32 devices in a mesh: section: 2 (over core), dp: 16 (over z, y, x).
Axes of the slice: x: 2, y: 2, z: 4, core: 2. Of those that a mesh axis runs over, the one named last changes fastest.
Arguments:
- tokens: bfloat16 [2, 10240, 768], P(None, 'dp'), may hold values from -6 to 6
- lengths: int32 [2, 16, 8], P(None, 'dp'), may hold values from 20 to 197, as said below
- route_mask: int32 [2, 10240], P(None, 'dp'), may hold values from 0 to 1, as said below
- router_weight: bfloat16 [768], replicated, may hold values from -0.21875 to 0.21875
- gains: float32 [2, 1536], P('section'), may hold values from 0.5 to 1.5
- biases: float32 [2, 7680], P('section'), may hold values from -2 to 2
- w_qkv: bfloat16 [2, 768, 2304], P('section'), may hold values from -0.21875 to 0.21875
- w_out: bfloat16 [2, 768, 768], P('section'), may hold values from -0.625 to 0.625
- w_up: bfloat16 [2, 768, 3072], P('section'), may hold values from -0.21875 to 0.21875
- w_down: bfloat16 [2, 3072, 768], P('section'), may hold values from -0.109375 to 0.109375
- cotangent: bfloat16 [2, 10240, 768], P(None, 'dp'), may hold values from -6 to 6
Outputs:
- activations: bfloat16 [2, 2, 10240, 768], P('section', None, 'dp')
- input_grads: bfloat16 [2, 2, 10240, 768], P('section', None, 'dp')
- grad_qkv: float32 [2, 768, 2304], P('section')
- grad_out: float32 [2, 768, 768], P('section')
- grad_up: float32 [2, 768, 3072], P('section')
- grad_down: float32 [2, 3072, 768], P('section')
- grad_gains: float32 [2, 1536], P('section')
- grad_biases: float32 [2, 7680], P('section')
- grad_router: float32 [768], replicated
- router_score_mean: float32 [2], replicated
The draws below stay inside these ranges and needn't reach their ends.
Inputs may be any that keep to these rules, and one draw needn't show every extreme that they name: In each device's block the 8 lengths sum to 640: two are 197, the other six form three pairs that each sum to 82, in a drawn order. `route_mask`: in every crop exactly half of the positions, rounded down, are 1.
All inputs are finite; a program needn't handle non-finite values.
Results may differ from the reference program's by a relative error of at most 0.015.
Values may be sent and summed in bfloat16 or wider, within the bound.
A program may use at most 256 MiB of HBM per device.

```python
from functools import partial
import jax
import jax.numpy as jnp
from jax import lax

D = 768
FF = 3072
HEADS = 12
HEAD = 64
GLOBAL = 197
PAIR = 82
CROPS = 8
MICRO = 2
ROWS = 640
TOKENS = 10240
BIAS_LEN = 7680
N_DP = 16


def crop_layout(key):
    blocks = MICRO * (TOKENS // ROWS)
    pair_key = jax.random.fold_in(key, 101)
    order_key = jax.random.fold_in(key, 202)
    lowest = PAIR // 4
    first_half = jax.random.randint(pair_key, (blocks, 3), lowest, PAIR - lowest + 1)
    crop_lengths = jnp.concatenate([jnp.full((blocks, 2), GLOBAL, jnp.int32), first_half.astype(jnp.int32), (PAIR - first_half).astype(jnp.int32)], axis=1)
    ranking = jax.random.randint(order_key, (blocks, CROPS), 0, 1024) * CROPS + jnp.arange(CROPS)[None, :]
    order = jnp.argsort(ranking, axis=1)
    return jnp.take_along_axis(crop_lengths, order, axis=1).astype(jnp.int32)


def draw_lengths(key, part):
    crop_lengths = crop_layout(key)
    return crop_lengths.reshape(MICRO, TOKENS // ROWS, CROPS)


def draw_route_mask(key, part):
    crop_lengths = crop_layout(key)
    key = jax.random.fold_in(key, 7)
    blocks = crop_lengths.shape[0]
    priority = jax.random.randint(key, (blocks, ROWS), 0, 2 ** 20) * ROWS + jnp.arange(ROWS)[None, :]
    positions = jnp.arange(ROWS, dtype=jnp.int32)

    def one_block(items):
        block_lengths, block_priority = items
        ends = jnp.cumsum(block_lengths)
        crops = jnp.sum((positions[:, None] >= ends[None, :-1]).astype(jnp.int32), axis=1)
        same_crop = crops[:, None] == crops[None, :]
        ranked = jnp.sum((same_crop & (block_priority[None, :] < block_priority[:, None])).astype(jnp.int32), axis=1)
        halves = block_lengths[crops] // 2
        return (ranked < halves).astype(jnp.int32)
    chosen = lax.map(one_block, (crop_lengths, priority))
    return chosen.reshape(MICRO, TOKENS).astype(jnp.int32)


def shard_levels(own_key, extent, cuts, low, top_value):
    loudness = 1.0
    for position, blocks in cuts:
        steps = jax.random.uniform(jax.random.fold_in(jax.random.fold_in(own_key, 6), position), (blocks,), jnp.float32, low / len(cuts), top_value / len(cuts))
        loudness = loudness * jnp.repeat(jnp.exp(steps), extent[position] // blocks).reshape((-1,) + (1,) * (len(extent) - 1 - position))
    return loudness


def gaussian(key, extent, width, reach, pieces=(), kind=jnp.bfloat16):
    level = shard_levels(key, extent, pieces, -0.22, 0.18) if pieces else 1.0
    drawn = jax.random.normal(key, extent, jnp.float32) * width * level
    return jnp.minimum(jnp.maximum(drawn, -reach), reach).astype(kind)


def setup_inputs(seed: int = 0) -> dict:
    key_of = jax.random.split(jax.random.key(seed), 12)
    return {
        "tokens": gaussian(key_of[0], (MICRO, TOKENS, D), 1.0, 6.0, ((1, 16),)),
        "lengths": draw_lengths(jax.random.fold_in(key_of[11], 71), 0),
        "route_mask": draw_route_mask(jax.random.fold_in(key_of[11], 71), 0),
        "router_weight": gaussian(key_of[3], (D,), D ** -0.5, 0.21875),
        "gains": jnp.clip(1.0 + 0.1 * jax.random.normal(key_of[4], (2, 2 * D), jnp.float32), 0.5, 1.5),
        "biases": gaussian(key_of[5], (2, BIAS_LEN), 0.3, 2.0, ((0, 2),), jnp.float32),
        "w_qkv": gaussian(key_of[6], (2, D, 3 * D), D ** -0.5, 0.21875, ((0, 2),)),
        "w_out": gaussian(key_of[7], (2, D, D), (D // 8) ** -0.5, 0.625, ((0, 2),)),
        "w_up": gaussian(key_of[8], (2, D, FF), D ** -0.5, 0.21875, ((0, 2),)),
        "w_down": gaussian(key_of[9], (2, FF, D), FF ** -0.5, 0.109375, ((0, 2),)),
        "cotangent": gaussian(key_of[10], (MICRO, TOKENS, D), 1.0, 6.0, ((1, 16),)),
    }


@jax.custom_vjp
def low(v):
    return lax.optimization_barrier(v.astype(jnp.bfloat16)).astype(jnp.float32)

@jax.custom_vjp
def low_back(v):
    return v

def low_keep(v):
    return (low(v), None)

def low_pass(kept, grad):
    return (grad,)

def back_keep(v):
    return (v, None)

def back_low(kept, grad):
    return (low(grad),)
low.defvjp(low_keep, low_pass)
low_back.defvjp(back_keep, back_low)
HIGH = lax.Precision.HIGHEST

def matmul(left, right):
    return jnp.dot(left, right, precision=HIGH)

def layer_norm(values, gain_row, bias_row):
    centred = values - lax.optimization_barrier(jnp.mean(values, axis=-1, keepdims=True))
    return centred * lax.rsqrt(lax.optimization_barrier(jnp.mean(centred * centred, axis=-1, keepdims=True)) + 1e-06) * gain_row + bias_row

def crop_ids(crop_lengths, row_count):
    ends = jnp.cumsum(crop_lengths)
    positions = jnp.arange(row_count, dtype=jnp.int32)
    return lax.optimization_barrier(jnp.sum((positions[:, None] >= ends[None, :-1]).astype(jnp.int32), axis=1))

def layer(inputs, gain_row, bias_row, w_qkv, w_out, w_up, w_down, allow, scale):
    row_count, model_width = inputs.shape
    hidden = w_up.shape[1]
    bias_q = bias_row[model_width:2 * model_width]
    bias_v = bias_row[2 * model_width:3 * model_width]
    normed = low(layer_norm(inputs, gain_row[:model_width], bias_row[:model_width]))
    joined = jnp.concatenate([bias_q, jnp.zeros_like(bias_q), bias_v])
    qkv = low(low_back(matmul(normed, w_qkv) + joined)).reshape(row_count, 3, HEADS, HEAD)
    queries, key_rows, value_rows = (qkv[:, 0], qkv[:, 1], qkv[:, 2])
    scores = jnp.einsum('qhd,khd->hqk', queries, key_rows, precision=HIGH) * 0.125
    scores = low_back(jnp.where(allow[None], scores, -1000000000.0))
    maximum = lax.optimization_barrier(jnp.max(scores, axis=-1, keepdims=True))
    exponent = jnp.exp(scores - maximum)
    probability = exponent / lax.optimization_barrier(jnp.sum(exponent, axis=-1, keepdims=True))
    mixture = jnp.einsum('hqk,khd->qhd', low(probability), value_rows, precision=HIGH).reshape(row_count, model_width)
    mixture = low(low_back(mixture))
    attended = low_back(matmul(mixture, w_out) + bias_row[3 * model_width:4 * model_width])
    between = inputs + attended
    second = low(layer_norm(between, gain_row[model_width:], bias_row[4 * model_width:5 * model_width]))
    pre_act = low_back(matmul(second, w_up) + bias_row[5 * model_width:5 * model_width + hidden])
    activated = low(jax.nn.gelu(pre_act, approximate=False))
    output_mlp = low_back(matmul(activated, w_down) + bias_row[5 * model_width + hidden:])
    return inputs + scale[:, None] * (attended + output_mlp)

def block(params, inputs, chosen_int, crop_lengths, probe):
    router, gains, biases, w_qkv, w_out, w_up, w_down = params
    row_count = inputs.shape[0]
    crops = crop_ids(crop_lengths, row_count)
    same_crop = crops[:, None] == crops[None, :]
    chosen = chosen_int == 1
    diagonal = jnp.arange(row_count)[:, None] == jnp.arange(row_count)[None, :]
    allow_one = same_crop & (chosen[:, None] & chosen[None, :] | diagonal)
    gate_value = jax.nn.sigmoid(matmul(inputs, router))
    scale_one = chosen.astype(jnp.float32) * gate_value
    first_out = layer(inputs, gains[0], biases[0], w_qkv[0], w_out[0], w_up[0], w_down[0], allow_one, scale_one)
    first_out = low(low_back(first_out))
    second_out = layer(first_out + probe, gains[1], biases[1], w_qkv[1], w_out[1], w_up[1], w_down[1], same_crop, jnp.ones((row_count,), jnp.float32))
    return ((first_out, second_out), jnp.sum(scale_one))

def reference(tokens, lengths, route_mask, router_weight, gains, biases, w_qkv, w_out, w_up, w_down, cotangent):
    blocks = MICRO * N_DP
    inputs = tokens.astype(jnp.float32).reshape(blocks, ROWS, D)
    chosen_all = route_mask.reshape(blocks, ROWS).astype(jnp.int32)
    lengths_all = lengths.reshape(blocks, CROPS).astype(jnp.int32)
    cot_all = cotangent.astype(jnp.float32).reshape(blocks, ROWS, D)
    params = (router_weight.astype(jnp.float32), gains.astype(jnp.float32), biases.astype(jnp.float32), w_qkv.astype(jnp.float32), w_out.astype(jnp.float32), w_up.astype(jnp.float32), w_down.astype(jnp.float32))
    probe = jnp.zeros_like(inputs)

    def total(params, inputs, probe):
        step_fn = jax.checkpoint(partial(block, params))

        def scan_step(carried, items):
            outputs, gate_total = step_fn(*items)
            return (carried, (outputs, gate_total))
        unused, (outputs, gate_totals) = lax.scan(scan_step, jnp.float32(0.0), (inputs, chosen_all, lengths_all, probe))
        return (outputs, gate_totals)
    outputs, pull_back, gate_totals = jax.vjp(total, params, inputs, probe, has_aux=True)
    first_out, second_out = outputs
    grads, grad_inputs, grad_probe = pull_back((jnp.zeros_like(first_out), cot_all))
    d_router, d_gains, d_biases, d_qkv, d_out, d_up, d_down = grads
    shape_out = (MICRO, TOKENS, D)
    activations = jnp.stack([first_out.reshape(shape_out), second_out.reshape(shape_out)]).astype(jnp.bfloat16)
    input_grads = jnp.stack([grad_inputs.reshape(shape_out), grad_probe.reshape(shape_out)]).astype(jnp.bfloat16)
    gate_sums = lax.optimization_barrier(jnp.sum(gate_totals.reshape(MICRO, N_DP), axis=1))
    counts = lax.optimization_barrier(jnp.sum(route_mask.astype(jnp.float32), axis=1))
    return (activations, input_grads, d_qkv, d_out, d_up, d_down, d_gains, d_biases, d_router, gate_sums / counts)
```

```python
import functools

import jax
import jax.numpy as jnp
from jax import lax
from jax.sharding import PartitionSpec as P

HEADS = 12
HEAD = 64
LONG = 197
F32 = jnp.float32
BF16 = jnp.bfloat16
NT = (((1,), (1,)), ((), ()))
TN = (((0,), (0,)), ((), ()))
NN = (((1,), (0,)), ((), ()))


def dot(left, right, dims=NN):
    return lax.dot_general(left, right, dims, preferred_element_type=F32)


def grid_axes(mesh):
    line = mesh.devices[0]
    count = len(line)
    try:
        spots = [tuple(device.coords) for device in line]
    except AttributeError:
        return [(count, 1)]
    axes = []
    for which in range(3):
        values = sorted({spot[which] for spot in spots})
        if len(values) > 1:
            stride = next(k for k in range(count) if spots[k][which] != spots[0][which])
            axes.append((len(values), stride))
    total = 1
    for size, _ in axes:
        total *= size
    good = total == count and all(
        spots[k][which] - spots[0][which] == (k // stride) % size
        for which, (size, stride) in zip(
            [w for w in range(3) if len({s[w] for s in spots}) > 1], axes
        )
        for k in range(count)
    )
    return sorted(axes) if good else [(count, 1)]


class Comm:
    def __init__(self, axes, count):
        self.axes, self.count = axes, count
        self.me = lax.axis_index("dp")

    def place(self, axis):
        size, stride = axis
        return lax.rem(self.me // stride, size)

    def pairs(self, axis, shift, keep):
        size, stride = axis
        found = []
        for k in range(self.count):
            at = (k // stride) % size
            if 0 <= at + shift < size and keep(at):
                found.append((k, k + shift * stride))
        return found

    def scatter(self, data, axis):
        size, _ = axis
        rows = data.shape[0] // size
        at = self.place(axis)

        def block(index):
            return lax.dynamic_slice_in_dim(data, index * rows, rows, 0)

        if size == 2:
            swap = self.pairs(axis, 1, lambda a: True) + self.pairs(axis, -1, lambda a: True)
            return block(at) + lax.ppermute(block(1 - at), "dp", swap)
        from_left = from_right = None
        for step in range(1, size):
            ahead = block(jnp.minimum(at + size - step, size - 1))
            behind = block(jnp.maximum(at - size + step, 0))
            if step > 1:
                ahead, behind = ahead + from_left, behind + from_right
            from_left = lax.ppermute(ahead, "dp", self.pairs(axis, 1, lambda a: a <= step - 1))
            from_right = lax.ppermute(behind, "dp", self.pairs(axis, -1, lambda a: a >= size - step))
        return block(at) + from_left + from_right

    def gather(self, data, axis):
        size, _ = axis
        rows = data.shape[0]
        at = self.place(axis)
        if size == 2:
            swap = self.pairs(axis, 1, lambda a: True) + self.pairs(axis, -1, lambda a: True)
            other = lax.ppermute(data, "dp", swap)
            low = jnp.where(at == 0, data, other)
            high = jnp.where(at == 0, other, data)
            return jnp.concatenate([low, high], axis=0)
        whole = jnp.zeros((size * rows, *data.shape[1:]), data.dtype)
        whole = lax.dynamic_update_slice_in_dim(whole, data, at * rows, 0)
        ahead = behind = data
        for step in range(1, size):
            ahead = lax.ppermute(ahead, "dp", self.pairs(axis, 1, lambda a: a >= step - 1))
            behind = lax.ppermute(behind, "dp", self.pairs(axis, -1, lambda a: a <= size - step))
            spot = jnp.where(at >= step, at - step, at)
            whole = lax.dynamic_update_slice_in_dim(whole, jnp.where(at >= step, ahead, data), spot * rows, 0)
            spot = jnp.where(at + step < size, at + step, at)
            whole = lax.dynamic_update_slice_in_dim(
                whole, jnp.where(at + step < size, behind, data), spot * rows, 0
            )
        return whole


def other_core(value):
    return lax.ppermute(value, "section", [(0, 1), (1, 0)])


def reduce_piece(comm, piece, order):
    section = lax.axis_index("section")
    half = piece.shape[0] // 2
    mine = lax.dynamic_slice_in_dim(piece, section * half, half, 0)
    theirs = lax.dynamic_slice_in_dim(piece, (1 - section) * half, half, 0)
    data = mine + other_core(theirs)
    for axis in order:
        data = comm.scatter(data, axis)
    return data


def gather_piece(comm, data, order):
    for axis in reversed(order):
        data = comm.gather(data, axis)
    return data


def layer_norm(values, gain_row, bias_row):
    centred = values - jnp.mean(values, axis=-1, keepdims=True)
    recip = lax.rsqrt(jnp.mean(centred * centred, axis=-1, keepdims=True) + 1e-06)
    normal = centred * recip
    return (normal * gain_row + bias_row, normal, recip)


def norm_back(grad_out, gain_row, normal, recip):
    grad_hat = grad_out * gain_row
    return recip * (
        grad_hat
        - jnp.mean(grad_hat, axis=-1, keepdims=True)
        - normal * jnp.mean(grad_hat * normal, axis=-1, keepdims=True)
    )


def bias_pieces(bias_row, width, hidden):
    cuts = [0, width, 2 * width, 3 * width, 4 * width, 5 * width, 5 * width + hidden, 6 * width + hidden]
    return [bias_row[cuts[k] : cuts[k + 1]] for k in range(7)]


def heads_of(block):
    return block.reshape(block.shape[0], HEADS, HEAD)


def layer_forward(inputs, scale, code, windows, weights):
    gain_row, bias_row, w_qkv, w_out, w_up, w_down = weights
    rows, width = inputs.shape
    b1, bq, bv, bo, b2, bu, bd = bias_pieces(bias_row, width, w_up.shape[1])
    g1, g2 = gain_row[:width], gain_row[width:]
    first, h1, r1 = layer_norm(inputs, g1, b1)
    n1 = first.astype(BF16)
    joined = jnp.concatenate([bq, jnp.zeros_like(bq), bv])
    qkv = (dot(n1, w_qkv) + joined).astype(BF16)
    probs, mixes = [], []
    for low, high in windows:
        part = qkv[low:high]
        q, k, v = (heads_of(part[:, c * width : (c + 1) * width]) for c in range(3))
        scores = jnp.einsum("qhd,khd->hqk", q, k, preferred_element_type=F32) * 0.125
        allow = code[low:high, None] == code[None, low:high]
        scores = jnp.where(allow[None], scores, -1e9)
        power = jnp.exp(scores - jnp.max(scores, axis=-1, keepdims=True))
        prob = power / jnp.sum(power, axis=-1, keepdims=True)
        mix = jnp.einsum("hqk,khd->qhd", prob.astype(BF16), v, preferred_element_type=F32)
        probs.append(prob)
        mixes.append(mix.reshape(high - low, width).astype(BF16))
    mix = jnp.concatenate(mixes, axis=0)
    attended = dot(mix, w_out) + bo
    between = inputs + attended
    second, h2, r2 = layer_norm(between, g2, b2)
    n2 = second.astype(BF16)
    pre = dot(n2, w_up) + bu
    half = 0.5 * (1.0 + lax.erf(pre * 0.7071067811865476))
    act = (pre * half).astype(BF16)
    slope = (half + pre * jnp.exp(-0.5 * pre * pre) * 0.3989422804014327).astype(F32)
    act, slope = lax.optimization_barrier((act, slope))
    mlp = dot(act, w_down) + bd
    delta = attended + mlp
    out = inputs + scale[:, None] * delta
    return out, delta, (n1, h1, r1, qkv, probs, mix, h2, r2, n2, slope, act)


def layer_back(dout, scale, windows, weights, kept):
    gain_row, bias_row, w_qkv, w_out, w_up, w_down = weights
    n1, h1, r1, qkv, probs, mix, h2, r2, n2, slope, act = kept
    rows, width = dout.shape
    g1, g2 = gain_row[:width], gain_row[width:]
    delta = dout * scale[:, None]
    dmlp = delta.astype(BF16)
    dbd = jnp.sum(dmlp.astype(F32), axis=0)
    grad_down = dot(act, dmlp, TN).astype(BF16)
    dpre = (dot(dmlp, w_down, NT) * slope).astype(BF16)
    dbu = jnp.sum(dpre.astype(F32), axis=0)
    grad_up = dot(n2, dpre, TN).astype(BF16)
    dn2 = dot(dpre, w_up, NT)
    dbetween = norm_back(dn2, g2, h2, r2)
    dg2, db2 = jnp.sum(dn2 * h2, axis=0), jnp.sum(dn2, axis=0)
    dattended = (delta + dbetween).astype(BF16)
    dbo = jnp.sum(dattended.astype(F32), axis=0)
    grad_out = dot(mix, dattended, TN).astype(BF16)
    dmix = dot(dattended, w_out, NT).astype(BF16)
    parts = []
    for (low, high), prob in zip(windows, probs):
        part = qkv[low:high]
        q, k, v = (heads_of(part[:, c * width : (c + 1) * width]) for c in range(3))
        dm = heads_of(dmix[low:high])
        dv = jnp.einsum("hqk,qhd->khd", prob.astype(BF16), dm, preferred_element_type=F32)
        dprob = jnp.einsum("qhd,khd->hqk", dm, v, preferred_element_type=F32)
        dscore = prob * (dprob - jnp.sum(prob * dprob, axis=-1, keepdims=True))
        dscore = dscore.astype(BF16)
        dq = jnp.einsum("hqk,khd->qhd", dscore, k, preferred_element_type=F32) * 0.125
        dk = jnp.einsum("hqk,qhd->khd", dscore, q, preferred_element_type=F32) * 0.125
        joined = jnp.concatenate([t.reshape(high - low, width) for t in (dq, dk, dv)], axis=1)
        parts.append(joined.astype(BF16))
    dqkv = jnp.concatenate(parts, axis=0)
    sums = jnp.sum(dqkv.astype(F32), axis=0)
    grad_qkv = dot(n1, dqkv, TN).astype(BF16)
    dn1 = dot(dqkv, w_qkv, NT)
    dg1, db1 = jnp.sum(dn1 * h1, axis=0), jnp.sum(dn1, axis=0)
    du = dout + dbetween + norm_back(dn1, g1, h1, r1)
    small = jnp.concatenate([dg1, dg2, db1, sums[:width], sums[2 * width :], dbo, db2, dbu, dbd])
    return du, (grad_qkv, grad_out, grad_up, grad_down), small


def row_plan(crop_lengths, chosen):
    rows = chosen.shape[0]
    ends = jnp.cumsum(crop_lengths)
    starts = ends - crop_lengths
    is_long = crop_lengths == LONG
    long_before = jnp.cumsum(is_long.astype(jnp.int32)) - is_long
    short = jnp.where(is_long, 0, crop_lengths)
    short_before = jnp.cumsum(short) - short
    base = jnp.where(is_long, long_before * LONG, 2 * LONG + short_before)
    at = jnp.arange(rows, dtype=jnp.int32)
    inside = (at[:, None] >= starts[None]) & (at[:, None] < ends[None])
    target = at + jnp.sum(jnp.where(inside, (base - starts)[None], 0), axis=1)
    order = target[None, :] == at[:, None]
    code = jnp.sum((at[:, None] >= base[None]).astype(jnp.int32), axis=1)
    chosen_in = jnp.sum(jnp.where(order, chosen[None, :], 0), axis=1)
    rank = jnp.sum(jnp.where(at[:, None] > at[None, :], chosen_in[None, :], 0), axis=1)
    slot = jnp.arange(rows // 2, dtype=jnp.int32)
    pick = (rank[None, :] == slot[:, None]) & (chosen_in[None, :] == 1)
    routed_code = jnp.sum(jnp.where(pick, code[None, :], 0), axis=1)
    return order.astype(BF16), pick.astype(BF16), code, routed_code, chosen_in


def body(axes, tokens, lengths, route_mask, router_weight, gains, biases, w_qkv, w_out, w_up, w_down, cotangent):
    section = lax.axis_index("section")
    count = lax.axis_size("dp")
    comm = Comm(axes, count)
    micro, rows, width = tokens.shape
    own = (gains[0], biases[0], w_qkv[0], w_out[0], w_up[0], w_down[0])
    far = tuple(other_core(value) for value in own)
    weights = [
        tuple(jnp.where(section == layer, mine, theirs) for mine, theirs in zip(own, far))
        for layer in range(2)
    ]
    router_f = router_weight.astype(F32)

    def pick_micro(array):
        return lax.dynamic_index_in_dim(array, section, 0, False)

    crop_lengths, chosen = pick_micro(lengths)[0], pick_micro(route_mask)
    order, pick, code, routed_code, chosen_in = row_plan(crop_lengths, chosen)
    is_routed = (chosen_in == 1)[:, None]
    x = dot(order, pick_micro(tokens)).astype(BF16)
    cot = dot(order, pick_micro(cotangent)).astype(BF16)
    routed = dot(pick, x).astype(BF16)
    inputs_one = routed.astype(F32)
    held = (routed_code > 0).astype(F32)
    gate = jax.nn.sigmoid(jnp.sum(inputs_one * router_f[None, :], axis=1))
    scale_one = held * gate
    windows_one = [(0, rows // 2)]
    windows_two = [(0, LONG), (LONG, 2 * LONG), (2 * LONG, rows)]

    out_one, delta_one, kept_one = layer_forward(inputs_one, scale_one, routed_code, windows_one, weights[0])
    y1 = jnp.where(is_routed, dot(pick, out_one.astype(BF16), TN).astype(BF16), x)
    ones = jnp.ones((rows,), F32)
    out_two, _, kept_two = layer_forward(y1.astype(F32), ones, code, windows_two, weights[1])
    y2 = out_two.astype(BF16)
    du_two, grads_two, small_two = layer_back(cot.astype(F32), ones, windows_two, weights[1], kept_two)
    dout = du_two.astype(BF16)
    dout_one = dot(pick, dout).astype(BF16).astype(F32)
    du_one, grads_one, small_one = layer_back(dout_one, scale_one, windows_one, weights[0], kept_one)
    slope = jnp.sum(dout_one * delta_one, axis=1) * held * gate * (1.0 - gate)
    du_one = (du_one + slope[:, None] * router_f[None, :]).astype(BF16)
    grad_router = jnp.sum(slope[:, None] * inputs_one, axis=0)
    du_one = jnp.where(is_routed, dot(pick, du_one, TN).astype(BF16), dout)

    def unsort(value):
        return dot(order, value, TN).astype(BF16)

    def spread(first, second):
        mine = jnp.where(section == 0, first, second)
        theirs = other_core(jnp.where(section == 0, second, first))
        return jnp.where(section == 0, jnp.stack([mine, theirs]), jnp.stack([theirs, mine]))

    activations = spread(unsort(y1), unsort(y2))
    input_grads = spread(unsort(du_one), unsort(dout))

    micro_ids = jnp.arange(micro)
    here = (micro_ids == section).astype(F32)
    counts = jnp.where(section == 0, jnp.sum(route_mask.astype(F32), axis=1), 0.0)
    small = jnp.concatenate([small_one, small_two, grad_router, here * jnp.sum(scale_one), counts])
    small = lax.psum(small, ("section", "dp"))
    span = small_one.shape[0]
    small_mine = jnp.where(section == 0, small[:span], small[span : 2 * span])
    tail = small[2 * span :]

    def order_of(ids):
        return [axes[k] for k in ids if k < len(axes)]

    plan = {
        (1, 3): (0, 2, 1),
        (1, 2): (1, 2, 0),
        (1, 1): (1, 0, 2),
        (1, 0): (0, 1, 2),
        (0, 3): (1, 2, 0),
        (0, 2): (0, 2, 1),
        (0, 1): (0, 1, 2),
        (0, 0): (1, 0, 2),
    }
    whole = {}
    for (layer, which), ids in plan.items():
        piece = (grads_one, grads_two)[layer][which]
        chosen_order = order_of(ids)
        part = reduce_piece(comm, piece, chosen_order)
        part = gather_piece(comm, part, chosen_order)
        far_part = lax.ppermute(part, "section", [(1 - layer, layer)])
        low = jnp.where(section == 0, part, far_part)
        high = jnp.where(section == 0, far_part, part)
        whole[layer, which] = (low, high)

    def final(which):
        low = jnp.where(section == 0, whole[0, which][0], whole[1, which][0])
        high = jnp.where(section == 0, whole[0, which][1], whole[1, which][1])
        return jnp.concatenate([low, high], axis=0).astype(F32)[None]

    return (
        activations[None],
        input_grads[None],
        final(0),
        final(1),
        final(2),
        final(3),
        small_mine[: 2 * width][None],
        small_mine[2 * width :][None],
        tail[:width],
        tail[width : width + micro] / tail[width + micro :],
    )


def solution(mesh):
    in_specs = (
        P(None, "dp", None),
        P(None, "dp", None),
        P(None, "dp"),
        P(),
        P("section", None),
        P("section", None),
        P("section", None, None),
        P("section", None, None),
        P("section", None, None),
        P("section", None, None),
        P(None, "dp", None),
    )
    out_specs = (
        P("section", None, "dp", None),
        P("section", None, "dp", None),
        P("section", None, None),
        P("section", None, None),
        P("section", None, None),
        P("section", None, None),
        P("section", None),
        P("section", None),
        P(),
        P(),
    )
    step = functools.partial(body, grid_axes(mesh))
    return jax.shard_map(step, mesh=mesh, in_specs=in_specs, out_specs=out_specs, check_vma=False)
```

```python
import functools

import jax
import jax.numpy as jnp
from jax import lax
from jax.experimental import pallas as pl
from jax.experimental.pallas import tpu as pltpu
from jax.sharding import PartitionSpec as P

HEADS = 12
HEAD = 64
LONG = 197
F32 = jnp.float32
BF16 = jnp.bfloat16
NT = (((1,), (1,)), ((), ()))
TN = (((0,), (0,)), ((), ()))
NN = (((1,), (0,)), ((), ()))


def dot(left, right, dims=NN):
    return lax.dot_general(left, right, dims, preferred_element_type=F32)


LANES = 768
TILE = 16


def axis_bits(mesh):
    line = mesh.devices[0]
    bits = len(line).bit_length() - 1
    try:
        spots = [tuple(device.coords) for device in line]
    except AttributeError:
        return [0] * bits
    return [
        next((w for w in range(3) if spots[1 << b][w] != spots[0][w]), 0) for b in range(bits)
    ]


def bit_orders(axis_of):
    groups = {}
    for bit, axis in enumerate(axis_of):
        groups.setdefault(axis, []).append(bit)
    lists = sorted(groups.values(), key=len)
    if len(lists) < 3:
        return [sum(lists, []), sum(lists, [])]
    one, two, three = lists[:3]
    return [
        one + three + two,
        two + three + one,
        one + three + two,
        two + three + one,
        one + two + three,
        two + one + three,
    ]


def block_of(refs, index):
    w_qkv, w_out, w_up, w_down = refs
    if index < 4:
        return w_down.at[pl.ds(index * LANES, LANES), :]
    if index < 8:
        return w_up.at[:, pl.ds((index - 4) * LANES, LANES)]
    if index < 9:
        return w_out
    return w_qkv.at[:, pl.ds((index - 9) * LANES, LANES)]


def add_rows(into, source, start, other, other_start, count):
    tile = next(t for t in (96, 64, 48, 32, 16) if count % t == 0)

    def step(k, carry):
        here = pl.ds(pl.multiple_of(start + k * tile, TILE), tile)
        there = pl.ds(pl.multiple_of(other_start + k * tile, TILE), tile)
        into[here, :] = source[here, :] + other[there, :]
        return carry

    lax.fori_loop(0, count // tile, step, 0)


def sum_kernel(orders, chunk, chunks, *refs):
    grads = (refs[0:4], refs[4:8])
    small_in = refs[8]
    outs, small_out = refs[9:13], refs[13]
    acc, mate, *rest = refs[14:]
    bits = len(orders[0])
    got, small_got = rest[:bits], rest[bits]
    load_sem, mate_send, mate_recv, out_sem, send, recv, back_send, back_recv, small_send, small_recv = rest[bits + 1 :]
    blocks = 12
    core = lax.axis_index("section")
    me = lax.axis_index("dp")

    def bit_at(bit):
        return lax.rem(me // (1 << bit), 2)

    def partner(bit):
        return (core, me + (1 - 2 * bit_at(bit)) * (1 << bit))

    across = (1 - core, me)
    friends = [across] + [partner(bit) for bit in range(bits)]
    barrier = pltpu.get_barrier_semaphore()
    for friend in friends:
        pl.semaphore_signal(barrier, inc=1, device_id=friend, device_id_type=pl.DeviceIdType.MESH)
    pl.semaphore_wait(barrier, len(friends))

    def remote(source, target, one, two, friend):
        return pltpu.make_async_remote_copy(
            src_ref=source,
            dst_ref=target,
            send_sem=one,
            recv_sem=two,
            device_id=friend,
            device_id_type=pl.DeviceIdType.MESH,
        )

    def small_step(k):
        friend = across if k == 0 else partner(k - 1)
        return remote(small_out, small_got.at[k], small_send.at[k], small_recv.at[k], friend)

    def small_first(layer):
        return remote(small_in.at[1 - layer], small_got.at[0], small_send.at[0], small_recv.at[0], across)

    def rows_of(index):
        return pl.ds(index * LANES, LANES)

    def load(layer, index):
        return pltpu.make_async_copy(block_of(grads[layer], index), acc.at[rows_of(index), :], load_sem.at[index])

    def swap(layer, index):
        return remote(
            block_of(grads[1 - layer], index),
            mate.at[rows_of(index), :],
            mate_send.at[index],
            mate_recv.at[index],
            across,
        )

    def begin(index):
        for layer in range(2):

            @pl.when(core == layer)
            def _():
                swap(layer, index).start()
                load(layer, index).start()

    def needed(upto):
        return min(blocks, -(-upto // LANES))

    for layer in range(2):

        @pl.when(core == layer)
        def _():
            small_out[...] = small_in[layer]
            small_first(layer).start()

    if chunk * chunks > blocks * LANES:
        acc[blocks * LANES :, :] = jnp.zeros((chunk * chunks - blocks * LANES, LANES), BF16)

    begun, joined = 0, 0

    def span(k, depth):
        start = k * chunk
        size = chunk
        for bit in orders[k % len(orders)][:depth]:
            size //= 2
            start = start + bit_at(bit) * size
        return start, size

    def down(k, depth):
        bit = orders[k % len(orders)][depth]
        start, size = span(k, depth)
        size //= 2
        away = pl.multiple_of(start + (1 - bit_at(bit)) * size, TILE)
        return remote(
            acc.at[pl.ds(away, size), :],
            got[depth].at[pl.ds(k * size, size), :],
            send.at[k, depth],
            recv.at[k, depth],
            partner(bit),
        )

    def up(k, depth):
        bit = orders[k % len(orders)][depth]
        start, size = span(k, depth + 1)
        here = mate.at[pl.ds(pl.multiple_of(start, TILE), size), :]
        return remote(here, here, back_send.at[k, depth], back_recv.at[k, depth], partner(bit))

    def put(index):
        out = block_of(outs, index)
        return pltpu.make_async_copy(mate.at[rows_of(index), :], out, out_sem.at[index])

    stages = 2 * bits + 1
    pairs = -(-chunks // 2)
    finished, small_done = 0, 0
    for moment in range(pairs + stages - 1):
        ahead = needed(min(chunks, 2 * (moment + 2)) * chunk)
        for index in range(begun, ahead):
            begin(index)
        begun = max(begun, ahead)
        for stage in [0] + list(range(stages - 1, 0, -1)):
            pair = moment - stage
            if not 0 <= pair < pairs:
                continue
            for k in range(2 * pair, min(2 * pair + 2, chunks)):
                if stage == 0:
                    for index in range(joined, needed((k + 1) * chunk)):
                        swap(0, index).wait_recv()
                        load(0, index).wait()
                        add_rows(acc, acc, index * LANES, mate, index * LANES, LANES)
                    joined = max(joined, needed((k + 1) * chunk))
                    down(k, 0).start()
                elif stage <= bits:
                    depth = stage - 1
                    down(k, depth).wait_recv()
                    start, size = span(k, stage)
                    add_rows(acc if stage < bits else mate, acc, start, got[depth], k * size, size)
                    if stage < bits:
                        down(k, stage).start()
                    else:
                        up(k, bits - 1).start()
                else:
                    depth = 2 * bits - stage
                    up(k, depth).wait_recv()
                    if depth > 0:
                        up(k, depth - 1).start()
                    else:
                        ready = blocks if k == chunks - 1 else (k + 1) * chunk // LANES
                        for index in range(finished, ready):
                            put(index).start()
                        finished = ready
        if small_done <= bits:
            small_step(small_done).wait()
            small_out[...] = small_out[...] + small_got[small_done]
            small_done += 1
            if small_done <= bits:
                small_step(small_done).start()

    for index in range(blocks):
        swap(0, index).wait_send()
        put(index).wait()
    for k in range(chunks):
        for depth in range(bits):
            down(k, depth).wait_send()
            up(k, depth).wait_send()


def sum_gradients(axis_of, first, second, small):
    bits = len(axis_of)
    orders = bit_orders(axis_of)
    unit = TILE << bits
    chunk = LANES if LANES % unit == 0 else unit
    chunks = -(-12 * LANES // chunk)
    scratch = [
        pltpu.VMEM((chunks * chunk, LANES), BF16),
        pltpu.VMEM((chunks * chunk, LANES), BF16),
    ]
    scratch += [pltpu.VMEM((chunks * chunk >> (depth + 1), LANES), BF16) for depth in range(bits)]
    scratch += [pltpu.VMEM((bits + 1, *small.shape[1:]), F32)]
    scratch += [pltpu.SemaphoreType.DMA((12,))] * 4
    scratch += [pltpu.SemaphoreType.DMA((chunks, bits))] * 4
    scratch += [pltpu.SemaphoreType.DMA((bits + 1,))] * 2
    shapes = [jax.ShapeDtypeStruct(value.shape, BF16) for value in first]
    anywhere = pl.BlockSpec(memory_space=pl.ANY)
    inside = pl.BlockSpec(memory_space=pltpu.VMEM)
    *sums, small_sum = pl.pallas_call(
        functools.partial(sum_kernel, orders, chunk, chunks),
        out_shape=shapes + [jax.ShapeDtypeStruct(small.shape[1:], F32)],
        in_specs=[anywhere] * 8 + [inside],
        out_specs=[anywhere] * 4 + [inside],
        scratch_shapes=scratch,
        compiler_params=pltpu.CompilerParams(
            collective_id=0, has_side_effects=True, vmem_limit_bytes=60 * 1024 * 1024
        ),
        cost_estimate=pl.CostEstimate(flops=10**8, bytes_accessed=6 * 10**8, transcendentals=0),
        name="sum_gradients",
    )(*first, *second, small)
    return sums, small_sum


def other_core(value):
    return lax.ppermute(value, "section", [(0, 1), (1, 0)])


def layer_norm(values, gain_row, bias_row):
    centred = values - jnp.mean(values, axis=-1, keepdims=True)
    recip = lax.rsqrt(jnp.mean(centred * centred, axis=-1, keepdims=True) + 1e-06)
    normal = centred * recip
    return (normal * gain_row + bias_row, normal, recip)


def norm_back(grad_out, gain_row, normal, recip):
    grad_hat = grad_out * gain_row
    return recip * (
        grad_hat
        - jnp.mean(grad_hat, axis=-1, keepdims=True)
        - normal * jnp.mean(grad_hat * normal, axis=-1, keepdims=True)
    )


def bias_pieces(bias_row, width, hidden):
    cuts = [0, width, 2 * width, 3 * width, 4 * width, 5 * width, 5 * width + hidden, 6 * width + hidden]
    return [bias_row[cuts[k] : cuts[k + 1]] for k in range(7)]


def heads_of(block):
    return block.reshape(block.shape[0], HEADS, HEAD)


def layer_forward(inputs, scale, code, windows, weights):
    gain_row, bias_row, w_qkv, w_out, w_up, w_down = weights
    rows, width = inputs.shape
    b1, bq, bv, bo, b2, bu, bd = bias_pieces(bias_row, width, w_up.shape[1])
    g1, g2 = gain_row[:width], gain_row[width:]
    first, h1, r1 = layer_norm(inputs, g1, b1)
    n1 = first.astype(BF16)
    joined = jnp.concatenate([bq, jnp.zeros_like(bq), bv])
    qkv = (dot(n1, w_qkv) + joined).astype(BF16)
    probs, mixes = [], []
    for low, high in windows:
        part = qkv[low:high]
        q, k, v = (heads_of(part[:, c * width : (c + 1) * width]) for c in range(3))
        scores = jnp.einsum("qhd,khd->hqk", q, k, preferred_element_type=F32) * 0.125
        allow = code[low:high, None] == code[None, low:high]
        scores = jnp.where(allow[None], scores, -1e9)
        power = jnp.exp(scores - jnp.max(scores, axis=-1, keepdims=True))
        prob = power / jnp.sum(power, axis=-1, keepdims=True)
        mix = jnp.einsum("hqk,khd->qhd", prob.astype(BF16), v, preferred_element_type=F32)
        probs.append(prob)
        mixes.append(mix.reshape(high - low, width).astype(BF16))
    mix = jnp.concatenate(mixes, axis=0)
    attended = dot(mix, w_out) + bo
    between = inputs + attended
    second, h2, r2 = layer_norm(between, g2, b2)
    n2 = second.astype(BF16)
    pre = dot(n2, w_up) + bu
    half = 0.5 * (1.0 + lax.erf(pre * 0.7071067811865476))
    act = (pre * half).astype(BF16)
    slope = (half + pre * jnp.exp(-0.5 * pre * pre) * 0.3989422804014327).astype(F32)
    act, slope = lax.optimization_barrier((act, slope))
    mlp = dot(act, w_down) + bd
    delta = attended + mlp
    out = inputs + scale[:, None] * delta
    return out, delta, (n1, h1, r1, qkv, probs, mix, h2, r2, n2, slope, act)


def layer_back(dout, scale, windows, weights, kept):
    gain_row, bias_row, w_qkv, w_out, w_up, w_down = weights
    n1, h1, r1, qkv, probs, mix, h2, r2, n2, slope, act = kept
    rows, width = dout.shape
    g1, g2 = gain_row[:width], gain_row[width:]
    delta = dout * scale[:, None]
    dmlp = delta.astype(BF16)
    dbd = jnp.sum(dmlp.astype(F32), axis=0)
    grad_down = dot(act, dmlp, TN).astype(BF16)
    dpre = (dot(dmlp, w_down, NT) * slope).astype(BF16)
    dbu = jnp.sum(dpre.astype(F32), axis=0)
    grad_up = dot(n2, dpre, TN).astype(BF16)
    dn2 = dot(dpre, w_up, NT)
    dbetween = norm_back(dn2, g2, h2, r2)
    dg2, db2 = jnp.sum(dn2 * h2, axis=0), jnp.sum(dn2, axis=0)
    dattended = (delta + dbetween).astype(BF16)
    dbo = jnp.sum(dattended.astype(F32), axis=0)
    grad_out = dot(mix, dattended, TN).astype(BF16)
    dmix = dot(dattended, w_out, NT).astype(BF16)
    parts = []
    for (low, high), prob in zip(windows, probs):
        part = qkv[low:high]
        q, k, v = (heads_of(part[:, c * width : (c + 1) * width]) for c in range(3))
        dm = heads_of(dmix[low:high])
        dv = jnp.einsum("hqk,qhd->khd", prob.astype(BF16), dm, preferred_element_type=F32)
        dprob = jnp.einsum("qhd,khd->hqk", dm, v, preferred_element_type=F32)
        dscore = prob * (dprob - jnp.sum(prob * dprob, axis=-1, keepdims=True))
        dscore = dscore.astype(BF16)
        dq = jnp.einsum("hqk,khd->qhd", dscore, k, preferred_element_type=F32) * 0.125
        dk = jnp.einsum("hqk,qhd->khd", dscore, q, preferred_element_type=F32) * 0.125
        joined = jnp.concatenate([t.reshape(high - low, width) for t in (dq, dk, dv)], axis=1)
        parts.append(joined.astype(BF16))
    dqkv = jnp.concatenate(parts, axis=0)
    sums = jnp.sum(dqkv.astype(F32), axis=0)
    grad_qkv = dot(n1, dqkv, TN).astype(BF16)
    dn1 = dot(dqkv, w_qkv, NT)
    dg1, db1 = jnp.sum(dn1 * h1, axis=0), jnp.sum(dn1, axis=0)
    du = dout + dbetween + norm_back(dn1, g1, h1, r1)
    small = jnp.concatenate([dg1, dg2, db1, sums[:width], sums[2 * width :], dbo, db2, dbu, dbd])
    return du, (grad_qkv, grad_out, grad_up, grad_down), small


def row_plan(crop_lengths, chosen):
    rows = chosen.shape[0]
    ends = jnp.cumsum(crop_lengths)
    starts = ends - crop_lengths
    is_long = crop_lengths == LONG
    long_before = jnp.cumsum(is_long.astype(jnp.int32)) - is_long
    short = jnp.where(is_long, 0, crop_lengths)
    short_before = jnp.cumsum(short) - short
    base = jnp.where(is_long, long_before * LONG, 2 * LONG + short_before)
    at = jnp.arange(rows, dtype=jnp.int32)
    inside = (at[:, None] >= starts[None]) & (at[:, None] < ends[None])
    target = at + jnp.sum(jnp.where(inside, (base - starts)[None], 0), axis=1)
    order = target[None, :] == at[:, None]
    code = jnp.sum((at[:, None] >= base[None]).astype(jnp.int32), axis=1)
    chosen_in = jnp.sum(jnp.where(order, chosen[None, :], 0), axis=1)
    rank = jnp.sum(jnp.where(at[:, None] > at[None, :], chosen_in[None, :], 0), axis=1)
    slot = jnp.arange(rows // 2, dtype=jnp.int32)
    pick = (rank[None, :] == slot[:, None]) & (chosen_in[None, :] == 1)
    routed_code = jnp.sum(jnp.where(pick, code[None, :], 0), axis=1)
    return order.astype(BF16), pick.astype(BF16), code, routed_code, chosen_in


def body(axis_of, tokens, lengths, route_mask, router_weight, gains, biases, w_qkv, w_out, w_up, w_down, cotangent):
    section = lax.axis_index("section")
    micro, rows, width = tokens.shape
    own = (gains[0], biases[0], w_qkv[0], w_out[0], w_up[0], w_down[0])
    far = tuple(other_core(value) for value in own)
    weights = [
        tuple(jnp.where(section == layer, mine, theirs) for mine, theirs in zip(own, far))
        for layer in range(2)
    ]
    router_f = router_weight.astype(F32)

    def pick_micro(array):
        return lax.dynamic_index_in_dim(array, section, 0, False)

    crop_lengths, chosen = pick_micro(lengths)[0], pick_micro(route_mask)
    order, pick, code, routed_code, chosen_in = row_plan(crop_lengths, chosen)
    is_routed = (chosen_in == 1)[:, None]
    x = dot(order, pick_micro(tokens)).astype(BF16)
    cot = dot(order, pick_micro(cotangent)).astype(BF16)
    routed = dot(pick, x).astype(BF16)
    inputs_one = routed.astype(F32)
    held = (routed_code > 0).astype(F32)
    gate = jax.nn.sigmoid(jnp.sum(inputs_one * router_f[None, :], axis=1))
    scale_one = held * gate
    windows_one = [(0, rows // 2)]
    windows_two = [(0, LONG), (LONG, 2 * LONG), (2 * LONG, rows)]

    out_one, delta_one, kept_one = layer_forward(inputs_one, scale_one, routed_code, windows_one, weights[0])
    y1 = jnp.where(is_routed, dot(pick, out_one.astype(BF16), TN).astype(BF16), x)
    ones = jnp.ones((rows,), F32)
    out_two, _, kept_two = layer_forward(y1.astype(F32), ones, code, windows_two, weights[1])
    y2 = out_two.astype(BF16)
    du_two, grads_two, small_two = layer_back(cot.astype(F32), ones, windows_two, weights[1], kept_two)
    dout = du_two.astype(BF16)
    dout_one = dot(pick, dout).astype(BF16).astype(F32)
    du_one, grads_one, small_one = layer_back(dout_one, scale_one, windows_one, weights[0], kept_one)
    slope = jnp.sum(dout_one * delta_one, axis=1) * held * gate * (1.0 - gate)
    du_one = (du_one + slope[:, None] * router_f[None, :]).astype(BF16)
    grad_router = jnp.sum(slope[:, None] * inputs_one, axis=0)
    du_one = jnp.where(is_routed, dot(pick, du_one, TN).astype(BF16), dout)

    def unsort(value):
        return dot(order, value, TN).astype(BF16)

    def spread(first, second):
        mine = jnp.where(section == 0, first, second)
        theirs = other_core(jnp.where(section == 0, second, first))
        return jnp.where(section == 0, jnp.stack([mine, theirs]), jnp.stack([theirs, mine]))

    activations = spread(unsort(y1), unsort(y2))
    input_grads = spread(unsort(du_one), unsort(dout))

    micro_ids = jnp.arange(micro)
    here = (micro_ids == section).astype(F32)
    counts = here * jnp.sum(route_mask.astype(F32), axis=1)
    extra = jnp.concatenate([here * jnp.sum(scale_one), counts])
    shared = [grad_router, extra]
    small = jnp.stack([jnp.concatenate([part, *shared]) for part in (small_one, small_two)])
    room = -(-small.shape[1] // (8 * LANES)) * 8 * LANES
    small = jnp.pad(small, ((0, 0), (0, room - small.shape[1]))).reshape(2, room // LANES, LANES)
    sums, small = sum_gradients(axis_of, grads_one, grads_two, small)
    small = small.reshape(-1)
    span = small_one.shape[0]
    tail = small[span:]

    return (
        activations[None],
        input_grads[None],
        *(value.astype(F32)[None] for value in sums),
        small[: 2 * width][None],
        small[2 * width : span][None],
        tail[:width],
        tail[width : width + micro] / tail[width + micro : width + 2 * micro],
    )


def solution(mesh):
    in_specs = (
        P(None, "dp", None),
        P(None, "dp", None),
        P(None, "dp"),
        P(),
        P("section", None),
        P("section", None),
        P("section", None, None),
        P("section", None, None),
        P("section", None, None),
        P("section", None, None),
        P(None, "dp", None),
    )
    out_specs = (
        P("section", None, "dp", None),
        P("section", None, "dp", None),
        P("section", None, None),
        P("section", None, None),
        P("section", None, None),
        P("section", None, None),
        P("section", None),
        P("section", None),
        P(),
        P(),
    )
    step = functools.partial(body, axis_bits(mesh))
    return jax.shard_map(step, mesh=mesh, in_specs=in_specs, out_specs=out_specs, check_vma=False)
```

```python
import functools

import jax
import jax.numpy as jnp
from jax import lax
from jax.experimental import pallas as pl
from jax.experimental.pallas import tpu as pltpu
from jax.sharding import PartitionSpec as P

HEADS = 12
HEAD = 64
LONG = 197
F32 = jnp.float32
BF16 = jnp.bfloat16
NT = (((1,), (1,)), ((), ()))
TN = (((0,), (0,)), ((), ()))
NN = (((1,), (0,)), ((), ()))


LANES = 768
TILE = 16


def axis_bits(mesh):
    line = mesh.devices[0]
    bits = len(line).bit_length() - 1
    try:
        spots = [tuple(device.coords) for device in line]
    except AttributeError:
        return [0] * bits
    return [
        next((w for w in range(3) if spots[1 << b][w] != spots[0][w]), 0) for b in range(bits)
    ]


def bit_orders(axis_of):
    groups = {}
    for bit, axis in enumerate(axis_of):
        groups.setdefault(axis, []).append(bit)
    lists = sorted(groups.values(), key=len)
    if len(lists) < 3:
        return [sum(lists, []), sum(lists, [])]
    one, two, three = lists[:3]
    return [
        one + three + two,
        two + three + one,
        one + three + two,
        two + three + one,
        one + two + three,
        two + one + three,
    ]


def block_of(refs, index):
    w_qkv, w_out, w_up, w_down = refs
    if index < 4:
        return w_down.at[pl.ds(index * LANES, LANES), :]
    if index < 8:
        return w_up.at[:, pl.ds((index - 4) * LANES, LANES)]
    if index < 9:
        return w_out
    return w_qkv.at[:, pl.ds((index - 9) * LANES, LANES)]


def add_rows(into, source, start, other, other_start, count):
    tile = next(t for t in (96, 64, 48, 32, 16) if count % t == 0)

    def step(k, carry):
        here = pl.ds(pl.multiple_of(start + k * tile, TILE), tile)
        there = pl.ds(pl.multiple_of(other_start + k * tile, TILE), tile)
        into[here, :] = source[here, :] + other[there, :]
        return carry

    lax.fori_loop(0, count // tile, step, 0)


def sum_kernel(orders, chunk, chunks, *refs):
    grads = (refs[0:4], refs[4:8])
    small_in = refs[8]
    outs, small_out = refs[9:13], refs[13]
    acc, mate, *rest = refs[14:]
    bits = len(orders[0])
    got, small_got = rest[:bits], rest[bits]
    load_sem, mate_send, mate_recv, out_sem, send, recv, back_send, back_recv, small_send, small_recv = rest[bits + 1 :]
    blocks = 12
    core = lax.axis_index("section")
    me = lax.axis_index("dp")

    def bit_at(bit):
        return lax.rem(me // (1 << bit), 2)

    def partner(bit):
        return (core, me + (1 - 2 * bit_at(bit)) * (1 << bit))

    across = (1 - core, me)
    friends = [across] + [partner(bit) for bit in range(bits)]
    barrier = pltpu.get_barrier_semaphore()
    for friend in friends:
        pl.semaphore_signal(barrier, inc=1, device_id=friend, device_id_type=pl.DeviceIdType.MESH)
    pl.semaphore_wait(barrier, len(friends))

    def remote(source, target, one, two, friend):
        return pltpu.make_async_remote_copy(
            src_ref=source,
            dst_ref=target,
            send_sem=one,
            recv_sem=two,
            device_id=friend,
            device_id_type=pl.DeviceIdType.MESH,
        )

    def small_step(k):
        friend = across if k == 0 else partner(k - 1)
        return remote(small_out, small_got.at[k], small_send.at[k], small_recv.at[k], friend)

    def small_first(layer):
        return remote(small_in.at[1 - layer], small_got.at[0], small_send.at[0], small_recv.at[0], across)

    def rows_of(index):
        return pl.ds(index * LANES, LANES)

    def load(layer, index):
        return pltpu.make_async_copy(block_of(grads[layer], index), acc.at[rows_of(index), :], load_sem.at[index])

    def swap(layer, index):
        return remote(
            block_of(grads[1 - layer], index),
            mate.at[rows_of(index), :],
            mate_send.at[index],
            mate_recv.at[index],
            across,
        )

    def begin(index):
        for layer in range(2):

            @pl.when(core == layer)
            def _():
                swap(layer, index).start()
                load(layer, index).start()

    def needed(upto):
        return min(blocks, -(-upto // LANES))

    for layer in range(2):

        @pl.when(core == layer)
        def _():
            small_out[...] = small_in[layer]
            small_first(layer).start()

    if chunk * chunks > blocks * LANES:
        acc[blocks * LANES :, :] = jnp.zeros((chunk * chunks - blocks * LANES, LANES), BF16)

    begun, joined = 0, 0

    def span(k, depth):
        start = k * chunk
        size = chunk
        for bit in orders[k % len(orders)][:depth]:
            size //= 2
            start = start + bit_at(bit) * size
        return start, size

    def down(k, depth):
        bit = orders[k % len(orders)][depth]
        start, size = span(k, depth)
        size //= 2
        away = pl.multiple_of(start + (1 - bit_at(bit)) * size, TILE)
        return remote(
            acc.at[pl.ds(away, size), :],
            got[depth].at[pl.ds(k * size, size), :],
            send.at[k, depth],
            recv.at[k, depth],
            partner(bit),
        )

    def up(k, depth):
        bit = orders[k % len(orders)][depth]
        start, size = span(k, depth + 1)
        here = mate.at[pl.ds(pl.multiple_of(start, TILE), size), :]
        return remote(here, here, back_send.at[k, depth], back_recv.at[k, depth], partner(bit))

    def put(index):
        out = block_of(outs, index)
        return pltpu.make_async_copy(mate.at[rows_of(index), :], out, out_sem.at[index])

    stages = 2 * bits + 1
    pairs = -(-chunks // 2)
    finished, small_done = 0, 0
    for moment in range(pairs + stages - 1):
        ahead = needed(min(chunks, 2 * (moment + 2)) * chunk)
        for index in range(begun, ahead):
            begin(index)
        begun = max(begun, ahead)
        for stage in [0] + list(range(stages - 1, 0, -1)):
            pair = moment - stage
            if not 0 <= pair < pairs:
                continue
            for k in range(2 * pair, min(2 * pair + 2, chunks)):
                if stage == 0:
                    for index in range(joined, needed((k + 1) * chunk)):
                        swap(0, index).wait_recv()
                        load(0, index).wait()
                        add_rows(acc, acc, index * LANES, mate, index * LANES, LANES)
                    joined = max(joined, needed((k + 1) * chunk))
                    down(k, 0).start()
                elif stage <= bits:
                    depth = stage - 1
                    down(k, depth).wait_recv()
                    start, size = span(k, stage)
                    add_rows(acc if stage < bits else mate, acc, start, got[depth], k * size, size)
                    if stage < bits:
                        down(k, stage).start()
                    else:
                        up(k, bits - 1).start()
                else:
                    depth = 2 * bits - stage
                    up(k, depth).wait_recv()
                    if depth > 0:
                        up(k, depth - 1).start()
                    else:
                        ready = blocks if k == chunks - 1 else (k + 1) * chunk // LANES
                        for index in range(finished, ready):
                            put(index).start()
                        finished = ready
        if small_done <= bits:
            small_step(small_done).wait()
            small_out[...] = small_out[...] + small_got[small_done]
            small_done += 1
            if small_done <= bits:
                small_step(small_done).start()

    for index in range(blocks):
        swap(0, index).wait_send()
        put(index).wait()
    for k in range(chunks):
        for depth in range(bits):
            down(k, depth).wait_send()
            up(k, depth).wait_send()


def sum_gradients(axis_of, first, second, small):
    bits = len(axis_of)
    orders = bit_orders(axis_of)
    unit = TILE << bits
    chunk = LANES if LANES % unit == 0 else unit
    chunks = -(-12 * LANES // chunk)
    scratch = [
        pltpu.VMEM((chunks * chunk, LANES), BF16),
        pltpu.VMEM((chunks * chunk, LANES), BF16),
    ]
    scratch += [pltpu.VMEM((chunks * chunk >> (depth + 1), LANES), BF16) for depth in range(bits)]
    scratch += [pltpu.VMEM((bits + 1, *small.shape[1:]), F32)]
    scratch += [pltpu.SemaphoreType.DMA((12,))] * 4
    scratch += [pltpu.SemaphoreType.DMA((chunks, bits))] * 4
    scratch += [pltpu.SemaphoreType.DMA((bits + 1,))] * 2
    shapes = [jax.ShapeDtypeStruct(value.shape, BF16) for value in first]
    anywhere = pl.BlockSpec(memory_space=pl.ANY)
    inside = pl.BlockSpec(memory_space=pltpu.VMEM)
    *sums, small_sum = pl.pallas_call(
        functools.partial(sum_kernel, orders, chunk, chunks),
        out_shape=shapes + [jax.ShapeDtypeStruct(small.shape[1:], F32)],
        in_specs=[anywhere] * 8 + [inside],
        out_specs=[anywhere] * 4 + [inside],
        scratch_shapes=scratch,
        compiler_params=pltpu.CompilerParams(
            collective_id=0, has_side_effects=True, vmem_limit_bytes=60 * 1024 * 1024
        ),
        cost_estimate=pl.CostEstimate(flops=10**8, bytes_accessed=6 * 10**8, transcendentals=0),
        name="sum_gradients",
    )(*first, *second, small)
    return sums, small_sum


def other_core(value):
    return lax.ppermute(value, "section", [(0, 1), (1, 0)])


STEP = 256
ROW_TILE = 64
NEGATIVE = -1e30


def dot(left, right, dims=NN):
    return lax.dot_general(left, right, dims, preferred_element_type=F32)


def gelu_parts(pre):
    bell = jnp.exp(pre * pre * -0.5)
    t = pl.reciprocal(1.0 + jnp.abs(pre) * (0.3275911 * 0.7071067811865476))
    poly = t * (0.1274147960 + t * (-0.142248368 + t * (0.710706871 + t * (-0.7265760135 + t * 0.5307027145))))
    tail = poly * bell
    return jnp.where(pre >= 0.0, 1.0 - tail, tail), bell


def norm_stats(values):
    centred = values - jnp.mean(values, axis=-1, keepdims=True)
    recip = lax.rsqrt(jnp.mean(centred * centred, axis=-1, keepdims=True) + 1e-06)
    return centred * recip, recip


def fold(tile):
    return jnp.sum(tile.reshape(tile.shape[0] // 8, 8, tile.shape[1]), axis=0)


def layer_kernel(layer, groups, window, full, is_router, *refs):
    names = ["x", "col_code", "row_code", "vec", "scale"]
    names += [f"{who}_{what}" for who in ("own", "far") for what in ("qkv", "out", "up", "down")]
    if full:
        names += ["dout"]
        names += ["delta", "factor", "router"] if is_router else []
        names += ["du", "small"]
        names += ["router_grad"] if is_router else ["y"]
        names += ["g_qkv", "g_out", "g_up", "g_down"]
    else:
        names += ["y", "delta"]
    names += ["w_qkv", "w_out", "w_up", "w_down", "w_sem", "n1", "qkv", "probs", "mask", "mix", "between", "n2", "act"]
    if full:
        names += ["n1t", "n2t", "mixt", "dmlp", "dpre", "dn", "datt", "dmix", "dqkv"]
        names += ["down_stage", "up_stage", "down_sem", "up_sem"]
    r = dict(zip(names, refs, strict=True))
    rows, width = r["x"].shape
    hidden = r["w_up"].shape[1]
    core = lax.axis_index("section")
    pairs = width // 128

    def weight(what, who):
        k = ("qkv", "out", "up", "down").index(what)
        return pltpu.make_async_copy(r[f"{who}_{what}"].at[0], r[f"w_{what}"], r["w_sem"].at[k])

    @pl.when(core == layer)
    def _():
        for what in ("qkv", "out", "up", "down"):
            weight(what, "own").start()

    @pl.when(core != layer)
    def _():
        for what in ("qkv", "out", "up", "down"):
            weight(what, "far").start()

    def vec(start, count=width):
        return r["vec"][:, start : start + count]

    g1, g2, b1, bq, bv, bo, b2 = (vec(k * width) for k in range(7))
    bu_at, bd_at = 7 * width, 7 * width + hidden

    def row_loop(step, init=0):
        def at(k, carry):
            return step(pl.ds(pl.multiple_of(k * ROW_TILE, ROW_TILE), ROW_TILE), carry)

        return lax.fori_loop(0, rows // ROW_TILE, at, init)

    def norm_step(source, gain, bias, target):
        def step(here, carry):
            normal, _ = norm_stats(source[here, :].astype(F32))
            target[here, :] = (normal * gain + bias).astype(BF16)
            return carry

        return step

    row_loop(norm_step(r["x"], g1, b1, r["n1"]))
    if full:

        def delta_step(here, carry):
            low = (r["dout"][here, :].astype(F32) * r["scale"][here, :]).astype(BF16)
            r["dmlp"][here, :] = low
            return carry + fold(low.astype(F32))

        dbd = row_loop(delta_step, jnp.zeros((8, width), F32))
        r["small"][:, bd_at:] = jnp.sum(dbd, axis=0, keepdims=True)

    for k, (start, low, high) in enumerate(groups):
        col = r["col_code"][start : start + window, :]
        row = r["row_code"][:, start : start + window]
        place = lax.broadcasted_iota(jnp.int32, (window, 1), 0) + start
        col = jnp.where((place >= low) & (place < high), col, -1)
        r["mask"][k] = jnp.where(col == row, 0.0, NEGATIVE)

    weight("qkv", "own").wait()
    for k in range(3 * width // STEP):
        span = slice(k * STEP, (k + 1) * STEP)
        value = dot(r["n1"][...], r["w_qkv"][:, span])
        if k < width // STEP:
            value = (value + bq[:, span]).astype(BF16).astype(F32) * 0.125
        elif k >= 2 * width // STEP:
            value = value + bv[:, k * STEP - 2 * width : (k + 1) * STEP - 2 * width]
        r["qkv"][:, span] = value.astype(BF16)

    lane = lax.broadcasted_iota(jnp.int32, (1, 128), 1)

    def halves(block):
        zero = jnp.zeros_like(block)
        return jnp.where(lane < 64, block, zero), jnp.where(lane < 64, zero, block)

    r["mix"][...] = jnp.zeros_like(r["mix"])

    def lanes(pair, part):
        return pl.ds(pl.multiple_of(pair * 128 + part * width, 128), 128)

    def attend(pair, carry):
        for k, (start, low, high) in enumerate(groups):
            here = slice(start, start + window)
            q, key, v = (r["qkv"][here, lanes(pair, part)] for part in range(3))
            vt = v.T
            place = lax.broadcasted_iota(jnp.int32, (1, window), 1) + start
            valid = (place >= low) & (place < high)
            parts = []
            for half, own_key in enumerate(halves(key)):
                scores = dot(own_key, q, NT) + r["mask"][k]
                power = jnp.exp(scores - jnp.max(scores, axis=0, keepdims=True))
                total = jnp.sum(power, axis=0, keepdims=True)
                prob = (power * jnp.where(valid, 1.0 / total, 0.0)).astype(BF16)
                if full:
                    r["probs"][(pair * 2 + half) * len(groups) + k] = prob
                parts.append(dot(vt[half * 64 : half * 64 + 64], prob))
            mixed = jnp.concatenate(parts, axis=0).T.astype(BF16)
            r["mix"][here, lanes(pair, 0)] = r["mix"][here, lanes(pair, 0)] + mixed
        return carry

    lax.fori_loop(0, pairs, attend, 0)

    weight("out", "own").wait()
    for k in range(width // STEP):
        span = slice(k * STEP, (k + 1) * STEP)
        value = dot(r["mix"][...], r["w_out"][:, span]) + bo[:, span]
        r["between"][:, span] = r["x"][:, span].astype(F32) + value
    row_loop(norm_step(r["between"], g2, b2, r["n2"]))
    if full:
        r["n1t"][...] = r["n1"][...].T
        r["n2t"][...] = r["n2"][...].T
        r["mixt"][...] = r["mix"][...].T

    weight("up", "own").wait()
    weight("down", "own").wait()

    def copy_out(stage, target, sem, slot):
        return pltpu.make_async_copy(r[stage].at[slot], target, r[sem].at[slot])

    def down_out(k, slot):
        return copy_out("down_stage", r["g_down"].at[pl.ds(pl.multiple_of(k * STEP, STEP), STEP), :], "down_sem", slot)

    def side_out(name, k, slot):
        return copy_out("up_stage", r[name].at[:, pl.ds(pl.multiple_of(k * STEP, STEP), STEP)], "up_sem", slot)

    def hidden_step(k, carry):
        at = pl.multiple_of(k * STEP, STEP)
        span = pl.ds(at, STEP)
        pre = dot(r["n2"][...], r["w_up"][:, span]) + r["vec"][:, pl.ds(at + bu_at, STEP)]
        cdf, bell = gelu_parts(pre)
        act = (pre * cdf).astype(BF16)
        r["act"][:, span] = act
        if full:
            slot = lax.rem(k, 2)

            @pl.when(k >= 2)
            def _():
                down_out(k, slot).wait()
                side_out("g_up", k, slot).wait()

            slope = cdf + pre * bell * 0.3989422804014327
            dact = dot(r["dmlp"][...], r["w_down"][span, :], NT)
            dpre = (dact * slope).astype(BF16)
            r["dpre"][:, span] = dpre
            r["small"][:, pl.ds(at + bu_at, STEP)] = jnp.sum(dpre.astype(F32), axis=0, keepdims=True)
            r["down_stage"][slot] = dot(act, r["dmlp"][...], TN).astype(BF16)
            down_out(k, slot).start()
            r["up_stage"][slot] = dot(r["n2t"][...], dpre).astype(BF16)
            side_out("g_up", k, slot).start()
        return carry

    lax.fori_loop(0, hidden // STEP, hidden_step, 0)
    if not (full and is_router):
        for k in range(width // STEP):
            span = slice(k * STEP, (k + 1) * STEP)
            value = dot(r["act"][...], r["w_down"][:, span]) + vec(bd_at)[:, span]
            source = r["x"][:, span].astype(F32)
            value = r["between"][:, span] - source + value
            if not full:
                r["delta"][:, span] = value
            r["y"][:, span] = (source + r["scale"][...] * value).astype(BF16)
    if not full:
        return

    for k in range(width // STEP):
        span = slice(k * STEP, (k + 1) * STEP)
        r["dn"][:, span] = dot(r["dpre"][...], r["w_up"][span, :], NT)

    def norm_back(source, gain, here):
        normal, recip = norm_stats(source[here, :].astype(F32))
        grad = r["dn"][here, :]
        hat = grad * gain
        back = recip * (
            hat - jnp.mean(hat, axis=-1, keepdims=True) - normal * jnp.mean(hat * normal, axis=-1, keepdims=True)
        )
        return back, fold(grad * normal), fold(grad)

    def second_back(here, carry):
        back, dg, db = norm_back(r["between"], g2, here)
        r["between"][here, :] = back
        total = (r["dout"][here, :].astype(F32) * r["scale"][here, :] + back).astype(BF16)
        r["datt"][here, :] = total
        return carry[0] + dg, carry[1] + db, carry[2] + fold(total.astype(F32))

    zero = jnp.zeros((8, width), F32)
    dg2, db2, dbo = row_loop(second_back, (zero, zero, zero))
    r["small"][:, width : 2 * width] = jnp.sum(dg2, axis=0, keepdims=True)
    r["small"][:, 6 * width : 7 * width] = jnp.sum(db2, axis=0, keepdims=True)
    r["small"][:, 5 * width : 6 * width] = jnp.sum(dbo, axis=0, keepdims=True)

    steps = hidden // STEP
    for k in range(width // STEP):
        span = slice(k * STEP, (k + 1) * STEP)
        r["dmix"][:, span] = dot(r["datt"][...], r["w_out"][span, :], NT).astype(BF16)
        slot = k % 2
        side_out("g_up", steps - 2 + slot, slot).wait()
        r["up_stage"][slot] = dot(r["mixt"][...], r["datt"][:, span]).astype(BF16)
        side_out("g_out", k, slot).start()

    r["dqkv"][...] = jnp.zeros_like(r["dqkv"])

    def attend_back(pair, carry):
        for k, (start, low, high) in enumerate(groups):
            here = slice(start, start + window)
            q, key, v = (r["qkv"][here, lanes(pair, part)] for part in range(3))
            dm = r["dmix"][here, lanes(pair, 0)]
            key_t = key.T
            dq, dk, dv = [], None, None
            for half, (own_q, own_v, own_dm) in enumerate(zip(halves(q), halves(v), halves(dm))):
                prob = r["probs"][(pair * 2 + half) * len(groups) + k]
                wide = prob.astype(F32)
                dprob = dot(own_v, dm, NT)
                product = wide * dprob
                ds = (product - wide * jnp.sum(product, axis=0, keepdims=True)).astype(BF16)
                dq.append(dot(key_t[half * 64 : half * 64 + 64], ds))
                one, two = dot(ds, own_q), dot(prob, own_dm)
                dk, dv = (one, two) if dk is None else (dk + one, dv + two)
            dq = jnp.concatenate(dq, axis=0).T * 0.125
            for part, value in enumerate((dq, dk, dv)):
                spot = lanes(pair, part)
                r["dqkv"][here, spot] = r["dqkv"][here, spot] + value.astype(BF16)
        return carry

    lax.fori_loop(0, pairs, attend_back, 0)

    for k in range(3 * width // STEP):
        span = slice(k * STEP, (k + 1) * STEP)
        block = r["dqkv"][:, span]
        if not width <= k * STEP < 2 * width:
            at = 3 * width + k * STEP - (width if k * STEP >= width else 0)
            r["small"][:, at : at + STEP] = jnp.sum(block.astype(F32), axis=0, keepdims=True)
        slot = (k + 1) % 2
        side_out("g_out", 0, slot).wait()
        r["up_stage"][slot] = dot(r["n1t"][...], block).astype(BF16)
        side_out("g_qkv", k, slot).start()

    for k in range(width // STEP):
        span = slice(k * STEP, (k + 1) * STEP)
        r["dn"][:, span] = dot(r["dqkv"][...], r["w_qkv"][span, :], NT)

    def first_back(here, carry):
        back, dg, db = norm_back(r["x"], g1, here)
        dout = r["dout"][here, :].astype(F32)
        total = dout + r["between"][here, :] + back
        sums = [carry[0] + dg, carry[1] + db]
        if is_router:
            slope = jnp.sum(dout * r["delta"][here, :], axis=1, keepdims=True) * r["factor"][here, :]
            total = total + slope * r["router"][...]
            sums.append(carry[2] + fold(slope * r["x"][here, :].astype(F32)))
        r["du"][here, :] = total.astype(BF16)
        return tuple(sums)

    sums = row_loop(first_back, (zero,) * (3 if is_router else 2))
    r["small"][:, :width] = jnp.sum(sums[0], axis=0, keepdims=True)
    r["small"][:, 2 * width : 3 * width] = jnp.sum(sums[1], axis=0, keepdims=True)
    if is_router:
        r["router_grad"][...] = jnp.sum(sums[2], axis=0, keepdims=True)
    for slot in range(2):
        down_out(0, slot).wait()
        side_out("g_up", 0, slot).wait()


def run_layer(layer, groups, window, x, code, vec, scale, own, far, back=None, router=None):
    rows, width = x.shape
    hidden = own[2].shape[2]
    full, is_router = back is not None, router is not None
    inside = pl.BlockSpec(memory_space=pltpu.VMEM)
    anywhere = pl.BlockSpec(memory_space=pl.ANY)
    args = [x, code[:, None], code[None, :], vec, scale[:, None], *own, *far]
    in_specs = [inside] * 5 + [anywhere] * 8
    if full:
        args += [back]
        if is_router:
            delta, factor, router_row = router
            args += [delta, factor[:, None], router_row]
        in_specs += [inside] * (len(args) - len(in_specs))
        outs = [((rows, width), BF16), ((1, vec.shape[1]), F32)]
        outs += [((1, width), F32)] if is_router else [((rows, width), BF16)]
        out_specs = [inside] * 3 + [anywhere] * 4
        outs += [((width, 3 * width), BF16), ((width, width), BF16), ((width, hidden), BF16), ((hidden, width), BF16)]
    else:
        outs = [((rows, width), BF16), ((rows, width), F32)]
        out_specs = [inside] * 2
    held = [
        ((width, 3 * width), BF16),
        ((width, width), BF16),
        ((width, hidden), BF16),
        ((hidden, width), BF16),
        None,
        ((rows, width), BF16),
        ((rows, 3 * width), BF16),
        ((HEADS * len(groups) if full else 1, window, window), BF16),
        ((len(groups), window, window), F32),
        ((rows, width), BF16),
        ((rows, width), F32),
        ((rows, width), BF16),
        ((rows, hidden), BF16),
    ]
    if full:
        held += [
            ((width, rows), BF16),
            ((width, rows), BF16),
            ((width, rows), BF16),
            ((rows, width), BF16),
            ((rows, hidden), BF16),
            ((rows, width), F32),
            ((rows, width), BF16),
            ((rows, width), BF16),
            ((rows, 3 * width), BF16),
            ((2, STEP, width), BF16),
            ((2, width, STEP), BF16),
        ]
    scratch = [pltpu.SemaphoreType.DMA((4,)) if one is None else pltpu.VMEM(*one) for one in held]
    if full:
        scratch += [pltpu.SemaphoreType.DMA((2,))] * 2
    flops = rows * width * (3 * width + width + 2 * hidden) * (6 if full else 2)
    return pl.pallas_call(
        functools.partial(layer_kernel, layer, groups, window, full, is_router),
        out_shape=[jax.ShapeDtypeStruct(*one) for one in outs],
        in_specs=in_specs,
        out_specs=out_specs,
        scratch_shapes=scratch,
        compiler_params=pltpu.CompilerParams(vmem_limit_bytes=60 * 1024 * 1024),
        cost_estimate=pl.CostEstimate(flops=flops, bytes_accessed=3 * 10**7, transcendentals=0),
        name=f"layer_{layer}_{'back' if full else 'forward'}",
    )(*args)


def row_plan(crop_lengths, chosen):
    rows = chosen.shape[0]
    ends = jnp.cumsum(crop_lengths)
    starts = ends - crop_lengths
    is_long = crop_lengths == LONG
    long_before = jnp.cumsum(is_long.astype(jnp.int32)) - is_long
    short = jnp.where(is_long, 0, crop_lengths)
    short_before = jnp.cumsum(short) - short
    base = jnp.where(is_long, long_before * LONG, 2 * LONG + short_before)
    at = jnp.arange(rows, dtype=jnp.int32)
    inside = (at[:, None] >= starts[None]) & (at[:, None] < ends[None])
    target = at + jnp.sum(jnp.where(inside, (base - starts)[None], 0), axis=1)
    order = target[None, :] == at[:, None]
    code = jnp.sum((at[:, None] >= base[None]).astype(jnp.int32), axis=1)
    chosen_in = jnp.sum(jnp.where(order, chosen[None, :], 0), axis=1)
    rank = jnp.sum(jnp.where(at[:, None] > at[None, :], chosen_in[None, :], 0), axis=1)
    slot = jnp.arange(rows // 2, dtype=jnp.int32)
    pick = (rank[None, :] == slot[:, None]) & (chosen_in[None, :] == 1)
    routed_code = jnp.sum(jnp.where(pick, code[None, :], 0), axis=1)
    return order.astype(BF16), pick.astype(BF16), code, routed_code, chosen_in


def body(axis_of, tokens, lengths, route_mask, router_weight, gains, biases, w_qkv, w_out, w_up, w_down, cotangent):
    section = lax.axis_index("section")
    micro, rows, width = tokens.shape
    own = (w_qkv, w_out, w_up, w_down)
    far = tuple(other_core(value) for value in own)
    own_vec = jnp.concatenate([gains, biases], axis=1)
    far_vec = other_core(own_vec)
    vecs = [jnp.where(section == layer, own_vec, far_vec) for layer in range(2)]
    router_f = router_weight.astype(F32)

    def pick_micro(array):
        return lax.dynamic_index_in_dim(array, section, 0, False)

    crop_lengths, chosen = pick_micro(lengths)[0], pick_micro(route_mask)
    order, pick, code, routed_code, chosen_in = row_plan(crop_lengths, chosen)
    is_routed = (chosen_in == 1)[:, None]
    x = dot(order, pick_micro(tokens)).astype(BF16)
    cot = dot(order, pick_micro(cotangent)).astype(BF16)
    routed = dot(pick, x).astype(BF16)
    inputs_one = routed.astype(F32)
    held = (routed_code > 0).astype(F32)
    gate = jax.nn.sigmoid(jnp.sum(inputs_one * router_f[None, :], axis=1))
    scale_one = held * gate
    half = LONG // 2
    groups_one = [(0, 0, half), (96, half, 2 * half), (192, 2 * half, rows // 2)]
    groups_two = [(0, 0, LONG), (192, LONG, 2 * LONG), (384, 2 * LONG, rows)]

    out_one, delta_one = run_layer(0, groups_one, 128, routed, routed_code, vecs[0], scale_one, own, far)
    y1 = jnp.where(is_routed, dot(pick, out_one, TN).astype(BF16), x)
    ones = jnp.ones((rows,), F32)
    dout, small_two, y2, *grads_two = run_layer(1, groups_two, 256, y1, code, vecs[1], ones, own, far, cot)
    dout_one = dot(pick, dout).astype(BF16)
    factor = held * gate * (1.0 - gate)
    du_one, small_one, grad_router, *grads_one = run_layer(
        0, groups_one, 128, routed, routed_code, vecs[0], scale_one, own, far, dout_one,
        (delta_one, factor, router_f[None, :]),
    )
    du_one = jnp.where(is_routed, dot(pick, du_one, TN).astype(BF16), dout)
    small_one, small_two, grad_router = small_one[0], small_two[0], grad_router[0]

    def unsort(value):
        return dot(order, value, TN).astype(BF16)

    def spread(first, second):
        mine = jnp.where(section == 0, first, second)
        theirs = other_core(jnp.where(section == 0, second, first))
        return jnp.where(section == 0, jnp.stack([mine, theirs]), jnp.stack([theirs, mine]))

    activations = spread(unsort(y1), unsort(y2))
    input_grads = spread(unsort(du_one), unsort(dout))

    micro_ids = jnp.arange(micro)
    here = (micro_ids == section).astype(F32)
    counts = here * jnp.sum(route_mask.astype(F32), axis=1)
    extra = jnp.concatenate([here * jnp.sum(scale_one), counts])
    shared = [grad_router, extra]
    small = jnp.stack([jnp.concatenate([part, *shared]) for part in (small_one, small_two)])
    room = -(-small.shape[1] // (8 * LANES)) * 8 * LANES
    small = jnp.pad(small, ((0, 0), (0, room - small.shape[1]))).reshape(2, room // LANES, LANES)
    sums, small = sum_gradients(axis_of, grads_one, grads_two, small)
    small = small.reshape(-1)
    span = small_one.shape[0]
    tail = small[span:]

    return (
        activations[None],
        input_grads[None],
        *(value.astype(F32)[None] for value in sums),
        small[: 2 * width][None],
        small[2 * width : span][None],
        tail[:width],
        tail[width : width + micro] / tail[width + micro : width + 2 * micro],
    )


def solution(mesh):
    in_specs = (
        P(None, "dp", None),
        P(None, "dp", None),
        P(None, "dp"),
        P(),
        P("section", None),
        P("section", None),
        P("section", None, None),
        P("section", None, None),
        P("section", None, None),
        P("section", None, None),
        P(None, "dp", None),
    )
    out_specs = (
        P("section", None, "dp", None),
        P("section", None, "dp", None),
        P("section", None, None),
        P("section", None, None),
        P("section", None, None),
        P("section", None, None),
        P("section", None),
        P("section", None),
        P(),
        P(),
    )
    step = functools.partial(body, axis_bits(mesh))
    return jax.shard_map(step, mesh=mesh, in_specs=in_specs, out_specs=out_specs, check_vma=False)
```

```python
import functools

import jax
import jax.numpy as jnp
from jax import lax
from jax.experimental import pallas as pl
from jax.experimental.pallas import tpu as pltpu
from jax.sharding import PartitionSpec as P

HEADS = 12
HEAD = 64
LONG = 197
F32 = jnp.float32
BF16 = jnp.bfloat16
NT = (((1,), (1,)), ((), ()))
TN = (((0,), (0,)), ((), ()))
NN = (((1,), (0,)), ((), ()))


LANES = 768
TILE = 16
GRAD_ROWS = 12 * LANES


def axis_bits(mesh):
    line = mesh.devices[0]
    bits = len(line).bit_length() - 1
    try:
        spots = [tuple(device.coords) for device in line]
    except AttributeError:
        return [0] * bits
    return [
        next((w for w in range(3) if spots[1 << b][w] != spots[0][w]), 0) for b in range(bits)
    ]


def sum_plan(axis_of):
    bits = len(axis_of)
    lists = {}
    for bit, axis in enumerate(axis_of):
        lists.setdefault(axis, []).append(bit)
    lists = sorted(lists.values(), key=len)
    while len(lists) < 3:
        lists.append([])
    one, two, three = lists[:3]
    three = three + sum(lists[3:], [])
    orders = [one + three + two, two + three + one, one + two + three, two + one + three]
    sizes = [512, 512, 256, 256]
    if any(size % (TILE << bits) for size in sizes) or GRAD_ROWS % sum(sizes):
        sizes = [TILE << bits] * 4
    groups, start = [], 0
    while start < GRAD_ROWS:
        group = []
        for size, order in zip(sizes, orders):
            if start < GRAD_ROWS:
                group.append((start, size, order))
                start += size
        groups.append(group)
    return groups, start


def add_rows(into, into_start, source, start, other, other_start, count):
    tile = next(t for t in (64, 32, 16) if count % t == 0)

    def step(k, carry):
        target, here, there = (
            pl.ds(pl.multiple_of(first + k * tile, TILE), tile) for first in (into_start, start, other_start)
        )
        into[target, :] = source[here, :] + other[there, :]
        return carry

    lax.fori_loop(0, count // tile, step, 0)


def sum_kernel(groups, *refs):
    grads, small_in, shown = refs[0:2], refs[2], refs[3:7]
    out, landed, small_out, shown_out = refs[7], refs[8], refs[9], refs[10:12]
    chunks = [chunk for group in groups for chunk in group]
    bits = len(chunks[0][2])
    acc, mate, *rest = refs[12:]
    got, small_got = rest[:bits], rest[bits]
    (
        load_sem, mate_sem, swap_send, swap_recv, shard_sem, send, recv, back_send, back_recv,
        small_send, small_recv, shown_sem, shown_send, shown_recv,
    ) = rest[bits + 1 :]
    core = lax.axis_index("section")
    me = lax.axis_index("dp")
    slots = mate.shape[0]

    def bit_at(bit):
        return lax.rem(me // (1 << bit), 2)

    def partner(bit):
        return (core, me + (1 - 2 * bit_at(bit)) * (1 << bit))

    across = (1 - core, me)
    friends = [across] + [partner(bit) for bit in range(bits)]
    barrier = pltpu.get_barrier_semaphore()
    for friend in friends:
        pl.semaphore_signal(barrier, inc=1, device_id=friend, device_id_type=pl.DeviceIdType.MESH)
    pl.semaphore_wait(barrier, len(friends))

    def remote(source, target, one, two, friend):
        return pltpu.make_async_remote_copy(
            src_ref=source,
            dst_ref=target,
            send_sem=one,
            recv_sem=two,
            device_id=friend,
            device_id_type=pl.DeviceIdType.MESH,
        )

    def small_step(k):
        friend = across if k == 0 else partner(k - 1)
        return remote(small_out, small_got.at[k], small_send.at[k], small_recv.at[k], friend)

    def small_first(layer):
        return remote(small_in.at[1 - layer], small_got.at[0], small_send.at[0], small_recv.at[0], across)

    def shown_keep(layer, k):
        return pltpu.make_async_copy(shown[2 * k + layer], shown_out[k].at[core], shown_sem.at[k])

    def shown_give(layer, k):
        return remote(
            shown[2 * k + 1 - layer], shown_out[k].at[core], shown_send.at[k], shown_recv.at[k], across
        )

    def held(k):
        start, size, _ = chunks[k]
        return pl.ds(start, min(size, GRAD_ROWS - start))

    def swap(layer, k):
        rows = held(k)
        return remote(grads[1 - layer].at[rows, :], landed.at[rows, :], swap_send.at[k], swap_recv.at[k], across)

    def load(layer, k):
        rows = held(k)
        return pltpu.make_async_copy(grads[layer].at[rows, :], acc.at[rows, :], load_sem.at[k])

    def load_mate(k):
        rows = held(k)
        return pltpu.make_async_copy(
            landed.at[rows, :], mate.at[k % slots, pl.ds(0, rows.size), :], mate_sem.at[k]
        )

    for layer in range(2):

        @pl.when(core == layer)
        def _():
            small_out[...] = small_in[layer]
            small_first(layer).start()
            for k in range(2):
                shown_keep(layer, k).start()

    total_rows = acc.shape[0]
    if total_rows > GRAD_ROWS:
        acc[GRAD_ROWS:, :] = jnp.zeros((total_rows - GRAD_ROWS, LANES), BF16)

    def begin(which):
        for layer in range(2):

            @pl.when(core == layer)
            def _():
                for k in which:
                    swap(layer, k).start()
                    load(layer, k).start()

    def span(k, depth):
        start, size, order = chunks[k]
        for bit in order[:depth]:
            size //= 2
            start = start + bit_at(bit) * size
        return start, size

    def down(k, depth):
        bit = chunks[k][2][depth]
        start, size = span(k, depth)
        size //= 2
        away = pl.multiple_of(start + (1 - bit_at(bit)) * size, TILE)
        return remote(
            acc.at[pl.ds(away, size), :],
            got[depth].at[pl.ds(chunks[k][0] >> (depth + 1), size), :],
            send.at[k, depth],
            recv.at[k, depth],
            partner(bit),
        )

    def shard(k):
        start, size = span(k, bits)
        here = pl.ds(pl.multiple_of(start, TILE), size)
        return pltpu.make_async_copy(acc.at[here, :], out.at[here, :], shard_sem.at[k])

    def up(k, depth):
        bit = chunks[k][2][depth]
        start, size = span(k, depth + 1)
        here = pl.ds(pl.multiple_of(start, TILE), size)
        source = acc if depth == bits - 1 else out
        return remote(
            source.at[here, :], out.at[here, :], back_send.at[k, depth], back_recv.at[k, depth], partner(bit)
        )

    first_of = [0]
    for group in groups:
        first_of.append(first_of[-1] + len(group))

    def members(group):
        return range(first_of[group], first_of[group + 1]) if 0 <= group < len(groups) else range(0)

    begin(members(0))
    begin(members(1))
    for layer in range(2):

        @pl.when(core == layer)
        def _():
            for k in range(2):
                shown_give(layer, k).start()

    for k in members(0):
        swap(0, k).wait_recv()
        load_mate(k).start()
    small_done = 0
    stages = 2 * bits + 1
    for moment in range(len(groups) + stages - 1):
        for k in members(moment):
            load(0, k).wait()
            load_mate(k).wait()
            start, size, _ = chunks[k]
            rows = min(size, GRAD_ROWS - start)
            add_rows(acc, start, acc, start, mate.at[k % slots], 0, rows)
            down(k, 0).start()
        begin(members(moment + 2))
        for stage in range(stages - 1, 0, -1):
            for k in members(moment - stage):
                if stage <= bits:
                    depth = stage - 1
                    down(k, depth).wait_recv()
                    start, size = span(k, stage)
                    add_rows(acc, start, acc, start, got[depth], chunks[k][0] >> stage, size)
                    if stage < bits:
                        down(k, stage).start()
                    else:
                        up(k, bits - 1).start()
                        shard(k).start()
                else:
                    depth = 2 * bits - stage
                    up(k, depth).wait_recv()
                    if depth == bits - 1:
                        shard(k).wait()
                    if depth > 0:
                        up(k, depth - 1).start()
        for k in members(moment + 1):
            swap(0, k).wait_recv()
            load_mate(k).start()
        if small_done <= bits:
            small_step(small_done).wait()
            small_out[...] = small_out[...] + small_got[small_done]
            small_done += 1
            if small_done <= bits:
                small_step(small_done).start()

    for k in range(2):
        shown_keep(0, k).wait()
        shown_give(0, k).wait()
    for k in range(len(chunks)):
        swap(0, k).wait_send()
        for depth in range(bits):
            down(k, depth).wait_send()
            up(k, depth).wait_send()


def sum_gradients(axis_of, grads, small, shown):
    bits = len(axis_of)
    groups, total = sum_plan(axis_of)
    count = sum(len(group) for group in groups)
    largest = max(chunk[1] for group in groups for chunk in group)
    most = max(len(group) for group in groups)
    scratch = [pltpu.VMEM((total, LANES), BF16), pltpu.VMEM((2 * most, largest, LANES), BF16)]
    scratch += [pltpu.VMEM((total >> (depth + 1), LANES), BF16) for depth in range(bits)]
    scratch += [pltpu.VMEM((bits + 1, *small.shape[1:]), F32)]
    scratch += [pltpu.SemaphoreType.DMA((count,))] * 5
    scratch += [pltpu.SemaphoreType.DMA((count, bits))] * 4
    scratch += [pltpu.SemaphoreType.DMA((bits + 1,))] * 2
    scratch += [pltpu.SemaphoreType.DMA((2,))] * 3
    anywhere = pl.BlockSpec(memory_space=pl.ANY)
    inside = pl.BlockSpec(memory_space=pltpu.VMEM)
    sums, _, small_sum, *shown_sum = pl.pallas_call(
        functools.partial(sum_kernel, groups),
        out_shape=[
            jax.ShapeDtypeStruct((total, LANES), BF16),
            jax.ShapeDtypeStruct((GRAD_ROWS, LANES), BF16),
            jax.ShapeDtypeStruct(small.shape[1:], F32),
            *(jax.ShapeDtypeStruct((2, *shown[0].shape), BF16) for _ in range(2)),
        ],
        in_specs=[anywhere] * 2 + [inside] + [anywhere] * 4,
        out_specs=[anywhere] * 2 + [inside] + [anywhere] * 2,
        scratch_shapes=scratch,
        compiler_params=pltpu.CompilerParams(
            collective_id=0, has_side_effects=True, vmem_limit_bytes=60 * 1024 * 1024
        ),
        cost_estimate=pl.CostEstimate(flops=10**8, bytes_accessed=6 * 10**8, transcendentals=0),
        name="sum_gradients",
    )(*grads, small, *shown)
    return sums, small_sum, shown_sum


def other_core(value):
    return lax.ppermute(value, "section", [(0, 1), (1, 0)])


STEP = 256
ROW_TILE = 64
NEGATIVE = -1e30


def dot(left, right, dims=NN):
    return lax.dot_general(left, right, dims, preferred_element_type=F32)


def gelu_parts(pre):
    bell = jnp.exp(pre * pre * -0.5)
    t = pl.reciprocal(1.0 + jnp.abs(pre) * (0.3275911 * 0.7071067811865476))
    poly = t * (0.1274147960 + t * (-0.142248368 + t * (0.710706871 + t * (-0.7265760135 + t * 0.5307027145))))
    tail = poly * bell
    return jnp.where(pre >= 0.0, 1.0 - tail, tail), bell


def norm_stats(values):
    centred = values - jnp.mean(values, axis=-1, keepdims=True)
    recip = lax.rsqrt(jnp.mean(centred * centred, axis=-1, keepdims=True) + 1e-06)
    return centred * recip, recip


def fold(tile):
    return jnp.sum(tile.reshape(tile.shape[0] // 8, 8, tile.shape[1]), axis=0)


class Names:
    pass


def layer_kernel(layer, groups, window, full, is_router, *refs):
    r = Names()
    given = iter(refs)
    r.x, r.col_code, r.row_code, r.vec, r.scale = (next(given) for _ in range(5))
    r.own = [next(given) for _ in range(4)]
    r.far = [next(given) for _ in range(4)]
    r.unsort = next(given)
    if full and is_router:
        r.all_dout, r.pick, r.unpick, r.skipped, r.delta, r.factor, r.router = (next(given) for _ in range(7))
    elif full:
        r.dout = next(given)
    else:
        r.all_x, r.unpick, r.skipped = (next(given) for _ in range(3))
    if full:
        r.shown_du, r.small, r.grads = (next(given) for _ in range(3))
        if is_router:
            r.router_grad = next(given)
        else:
            r.du, r.shown_y = (next(given) for _ in range(2))
    else:
        r.all_y, r.shown_y, r.delta = (next(given) for _ in range(3))
    r.weights = [next(given) for _ in range(4)]
    r.w_qkv, r.w_out, r.w_up, r.w_down = r.weights
    r.w_sem, r.n1, r.qkv, r.probs, r.mask, r.mix, r.between, r.n2, r.act = (next(given) for _ in range(9))
    if full:
        r.n1t, r.n2t, r.mixt, r.dmlp, r.dpre, r.dn, r.datt, r.dmix, r.dqkv = (next(given) for _ in range(9))
        r.down_stage, r.up_stage = (next(given) for _ in range(2))
        if is_router:
            r.dout, r.du = (next(given) for _ in range(2))
        else:
            r.y = next(given)
        r.down_sem, r.up_sem = (next(given) for _ in range(2))
    else:
        r.y = next(given)
    rows, width = r.x.shape
    hidden = r.w_up.shape[1]
    core = lax.axis_index("section")
    pairs = width // 128

    def weight(which, source):
        return pltpu.make_async_copy(source[which].at[0], r.weights[which], r.w_sem.at[which])

    for near, source in ((core == layer, r.own), (core != layer, r.far)):

        @pl.when(near)
        def _():
            for which in range(4):
                weight(which, source).start()

    def vec(start, count=width):
        return r.vec[:, start : start + count]

    g1, g2, b1, bq, bv, bo, b2 = (vec(k * width) for k in range(7))
    bu_at, bd_at = 7 * width, 7 * width + hidden

    def row_loop(step, init=0):
        def at(k, carry):
            return step(pl.ds(pl.multiple_of(k * ROW_TILE, ROW_TILE), ROW_TILE), carry)

        return lax.fori_loop(0, rows // ROW_TILE, at, init)

    def norm_step(source, gain, bias, target):
        def step(here, carry):
            normal, _ = norm_stats(source[here, :].astype(F32))
            target[here, :] = (normal * gain + bias).astype(BF16)
            return carry

        return step

    def tiles(step):
        for k in range(width // STEP):
            step(slice(k * STEP, (k + 1) * STEP))

    def show(source, target):
        def step(span):
            target[:, span] = dot(r.unsort[...], source[:, span]).astype(BF16)

        tiles(step)

    def spread(routed, others, target, shown):
        def step(span):
            value = dot(r.unpick[...], routed[:, span]) + others[:, span].astype(F32) * r.skipped[...]
            if target is not None:
                target[:, span] = value.astype(BF16)
            shown[:, span] = dot(r.unsort[...], value.astype(BF16)).astype(BF16)

        tiles(step)

    row_loop(norm_step(r.x, g1, b1, r.n1))
    if full and is_router:

        def route_step(span):
            r.dout[:, span] = dot(r.pick[...], r.all_dout[:, span]).astype(BF16)

        tiles(route_step)
    if full:

        def delta_step(here, carry):
            low = (r.dout[here, :].astype(F32) * r.scale[here, :]).astype(BF16)
            r.dmlp[here, :] = low
            return carry + fold(low.astype(F32))

        dbd = row_loop(delta_step, jnp.zeros((8, width), F32))
        r.small[:, bd_at:] = jnp.sum(dbd, axis=0, keepdims=True)

    for k, (start, low, high) in enumerate(groups):
        col = r.col_code[start : start + window, :]
        row = r.row_code[:, start : start + window]
        place = lax.broadcasted_iota(jnp.int32, (window, 1), 0) + start
        col = jnp.where((place >= low) & (place < high), col, -1)
        r.mask[k] = jnp.where(col == row, 0.0, NEGATIVE)

    weight(0, r.own).wait()
    for k in range(3 * width // STEP):
        span = slice(k * STEP, (k + 1) * STEP)
        value = dot(r.n1[...], r.w_qkv[:, span])
        if k < width // STEP:
            value = (value + bq[:, span]).astype(BF16).astype(F32) * 0.125
        elif k >= 2 * width // STEP:
            value = value + bv[:, k * STEP - 2 * width : (k + 1) * STEP - 2 * width]
        r.qkv[:, span] = value.astype(BF16)

    lane = lax.broadcasted_iota(jnp.int32, (1, 128), 1)

    def halves(block):
        zero = jnp.zeros_like(block)
        return jnp.where(lane < 64, block, zero), jnp.where(lane < 64, zero, block)

    r.mix[...] = jnp.zeros_like(r.mix)

    def lanes(pair, part):
        return pl.ds(pl.multiple_of(pair * 128 + part * width, 128), 128)

    def attend(pair, carry):
        for k, (start, low, high) in enumerate(groups):
            here = slice(start, start + window)
            q, key, v = (r.qkv[here, lanes(pair, part)] for part in range(3))
            vt = v.T
            place = lax.broadcasted_iota(jnp.int32, (1, window), 1) + start
            valid = (place >= low) & (place < high)
            parts = []
            for half, own_key in enumerate(halves(key)):
                scores = dot(own_key, q, NT) + r.mask[k]
                power = jnp.exp(scores - jnp.max(scores, axis=0, keepdims=True))
                total = jnp.sum(power, axis=0, keepdims=True)
                prob = (power * jnp.where(valid, 1.0 / total, 0.0)).astype(BF16)
                if full:
                    r.probs[(pair * 2 + half) * len(groups) + k] = prob
                parts.append(dot(vt[half * 64 : half * 64 + 64], prob))
            mixed = jnp.concatenate(parts, axis=0).T.astype(BF16)
            r.mix[here, lanes(pair, 0)] = r.mix[here, lanes(pair, 0)] + mixed
        return carry

    lax.fori_loop(0, pairs, attend, 0)

    weight(1, r.own).wait()
    for k in range(width // STEP):
        span = slice(k * STEP, (k + 1) * STEP)
        value = dot(r.mix[...], r.w_out[:, span]) + bo[:, span]
        r.between[:, span] = r.x[:, span].astype(F32) + value
    row_loop(norm_step(r.between, g2, b2, r.n2))
    if full:
        r.n1t[...] = r.n1[...].T
        r.n2t[...] = r.n2[...].T
        r.mixt[...] = r.mix[...].T

    weight(2, r.own).wait()
    weight(3, r.own).wait()

    def copy_out(stage, target, sem, slot):
        return pltpu.make_async_copy(stage.at[slot], target, sem.at[slot])

    def down_out(k, slot):
        return copy_out(r.down_stage, r.grads.at[pl.ds(pl.multiple_of(k * STEP, STEP), STEP), :], r.down_sem, slot)

    def side_out(block, k, slot):
        row = pl.multiple_of((block + k // 3) * width, width)
        column = pl.multiple_of(k % 3 * STEP, STEP)
        return copy_out(r.up_stage, r.grads.at[pl.ds(row, width), pl.ds(column, STEP)], r.up_sem, slot)

    def hidden_step(k, carry):
        at = pl.multiple_of(k * STEP, STEP)
        span = pl.ds(at, STEP)
        pre = dot(r.n2[...], r.w_up[:, span]) + r.vec[:, pl.ds(at + bu_at, STEP)]
        cdf, bell = gelu_parts(pre)
        act = (pre * cdf).astype(BF16)
        r.act[:, span] = act
        if full:
            slot = lax.rem(k, 2)

            @pl.when(k >= 2)
            def _():
                down_out(k, slot).wait()
                side_out(4, k, slot).wait()

            slope = cdf + pre * bell * 0.3989422804014327
            dact = dot(r.dmlp[...], r.w_down[span, :], NT)
            dpre = (dact * slope).astype(BF16)
            r.dpre[:, span] = dpre
            r.small[:, pl.ds(at + bu_at, STEP)] = jnp.sum(dpre.astype(F32), axis=0, keepdims=True)
            r.down_stage[slot] = dot(act, r.dmlp[...], TN).astype(BF16)
            down_out(k, slot).start()
            r.up_stage[slot] = dot(r.n2t[...], dpre).astype(BF16)
            side_out(4, k, slot).start()
        return carry

    lax.fori_loop(0, hidden // STEP, hidden_step, 0)
    if not (full and is_router):
        for k in range(width // STEP):
            span = slice(k * STEP, (k + 1) * STEP)
            value = dot(r.act[...], r.w_down[:, span]) + vec(bd_at)[:, span]
            source = r.x[:, span].astype(F32)
            value = r.between[:, span] - source + value
            if not full:
                r.delta[:, span] = value
            r.y[:, span] = (source + r.scale[...] * value).astype(BF16)
    if not full:
        spread(r.y, r.all_x, r.all_y, r.shown_y)
        return
    if not is_router:
        show(r.y, r.shown_y)

    for k in range(width // STEP):
        span = slice(k * STEP, (k + 1) * STEP)
        r.dn[:, span] = dot(r.dpre[...], r.w_up[span, :], NT)

    def norm_back(source, gain, here):
        normal, recip = norm_stats(source[here, :].astype(F32))
        grad = r.dn[here, :]
        hat = grad * gain
        back = recip * (
            hat - jnp.mean(hat, axis=-1, keepdims=True) - normal * jnp.mean(hat * normal, axis=-1, keepdims=True)
        )
        return back, fold(grad * normal), fold(grad)

    def second_back(here, carry):
        back, dg, db = norm_back(r.between, g2, here)
        r.between[here, :] = back
        total = (r.dout[here, :].astype(F32) * r.scale[here, :] + back).astype(BF16)
        r.datt[here, :] = total
        return carry[0] + dg, carry[1] + db, carry[2] + fold(total.astype(F32))

    zero = jnp.zeros((8, width), F32)
    dg2, db2, dbo = row_loop(second_back, (zero, zero, zero))
    r.small[:, width : 2 * width] = jnp.sum(dg2, axis=0, keepdims=True)
    r.small[:, 6 * width : 7 * width] = jnp.sum(db2, axis=0, keepdims=True)
    r.small[:, 5 * width : 6 * width] = jnp.sum(dbo, axis=0, keepdims=True)

    steps = hidden // STEP
    for k in range(width // STEP):
        span = slice(k * STEP, (k + 1) * STEP)
        r.dmix[:, span] = dot(r.datt[...], r.w_out[span, :], NT).astype(BF16)
        slot = k % 2
        side_out(4, steps - 2 + slot, slot).wait()
        r.up_stage[slot] = dot(r.mixt[...], r.datt[:, span]).astype(BF16)
        side_out(8, k, slot).start()

    r.dqkv[...] = jnp.zeros_like(r.dqkv)

    def attend_back(pair, carry):
        for k, (start, low, high) in enumerate(groups):
            here = slice(start, start + window)
            q, key, v = (r.qkv[here, lanes(pair, part)] for part in range(3))
            dm = r.dmix[here, lanes(pair, 0)]
            key_t = key.T
            dq, dk, dv = [], None, None
            for half, (own_q, own_v, own_dm) in enumerate(zip(halves(q), halves(v), halves(dm))):
                prob = r.probs[(pair * 2 + half) * len(groups) + k]
                wide = prob.astype(F32)
                dprob = dot(own_v, dm, NT)
                product = wide * dprob
                ds = (product - wide * jnp.sum(product, axis=0, keepdims=True)).astype(BF16)
                dq.append(dot(key_t[half * 64 : half * 64 + 64], ds))
                one, two = dot(ds, own_q), dot(prob, own_dm)
                dk, dv = (one, two) if dk is None else (dk + one, dv + two)
            dq = jnp.concatenate(dq, axis=0).T * 0.125
            for part, value in enumerate((dq, dk, dv)):
                spot = lanes(pair, part)
                r.dqkv[here, spot] = r.dqkv[here, spot] + value.astype(BF16)
        return carry

    lax.fori_loop(0, pairs, attend_back, 0)

    for k in range(3 * width // STEP):
        span = slice(k * STEP, (k + 1) * STEP)
        block = r.dqkv[:, span]
        if not width <= k * STEP < 2 * width:
            at = 3 * width + k * STEP - (width if k * STEP >= width else 0)
            r.small[:, at : at + STEP] = jnp.sum(block.astype(F32), axis=0, keepdims=True)
        slot = (k + 1) % 2
        side_out(8, 0, slot).wait()
        r.up_stage[slot] = dot(r.n1t[...], block).astype(BF16)
        side_out(9, k, slot).start()

    for k in range(width // STEP):
        span = slice(k * STEP, (k + 1) * STEP)
        r.dn[:, span] = dot(r.dqkv[...], r.w_qkv[span, :], NT)

    def first_back(here, carry):
        back, dg, db = norm_back(r.x, g1, here)
        dout = r.dout[here, :].astype(F32)
        total = dout + r.between[here, :] + back
        sums = [carry[0] + dg, carry[1] + db]
        if is_router:
            slope = jnp.sum(dout * r.delta[here, :], axis=1, keepdims=True) * r.factor[here, :]
            total = total + slope * r.router[...]
            sums.append(carry[2] + fold(slope * r.x[here, :].astype(F32)))
        r.du[here, :] = total.astype(BF16)
        return tuple(sums)

    sums = row_loop(first_back, (zero,) * (3 if is_router else 2))
    r.small[:, :width] = jnp.sum(sums[0], axis=0, keepdims=True)
    r.small[:, 2 * width : 3 * width] = jnp.sum(sums[1], axis=0, keepdims=True)
    if is_router:
        r.router_grad[...] = jnp.sum(sums[2], axis=0, keepdims=True)
        spread(r.du, r.all_dout, None, r.shown_du)
    else:
        show(r.du, r.shown_du)
    for slot in range(2):
        down_out(0, slot).wait()
        side_out(4, 0, slot).wait()


def run_layer(layer, groups, window, x, code, vec, scale, own, far, rows_of, all_x=None, back=None, router=None):
    rows, width = x.shape
    hidden = own[2].shape[2]
    full, is_router = back is not None, router is not None
    inside = pl.BlockSpec(memory_space=pltpu.VMEM)
    anywhere = pl.BlockSpec(memory_space=pl.ANY)
    unsort, pick, unpick, skipped = rows_of
    args = [x, code[:, None], code[None, :], vec, scale[:, None], *own, *far, unsort]
    every = unsort.shape[0]
    if full:
        args += [back]
        if is_router:
            delta, factor, router_row = router
            args += [pick, unpick, skipped, delta, factor[:, None], router_row]
        outs = [((every, width), BF16), ((1, vec.shape[1]), F32), ((GRAD_ROWS, LANES), BF16)]
        outs += [((1, width), F32)] if is_router else [((rows, width), BF16)] * 2
    else:
        args += [all_x, unpick, skipped]
        outs = [((every, width), BF16), ((every, width), BF16), ((rows, width), F32)]
    in_specs = [inside] * 5 + [anywhere] * 8 + [inside] * (len(args) - 13)
    out_specs = [anywhere if full and k == 2 else inside for k in range(len(outs))]
    held = [
        ((width, 3 * width), BF16),
        ((width, width), BF16),
        ((width, hidden), BF16),
        ((hidden, width), BF16),
        None,
        ((rows, width), BF16),
        ((rows, 3 * width), BF16),
        ((HEADS * len(groups) if full else 1, window, window), BF16),
        ((len(groups), window, window), F32),
        ((rows, width), BF16),
        ((rows, width), F32),
        ((rows, width), BF16),
        ((rows, hidden), BF16),
    ]
    if full:
        held += [
            ((width, rows), BF16),
            ((width, rows), BF16),
            ((width, rows), BF16),
            ((rows, width), BF16),
            ((rows, hidden), BF16),
            ((rows, width), F32),
            ((rows, width), BF16),
            ((rows, width), BF16),
            ((rows, 3 * width), BF16),
            ((2, STEP, width), BF16),
            ((2, width, STEP), BF16),
        ]
        held += [((rows, width), BF16)] * (2 if is_router else 1)
    else:
        held += [((rows, width), BF16)]
    scratch = [pltpu.SemaphoreType.DMA((4,)) if one is None else pltpu.VMEM(*one) for one in held]
    if full:
        scratch += [pltpu.SemaphoreType.DMA((2,))] * 2
    flops = rows * width * (3 * width + width + 2 * hidden) * (6 if full else 2)
    return pl.pallas_call(
        functools.partial(layer_kernel, layer, groups, window, full, is_router),
        out_shape=[jax.ShapeDtypeStruct(*one) for one in outs],
        in_specs=in_specs,
        out_specs=out_specs,
        scratch_shapes=scratch,
        compiler_params=pltpu.CompilerParams(vmem_limit_bytes=60 * 1024 * 1024),
        cost_estimate=pl.CostEstimate(flops=flops, bytes_accessed=3 * 10**7, transcendentals=0),
        name="back" if full else "forward",
    )(*args)


def row_plan(crop_lengths, chosen):
    rows = chosen.shape[0]
    ends = jnp.cumsum(crop_lengths)
    starts = ends - crop_lengths
    is_long = crop_lengths == LONG
    long_before = jnp.cumsum(is_long.astype(jnp.int32)) - is_long
    short = jnp.where(is_long, 0, crop_lengths)
    short_before = jnp.cumsum(short) - short
    base = jnp.where(is_long, long_before * LONG, 2 * LONG + short_before)
    at = jnp.arange(rows, dtype=jnp.int32)
    inside = (at[:, None] >= starts[None]) & (at[:, None] < ends[None])
    target = at + jnp.sum(jnp.where(inside, (base - starts)[None], 0), axis=1)
    order = target[None, :] == at[:, None]
    code = jnp.sum((at[:, None] >= base[None]).astype(jnp.int32), axis=1)
    chosen_in = jnp.sum(jnp.where(order, chosen[None, :], 0), axis=1)
    rank = jnp.sum(jnp.where(at[:, None] > at[None, :], chosen_in[None, :], 0), axis=1)
    slot = jnp.arange(rows // 2, dtype=jnp.int32)
    pick = (rank[None, :] == slot[:, None]) & (chosen_in[None, :] == 1)
    routed_code = jnp.sum(jnp.where(pick, code[None, :], 0), axis=1)
    unsort = target[:, None] == at[None, :]
    at_slot = at[None, : rows // 2]
    unpick = (rank[:, None] == at_slot) & (chosen_in[:, None] == 1)
    skipped = (1 - chosen_in)[:, None].astype(F32)
    return order.astype(BF16), code, routed_code, (unsort.astype(BF16), pick.astype(BF16), unpick.astype(BF16), skipped)


def body(axis_of, tokens, lengths, route_mask, router_weight, gains, biases, w_qkv, w_out, w_up, w_down, cotangent):
    section = lax.axis_index("section")
    micro, rows, width = tokens.shape
    own = (w_qkv, w_out, w_up, w_down)
    far = tuple(other_core(value) for value in own)
    own_vec = jnp.concatenate([gains, biases], axis=1)
    far_vec = other_core(own_vec)
    vecs = [jnp.where(section == layer, own_vec, far_vec) for layer in range(2)]
    router_f = router_weight.astype(F32)

    def pick_micro(array):
        return lax.dynamic_index_in_dim(array, section, 0, False)

    crop_lengths, chosen = pick_micro(lengths)[0], pick_micro(route_mask)
    order, code, routed_code, rows_of = row_plan(crop_lengths, chosen)
    x = dot(order, pick_micro(tokens)).astype(BF16)
    cot = dot(order, pick_micro(cotangent)).astype(BF16)
    routed = dot(rows_of[1], x).astype(BF16)
    inputs_one = routed.astype(F32)
    held = (routed_code > 0).astype(F32)
    gate = jax.nn.sigmoid(jnp.sum(inputs_one * router_f[None, :], axis=1))
    scale_one = held * gate
    half = LONG // 2
    groups_one = [(0, 0, half), (96, half, 2 * half), (192, 2 * half, rows // 2)]
    groups_two = [(0, 0, LONG), (192, LONG, 2 * LONG), (384, 2 * LONG, rows)]

    y1, shown_y1, delta_one = run_layer(
        0, groups_one, 128, routed, routed_code, vecs[0], scale_one, own, far, rows_of, all_x=x
    )
    ones = jnp.ones((rows,), F32)
    shown_du2, small_two, grads_two, dout, shown_y2 = run_layer(
        1, groups_two, 256, y1, code, vecs[1], ones, own, far, rows_of, back=cot
    )
    factor = held * gate * (1.0 - gate)
    shown_du1, small_one, grads_one, grad_router = run_layer(
        0, groups_one, 128, routed, routed_code, vecs[0], scale_one, own, far, rows_of, back=dout,
        router=(delta_one, factor, router_f[None, :]),
    )
    small_one, small_two, grad_router = small_one[0], small_two[0], grad_router[0]

    micro_ids = jnp.arange(micro)
    here = (micro_ids == section).astype(F32)
    counts = here * jnp.sum(route_mask.astype(F32), axis=1)
    extra = jnp.concatenate([here * jnp.sum(scale_one), counts])
    shared = [grad_router, extra]
    small = jnp.stack([jnp.concatenate([part, *shared]) for part in (small_one, small_two)])
    room = -(-small.shape[1] // (8 * LANES)) * 8 * LANES
    small = jnp.pad(small, ((0, 0), (0, room - small.shape[1]))).reshape(2, room // LANES, LANES)
    sums, small, (activations, input_grads) = sum_gradients(
        axis_of, (grads_one, grads_two), small, (shown_y1, shown_y2, shown_du1, shown_du2)
    )
    down, up, out, qkv = (
        sums[first * LANES : last * LANES].astype(F32) for first, last in ((0, 4), (4, 8), (8, 9), (9, 12))
    )

    def beside(value):
        return jnp.concatenate(jnp.split(value, value.shape[0] // LANES, axis=0), axis=1)

    small = small.reshape(-1)
    span = small_one.shape[0]
    tail = small[span:]

    return (
        activations[None],
        input_grads[None],
        beside(qkv)[None],
        out[None],
        beside(up)[None],
        down[None],
        small[: 2 * width][None],
        small[2 * width : span][None],
        tail[:width],
        tail[width : width + micro] / tail[width + micro : width + 2 * micro],
    )


def solution(mesh):
    in_specs = (
        P(None, "dp", None),
        P(None, "dp", None),
        P(None, "dp"),
        P(),
        P("section", None),
        P("section", None),
        P("section", None, None),
        P("section", None, None),
        P("section", None, None),
        P("section", None, None),
        P(None, "dp", None),
    )
    out_specs = (
        P("section", None, "dp", None),
        P("section", None, "dp", None),
        P("section", None, None),
        P("section", None, None),
        P("section", None, None),
        P("section", None, None),
        P("section", None),
        P("section", None),
        P(),
        P(),
    )
    step = functools.partial(body, axis_bits(mesh))
    return jax.shard_map(step, mesh=mesh, in_specs=in_specs, out_specs=out_specs, check_vma=False)
```

```python
import functools

import jax
import jax.numpy as jnp
from jax import lax
from jax.experimental import pallas as pl
from jax.experimental.pallas import tpu as pltpu
from jax.sharding import PartitionSpec as P

HEADS = 12
HEAD = 64
LONG = 197
F32 = jnp.float32
BF16 = jnp.bfloat16
NT = (((1,), (1,)), ((), ()))
TN = (((0,), (0,)), ((), ()))
NN = (((1,), (0,)), ((), ()))


LANES = 768
TILE = 16
GRAD_ROWS = 12 * LANES


def axis_bits(mesh):
    line = mesh.devices[0]
    bits = len(line).bit_length() - 1
    try:
        spots = [tuple(device.coords) for device in line]
    except AttributeError:
        return [0] * bits
    return [
        next((w for w in range(3) if spots[1 << b][w] != spots[0][w]), 0) for b in range(bits)
    ]


def sum_plan(axis_of):
    bits = len(axis_of)
    lists = {}
    for bit, axis in enumerate(axis_of):
        lists.setdefault(axis, []).append(bit)
    lists = sorted(lists.values(), key=len)
    while len(lists) < 3:
        lists.append([])
    one, two, three = lists[:3]
    three = three + sum(lists[3:], [])
    orders = [one + three + two, two + three + one, one + two + three, two + one + three]
    sizes = [512, 512, 256, 256]
    if any(size % (TILE << bits) for size in sizes) or GRAD_ROWS % sum(sizes):
        sizes = [TILE << bits] * 2
    groups, start = [], 0
    while start < GRAD_ROWS:
        group = []
        for size, order in zip(sizes, orders):
            if start < GRAD_ROWS:
                group.append((start, size, order))
                start += size
        groups.append(group)
    return groups, start


def add_rows(into, into_start, source, start, other, other_start, count):
    tile = next(t for t in (64, 32, 16) if count % t == 0)

    def step(k, carry):
        target, here, there = (
            pl.ds(pl.multiple_of(first + k * tile, TILE), tile) for first in (into_start, start, other_start)
        )
        into[target, :] = source[here, :] + other[there, :]
        return carry

    lax.fori_loop(0, count // tile, step, 0)


class Names:
    pass


def copy_far(source, target, one, two, friend):
    return pltpu.make_async_remote_copy(
        src_ref=source,
        dst_ref=target,
        send_sem=one,
        recv_sem=two,
        device_id=friend,
        device_id_type=pl.DeviceIdType.MESH,
    )


def at_core(core, index, step):
    pl.when(core == index)(step)


GRAD_TILES = 36


class Sums:
    def __init__(self, groups, given):
        self.groups = groups
        self.chunks = [chunk for group in groups for chunk in group]
        self.bits = bits = len(self.chunks[0][2])
        self.first_of = [0]
        for group in groups:
            self.first_of.append(self.first_of[-1] + len(group))
        self.acc, self.mate = next(given), next(given)
        self.got = [next(given) for _ in range(bits)]
        self.small_got, self.small = next(given), next(given)
        self.load_sem, self.mate_sem, self.swap_send, self.swap_recv, self.shard_sem = (next(given) for _ in range(5))
        self.send, self.recv, self.back_send, self.back_recv = (next(given) for _ in range(4))
        self.small_send, self.small_recv = (next(given) for _ in range(2))
        self.shown_sem, self.shown_send, self.shown_recv = (next(given) for _ in range(3))
        self.tile_recv = next(given)
        self.core = lax.axis_index("section")
        self.me = lax.axis_index("dp")
        self.across = (1 - self.core, self.me)
        self.last = len(groups) + 2 * bits

    @staticmethod
    def scratch(groups, total, small_rows):
        bits = len(groups[0][0][2])
        count = sum(len(group) for group in groups)
        largest = max(chunk[1] for group in groups for chunk in group)
        most = max(len(group) for group in groups)
        held = [pltpu.VMEM((total, LANES), BF16), pltpu.VMEM((most, largest, LANES), BF16)]
        held += [pltpu.VMEM((total >> (depth + 1), LANES), BF16) for depth in range(bits)]
        held += [pltpu.VMEM((bits + 1, small_rows, LANES), F32), pltpu.VMEM((2, small_rows, LANES), F32)]
        held += [pltpu.SemaphoreType.DMA((count,))] * 5
        held += [pltpu.SemaphoreType.DMA((count, bits))] * 4
        held += [pltpu.SemaphoreType.DMA((bits + 1,))] * 2
        held += [pltpu.SemaphoreType.DMA((2,))] * 3
        return held + [pltpu.SemaphoreType.DMA((GRAD_TILES,))]

    def bit_at(self, bit):
        return lax.rem(self.me // (1 << bit), 2)

    def partner(self, bit):
        return (self.core, self.me + (1 - 2 * self.bit_at(bit)) * (1 << bit))

    def open(self):
        friends = [self.across] + [self.partner(bit) for bit in range(self.bits)]
        barrier = pltpu.get_barrier_semaphore()
        for friend in friends:
            pl.semaphore_signal(barrier, inc=1, device_id=friend, device_id_type=pl.DeviceIdType.MESH)
        pl.semaphore_wait(barrier, len(friends))
        total_rows = self.acc.shape[0]
        if total_rows > GRAD_ROWS:
            self.acc[GRAD_ROWS:, :] = jnp.zeros((total_rows - GRAD_ROWS, LANES), BF16)

    def members(self, group):
        return range(self.first_of[group], self.first_of[group + 1]) if 0 <= group < len(self.groups) else range(0)

    def rows_of(self, k):
        start, size, _ = self.chunks[k]
        return pl.ds(start, min(size, GRAD_ROWS - start))

    def swap(self, k):
        rows = self.rows_of(k)
        return copy_far(
            self.grads[1].at[rows, :], self.landed.at[rows, :], self.swap_send.at[k], self.swap_recv.at[k], self.across
        )

    def load(self, layer, k):
        rows = self.rows_of(k)
        return pltpu.make_async_copy(self.grads[layer].at[rows, :], self.acc.at[rows, :], self.load_sem.at[k])

    def load_mate(self, k):
        rows = self.rows_of(k)
        slot = self.mate.at[k % self.mate.shape[0], pl.ds(0, rows.size), :]
        return pltpu.make_async_copy(self.landed.at[rows, :], slot, self.mate_sem.at[k])

    def span(self, k, depth):
        start, size, order = self.chunks[k]
        for bit in order[:depth]:
            size //= 2
            start = start + self.bit_at(bit) * size
        return start, size

    def down(self, k, depth):
        bit = self.chunks[k][2][depth]
        start, size = self.span(k, depth)
        size //= 2
        away = pl.multiple_of(start + (1 - self.bit_at(bit)) * size, TILE)
        return copy_far(
            self.acc.at[pl.ds(away, size), :],
            self.got[depth].at[pl.ds(self.chunks[k][0] >> (depth + 1), size), :],
            self.send.at[k, depth],
            self.recv.at[k, depth],
            self.partner(bit),
        )

    def shard(self, k):
        start, size = self.span(k, self.bits)
        here = pl.ds(pl.multiple_of(start, TILE), size)
        return pltpu.make_async_copy(self.acc.at[here, :], self.out.at[here, :], self.shard_sem.at[k])

    def up(self, k, depth):
        bit = self.chunks[k][2][depth]
        start, size = self.span(k, depth + 1)
        here = pl.ds(pl.multiple_of(start, TILE), size)
        source = self.acc if depth == self.bits - 1 else self.out
        return copy_far(
            source.at[here, :], self.out.at[here, :], self.back_send.at[k, depth], self.back_recv.at[k, depth],
            self.partner(bit),
        )

    def start_swaps(self, group):
        def step():
            for k in self.members(group):
                self.swap(k).start()

        at_core(self.core, 0, step)

    def begin(self, layer, group):
        for k in self.members(group):
            self.load(layer, k).start()

    def fetch(self, layer, group):
        for k in self.members(group):
            if layer == 1:
                self.swap(k).wait_recv()
            self.load_mate(k).start()

    def moment(self, now, before=None):
        bits = self.bits
        stages = 2 * bits + 1
        for k in self.members(now):
            self.load(1, k).wait()
            self.load_mate(k).wait()
            rows = self.rows_of(k)
            add_rows(self.acc, rows.start, self.acc, rows.start, self.mate.at[k % self.mate.shape[0]], 0, rows.size)
            self.down(k, 0).start()
        before(now)
        for stage in range(stages - 1, 0, -1):
            for k in self.members(now - stage):
                if stage <= bits:
                    depth = stage - 1
                    self.down(k, depth).wait_recv()
                    start, size = self.span(k, stage)
                    add_rows(self.acc, start, self.acc, start, self.got[depth], self.chunks[k][0] >> stage, size)
                    if stage < bits:
                        self.down(k, stage).start()
                    else:
                        self.up(k, bits - 1).start()
                        self.shard(k).start()
                else:
                    depth = 2 * bits - stage
                    self.up(k, depth).wait_recv()
                    if depth == bits - 1:
                        self.shard(k).wait()
                    if depth > 0:
                        self.up(k, depth - 1).start()

    def run(self, layer, now):
        def before(moment):
            self.begin(layer, moment + 2)

        self.moment(now, before)
        self.fetch(layer, now + 1)

    def run_any(self, now):
        def before(moment):
            if self.members(moment + 2):
                for layer in range(2):
                    at_core(self.core, layer, functools.partial(self.begin, layer, moment + 2))

        self.moment(now, before)
        if self.members(now + 1):
            for layer in range(2):
                at_core(self.core, layer, functools.partial(self.fetch, layer, now + 1))

    def small_step(self, k):
        friend = self.across if k == 0 else self.partner(k - 1)
        return copy_far(
            self.small_out, self.small_got.at[k], self.small_send.at[k], self.small_recv.at[k], friend
        )

    def small_begin(self):
        for layer in range(2):

            def step(layer=layer):
                self.small_out[...] = self.small[layer]
                copy_far(
                    self.small.at[1 - layer], self.small_got.at[0], self.small_send.at[0], self.small_recv.at[0],
                    self.across,
                ).start()

            at_core(self.core, layer, step)

    def small_turn(self, k):
        self.small_step(k).wait()
        self.small_out[...] = self.small_out[...] + self.small_got[k]
        if k < self.bits:
            self.small_step(k + 1).start()

    def shown_keep(self, layer, k):
        return pltpu.make_async_copy(self.shown[2 * k + layer], self.shown_out[k].at[self.core], self.shown_sem.at[k])

    def shown_give(self, layer, k):
        return copy_far(
            self.shown[2 * k + 1 - layer], self.shown_out[k].at[self.core], self.shown_send.at[k],
            self.shown_recv.at[k], self.across,
        )

    def show(self):
        for layer in range(2):

            def step(layer=layer):
                for k in range(2):
                    self.shown_keep(layer, k).start()
                    self.shown_give(layer, k).start()

            at_core(self.core, layer, step)

    def close(self):
        for k in range(2):
            self.shown_keep(0, k).wait()
            self.shown_give(0, k).wait()

        def sent():
            for k in range(len(self.chunks)):
                self.swap(k).wait_send()

        at_core(self.core, 0, sent)
        for k in range(len(self.chunks)):
            for depth in range(self.bits):
                self.down(k, depth).wait_send()
                self.up(k, depth).wait_send()


def cast_kernel(source, qkv, out, up, down, low, high, in_sem, out_sem):
    rows = low.shape[1]
    per = LANES // rows
    slots = low.shape[0]
    count = 12 * per

    def take(k):
        return pltpu.make_async_copy(source.at[pl.ds(k * rows, rows), :], low.at[k % slots], in_sem.at[k % slots])

    def give(k):
        block, part = divmod(k, per)
        if block < 4:
            target = down.at[0, pl.ds(k * rows, rows), :]
        elif block < 8:
            target = up.at[0, pl.ds(part * rows, rows), pl.ds((block - 4) * LANES, LANES)]
        elif block < 9:
            target = out.at[0, pl.ds(part * rows, rows), :]
        else:
            target = qkv.at[0, pl.ds(part * rows, rows), pl.ds((block - 9) * LANES, LANES)]
        return pltpu.make_async_copy(high.at[k % slots], target, out_sem.at[k % slots])

    for k in range(slots):
        take(k).start()
    for k in range(count):
        take(k).wait()
        if k >= slots:
            give(k - slots).wait()
        high[k % slots] = low[k % slots].astype(F32)
        give(k).start()
        if k + slots < count:
            take(k + slots).start()
    for k in range(count - slots, count):
        give(k).wait()


def cast_sums(sums, shapes):
    anywhere = pl.BlockSpec(memory_space=pl.ANY)
    return pl.pallas_call(
        cast_kernel,
        out_shape=[jax.ShapeDtypeStruct(shape, F32) for shape in shapes],
        in_specs=[anywhere],
        out_specs=[anywhere] * 4,
        scratch_shapes=[
            pltpu.VMEM((6, 256, LANES), BF16),
            pltpu.VMEM((6, 256, LANES), F32),
            pltpu.SemaphoreType.DMA((6,)),
            pltpu.SemaphoreType.DMA((6,)),
        ],
        compiler_params=pltpu.CompilerParams(vmem_limit_bytes=32 * 1024 * 1024),
        cost_estimate=pl.CostEstimate(flops=0, bytes_accessed=42 * 10**6, transcendentals=0),
        name="cast",
    )(sums)


def other_core(value):
    return lax.ppermute(value, "section", [(0, 1), (1, 0)])


STEP = 256
ROW_TILE = 64
NEGATIVE = -1e30


def dot(left, right, dims=NN):
    return lax.dot_general(left, right, dims, preferred_element_type=F32)


def gelu_parts(pre):
    bell = jnp.exp(pre * pre * -0.5)
    t = pl.reciprocal(1.0 + jnp.abs(pre) * (0.3275911 * 0.7071067811865476))
    poly = t * (0.1274147960 + t * (-0.142248368 + t * (0.710706871 + t * (-0.7265760135 + t * 0.5307027145))))
    tail = poly * bell
    return jnp.where(pre >= 0.0, 1.0 - tail, tail), bell


def norm_stats(values):
    centred = values - jnp.mean(values, axis=-1, keepdims=True)
    recip = lax.rsqrt(jnp.mean(centred * centred, axis=-1, keepdims=True) + 1e-06)
    return centred * recip, recip


def fold(tile):
    return jnp.sum(tile.reshape(tile.shape[0] // 8, 8, tile.shape[1]), axis=0)


def layer_kernel(layer, groups, window, full, *refs):
    r = Names()
    given = iter(refs)
    r.x, r.col_code, r.row_code, r.vec, r.scale = (next(given) for _ in range(5))
    r.own = [next(given) for _ in range(4)]
    r.far = [next(given) for _ in range(4)]
    r.unsort = next(given)
    if full:
        r.dout = next(given)
        r.shown_du, r.small, r.grads, r.du, r.shown_y = (next(given) for _ in range(5))
    else:
        r.all_x, r.unpick, r.skipped = (next(given) for _ in range(3))
        r.all_y, r.shown_y, r.delta = (next(given) for _ in range(3))
    r.weights = [next(given) for _ in range(4)]
    r.w_sem, r.n1, r.qkv, r.probs, r.mask, r.mix, r.between, r.n2, r.act = (next(given) for _ in range(9))
    if full:
        back_names(r, given)
    r.y = next(given)
    layer_body(r, layer, groups, window, full, False)


def back_names(r, given):
    r.n1t, r.n2t, r.mixt, r.dmlp, r.dpre, r.dn, r.datt, r.dmix, r.dqkv = (next(given) for _ in range(9))
    r.down_stage, r.up_stage, r.down_sem, r.up_sem = (next(given) for _ in range(4))


def fused_kernel(groups, window, sum_groups, *refs):
    r = Names()
    given = iter(refs)
    r.x, r.col_code, r.row_code, r.vec, r.scale = (next(given) for _ in range(5))
    r.own = [next(given) for _ in range(4)]
    r.far = [next(given) for _ in range(4)]
    r.unsort = next(given)
    r.all_dout, r.pick, r.unpick, r.skipped, r.delta, r.factor, r.router = (next(given) for _ in range(7))
    second, second_small, extra = (next(given) for _ in range(3))
    shown = [next(given) for _ in range(3)]
    out, landed, first, small_out = (next(given) for _ in range(4))
    shown_out = [next(given) for _ in range(2)]
    r.weights = [next(given) for _ in range(2)]
    r.w_sem, r.n1, r.qkv, r.probs, r.mask, r.mix, r.between, r.n2 = (next(given) for _ in range(8))
    back_names(r, given)
    r.dout, r.du, r.shown_du, r.small, r.router_grad = (next(given) for _ in range(5))
    r.up_tile, r.down_tile, r.tile_sem = (next(given) for _ in range(3))
    sums = Sums(sum_groups, given)
    sums.grads, sums.landed, sums.out, sums.small_out = (first, second), landed, out, small_out
    sums.shown, sums.shown_out = (shown[0], shown[1], r.shown_du, shown[2]), shown_out
    r.grads = first
    core = sums.core
    sums.open()
    sums.start_swaps(0)
    sums.start_swaps(1)

    def begin():
        sums.begin(1, 0)
        sums.begin(1, 1)
        sums.fetch(1, 0)

    at_core(core, 1, begin)
    early = [0]

    def hook():
        now = early[0]
        sums.start_swaps(now + 2)
        at_core(core, 1, functools.partial(sums.run, 1, now))
        early[0] = now + 1

    def tile_out(stage, row, column, shape, sem, tile):
        area = (pl.ds(row, shape[0]), pl.ds(column, shape[1]))

        def keep():
            pltpu.make_async_copy(stage, first.at[area], sem).start()

        def give():
            copy_far(stage, landed.at[area], sem, sums.tile_recv.at[tile], sums.across).start()

        at_core(core, 0, keep)
        at_core(core, 1, give)

    r.hook, r.tile_out = hook, tile_out
    layer_body(r, 0, groups, window, True, True)

    for index, source in enumerate((r.small, second_small)):
        for row in range(source.shape[1] // LANES):
            sums.small[index, row : row + 1, :] = source[:, row * LANES : (row + 1) * LANES]
        row = source.shape[1] // LANES
        sums.small[index, row : row + 1, :] = r.router_grad[...]
        sums.small[index, row + 1 : row + 2, :] = extra[...]
        left = sums.small.shape[1] - row - 2
        sums.small[index, row + 2 :, :] = jnp.zeros((left, LANES), F32)
    sums.small_begin()
    sums.show()

    def landed_all():
        for tile in range(GRAD_TILES):
            shape = (STEP, LANES) if tile < 12 else (LANES, STEP)
            area = landed.at[pl.ds(0, shape[0]), pl.ds(0, shape[1])]
            copy_far(area, area, sums.tile_recv.at[tile], sums.tile_recv.at[tile], sums.across).wait_recv()
        sums.begin(0, 0)
        sums.begin(0, 1)
        sums.fetch(0, 0)
        for now in range(min(early[0], sums.last)):
            sums.run(0, now)

    at_core(core, 0, landed_all)
    for turn, now in enumerate(range(early[0], max(sums.last, early[0] + sums.bits + 1))):
        if now < sums.last:
            sums.run_any(now)
        if turn <= sums.bits:
            sums.small_turn(turn)
    sums.close()


def layer_body(r, layer, groups, window, full, is_router):
    hook = r.hook if is_router else lambda: None
    rows, width = r.x.shape
    hidden = r.own[2].shape[2]
    core = lax.axis_index("section")
    pairs = width // 128

    kept = {0: 0, 1: 1, 2: 2, 3: 3} if not is_router else {0: 0, 1: 1}

    def weight(which, source):
        return pltpu.make_async_copy(source[which].at[0], r.weights[which], r.w_sem.at[which])

    def up_tile(source, k, slot):
        span = pl.ds(pl.multiple_of(k * STEP, STEP), STEP)
        return pltpu.make_async_copy(source[2].at[0, :, span], r.up_tile.at[slot], r.tile_sem.at[0, slot])

    def down_tile(source, k, slot):
        span = pl.ds(pl.multiple_of(k * STEP, STEP), STEP)
        return pltpu.make_async_copy(source[3].at[0, span, :], r.down_tile.at[slot], r.tile_sem.at[1, slot])

    def start_tiles(k, slot):
        for near, source in ((core == layer, r.own), (core != layer, r.far)):

            @pl.when(near)
            def _():
                up_tile(source, k, slot).start()
                down_tile(source, k, slot).start()

    for near, source in ((core == layer, r.own), (core != layer, r.far)):

        @pl.when(near)
        def _():
            for which in kept:
                weight(which, source).start()

    if is_router:
        start_tiles(0, 0)
        start_tiles(1, 1)

    def vec(start, count=width):
        return r.vec[:, start : start + count]

    g1, g2, b1, bq, bv, bo, b2 = (vec(k * width) for k in range(7))
    bu_at, bd_at = 7 * width, 7 * width + hidden

    def row_loop(step, init=0):
        def at(k, carry):
            return step(pl.ds(pl.multiple_of(k * ROW_TILE, ROW_TILE), ROW_TILE), carry)

        return lax.fori_loop(0, rows // ROW_TILE, at, init)

    def norm_step(source, gain, bias, target):
        def step(here, carry):
            normal, _ = norm_stats(source[here, :].astype(F32))
            target[here, :] = (normal * gain + bias).astype(BF16)
            return carry

        return step

    def tiles(step):
        for k in range(width // STEP):
            step(slice(k * STEP, (k + 1) * STEP))

    def show(source, target):
        def step(span):
            target[:, span] = dot(r.unsort[...], source[:, span]).astype(BF16)

        tiles(step)

    def spread(routed, others, target, shown):
        def step(span):
            value = dot(r.unpick[...], routed[:, span]) + others[:, span].astype(F32) * r.skipped[...]
            if target is not None:
                target[:, span] = value.astype(BF16)
            shown[:, span] = dot(r.unsort[...], value.astype(BF16)).astype(BF16)

        tiles(step)

    row_loop(norm_step(r.x, g1, b1, r.n1))
    if full and is_router:

        def route_step(span):
            r.dout[:, span] = dot(r.pick[...], r.all_dout[:, span]).astype(BF16)

        tiles(route_step)
    if full:

        def delta_step(here, carry):
            low = (r.dout[here, :].astype(F32) * r.scale[here, :]).astype(BF16)
            r.dmlp[here, :] = low
            return carry + fold(low.astype(F32))

        dbd = row_loop(delta_step, jnp.zeros((8, width), F32))
        r.small[:, bd_at:] = jnp.sum(dbd, axis=0, keepdims=True)

    for k, (start, low, high) in enumerate(groups):
        col = r.col_code[start : start + window, :]
        row = r.row_code[:, start : start + window]
        place = lax.broadcasted_iota(jnp.int32, (window, 1), 0) + start
        col = jnp.where((place >= low) & (place < high), col, -1)
        r.mask[k] = jnp.where(col == row, 0.0, NEGATIVE)

    weight(0, r.own).wait()
    for k in range(3 * width // STEP):
        span = slice(k * STEP, (k + 1) * STEP)
        value = dot(r.n1[...], r.weights[0][:, span])
        if k < width // STEP:
            value = (value + bq[:, span]).astype(BF16).astype(F32) * 0.125
        elif k >= 2 * width // STEP:
            value = value + bv[:, k * STEP - 2 * width : (k + 1) * STEP - 2 * width]
        r.qkv[:, span] = value.astype(BF16)

    hook()
    lane = lax.broadcasted_iota(jnp.int32, (1, 128), 1)

    def halves(block):
        zero = jnp.zeros_like(block)
        return jnp.where(lane < 64, block, zero), jnp.where(lane < 64, zero, block)

    r.mix[...] = jnp.zeros_like(r.mix)

    def lanes(pair, part):
        return pl.ds(pl.multiple_of(pair * 128 + part * width, 128), 128)

    def attend(pair, carry):
        for k, (start, low, high) in enumerate(groups):
            here = slice(start, start + window)
            q, key, v = (r.qkv[here, lanes(pair, part)] for part in range(3))
            vt = v.T
            place = lax.broadcasted_iota(jnp.int32, (1, window), 1) + start
            valid = (place >= low) & (place < high)
            parts = []
            for half, own_key in enumerate(halves(key)):
                scores = dot(own_key, q, NT) + r.mask[k]
                power = jnp.exp(scores - jnp.max(scores, axis=0, keepdims=True))
                total = jnp.sum(power, axis=0, keepdims=True)
                prob = (power * jnp.where(valid, 1.0 / total, 0.0)).astype(BF16)
                if full:
                    r.probs[(pair * 2 + half) * len(groups) + k] = prob
                parts.append(dot(vt[half * 64 : half * 64 + 64], prob))
            mixed = jnp.concatenate(parts, axis=0).T.astype(BF16)
            r.mix[here, lanes(pair, 0)] = r.mix[here, lanes(pair, 0)] + mixed
        return carry

    lax.fori_loop(0, pairs, attend, 0)
    hook()

    weight(1, r.own).wait()
    for k in range(width // STEP):
        span = slice(k * STEP, (k + 1) * STEP)
        value = dot(r.mix[...], r.weights[1][:, span]) + bo[:, span]
        r.between[:, span] = r.x[:, span].astype(F32) + value
    row_loop(norm_step(r.between, g2, b2, r.n2))
    if full:
        r.n1t[...] = r.n1[...].T
        r.n2t[...] = r.n2[...].T
        r.mixt[...] = r.mix[...].T

    if not is_router:
        weight(2, r.own).wait()
        weight(3, r.own).wait()

    def tile_out(stage, row, column, shape, sem, tile):
        target = r.grads.at[pl.ds(row, shape[0]), pl.ds(column, shape[1])]
        pltpu.make_async_copy(stage, target, sem).start()

    tile_out = r.tile_out if is_router else tile_out

    def down_out(k, slot):
        tile_out(
            r.down_stage.at[slot], pl.multiple_of(k * STEP, STEP), 0, (STEP, width), r.down_sem.at[slot], k
        )

    def side_out(block, k, slot):
        row = pl.multiple_of((block + k // 3) * width, width)
        column = pl.multiple_of(k % 3 * STEP, STEP)
        tile = k + {4: 12, 8: 24, 9: 27}[block]
        tile_out(r.up_stage.at[slot], row, column, (width, STEP), r.up_sem.at[slot], tile)

    def down_free(slot):
        target = r.grads.at[pl.ds(0, STEP), pl.ds(0, width)]
        pltpu.make_async_copy(r.down_stage.at[slot], target, r.down_sem.at[slot]).wait()

    def side_free(slot):
        target = r.grads.at[pl.ds(0, width), pl.ds(0, STEP)]
        pltpu.make_async_copy(r.up_stage.at[slot], target, r.up_sem.at[slot]).wait()

    def hidden_step(k, carry):
        at = pl.multiple_of(k * STEP, STEP)
        span = pl.ds(at, STEP)
        slot = lax.rem(k, 2)
        if is_router:
            up_tile(r.own, k, slot).wait()
            down_tile(r.own, k, slot).wait()
            w_up, w_down = r.up_tile[slot], r.down_tile[slot]
        else:
            w_up, w_down = r.weights[2][:, span], r.weights[3][span, :]
        pre = dot(r.n2[...], w_up) + r.vec[:, pl.ds(at + bu_at, STEP)]
        cdf, bell = gelu_parts(pre)
        act = (pre * cdf).astype(BF16)
        if not is_router:
            r.act[:, span] = act
        if full:

            @pl.when(k >= 2)
            def _():
                down_free(slot)
                side_free(slot)

            slope = cdf + pre * bell * 0.3989422804014327
            dact = dot(r.dmlp[...], w_down, NT)
            dpre = (dact * slope).astype(BF16)
            if is_router:
                r.dn[...] = r.dn[...] + dot(dpre, w_up, NT)
            else:
                r.dpre[:, span] = dpre
            r.small[:, pl.ds(at + bu_at, STEP)] = jnp.sum(dpre.astype(F32), axis=0, keepdims=True)
            r.down_stage[slot] = dot(act, r.dmlp[...], TN).astype(BF16)
            down_out(k, slot)
            r.up_stage[slot] = dot(r.n2t[...], dpre).astype(BF16)
            side_out(4, k, slot)
        if is_router:

            @pl.when(k + 2 < hidden // STEP)
            def _():
                start_tiles(k + 2, slot)

        return carry

    steps = hidden // STEP
    if is_router:
        r.dn[...] = jnp.zeros_like(r.dn)
        for part in range(3):
            lax.fori_loop(part * steps // 3, (part + 1) * steps // 3, hidden_step, 0)
            hook()
    else:
        lax.fori_loop(0, steps, hidden_step, 0)
    if not (full and is_router):
        for k in range(width // STEP):
            span = slice(k * STEP, (k + 1) * STEP)
            value = dot(r.act[...], r.weights[3][:, span]) + vec(bd_at)[:, span]
            source = r.x[:, span].astype(F32)
            value = r.between[:, span] - source + value
            if not full:
                r.delta[:, span] = value
            r.y[:, span] = (source + r.scale[...] * value).astype(BF16)
    if not full:
        spread(r.y, r.all_x, r.all_y, r.shown_y)
        return
    if not is_router:
        show(r.y, r.shown_y)

    if not is_router:
        for k in range(width // STEP):
            span = slice(k * STEP, (k + 1) * STEP)
            r.dn[:, span] = dot(r.dpre[...], r.weights[2][span, :], NT)

    def norm_back(source, gain, here):
        normal, recip = norm_stats(source[here, :].astype(F32))
        grad = r.dn[here, :]
        hat = grad * gain
        back = recip * (
            hat - jnp.mean(hat, axis=-1, keepdims=True) - normal * jnp.mean(hat * normal, axis=-1, keepdims=True)
        )
        return back, fold(grad * normal), fold(grad)

    def second_back(here, carry):
        back, dg, db = norm_back(r.between, g2, here)
        r.between[here, :] = back
        total = (r.dout[here, :].astype(F32) * r.scale[here, :] + back).astype(BF16)
        r.datt[here, :] = total
        return carry[0] + dg, carry[1] + db, carry[2] + fold(total.astype(F32))

    zero = jnp.zeros((8, width), F32)
    dg2, db2, dbo = row_loop(second_back, (zero, zero, zero))
    r.small[:, width : 2 * width] = jnp.sum(dg2, axis=0, keepdims=True)
    r.small[:, 6 * width : 7 * width] = jnp.sum(db2, axis=0, keepdims=True)
    r.small[:, 5 * width : 6 * width] = jnp.sum(dbo, axis=0, keepdims=True)

    for k in range(width // STEP):
        span = slice(k * STEP, (k + 1) * STEP)
        r.dmix[:, span] = dot(r.datt[...], r.weights[1][span, :], NT).astype(BF16)
        slot = k % 2
        side_free(slot)
        r.up_stage[slot] = dot(r.mixt[...], r.datt[:, span]).astype(BF16)
        side_out(8, k, slot)
    hook()

    r.dqkv[...] = jnp.zeros_like(r.dqkv)

    def attend_back(pair, carry):
        for k, (start, low, high) in enumerate(groups):
            here = slice(start, start + window)
            q, key, v = (r.qkv[here, lanes(pair, part)] for part in range(3))
            dm = r.dmix[here, lanes(pair, 0)]
            key_t = key.T
            dq, dk, dv = [], None, None
            for half, (own_q, own_v, own_dm) in enumerate(zip(halves(q), halves(v), halves(dm))):
                prob = r.probs[(pair * 2 + half) * len(groups) + k]
                wide = prob.astype(F32)
                dprob = dot(own_v, dm, NT)
                product = wide * dprob
                ds = (product - wide * jnp.sum(product, axis=0, keepdims=True)).astype(BF16)
                dq.append(dot(key_t[half * 64 : half * 64 + 64], ds))
                one, two = dot(ds, own_q), dot(prob, own_dm)
                dk, dv = (one, two) if dk is None else (dk + one, dv + two)
            dq = jnp.concatenate(dq, axis=0).T * 0.125
            for part, value in enumerate((dq, dk, dv)):
                spot = lanes(pair, part)
                r.dqkv[here, spot] = r.dqkv[here, spot] + value.astype(BF16)
        return carry

    lax.fori_loop(0, pairs, attend_back, 0)
    hook()

    for k in range(3 * width // STEP):
        span = slice(k * STEP, (k + 1) * STEP)
        block = r.dqkv[:, span]
        if not width <= k * STEP < 2 * width:
            at = 3 * width + k * STEP - (width if k * STEP >= width else 0)
            r.small[:, at : at + STEP] = jnp.sum(block.astype(F32), axis=0, keepdims=True)
        slot = (k + 1) % 2
        side_free(slot)
        r.up_stage[slot] = dot(r.n1t[...], block).astype(BF16)
        side_out(9, k, slot)

    for k in range(width // STEP):
        span = slice(k * STEP, (k + 1) * STEP)
        r.dn[:, span] = dot(r.dqkv[...], r.weights[0][span, :], NT)

    def first_back(here, carry):
        back, dg, db = norm_back(r.x, g1, here)
        dout = r.dout[here, :].astype(F32)
        total = dout + r.between[here, :] + back
        sums = [carry[0] + dg, carry[1] + db]
        if is_router:
            slope = jnp.sum(dout * r.delta[here, :], axis=1, keepdims=True) * r.factor[here, :]
            total = total + slope * r.router[...]
            sums.append(carry[2] + fold(slope * r.x[here, :].astype(F32)))
        r.du[here, :] = total.astype(BF16)
        return tuple(sums)

    sums = row_loop(first_back, (zero,) * (3 if is_router else 2))
    r.small[:, :width] = jnp.sum(sums[0], axis=0, keepdims=True)
    r.small[:, 2 * width : 3 * width] = jnp.sum(sums[1], axis=0, keepdims=True)
    if is_router:
        r.router_grad[...] = jnp.sum(sums[2], axis=0, keepdims=True)
        spread(r.du, r.all_dout, None, r.shown_du)
    else:
        show(r.du, r.shown_du)
    for slot in range(2):
        down_free(slot)
        side_free(slot)


def front_scratch(rows, width, hidden, groups, window, full, kept):
    sizes = [(width, 3 * width), (width, width), (width, hidden), (hidden, width)][:kept]
    held = [pltpu.VMEM(size, BF16) for size in sizes]
    held += [pltpu.SemaphoreType.DMA((4,))]
    held += [pltpu.VMEM((rows, width), BF16), pltpu.VMEM((rows, 3 * width), BF16)]
    held += [pltpu.VMEM((HEADS * len(groups) if full else 1, window, window), BF16)]
    held += [pltpu.VMEM((len(groups), window, window), F32), pltpu.VMEM((rows, width), BF16)]
    return held + [pltpu.VMEM((rows, width), F32), pltpu.VMEM((rows, width), BF16)]


def back_scratch(rows, width, hidden):
    held = [pltpu.VMEM((width, rows), BF16)] * 3 + [pltpu.VMEM((rows, width), BF16)]
    held += [pltpu.VMEM((rows, hidden), BF16), pltpu.VMEM((rows, width), F32)]
    held += [pltpu.VMEM((rows, width), BF16)] * 2 + [pltpu.VMEM((rows, 3 * width), BF16)]
    held += [pltpu.VMEM((2, STEP, width), BF16), pltpu.VMEM((2, width, STEP), BF16)]
    return held + [pltpu.SemaphoreType.DMA((2,))] * 2


def run_layer(layer, groups, window, x, code, vec, scale, own, far, rows_of, all_x=None, back=None):
    rows, width = x.shape
    hidden = own[2].shape[2]
    full = back is not None
    inside = pl.BlockSpec(memory_space=pltpu.VMEM)
    anywhere = pl.BlockSpec(memory_space=pl.ANY)
    unsort, pick, unpick, skipped = rows_of
    args = [x, code[:, None], code[None, :], vec, scale[:, None], *own, *far, unsort]
    every = unsort.shape[0]
    if full:
        args += [back]
        outs = [((every, width), BF16), ((1, vec.shape[1]), F32), ((GRAD_ROWS, LANES), BF16)]
        outs += [((rows, width), BF16)] * 2
    else:
        args += [all_x, unpick, skipped]
        outs = [((every, width), BF16), ((every, width), BF16), ((rows, width), F32)]
    in_specs = [inside] * 5 + [anywhere] * 8 + [inside] * (len(args) - 13)
    out_specs = [anywhere if full and k == 2 else inside for k in range(len(outs))]
    scratch = front_scratch(rows, width, hidden, groups, window, full, 4)
    scratch += [pltpu.VMEM((rows, hidden), BF16)]
    if full:
        scratch += back_scratch(rows, width, hidden)
    scratch += [pltpu.VMEM((rows, width), BF16)]
    flops = rows * width * (3 * width + width + 2 * hidden) * (6 if full else 2)
    return pl.pallas_call(
        functools.partial(layer_kernel, layer, groups, window, full),
        out_shape=[jax.ShapeDtypeStruct(*one) for one in outs],
        in_specs=in_specs,
        out_specs=out_specs,
        scratch_shapes=scratch,
        compiler_params=pltpu.CompilerParams(vmem_limit_bytes=60 * 1024 * 1024),
        cost_estimate=pl.CostEstimate(flops=flops, bytes_accessed=3 * 10**7, transcendentals=0),
        name="back" if full else "forward",
    )(*args)


def run_fused(axis_of, groups, window, x, code, vec, scale, own, far, rows_of, back, router, second, second_small, extra, shown):
    rows, width = x.shape
    hidden = own[2].shape[2]
    sum_groups, total = sum_plan(axis_of)
    inside = pl.BlockSpec(memory_space=pltpu.VMEM)
    anywhere = pl.BlockSpec(memory_space=pl.ANY)
    unsort, pick, unpick, skipped = rows_of
    delta, factor, router_row = router
    every = unsort.shape[0]
    args = [x, code[:, None], code[None, :], vec, scale[:, None], *own, *far, unsort]
    args += [back, pick, unpick, skipped, delta, factor[:, None], router_row]
    args += [second, second_small, extra, *shown]
    small_rows = -(-(vec.shape[1] // LANES + 2) // 8) * 8
    outs = [((total, LANES), BF16), ((GRAD_ROWS, LANES), BF16), ((GRAD_ROWS, LANES), BF16)]
    outs += [((small_rows, LANES), F32)] + [((2, every, width), BF16)] * 2
    scratch = front_scratch(rows, width, hidden, groups, window, True, 2)
    scratch += back_scratch(rows, width, hidden)
    scratch += [pltpu.VMEM((rows, width), BF16)] * 2 + [pltpu.VMEM((every, width), BF16)]
    scratch += [pltpu.VMEM((1, vec.shape[1]), F32), pltpu.VMEM((1, width), F32)]
    scratch += [pltpu.VMEM((2, width, STEP), BF16), pltpu.VMEM((2, STEP, width), BF16)]
    scratch += [pltpu.SemaphoreType.DMA((2, 2))]
    scratch += Sums.scratch(sum_groups, total, small_rows)
    sums, _, _, small, *shown = pl.pallas_call(
        functools.partial(fused_kernel, groups, window, sum_groups),
        out_shape=[jax.ShapeDtypeStruct(*one) for one in outs],
        in_specs=[inside] * 5 + [anywhere] * 8 + [inside] * 8 + [anywhere] + [inside] * 2 + [anywhere] * 3,
        out_specs=[anywhere] * 3 + [inside] + [anywhere] * 2,
        scratch_shapes=scratch,
        compiler_params=pltpu.CompilerParams(
            collective_id=0, has_side_effects=True, vmem_limit_bytes=64 * 1024 * 1024
        ),
        cost_estimate=pl.CostEstimate(flops=10**10, bytes_accessed=6 * 10**8, transcendentals=0),
        name="fused",
    )(*args)
    return sums, small, shown


def row_plan(crop_lengths, chosen):
    rows = chosen.shape[0]
    ends = jnp.cumsum(crop_lengths)
    starts = ends - crop_lengths
    is_long = crop_lengths == LONG
    long_before = jnp.cumsum(is_long.astype(jnp.int32)) - is_long
    short = jnp.where(is_long, 0, crop_lengths)
    short_before = jnp.cumsum(short) - short
    base = jnp.where(is_long, long_before * LONG, 2 * LONG + short_before)
    at = jnp.arange(rows, dtype=jnp.int32)
    inside = (at[:, None] >= starts[None]) & (at[:, None] < ends[None])
    target = at + jnp.sum(jnp.where(inside, (base - starts)[None], 0), axis=1)
    order = target[None, :] == at[:, None]
    code = jnp.sum((at[:, None] >= base[None]).astype(jnp.int32), axis=1)
    chosen_in = jnp.sum(jnp.where(order, chosen[None, :], 0), axis=1)
    rank = jnp.sum(jnp.where(at[:, None] > at[None, :], chosen_in[None, :], 0), axis=1)
    slot = jnp.arange(rows // 2, dtype=jnp.int32)
    pick = (rank[None, :] == slot[:, None]) & (chosen_in[None, :] == 1)
    routed_code = jnp.sum(jnp.where(pick, code[None, :], 0), axis=1)
    unsort = target[:, None] == at[None, :]
    at_slot = at[None, : rows // 2]
    unpick = (rank[:, None] == at_slot) & (chosen_in[:, None] == 1)
    skipped = (1 - chosen_in)[:, None].astype(F32)
    return order.astype(BF16), code, routed_code, (unsort.astype(BF16), pick.astype(BF16), unpick.astype(BF16), skipped)


def body(axis_of, tokens, lengths, route_mask, router_weight, gains, biases, w_qkv, w_out, w_up, w_down, cotangent):
    section = lax.axis_index("section")
    micro, rows, width = tokens.shape
    own = (w_qkv, w_out, w_up, w_down)
    far = tuple(other_core(value) for value in own)
    own_vec = jnp.concatenate([gains, biases], axis=1)
    far_vec = other_core(own_vec)
    vecs = [jnp.where(section == layer, own_vec, far_vec) for layer in range(2)]
    router_f = router_weight.astype(F32)

    def pick_micro(array):
        return lax.dynamic_index_in_dim(array, section, 0, False)

    crop_lengths, chosen = pick_micro(lengths)[0], pick_micro(route_mask)
    order, code, routed_code, rows_of = row_plan(crop_lengths, chosen)
    x = dot(order, pick_micro(tokens)).astype(BF16)
    cot = dot(order, pick_micro(cotangent)).astype(BF16)
    routed = dot(rows_of[1], x).astype(BF16)
    inputs_one = routed.astype(F32)
    held = (routed_code > 0).astype(F32)
    gate = jax.nn.sigmoid(jnp.sum(inputs_one * router_f[None, :], axis=1))
    scale_one = held * gate
    half = LONG // 2
    groups_one = [(0, 0, half), (96, half, 2 * half), (192, 2 * half, rows // 2)]
    groups_two = [(0, 0, LONG), (192, LONG, 2 * LONG), (384, 2 * LONG, rows)]

    y1, shown_y1, delta_one = run_layer(
        0, groups_one, 128, routed, routed_code, vecs[0], scale_one, own, far, rows_of, all_x=x
    )
    ones = jnp.ones((rows,), F32)
    shown_du2, small_two, grads_two, dout, shown_y2 = run_layer(
        1, groups_two, 256, y1, code, vecs[1], ones, own, far, rows_of, back=cot
    )
    factor = held * gate * (1.0 - gate)
    micro_ids = jnp.arange(micro)
    here = (micro_ids == section).astype(F32)
    counts = here * jnp.sum(route_mask.astype(F32), axis=1)
    extra = jnp.concatenate([here * jnp.sum(scale_one), counts])
    extra = jnp.pad(extra, (0, width - extra.shape[0]))[None]
    factor = held * gate * (1.0 - gate)
    sums, small, (activations, input_grads) = run_fused(
        axis_of, groups_one, 128, routed, routed_code, vecs[0], scale_one, own, far, rows_of, dout,
        (delta_one, factor, router_f[None, :]), grads_two, small_two, extra, (shown_y1, shown_y2, shown_du2),
    )
    small = small.reshape(-1)
    span = vecs[0].shape[1]
    tail = small[span:]
    grads = cast_sums(sums, [value.shape for value in own])

    return (
        activations[None],
        input_grads[None],
        *grads,
        small[: 2 * width][None],
        small[2 * width : span][None],
        tail[:width],
        tail[width : width + micro] / tail[width + micro : width + 2 * micro],
    )


def solution(mesh):
    in_specs = (
        P(None, "dp", None),
        P(None, "dp", None),
        P(None, "dp"),
        P(),
        P("section", None),
        P("section", None),
        P("section", None, None),
        P("section", None, None),
        P("section", None, None),
        P("section", None, None),
        P(None, "dp", None),
    )
    out_specs = (
        P("section", None, "dp", None),
        P("section", None, "dp", None),
        P("section", None, None),
        P("section", None, None),
        P("section", None, None),
        P("section", None, None),
        P("section", None),
        P("section", None),
        P(),
        P(),
    )
    step = functools.partial(body, axis_bits(mesh))
    return jax.shard_map(step, mesh=mesh, in_specs=in_specs, out_specs=out_specs, check_vma=False)
```

```python
import functools

import jax
import jax.numpy as jnp
from jax import lax
from jax.experimental import pallas as pl
from jax.experimental.pallas import tpu as pltpu
from jax.sharding import PartitionSpec as P

HEADS = 12
HEAD = 64
LONG = 197
F32 = jnp.float32
BF16 = jnp.bfloat16
NT = (((1,), (1,)), ((), ()))
TN = (((0,), (0,)), ((), ()))
NN = (((1,), (0,)), ((), ()))


LANES = 768
TILE = 16
GRAD_ROWS = 12 * LANES


def axis_bits(mesh):
    line = mesh.devices[0]
    bits = len(line).bit_length() - 1
    try:
        spots = [tuple(device.coords) for device in line]
    except AttributeError:
        return [0] * bits
    return [
        next((w for w in range(3) if spots[1 << b][w] != spots[0][w]), 0) for b in range(bits)
    ]


HALVINGS = 4
GROUPS = 6
SLOTS = 4


def sum_plan(axis_of):
    lists = {}
    for bit, axis in enumerate(axis_of):
        lists.setdefault(axis, []).append(bit)
    lists = sorted(lists.values(), key=len)
    while len(lists) < 3:
        lists.append([])
    one, two, three = lists[:3]
    three = three + sum(lists[3:], [])
    orders = [one + three + two, two + three + one, one + two + three, two + one + three]
    chunks, start = [], 0
    for size, order in zip((512, 512, 256, 256), orders):
        chunks.append((start, size, order))
        start += size
    return chunks


def add_rows(into, into_start, source, start, other, other_start, count):
    tile = next(t for t in (64, 32, 16) if count % t == 0)

    def step(k, carry):
        target, here, there = (
            pl.ds(pl.multiple_of(first + k * tile, TILE), tile) for first in (into_start, start, other_start)
        )
        into[target, :] = source[here, :] + other[there, :]
        return carry

    lax.fori_loop(0, count // tile, step, 0)


class Names:
    pass


def copy_far(source, target, one, two, friend):
    return pltpu.make_async_remote_copy(
        src_ref=source,
        dst_ref=target,
        send_sem=one,
        recv_sem=two,
        device_id=friend,
        device_id_type=pl.DeviceIdType.MESH,
    )


def at_core(core, index, step):
    pl.when(core == index)(step)


GRAD_TILES = 36
GROUP_ROWS = GRAD_ROWS // GROUPS


class Sums:
    def __init__(self, chunks, starts, given):
        self.chunks, self.starts = chunks, starts
        self.bits = bits = len(chunks[0][2])
        self.halvings = min(bits, HALVINGS)
        self.acc, self.mate = next(given), next(given)
        self.got = [next(given) for _ in range(bits)]
        self.small_got, self.small = next(given), next(given)
        self.load_sem, self.mate_sem, self.swap_send, self.swap_recv, self.shard_sem = (next(given) for _ in range(5))
        self.send, self.recv, self.back_send, self.back_recv = (next(given) for _ in range(4))
        self.small_send, self.small_recv = (next(given) for _ in range(2))
        self.shown_sem, self.shown_send, self.shown_recv = (next(given) for _ in range(3))
        self.tile_recv, self.give_send, self.give_recv = (next(given) for _ in range(3))
        self.core = lax.axis_index("section")
        self.me = lax.axis_index("dp")
        self.across = (1 - self.core, self.me)
        self.end = starts[-1] + bits + self.halvings + 1

    @staticmethod
    def scratch(chunks, small_rows):
        bits = len(chunks[0][2])
        count = GROUPS * len(chunks)
        largest = max(chunk[1] for chunk in chunks)
        rows = SLOTS * GROUP_ROWS
        held = [pltpu.VMEM((rows, LANES), BF16), pltpu.VMEM((len(chunks), largest, LANES), BF16)]
        held += [pltpu.VMEM((rows >> min(depth + 1, HALVINGS), LANES), BF16) for depth in range(bits)]
        held += [pltpu.VMEM((bits + 1, small_rows, LANES), F32), pltpu.VMEM((2, small_rows, LANES), F32)]
        held += [pltpu.SemaphoreType.DMA((count,))] * 5
        held += [pltpu.SemaphoreType.DMA((count, bits))] * 4
        held += [pltpu.SemaphoreType.DMA((bits + 1,))] * 2
        held += [pltpu.SemaphoreType.DMA((2,))] * 3
        held += [pltpu.SemaphoreType.DMA((GRAD_TILES,))]
        return held + [pltpu.SemaphoreType.DMA((GROUPS,))] * 2

    def bit_at(self, bit):
        return lax.rem(self.me // (1 << bit), 2)

    def partner(self, bit):
        return (self.core, self.me + (1 - 2 * self.bit_at(bit)) * (1 << bit))

    def open(self):
        friends = [self.across] + [self.partner(bit) for bit in range(self.bits)]
        barrier = pltpu.get_barrier_semaphore()
        for friend in friends:
            pl.semaphore_signal(barrier, inc=1, device_id=friend, device_id_type=pl.DeviceIdType.MESH)
        pl.semaphore_wait(barrier, len(friends))

    @staticmethod
    def layer_of(j):
        return 1 if j < GROUPS // 2 else 0

    def base(self, j, core):
        return (2 * (j % (GROUPS // 2)) + core) * GROUP_ROWS

    def rows_at(self, j, core, c):
        start, size, _ = self.chunks[c]
        return pl.ds(pl.multiple_of(self.base(j, core) + start, TILE), size)

    def index(self, j, c):
        return j * len(self.chunks) + c

    def swap(self, j, c):
        rows, k = self.rows_at(j, 1 - self.core, c), self.index(j, c)
        return copy_far(
            self.grads[1].at[rows, :], self.landed[1].at[rows, :], self.swap_send.at[k], self.swap_recv.at[k],
            self.across,
        )

    def load(self, j, c):
        start, size, _ = self.chunks[c]
        target = self.acc.at[pl.ds(j % SLOTS * GROUP_ROWS + start, size), :]
        source = self.grads[self.layer_of(j)].at[self.rows_at(j, self.core, c), :]
        return pltpu.make_async_copy(source, target, self.load_sem.at[self.index(j, c)])

    def load_mate(self, j, c):
        source = self.landed[self.layer_of(j)].at[self.rows_at(j, self.core, c), :]
        target = self.mate.at[c, pl.ds(0, self.chunks[c][1]), :]
        return pltpu.make_async_copy(source, target, self.mate_sem.at[self.index(j, c)])

    def span(self, c, depth):
        start, size, order = self.chunks[c]
        for bit in order[: min(depth, self.halvings)]:
            size //= 2
            start = start + self.bit_at(bit) * size
        return start, size

    def in_acc(self, j, start, size):
        return pl.ds(pl.multiple_of(j % SLOTS * GROUP_ROWS + start, TILE), size)

    def got_at(self, j, c, depth):
        return (j % SLOTS * GROUP_ROWS + self.chunks[c][0]) >> min(depth + 1, HALVINGS)

    def down(self, j, c, depth):
        bit = self.chunks[c][2][depth]
        start, size = self.span(c, depth)
        if depth < self.halvings:
            size //= 2
            start = start + (1 - self.bit_at(bit)) * size
        k = self.index(j, c)
        return copy_far(
            self.acc.at[self.in_acc(j, start, size), :],
            self.got[depth].at[pl.ds(self.got_at(j, c, depth), size), :],
            self.send.at[k, depth],
            self.recv.at[k, depth],
            self.partner(bit),
        )

    def shard(self, j, c):
        start, size = self.span(c, self.halvings)
        there = pl.ds(pl.multiple_of(self.base(j, self.core) + start, TILE), size)
        target = self.full[self.layer_of(j)].at[there, :]
        return pltpu.make_async_copy(
            self.acc.at[self.in_acc(j, start, size), :], target, self.shard_sem.at[self.index(j, c)]
        )

    def up(self, j, c, depth):
        bit = self.chunks[c][2][depth]
        start, size = self.span(c, depth + 1)
        full = self.full[self.layer_of(j)]
        target = full.at[pl.ds(pl.multiple_of(self.base(j, self.core) + start, TILE), size), :]
        source = self.acc.at[self.in_acc(j, start, size), :] if depth == self.halvings - 1 else target
        k = self.index(j, c)
        return copy_far(source, target, self.back_send.at[k, depth], self.back_recv.at[k, depth], self.partner(bit))

    def give(self, j, core):
        full = self.full[self.layer_of(j)]
        rows = pl.ds(self.base(j, core), GROUP_ROWS)
        return copy_far(full.at[rows, :], full.at[rows, :], self.give_send.at[j], self.give_recv.at[j], self.across)

    def each(self):
        return range(len(self.chunks))

    def start_swaps(self, j):
        for c in self.each():
            self.swap(j, c).start()

    def emptied(self, j):
        for c in self.each():
            for depth in range(self.halvings):
                self.down(j, c, depth).wait_send()
            self.up(j, c, self.halvings - 1).wait_send()

    def prepare(self, j):
        if j >= SLOTS:
            self.emptied(j - SLOTS)
        for c in self.each():
            self.load(j, c).start()
        if self.layer_of(j) == 0:
            for tile in range(6):
                area = self.landed[0].at[pl.ds(0, LANES), pl.ds(0, STEP)]
                sem = self.tile_recv.at[(j - GROUPS // 2) * 12 + self.core * 6 + tile]
                copy_far(area, area, sem, sem, self.across).wait_recv()
        for c in self.each():
            if self.layer_of(j) == 1:
                self.swap(j, c).wait_recv()
            self.load_mate(j, c).start()

    def moment(self, now):
        bits, halvings = self.bits, self.halvings
        for j, start in enumerate(self.starts):
            if start == now:
                for c in self.each():
                    self.load(j, c).wait()
                    self.load_mate(j, c).wait()
                    first, size, _ = self.chunks[c]
                    at = j % SLOTS * GROUP_ROWS + first
                    add_rows(self.acc, at, self.acc, at, self.mate.at[c], 0, size)
                    self.down(j, c, 0).start()
            if self.layer_of(j) == 1 and start == now + 2:
                self.start_swaps(j)
        for j, begun in enumerate(self.starts):
            stage = now - begun
            if not 0 < stage <= bits + halvings:
                continue
            for c in self.each():
                if stage <= bits:
                    depth = stage - 1
                    if depth < halvings:
                        self.down(j, c, depth).wait_recv()
                    else:
                        self.down(j, c, depth).wait()
                    first, size = self.span(c, stage)
                    at = j % SLOTS * GROUP_ROWS + first
                    add_rows(self.acc, at, self.acc, at, self.got[depth], self.got_at(j, c, depth), size)
                    if stage < bits:
                        self.down(j, c, stage).start()
                    else:
                        self.up(j, c, halvings - 1).start()
                        self.shard(j, c).start()
                else:
                    depth = bits + halvings - stage
                    self.up(j, c, depth).wait_recv()
                    if depth == halvings - 1:
                        self.shard(j, c).wait()
                    if depth > 0:
                        self.up(j, c, depth - 1).start()
            if stage == bits + halvings:
                core = 1 - self.layer_of(j)
                at_core(self.core, core, lambda j=j, core=core: self.give(j, core).start())
        for j, start in enumerate(self.starts):
            if start == now + 1:
                self.prepare(j)

    def small_step(self, k):
        friend = self.across if k == 0 else self.partner(k - 1)
        return copy_far(
            self.small_out, self.small_got.at[k], self.small_send.at[k], self.small_recv.at[k], friend
        )

    def small_begin(self):
        for layer in range(2):

            def step(layer=layer):
                self.small_out[...] = self.small[layer]
                copy_far(
                    self.small.at[1 - layer], self.small_got.at[0], self.small_send.at[0], self.small_recv.at[0],
                    self.across,
                ).start()

            at_core(self.core, layer, step)

    def small_turn(self, k):
        self.small_step(k).wait()
        self.small_out[...] = self.small_out[...] + self.small_got[k]
        if k < self.bits:
            self.small_step(k + 1).start()

    def shown_keep(self, layer, k):
        return pltpu.make_async_copy(self.shown[2 * k + layer], self.shown_out[k].at[self.core], self.shown_sem.at[k])

    def shown_give(self, layer, k):
        return copy_far(
            self.shown[2 * k + 1 - layer], self.shown_out[k].at[self.core], self.shown_send.at[k],
            self.shown_recv.at[k], self.across,
        )

    def show(self):
        for layer in range(2):

            def step(layer=layer):
                for k in range(2):
                    self.shown_keep(layer, k).start()
                    self.shown_give(layer, k).start()

            at_core(self.core, layer, step)

    def close(self):
        for k in range(2):
            self.shown_keep(0, k).wait()
            self.shown_give(0, k).wait()
        for j in range(GROUPS):
            layer = self.layer_of(j)
            at_core(self.core, layer, lambda j=j: self.give(j, 1 - self.layer_of(j)).wait_recv())
            at_core(self.core, 1 - layer, lambda j=j: self.give(j, 1 - self.layer_of(j)).wait_send())
            if j >= GROUPS - SLOTS:
                self.emptied(j)
            for c in self.each():
                if layer == 1:
                    self.swap(j, c).wait_send()
                for depth in range(self.halvings - 1):
                    self.up(j, c, depth).wait_send()


def cast_kernel(first, second, qkv, out, up, down, low, high, in_sem, out_sem):
    rows = low.shape[1]
    per = LANES // rows
    slots = low.shape[0]
    count = 12 * per

    core = lax.axis_index("section")

    def take(k, source=first):
        return pltpu.make_async_copy(source.at[pl.ds(k * rows, rows), :], low.at[k % slots], in_sem.at[k % slots])

    def give(k):
        block, part = divmod(k, per)
        if block < 4:
            target = down.at[0, pl.ds(k * rows, rows), :]
        elif block < 8:
            target = up.at[0, pl.ds(part * rows, rows), pl.ds((block - 4) * LANES, LANES)]
        elif block < 9:
            target = out.at[0, pl.ds(part * rows, rows), :]
        else:
            target = qkv.at[0, pl.ds(part * rows, rows), pl.ds((block - 9) * LANES, LANES)]
        return pltpu.make_async_copy(high.at[k % slots], target, out_sem.at[k % slots])

    def fetch(k):
        at_core(core, 0, lambda: take(k).start())
        at_core(core, 1, lambda: take(k, second).start())

    for k in range(slots):
        fetch(k)
    for k in range(count):
        take(k).wait()
        if k >= slots:
            give(k - slots).wait()
        high[k % slots] = low[k % slots].astype(F32)
        give(k).start()
        if k + slots < count:
            fetch(k + slots)
    for k in range(count - slots, count):
        give(k).wait()


def cast_sums(sums, shapes):
    anywhere = pl.BlockSpec(memory_space=pl.ANY)
    return pl.pallas_call(
        cast_kernel,
        out_shape=[jax.ShapeDtypeStruct(shape, F32) for shape in shapes],
        in_specs=[anywhere] * 2,
        out_specs=[anywhere] * 4,
        scratch_shapes=[
            pltpu.VMEM((6, 256, LANES), BF16),
            pltpu.VMEM((6, 256, LANES), F32),
            pltpu.SemaphoreType.DMA((6,)),
            pltpu.SemaphoreType.DMA((6,)),
        ],
        compiler_params=pltpu.CompilerParams(vmem_limit_bytes=60 * 1024 * 1024),
        cost_estimate=pl.CostEstimate(flops=0, bytes_accessed=42 * 10**6, transcendentals=0),
        name="cast",
    )(*sums)


def other_core(value):
    return lax.ppermute(value, "section", [(0, 1), (1, 0)])


STEP = 256
ROW_TILE = 64
NEGATIVE = -1e30


def dot(left, right, dims=NN):
    return lax.dot_general(left, right, dims, preferred_element_type=F32)


def gelu_parts(pre):
    bell = jnp.exp(pre * pre * -0.5)
    t = pl.reciprocal(1.0 + jnp.abs(pre) * (0.3275911 * 0.7071067811865476))
    poly = t * (0.1274147960 + t * (-0.142248368 + t * (0.710706871 + t * (-0.7265760135 + t * 0.5307027145))))
    tail = poly * bell
    return jnp.where(pre >= 0.0, 1.0 - tail, tail), bell


def norm_stats(values):
    centred = values - jnp.mean(values, axis=-1, keepdims=True)
    recip = lax.rsqrt(jnp.mean(centred * centred, axis=-1, keepdims=True) + 1e-06)
    return centred * recip, recip


def fold(tile):
    return jnp.sum(tile.reshape(tile.shape[0] // 8, 8, tile.shape[1]), axis=0)


def layer_kernel(layer, groups, window, full, *refs):
    r = Names()
    given = iter(refs)
    r.x, r.col_code, r.row_code, r.vec, r.scale = (next(given) for _ in range(5))
    r.own = [next(given) for _ in range(4)]
    r.far = [next(given) for _ in range(4)]
    r.unsort = next(given)
    if full:
        r.dout = next(given)
        r.shown_du, r.small, r.grads, r.du, r.shown_y = (next(given) for _ in range(5))
    else:
        r.all_x, r.unpick, r.skipped = (next(given) for _ in range(3))
        r.all_y, r.shown_y, r.delta = (next(given) for _ in range(3))
    r.weights = [next(given) for _ in range(4)]
    r.w_sem, r.n1, r.qkv, r.probs, r.mask, r.mix, r.between, r.n2, r.act = (next(given) for _ in range(9))
    if full:
        back_names(r, given)
    r.y = next(given)
    layer_body(r, layer, groups, window, full, False)


def back_names(r, given):
    r.n1t, r.n2t, r.mixt, r.dmlp, r.dpre, r.dn, r.datt, r.dmix, r.dqkv = (next(given) for _ in range(9))
    r.down_stage, r.up_stage, r.down_sem, r.up_sem = (next(given) for _ in range(4))


def fused_kernel(groups, window, chunks, *refs):
    r = Names()
    given = iter(refs)
    r.x, r.col_code, r.row_code, r.vec, r.scale = (next(given) for _ in range(5))
    r.own = [next(given) for _ in range(4)]
    r.far = [next(given) for _ in range(4)]
    r.unsort = next(given)
    r.all_dout, r.pick, r.unpick, r.skipped, r.delta, r.factor, r.router = (next(given) for _ in range(7))
    second, second_small, extra = (next(given) for _ in range(3))
    shown = [next(given) for _ in range(3)]
    full = [next(given) for _ in range(2)]
    landed = [next(given) for _ in range(2)]
    first, small_out = (next(given) for _ in range(2))
    shown_out = [next(given) for _ in range(2)]
    r.weights = [next(given) for _ in range(2)]
    r.w_sem, r.n1, r.qkv, r.probs, r.mask, r.mix, r.between, r.n2 = (next(given) for _ in range(8))
    back_names(r, given)
    r.dout, r.du, r.shown_du, r.small, r.router_grad = (next(given) for _ in range(5))
    r.up_tile, r.down_tile, r.tile_sem = (next(given) for _ in range(3))
    sums = Sums(chunks, (0, 1, 2, 5, 6, 8), given)
    sums.grads, sums.landed, sums.full, sums.small_out = (first, second), landed, full, small_out
    sums.shown, sums.shown_out = (shown[0], shown[1], r.shown_du, shown[2]), shown_out
    r.grads = first
    core = sums.core
    sums.open()
    sums.start_swaps(0)
    sums.start_swaps(1)
    sums.prepare(0)
    early = [0]

    def hook():
        sums.moment(early[0])
        early[0] += 1

    def tile_out(stage, row, column, shape, sem, tile):
        area = (pl.ds(row, shape[0]), pl.ds(column, shape[1]))
        owner = lax.rem(tile // 6, 2)

        @pl.when(core == owner)
        def _():
            pltpu.make_async_copy(stage, first.at[area], sem).start()

        @pl.when(core != owner)
        def _():
            copy_far(stage, landed[0].at[area], sem, sums.tile_recv.at[tile], sums.across).start()

    r.hook, r.tile_out = hook, tile_out
    layer_body(r, 0, groups, window, True, True)

    for index, source in enumerate((r.small, second_small)):
        for row in range(source.shape[1] // LANES):
            sums.small[index, row : row + 1, :] = source[:, row * LANES : (row + 1) * LANES]
        row = source.shape[1] // LANES
        sums.small[index, row : row + 1, :] = r.router_grad[...]
        sums.small[index, row + 1 : row + 2, :] = extra[...]
        left = sums.small.shape[1] - row - 2
        sums.small[index, row + 2 :, :] = jnp.zeros((left, LANES), F32)
    sums.small_begin()
    sums.show()

    for turn, now in enumerate(range(early[0], max(sums.end, early[0] + sums.bits + 1))):
        if now < sums.end:
            sums.moment(now)
        if turn <= sums.bits:
            sums.small_turn(turn)
    sums.close()


def layer_body(r, layer, groups, window, full, is_router):
    hook = r.hook if is_router else lambda: None
    rows, width = r.x.shape
    hidden = r.own[2].shape[2]
    core = lax.axis_index("section")
    pairs = width // 128

    kept = {0: 0, 1: 1, 2: 2, 3: 3} if not is_router else {0: 0, 1: 1}

    def weight(which, source):
        return pltpu.make_async_copy(source[which].at[0], r.weights[which], r.w_sem.at[which])

    def up_tile(source, k, slot):
        span = pl.ds(pl.multiple_of(k * STEP, STEP), STEP)
        return pltpu.make_async_copy(source[2].at[0, :, span], r.up_tile.at[slot], r.tile_sem.at[0, slot])

    def down_tile(source, k, slot):
        span = pl.ds(pl.multiple_of(k * STEP, STEP), STEP)
        return pltpu.make_async_copy(source[3].at[0, span, :], r.down_tile.at[slot], r.tile_sem.at[1, slot])

    def start_tiles(k, slot):
        for near, source in ((core == layer, r.own), (core != layer, r.far)):

            @pl.when(near)
            def _():
                up_tile(source, k, slot).start()
                down_tile(source, k, slot).start()

    for near, source in ((core == layer, r.own), (core != layer, r.far)):

        @pl.when(near)
        def _():
            for which in kept:
                weight(which, source).start()

    if is_router:
        start_tiles(0, 0)
        start_tiles(1, 1)

    def vec(start, count=width):
        return r.vec[:, start : start + count]

    g1, g2, b1, bq, bv, bo, b2 = (vec(k * width) for k in range(7))
    bu_at, bd_at = 7 * width, 7 * width + hidden

    def row_loop(step, init=0):
        def at(k, carry):
            return step(pl.ds(pl.multiple_of(k * ROW_TILE, ROW_TILE), ROW_TILE), carry)

        return lax.fori_loop(0, rows // ROW_TILE, at, init)

    def norm_step(source, gain, bias, target):
        def step(here, carry):
            normal, _ = norm_stats(source[here, :].astype(F32))
            target[here, :] = (normal * gain + bias).astype(BF16)
            return carry

        return step

    def tiles(step):
        for k in range(width // STEP):
            step(slice(k * STEP, (k + 1) * STEP))

    def show(source, target):
        def step(span):
            target[:, span] = dot(r.unsort[...], source[:, span]).astype(BF16)

        tiles(step)

    def spread(routed, others, target, shown):
        def step(span):
            value = dot(r.unpick[...], routed[:, span]) + others[:, span].astype(F32) * r.skipped[...]
            if target is not None:
                target[:, span] = value.astype(BF16)
            shown[:, span] = dot(r.unsort[...], value.astype(BF16)).astype(BF16)

        tiles(step)

    row_loop(norm_step(r.x, g1, b1, r.n1))
    if full and is_router:

        def route_step(span):
            r.dout[:, span] = dot(r.pick[...], r.all_dout[:, span]).astype(BF16)

        tiles(route_step)
    if full:

        def delta_step(here, carry):
            low = (r.dout[here, :].astype(F32) * r.scale[here, :]).astype(BF16)
            r.dmlp[here, :] = low
            return carry + fold(low.astype(F32))

        dbd = row_loop(delta_step, jnp.zeros((8, width), F32))
        r.small[:, bd_at:] = jnp.sum(dbd, axis=0, keepdims=True)

    for k, (start, low, high) in enumerate(groups):
        col = r.col_code[start : start + window, :]
        row = r.row_code[:, start : start + window]
        place = lax.broadcasted_iota(jnp.int32, (window, 1), 0) + start
        col = jnp.where((place >= low) & (place < high), col, -1)
        r.mask[k] = jnp.where(col == row, 0.0, NEGATIVE)

    weight(0, r.own).wait()
    for k in range(3 * width // STEP):
        span = slice(k * STEP, (k + 1) * STEP)
        value = dot(r.n1[...], r.weights[0][:, span])
        if k < width // STEP:
            value = (value + bq[:, span]).astype(BF16).astype(F32) * 0.125
        elif k >= 2 * width // STEP:
            value = value + bv[:, k * STEP - 2 * width : (k + 1) * STEP - 2 * width]
        r.qkv[:, span] = value.astype(BF16)

    hook()
    lane = lax.broadcasted_iota(jnp.int32, (1, 128), 1)

    def halves(block):
        zero = jnp.zeros_like(block)
        return jnp.where(lane < 64, block, zero), jnp.where(lane < 64, zero, block)

    r.mix[...] = jnp.zeros_like(r.mix)

    def lanes(pair, part):
        return pl.ds(pl.multiple_of(pair * 128 + part * width, 128), 128)

    def attend(pair, carry):
        for k, (start, low, high) in enumerate(groups):
            here = slice(start, start + window)
            q, key, v = (r.qkv[here, lanes(pair, part)] for part in range(3))
            vt = v.T
            place = lax.broadcasted_iota(jnp.int32, (1, window), 1) + start
            valid = (place >= low) & (place < high)
            parts = []
            for half, own_key in enumerate(halves(key)):
                scores = dot(own_key, q, NT) + r.mask[k]
                power = jnp.exp(scores - jnp.max(scores, axis=0, keepdims=True))
                total = jnp.sum(power, axis=0, keepdims=True)
                prob = (power * jnp.where(valid, 1.0 / total, 0.0)).astype(BF16)
                if full:
                    r.probs[(pair * 2 + half) * len(groups) + k] = prob
                parts.append(dot(vt[half * 64 : half * 64 + 64], prob))
            mixed = jnp.concatenate(parts, axis=0).T.astype(BF16)
            r.mix[here, lanes(pair, 0)] = r.mix[here, lanes(pair, 0)] + mixed
        return carry

    lax.fori_loop(0, pairs, attend, 0)
    hook()

    weight(1, r.own).wait()
    for k in range(width // STEP):
        span = slice(k * STEP, (k + 1) * STEP)
        value = dot(r.mix[...], r.weights[1][:, span]) + bo[:, span]
        r.between[:, span] = r.x[:, span].astype(F32) + value
    row_loop(norm_step(r.between, g2, b2, r.n2))
    if full:
        r.n1t[...] = r.n1[...].T
        r.n2t[...] = r.n2[...].T
        r.mixt[...] = r.mix[...].T

    if not is_router:
        weight(2, r.own).wait()
        weight(3, r.own).wait()

    def tile_out(stage, row, column, shape, sem, tile):
        target = r.grads.at[pl.ds(row, shape[0]), pl.ds(column, shape[1])]
        pltpu.make_async_copy(stage, target, sem).start()

    tile_out = r.tile_out if is_router else tile_out

    def down_out(k, slot):
        tile_out(
            r.down_stage.at[slot], pl.multiple_of(k * STEP, STEP), 0, (STEP, width), r.down_sem.at[slot], k
        )

    def side_out(block, k, slot):
        row = pl.multiple_of((block + k // 3) * width, width)
        column = pl.multiple_of(k % 3 * STEP, STEP)
        tile = k + {4: 12, 8: 24, 9: 27}[block]
        tile_out(r.up_stage.at[slot], row, column, (width, STEP), r.up_sem.at[slot], tile)

    def down_free(slot):
        target = r.grads.at[pl.ds(0, STEP), pl.ds(0, width)]
        pltpu.make_async_copy(r.down_stage.at[slot], target, r.down_sem.at[slot]).wait()

    def side_free(slot):
        target = r.grads.at[pl.ds(0, width), pl.ds(0, STEP)]
        pltpu.make_async_copy(r.up_stage.at[slot], target, r.up_sem.at[slot]).wait()

    def hidden_step(k, carry):
        at = pl.multiple_of(k * STEP, STEP)
        span = pl.ds(at, STEP)
        slot = lax.rem(k, 2)
        if is_router:
            up_tile(r.own, k, slot).wait()
            down_tile(r.own, k, slot).wait()
            w_up, w_down = r.up_tile[slot], r.down_tile[slot]
        else:
            w_up, w_down = r.weights[2][:, span], r.weights[3][span, :]
        pre = dot(r.n2[...], w_up) + r.vec[:, pl.ds(at + bu_at, STEP)]
        cdf, bell = gelu_parts(pre)
        act = (pre * cdf).astype(BF16)
        if not is_router:
            r.act[:, span] = act
        if full:

            @pl.when(k >= 2)
            def _():
                down_free(slot)
                side_free(slot)

            slope = cdf + pre * bell * 0.3989422804014327
            dact = dot(r.dmlp[...], w_down, NT)
            dpre = (dact * slope).astype(BF16)
            if is_router:
                r.dn[...] = r.dn[...] + dot(dpre, w_up, NT)
            else:
                r.dpre[:, span] = dpre
            r.small[:, pl.ds(at + bu_at, STEP)] = jnp.sum(dpre.astype(F32), axis=0, keepdims=True)
            r.down_stage[slot] = dot(act, r.dmlp[...], TN).astype(BF16)
            down_out(k, slot)
            r.up_stage[slot] = dot(r.n2t[...], dpre).astype(BF16)
            side_out(4, k, slot)
        if is_router:

            @pl.when(k + 2 < hidden // STEP)
            def _():
                start_tiles(k + 2, slot)

        return carry

    steps = hidden // STEP
    if is_router:
        r.dn[...] = jnp.zeros_like(r.dn)
        for part in range(3):
            lax.fori_loop(part * steps // 3, (part + 1) * steps // 3, hidden_step, 0)
            if part == 2:
                down_free(0)
                down_free(1)
            hook()
    else:
        lax.fori_loop(0, steps, hidden_step, 0)
    if not (full and is_router):
        for k in range(width // STEP):
            span = slice(k * STEP, (k + 1) * STEP)
            value = dot(r.act[...], r.weights[3][:, span]) + vec(bd_at)[:, span]
            source = r.x[:, span].astype(F32)
            value = r.between[:, span] - source + value
            if not full:
                r.delta[:, span] = value
            r.y[:, span] = (source + r.scale[...] * value).astype(BF16)
    if not full:
        spread(r.y, r.all_x, r.all_y, r.shown_y)
        return
    if not is_router:
        show(r.y, r.shown_y)

    if not is_router:
        for k in range(width // STEP):
            span = slice(k * STEP, (k + 1) * STEP)
            r.dn[:, span] = dot(r.dpre[...], r.weights[2][span, :], NT)

    def norm_back(source, gain, here):
        normal, recip = norm_stats(source[here, :].astype(F32))
        grad = r.dn[here, :]
        hat = grad * gain
        back = recip * (
            hat - jnp.mean(hat, axis=-1, keepdims=True) - normal * jnp.mean(hat * normal, axis=-1, keepdims=True)
        )
        return back, fold(grad * normal), fold(grad)

    def second_back(here, carry):
        back, dg, db = norm_back(r.between, g2, here)
        r.between[here, :] = back
        total = (r.dout[here, :].astype(F32) * r.scale[here, :] + back).astype(BF16)
        r.datt[here, :] = total
        return carry[0] + dg, carry[1] + db, carry[2] + fold(total.astype(F32))

    zero = jnp.zeros((8, width), F32)
    dg2, db2, dbo = row_loop(second_back, (zero, zero, zero))
    r.small[:, width : 2 * width] = jnp.sum(dg2, axis=0, keepdims=True)
    r.small[:, 6 * width : 7 * width] = jnp.sum(db2, axis=0, keepdims=True)
    r.small[:, 5 * width : 6 * width] = jnp.sum(dbo, axis=0, keepdims=True)

    for k in range(width // STEP):
        span = slice(k * STEP, (k + 1) * STEP)
        r.dmix[:, span] = dot(r.datt[...], r.weights[1][span, :], NT).astype(BF16)
        slot = k % 2
        side_free(slot)
        r.up_stage[slot] = dot(r.mixt[...], r.datt[:, span]).astype(BF16)
        side_out(8, k, slot)
    hook()

    r.dqkv[...] = jnp.zeros_like(r.dqkv)

    def attend_back(pair, carry):
        for k, (start, low, high) in enumerate(groups):
            here = slice(start, start + window)
            q, key, v = (r.qkv[here, lanes(pair, part)] for part in range(3))
            dm = r.dmix[here, lanes(pair, 0)]
            key_t = key.T
            dq, dk, dv = [], None, None
            for half, (own_q, own_v, own_dm) in enumerate(zip(halves(q), halves(v), halves(dm))):
                prob = r.probs[(pair * 2 + half) * len(groups) + k]
                wide = prob.astype(F32)
                dprob = dot(own_v, dm, NT)
                product = wide * dprob
                ds = (product - wide * jnp.sum(product, axis=0, keepdims=True)).astype(BF16)
                dq.append(dot(key_t[half * 64 : half * 64 + 64], ds))
                one, two = dot(ds, own_q), dot(prob, own_dm)
                dk, dv = (one, two) if dk is None else (dk + one, dv + two)
            dq = jnp.concatenate(dq, axis=0).T * 0.125
            for part, value in enumerate((dq, dk, dv)):
                spot = lanes(pair, part)
                r.dqkv[here, spot] = r.dqkv[here, spot] + value.astype(BF16)
        return carry

    lax.fori_loop(0, pairs, attend_back, 0)
    hook()

    for k in range(3 * width // STEP):
        span = slice(k * STEP, (k + 1) * STEP)
        block = r.dqkv[:, span]
        if not width <= k * STEP < 2 * width:
            at = 3 * width + k * STEP - (width if k * STEP >= width else 0)
            r.small[:, at : at + STEP] = jnp.sum(block.astype(F32), axis=0, keepdims=True)
        slot = (k + 1) % 2
        side_free(slot)
        r.up_stage[slot] = dot(r.n1t[...], block).astype(BF16)
        side_out(9, k, slot)
    side_free(0)
    side_free(1)
    hook()

    for k in range(width // STEP):
        span = slice(k * STEP, (k + 1) * STEP)
        r.dn[:, span] = dot(r.dqkv[...], r.weights[0][span, :], NT)

    def first_back(here, carry):
        back, dg, db = norm_back(r.x, g1, here)
        dout = r.dout[here, :].astype(F32)
        total = dout + r.between[here, :] + back
        sums = [carry[0] + dg, carry[1] + db]
        if is_router:
            slope = jnp.sum(dout * r.delta[here, :], axis=1, keepdims=True) * r.factor[here, :]
            total = total + slope * r.router[...]
            sums.append(carry[2] + fold(slope * r.x[here, :].astype(F32)))
        r.du[here, :] = total.astype(BF16)
        return tuple(sums)

    sums = row_loop(first_back, (zero,) * (3 if is_router else 2))
    r.small[:, :width] = jnp.sum(sums[0], axis=0, keepdims=True)
    r.small[:, 2 * width : 3 * width] = jnp.sum(sums[1], axis=0, keepdims=True)
    if is_router:
        r.router_grad[...] = jnp.sum(sums[2], axis=0, keepdims=True)
        spread(r.du, r.all_dout, None, r.shown_du)
    else:
        show(r.du, r.shown_du)
    if not is_router:
        down_free(0)
        down_free(1)


def front_scratch(rows, width, hidden, groups, window, full, kept):
    sizes = [(width, 3 * width), (width, width), (width, hidden), (hidden, width)][:kept]
    held = [pltpu.VMEM(size, BF16) for size in sizes]
    held += [pltpu.SemaphoreType.DMA((4,))]
    held += [pltpu.VMEM((rows, width), BF16), pltpu.VMEM((rows, 3 * width), BF16)]
    held += [pltpu.VMEM((HEADS * len(groups) if full else 1, window, window), BF16)]
    held += [pltpu.VMEM((len(groups), window, window), F32), pltpu.VMEM((rows, width), BF16)]
    return held + [pltpu.VMEM((rows, width), F32), pltpu.VMEM((rows, width), BF16)]


def back_scratch(rows, width, hidden):
    held = [pltpu.VMEM((width, rows), BF16)] * 3 + [pltpu.VMEM((rows, width), BF16)]
    held += [pltpu.VMEM((rows, hidden), BF16), pltpu.VMEM((rows, width), F32)]
    held += [pltpu.VMEM((rows, width), BF16)] * 2 + [pltpu.VMEM((rows, 3 * width), BF16)]
    held += [pltpu.VMEM((2, STEP, width), BF16), pltpu.VMEM((2, width, STEP), BF16)]
    return held + [pltpu.SemaphoreType.DMA((2,))] * 2


def run_layer(layer, groups, window, x, code, vec, scale, own, far, rows_of, all_x=None, back=None):
    rows, width = x.shape
    hidden = own[2].shape[2]
    full = back is not None
    inside = pl.BlockSpec(memory_space=pltpu.VMEM)
    anywhere = pl.BlockSpec(memory_space=pl.ANY)
    unsort, pick, unpick, skipped = rows_of
    args = [x, code[:, None], code[None, :], vec, scale[:, None], *own, *far, unsort]
    every = unsort.shape[0]
    if full:
        args += [back]
        outs = [((every, width), BF16), ((1, vec.shape[1]), F32), ((GRAD_ROWS, LANES), BF16)]
        outs += [((rows, width), BF16)] * 2
    else:
        args += [all_x, unpick, skipped]
        outs = [((every, width), BF16), ((every, width), BF16), ((rows, width), F32)]
    in_specs = [inside] * 5 + [anywhere] * 8 + [inside] * (len(args) - 13)
    out_specs = [anywhere if full and k == 2 else inside for k in range(len(outs))]
    scratch = front_scratch(rows, width, hidden, groups, window, full, 4)
    scratch += [pltpu.VMEM((rows, hidden), BF16)]
    if full:
        scratch += back_scratch(rows, width, hidden)
    scratch += [pltpu.VMEM((rows, width), BF16)]
    flops = rows * width * (3 * width + width + 2 * hidden) * (6 if full else 2)
    return pl.pallas_call(
        functools.partial(layer_kernel, layer, groups, window, full),
        out_shape=[jax.ShapeDtypeStruct(*one) for one in outs],
        in_specs=in_specs,
        out_specs=out_specs,
        scratch_shapes=scratch,
        compiler_params=pltpu.CompilerParams(vmem_limit_bytes=60 * 1024 * 1024),
        cost_estimate=pl.CostEstimate(flops=flops, bytes_accessed=3 * 10**7, transcendentals=0),
        name="back" if full else "forward",
    )(*args)


def run_fused(axis_of, groups, window, x, code, vec, scale, own, far, rows_of, back, router, second, second_small, extra, shown):
    rows, width = x.shape
    hidden = own[2].shape[2]
    chunks = sum_plan(axis_of)
    inside = pl.BlockSpec(memory_space=pltpu.VMEM)
    anywhere = pl.BlockSpec(memory_space=pl.ANY)
    unsort, pick, unpick, skipped = rows_of
    delta, factor, router_row = router
    every = unsort.shape[0]
    args = [x, code[:, None], code[None, :], vec, scale[:, None], *own, *far, unsort]
    args += [back, pick, unpick, skipped, delta, factor[:, None], router_row]
    args += [second, second_small, extra, *shown]
    small_rows = -(-(vec.shape[1] // LANES + 2) // 8) * 8
    outs = [((GRAD_ROWS, LANES), BF16)] * 5
    outs += [((small_rows, LANES), F32)] + [((2, every, width), BF16)] * 2
    scratch = front_scratch(rows, width, hidden, groups, window, True, 2)
    scratch += back_scratch(rows, width, hidden)
    scratch += [pltpu.VMEM((rows, width), BF16)] * 2 + [pltpu.VMEM((every, width), BF16)]
    scratch += [pltpu.VMEM((1, vec.shape[1]), F32), pltpu.VMEM((1, width), F32)]
    scratch += [pltpu.VMEM((2, width, STEP), BF16), pltpu.VMEM((2, STEP, width), BF16)]
    scratch += [pltpu.SemaphoreType.DMA((2, 2))]
    scratch += Sums.scratch(chunks, small_rows)
    *sums, _, _, _, small, acts, grads = pl.pallas_call(
        functools.partial(fused_kernel, groups, window, chunks),
        out_shape=[jax.ShapeDtypeStruct(*one) for one in outs],
        in_specs=[inside] * 5 + [anywhere] * 8 + [inside] * 8 + [anywhere] + [inside] * 2 + [anywhere] * 3,
        out_specs=[anywhere] * 5 + [inside] + [anywhere] * 2,
        scratch_shapes=scratch,
        compiler_params=pltpu.CompilerParams(
            collective_id=0, has_side_effects=True, vmem_limit_bytes=64 * 1024 * 1024
        ),
        cost_estimate=pl.CostEstimate(flops=10**10, bytes_accessed=6 * 10**8, transcendentals=0),
        name="fused",
    )(*args)
    return sums, small, (acts, grads)


def row_plan(crop_lengths, chosen):
    rows = chosen.shape[0]
    ends = jnp.cumsum(crop_lengths)
    starts = ends - crop_lengths
    is_long = crop_lengths == LONG
    long_before = jnp.cumsum(is_long.astype(jnp.int32)) - is_long
    short = jnp.where(is_long, 0, crop_lengths)
    short_before = jnp.cumsum(short) - short
    base = jnp.where(is_long, long_before * LONG, 2 * LONG + short_before)
    at = jnp.arange(rows, dtype=jnp.int32)
    inside = (at[:, None] >= starts[None]) & (at[:, None] < ends[None])
    target = at + jnp.sum(jnp.where(inside, (base - starts)[None], 0), axis=1)
    order = target[None, :] == at[:, None]
    code = jnp.sum((at[:, None] >= base[None]).astype(jnp.int32), axis=1)
    chosen_in = jnp.sum(jnp.where(order, chosen[None, :], 0), axis=1)
    rank = jnp.sum(jnp.where(at[:, None] > at[None, :], chosen_in[None, :], 0), axis=1)
    slot = jnp.arange(rows // 2, dtype=jnp.int32)
    pick = (rank[None, :] == slot[:, None]) & (chosen_in[None, :] == 1)
    routed_code = jnp.sum(jnp.where(pick, code[None, :], 0), axis=1)
    unsort = target[:, None] == at[None, :]
    at_slot = at[None, : rows // 2]
    unpick = (rank[:, None] == at_slot) & (chosen_in[:, None] == 1)
    skipped = (1 - chosen_in)[:, None].astype(F32)
    return order.astype(BF16), code, routed_code, (unsort.astype(BF16), pick.astype(BF16), unpick.astype(BF16), skipped)


def body(axis_of, tokens, lengths, route_mask, router_weight, gains, biases, w_qkv, w_out, w_up, w_down, cotangent):
    section = lax.axis_index("section")
    micro, rows, width = tokens.shape
    own = (w_qkv, w_out, w_up, w_down)
    far = tuple(other_core(value) for value in own)
    own_vec = jnp.concatenate([gains, biases], axis=1)
    far_vec = other_core(own_vec)
    vecs = [jnp.where(section == layer, own_vec, far_vec) for layer in range(2)]
    router_f = router_weight.astype(F32)

    def pick_micro(array):
        return lax.dynamic_index_in_dim(array, section, 0, False)

    crop_lengths, chosen = pick_micro(lengths)[0], pick_micro(route_mask)
    order, code, routed_code, rows_of = row_plan(crop_lengths, chosen)
    x = dot(order, pick_micro(tokens)).astype(BF16)
    cot = dot(order, pick_micro(cotangent)).astype(BF16)
    routed = dot(rows_of[1], x).astype(BF16)
    inputs_one = routed.astype(F32)
    held = (routed_code > 0).astype(F32)
    gate = jax.nn.sigmoid(jnp.sum(inputs_one * router_f[None, :], axis=1))
    scale_one = held * gate
    half = LONG // 2
    groups_one = [(0, 0, half), (96, half, 2 * half), (192, 2 * half, rows // 2)]
    groups_two = [(0, 0, LONG), (192, LONG, 2 * LONG), (384, 2 * LONG, rows)]

    y1, shown_y1, delta_one = run_layer(
        0, groups_one, 128, routed, routed_code, vecs[0], scale_one, own, far, rows_of, all_x=x
    )
    ones = jnp.ones((rows,), F32)
    shown_du2, small_two, grads_two, dout, shown_y2 = run_layer(
        1, groups_two, 256, y1, code, vecs[1], ones, own, far, rows_of, back=cot
    )
    factor = held * gate * (1.0 - gate)
    micro_ids = jnp.arange(micro)
    here = (micro_ids == section).astype(F32)
    counts = here * jnp.sum(route_mask.astype(F32), axis=1)
    extra = jnp.concatenate([here * jnp.sum(scale_one), counts])
    extra = jnp.pad(extra, (0, width - extra.shape[0]))[None]
    factor = held * gate * (1.0 - gate)
    sums, small, (activations, input_grads) = run_fused(
        axis_of, groups_one, 128, routed, routed_code, vecs[0], scale_one, own, far, rows_of, dout,
        (delta_one, factor, router_f[None, :]), grads_two, small_two, extra, (shown_y1, shown_y2, shown_du2),
    )
    small = small.reshape(-1)
    span = vecs[0].shape[1]
    tail = small[span:]
    grads = cast_sums(sums, [value.shape for value in own])

    return (
        activations[None],
        input_grads[None],
        *grads,
        small[: 2 * width][None],
        small[2 * width : span][None],
        tail[:width],
        tail[width : width + micro] / tail[width + micro : width + 2 * micro],
    )


def solution(mesh):
    in_specs = (
        P(None, "dp", None),
        P(None, "dp", None),
        P(None, "dp"),
        P(),
        P("section", None),
        P("section", None),
        P("section", None, None),
        P("section", None, None),
        P("section", None, None),
        P("section", None, None),
        P(None, "dp", None),
    )
    out_specs = (
        P("section", None, "dp", None),
        P("section", None, "dp", None),
        P("section", None, None),
        P("section", None, None),
        P("section", None, None),
        P("section", None, None),
        P("section", None),
        P("section", None),
        P(),
        P(),
    )
    step = functools.partial(body, axis_bits(mesh))
    return jax.shard_map(step, mesh=mesh, in_specs=in_specs, out_specs=out_specs, check_vma=False)
```

```python
import functools

import jax
import jax.numpy as jnp
from jax import lax
from jax.experimental import pallas as pl
from jax.experimental.pallas import tpu as pltpu
from jax.sharding import PartitionSpec as P

HEADS = 12
HEAD = 64
LONG = 197
F32 = jnp.float32
BF16 = jnp.bfloat16
NT = (((1,), (1,)), ((), ()))
TN = (((0,), (0,)), ((), ()))
NN = (((1,), (0,)), ((), ()))


LANES = 768
TILE = 16
GRAD_ROWS = 12 * LANES


def axis_bits(mesh):
    line = mesh.devices[0]
    bits = len(line).bit_length() - 1
    try:
        spots = [tuple(device.coords) for device in line]
    except AttributeError:
        return [0] * bits
    return [
        next((w for w in range(3) if spots[1 << b][w] != spots[0][w]), 0) for b in range(bits)
    ]


HALVINGS = 4
GROUPS = 6
SLOTS = 4


GROUP_PLAN = (
    ((512, 2013), (512, 1203), (512, 132)),
    ((512, 2013), (512, 1320), (512, 123)),
    ((512, 2013), (512, 1023), (512, 123)),
    ((768, 123), (512, 1203), (256, 2013)),
    ((512, 2013), (512, 1203), (512, 123)),
    ((512, 2310), (512, 1032), (512, 123)),
)
GROUP_STARTS = (0, 1, 2, 4, 5, 6)


def sum_plan(axis_of):
    lists = {}
    for bit, axis in enumerate(axis_of):
        lists.setdefault(axis, []).append(bit)
    lists = sorted(lists.values(), key=len)
    while len(lists) < 3:
        lists.append([])
    roles = [lists[0][:1], lists[1][:1], lists[2][:1], lists[2][1:2]]
    plan = []
    for group in GROUP_PLAN:
        chunks, start = [], 0
        for size, code in group:
            order = [bit for place in (1000, 100, 10, 1) for bit in roles[code // place % 10]]
            order += [bit for bit in range(len(axis_of)) if bit not in order]
            chunks.append((start, size, order))
            start += size
        plan.append(chunks)
    return plan


def add_rows(into, into_start, source, start, other, other_start, count):
    tile = next(t for t in (64, 32, 16) if count % t == 0)

    def step(k, carry):
        target, here, there = (
            pl.ds(pl.multiple_of(first + k * tile, TILE), tile) for first in (into_start, start, other_start)
        )
        into[target, :] = source[here, :] + other[there, :]
        return carry

    lax.fori_loop(0, count // tile, step, 0)


class Names:
    pass


def copy_far(source, target, one, two, friend):
    return pltpu.make_async_remote_copy(
        src_ref=source,
        dst_ref=target,
        send_sem=one,
        recv_sem=two,
        device_id=friend,
        device_id_type=pl.DeviceIdType.MESH,
    )


def at_core(core, index, step):
    pl.when(core == index)(step)


GRAD_TILES = 36
GROUP_ROWS = GRAD_ROWS // GROUPS


class Sums:
    def __init__(self, chunks, starts, given):
        self.chunks, self.starts = chunks, starts
        self.shards = set()
        self.bits = bits = len(chunks[0][0][2])
        self.halvings = min(bits, HALVINGS)
        self.acc, self.mate = next(given), next(given)
        self.got = [next(given) for _ in range(bits)]
        self.small_got, self.small = next(given), next(given)
        self.load_sem, self.mate_sem, self.swap_send, self.swap_recv, self.shard_sem = (next(given) for _ in range(5))
        self.send, self.recv, self.back_send, self.back_recv = (next(given) for _ in range(4))
        self.small_send, self.small_recv = (next(given) for _ in range(2))
        self.shown_sem, self.shown_send, self.shown_recv = (next(given) for _ in range(3))
        self.tile_recv, self.give_send, self.give_recv = (next(given) for _ in range(3))
        self.core = lax.axis_index("section")
        self.me = lax.axis_index("dp")
        self.across = (1 - self.core, self.me)
        self.end = starts[-1] + bits + self.halvings + 1

    @staticmethod
    def scratch(chunks, small_rows):
        bits = len(chunks[0][0][2])
        count = sum(len(group) for group in chunks)
        rows = SLOTS * GROUP_ROWS
        held = [pltpu.VMEM((rows, LANES), BF16), pltpu.VMEM((GROUP_ROWS, LANES), BF16)]
        held += [pltpu.VMEM((rows >> min(depth + 1, HALVINGS), LANES), BF16) for depth in range(bits)]
        held += [pltpu.VMEM((bits + 1, small_rows, LANES), F32), pltpu.VMEM((2, small_rows, LANES), F32)]
        held += [pltpu.SemaphoreType.DMA((count,))] * 5
        held += [pltpu.SemaphoreType.DMA((count, bits))] * 4
        held += [pltpu.SemaphoreType.DMA((bits + 1,))] * 2
        held += [pltpu.SemaphoreType.DMA((2,))] * 3
        held += [pltpu.SemaphoreType.DMA((GRAD_TILES,))]
        return held + [pltpu.SemaphoreType.DMA((GROUPS,))] * 2

    def bit_at(self, bit):
        return lax.rem(self.me // (1 << bit), 2)

    def partner(self, bit):
        return (self.core, self.me + (1 - 2 * self.bit_at(bit)) * (1 << bit))

    def open(self):
        friends = [self.across] + [self.partner(bit) for bit in range(self.bits)]
        barrier = pltpu.get_barrier_semaphore()
        for friend in friends:
            pl.semaphore_signal(barrier, inc=1, device_id=friend, device_id_type=pl.DeviceIdType.MESH)
        pl.semaphore_wait(barrier, len(friends))

    @staticmethod
    def layer_of(j):
        return 1 if j < GROUPS // 2 else 0

    def base(self, j, core):
        return (2 * (j % (GROUPS // 2)) + core) * GROUP_ROWS

    def rows_at(self, j, core, c):
        start, size, _ = self.chunks[j][c]
        return pl.ds(pl.multiple_of(self.base(j, core) + start, TILE), size)

    def index(self, j, c):
        return sum(len(group) for group in self.chunks[:j]) + c

    def swap(self, j, c):
        rows, k = self.rows_at(j, 1 - self.core, c), self.index(j, c)
        return copy_far(
            self.grads[1].at[rows, :], self.landed[1].at[rows, :], self.swap_send.at[k], self.swap_recv.at[k],
            self.across,
        )

    def load(self, j, c):
        start, size, _ = self.chunks[j][c]
        target = self.acc.at[pl.ds(j % SLOTS * GROUP_ROWS + start, size), :]
        source = self.grads[self.layer_of(j)].at[self.rows_at(j, self.core, c), :]
        return pltpu.make_async_copy(source, target, self.load_sem.at[self.index(j, c)])

    def load_mate(self, j, c):
        source = self.landed[self.layer_of(j)].at[self.rows_at(j, self.core, c), :]
        start, size, _ = self.chunks[j][c]
        target = self.mate.at[pl.ds(start, size), :]
        return pltpu.make_async_copy(source, target, self.mate_sem.at[self.index(j, c)])

    def span(self, j, c, depth):
        start, size, order = self.chunks[j][c]
        for bit in order[: min(depth, self.halvings)]:
            size //= 2
            start = start + self.bit_at(bit) * size
        return start, size

    def in_acc(self, j, start, size):
        return pl.ds(pl.multiple_of(j % SLOTS * GROUP_ROWS + start, TILE), size)

    def got_at(self, j, c, depth):
        return (j % SLOTS * GROUP_ROWS + self.chunks[j][c][0]) >> min(depth + 1, HALVINGS)

    def down(self, j, c, depth):
        bit = self.chunks[j][c][2][depth]
        start, size = self.span(j, c, depth)
        if depth < self.halvings:
            size //= 2
            start = start + (1 - self.bit_at(bit)) * size
        k = self.index(j, c)
        return copy_far(
            self.acc.at[self.in_acc(j, start, size), :],
            self.got[depth].at[pl.ds(self.got_at(j, c, depth), size), :],
            self.send.at[k, depth],
            self.recv.at[k, depth],
            self.partner(bit),
        )

    def shard(self, j, c):
        start, size = self.span(j, c, self.halvings)
        there = pl.ds(pl.multiple_of(self.base(j, self.core) + start, TILE), size)
        target = self.full[self.layer_of(j)].at[there, :]
        return pltpu.make_async_copy(
            self.acc.at[self.in_acc(j, start, size), :], target, self.shard_sem.at[self.index(j, c)]
        )

    def up(self, j, c, depth):
        bit = self.chunks[j][c][2][depth]
        start, size = self.span(j, c, depth + 1)
        full = self.full[self.layer_of(j)]
        target = full.at[pl.ds(pl.multiple_of(self.base(j, self.core) + start, TILE), size), :]
        source = self.acc.at[self.in_acc(j, start, size), :] if depth == self.halvings - 1 else target
        k = self.index(j, c)
        return copy_far(source, target, self.back_send.at[k, depth], self.back_recv.at[k, depth], self.partner(bit))

    def give(self, j, core):
        full = self.full[self.layer_of(j)]
        rows = pl.ds(self.base(j, core), GROUP_ROWS)
        return copy_far(full.at[rows, :], full.at[rows, :], self.give_send.at[j], self.give_recv.at[j], self.across)

    def each(self, j):
        return range(len(self.chunks[j]))

    def start_swaps(self, j):
        for c in self.each(j):
            self.swap(j, c).start()

    def emptied(self, j):
        for c in self.each(j):
            for depth in range(self.halvings):
                self.down(j, c, depth).wait_send()
            self.up(j, c, self.halvings - 1).wait_send()
            self.shard_done(j, c)

    def shard_done(self, j, c):
        if (j, c) not in self.shards:
            self.shard(j, c).wait()
            self.shards.add((j, c))

    def prepare(self, j):
        if j >= SLOTS:
            self.emptied(j - SLOTS)
        for c in self.each(j):
            self.load(j, c).start()
        if self.layer_of(j) == 0:
            for tile in range(6):
                area = self.landed[0].at[pl.ds(0, LANES), pl.ds(0, STEP)]
                sem = self.tile_recv.at[(j - GROUPS // 2) * 12 + self.core * 6 + tile]
                copy_far(area, area, sem, sem, self.across).wait_recv()
        for c in self.each(j):
            if self.layer_of(j) == 1:
                self.swap(j, c).wait_recv()
            self.load_mate(j, c).start()

    def moment(self, now):
        bits, halvings = self.bits, self.halvings
        for j, start in enumerate(self.starts):
            if start == now:
                for c in self.each(j):
                    self.load(j, c).wait()
                    self.load_mate(j, c).wait()
                    first, size, _ = self.chunks[j][c]
                    at = j % SLOTS * GROUP_ROWS + first
                    add_rows(self.acc, at, self.acc, at, self.mate, first, size)
                    self.down(j, c, 0).start()
            if self.layer_of(j) == 1 and start == now + 2:
                self.start_swaps(j)
        for j, begun in enumerate(self.starts):
            stage = now - begun
            if not 0 < stage <= bits + halvings:
                continue
            for c in self.each(j):
                if stage <= bits:
                    depth = stage - 1
                    if depth < halvings:
                        self.down(j, c, depth).wait_recv()
                    else:
                        self.down(j, c, depth).wait()
                    first, size = self.span(j, c, stage)
                    at = j % SLOTS * GROUP_ROWS + first
                    add_rows(self.acc, at, self.acc, at, self.got[depth], self.got_at(j, c, depth), size)
                    if stage < bits:
                        self.down(j, c, stage).start()
                    else:
                        self.up(j, c, halvings - 1).start()
                        self.shard(j, c).start()
                else:
                    depth = bits + halvings - stage
                    self.up(j, c, depth).wait_recv()
                    if depth == halvings - 1:
                        self.shard_done(j, c)
                    if depth > 0:
                        self.up(j, c, depth - 1).start()
            if stage == bits + halvings:
                core = 1 - self.layer_of(j)
                at_core(self.core, core, lambda j=j, core=core: self.give(j, core).start())
        for j, start in enumerate(self.starts):
            if start == now + 1:
                self.prepare(j)

    def small_step(self, k):
        friend = self.across if k == 0 else self.partner(k - 1)
        return copy_far(
            self.small_out, self.small_got.at[k], self.small_send.at[k], self.small_recv.at[k], friend
        )

    def small_begin(self):
        for layer in range(2):

            def step(layer=layer):
                self.small_out[...] = self.small[layer]
                copy_far(
                    self.small.at[1 - layer], self.small_got.at[0], self.small_send.at[0], self.small_recv.at[0],
                    self.across,
                ).start()

            at_core(self.core, layer, step)

    def small_turn(self, k):
        self.small_step(k).wait()
        self.small_out[...] = self.small_out[...] + self.small_got[k]
        if k < self.bits:
            self.small_step(k + 1).start()

    def shown_keep(self, layer, k):
        return pltpu.make_async_copy(self.shown[2 * k + layer], self.shown_out[k].at[self.core], self.shown_sem.at[k])

    def shown_give(self, layer, k):
        return copy_far(
            self.shown[2 * k + 1 - layer], self.shown_out[k].at[self.core], self.shown_send.at[k],
            self.shown_recv.at[k], self.across,
        )

    def show(self):
        for layer in range(2):

            def step(layer=layer):
                for k in range(2):
                    self.shown_keep(layer, k).start()
                    self.shown_give(layer, k).start()

            at_core(self.core, layer, step)

    def close(self):
        for k in range(2):
            self.shown_keep(0, k).wait()
            self.shown_give(0, k).wait()
        for j in range(GROUPS):
            layer = self.layer_of(j)
            at_core(self.core, layer, lambda j=j: self.give(j, 1 - self.layer_of(j)).wait_recv())
            at_core(self.core, 1 - layer, lambda j=j: self.give(j, 1 - self.layer_of(j)).wait_send())
            if j >= GROUPS - SLOTS:
                self.emptied(j)
            for c in self.each(j):
                if layer == 1:
                    self.swap(j, c).wait_send()
                for depth in range(self.halvings - 1):
                    self.up(j, c, depth).wait_send()


def cast_kernel(first, second, qkv, out, up, down, low, high, in_sem, out_sem):
    rows = low.shape[1]
    per = LANES // rows
    slots = low.shape[0]
    count = 12 * per

    core = lax.axis_index("section")

    def take(k, source=first):
        return pltpu.make_async_copy(source.at[pl.ds(k * rows, rows), :], low.at[k % slots], in_sem.at[k % slots])

    def give(k):
        block, part = divmod(k, per)
        if block < 4:
            target = down.at[0, pl.ds(k * rows, rows), :]
        elif block < 8:
            target = up.at[0, pl.ds(part * rows, rows), pl.ds((block - 4) * LANES, LANES)]
        elif block < 9:
            target = out.at[0, pl.ds(part * rows, rows), :]
        else:
            target = qkv.at[0, pl.ds(part * rows, rows), pl.ds((block - 9) * LANES, LANES)]
        return pltpu.make_async_copy(high.at[k % slots], target, out_sem.at[k % slots])

    def fetch(k):
        at_core(core, 0, lambda: take(k).start())
        at_core(core, 1, lambda: take(k, second).start())

    for k in range(slots):
        fetch(k)
    for k in range(count):
        take(k).wait()
        if k >= slots:
            give(k - slots).wait()
        high[k % slots] = low[k % slots].astype(F32)
        give(k).start()
        if k + slots < count:
            fetch(k + slots)
    for k in range(count - slots, count):
        give(k).wait()


def cast_sums(sums, shapes):
    anywhere = pl.BlockSpec(memory_space=pl.ANY)
    return pl.pallas_call(
        cast_kernel,
        out_shape=[jax.ShapeDtypeStruct(shape, F32) for shape in shapes],
        in_specs=[anywhere] * 2,
        out_specs=[anywhere] * 4,
        scratch_shapes=[
            pltpu.VMEM((6, 256, LANES), BF16),
            pltpu.VMEM((6, 256, LANES), F32),
            pltpu.SemaphoreType.DMA((6,)),
            pltpu.SemaphoreType.DMA((6,)),
        ],
        compiler_params=pltpu.CompilerParams(vmem_limit_bytes=60 * 1024 * 1024),
        cost_estimate=pl.CostEstimate(flops=0, bytes_accessed=42 * 10**6, transcendentals=0),
        name="cast",
    )(*sums)


def other_core(value):
    return lax.ppermute(value, "section", [(0, 1), (1, 0)])


STEP = 256
ROW_TILE = 64
NEGATIVE = -1e30


def dot(left, right, dims=NN):
    return lax.dot_general(left, right, dims, preferred_element_type=F32)


def gelu_parts(pre):
    bell = jnp.exp(pre * pre * -0.5)
    t = pl.reciprocal(1.0 + jnp.abs(pre) * (0.3275911 * 0.7071067811865476))
    poly = t * (0.1274147960 + t * (-0.142248368 + t * (0.710706871 + t * (-0.7265760135 + t * 0.5307027145))))
    tail = poly * bell
    return jnp.where(pre >= 0.0, 1.0 - tail, tail), bell


def norm_stats(values):
    centred = values - jnp.mean(values, axis=-1, keepdims=True)
    recip = lax.rsqrt(jnp.mean(centred * centred, axis=-1, keepdims=True) + 1e-06)
    return centred * recip, recip


def fold(tile):
    return jnp.sum(tile.reshape(tile.shape[0] // 8, 8, tile.shape[1]), axis=0)


def layer_kernel(layer, groups, window, full, *refs):
    r = Names()
    given = iter(refs)
    r.x, r.col_code, r.row_code, r.vec, r.scale = (next(given) for _ in range(5))
    r.own = [next(given) for _ in range(4)]
    r.far = [next(given) for _ in range(4)]
    r.unsort = next(given)
    if full:
        r.dout = next(given)
        r.shown_du, r.small, r.grads, r.du, r.shown_y = (next(given) for _ in range(5))
    else:
        r.all_x, r.unpick, r.skipped = (next(given) for _ in range(3))
        r.all_y, r.shown_y, r.delta = (next(given) for _ in range(3))
    r.weights = [next(given) for _ in range(4)]
    r.w_sem, r.n1, r.qkv, r.probs, r.mask, r.mix, r.between, r.n2, r.act = (next(given) for _ in range(9))
    if full:
        back_names(r, given)
    r.y = next(given)
    layer_body(r, layer, groups, window, full, False)


def back_names(r, given):
    r.n1t, r.n2t, r.mixt, r.dmlp, r.dpre, r.dn, r.datt, r.dmix, r.dqkv = (next(given) for _ in range(9))
    r.down_stage, r.up_stage, r.down_sem, r.up_sem = (next(given) for _ in range(4))


def fused_kernel(groups, window, chunks, *refs):
    r = Names()
    given = iter(refs)
    r.x, r.col_code, r.row_code, r.vec, r.scale = (next(given) for _ in range(5))
    r.own = [next(given) for _ in range(4)]
    r.far = [next(given) for _ in range(4)]
    r.unsort = next(given)
    r.all_dout, r.pick, r.unpick, r.skipped, r.delta, r.factor, r.router = (next(given) for _ in range(7))
    second, second_small, extra = (next(given) for _ in range(3))
    shown = [next(given) for _ in range(3)]
    full = [next(given) for _ in range(2)]
    landed = [next(given) for _ in range(2)]
    first, small_out = (next(given) for _ in range(2))
    shown_out = [next(given) for _ in range(2)]
    r.weights = [next(given) for _ in range(2)]
    r.w_sem, r.n1, r.qkv, r.probs, r.mask, r.mix, r.between, r.n2 = (next(given) for _ in range(8))
    back_names(r, given)
    r.dout, r.du, r.shown_du, r.small, r.router_grad = (next(given) for _ in range(5))
    r.up_tile, r.down_tile, r.tile_sem = (next(given) for _ in range(3))
    sums = Sums(chunks, GROUP_STARTS, given)
    sums.grads, sums.landed, sums.full, sums.small_out = (first, second), landed, full, small_out
    sums.shown, sums.shown_out = (shown[0], shown[1], r.shown_du, shown[2]), shown_out
    r.grads = first
    core = sums.core
    sums.open()
    sums.start_swaps(0)
    sums.start_swaps(1)
    sums.prepare(0)
    early = [0]

    def hook():
        sums.moment(early[0])
        early[0] += 1

    def tile_out(stage, row, column, shape, sem, tile):
        area = (pl.ds(row, shape[0]), pl.ds(column, shape[1]))
        owner = lax.rem(tile // 6, 2)

        @pl.when(core == owner)
        def _():
            pltpu.make_async_copy(stage, first.at[area], sem).start()

        @pl.when(core != owner)
        def _():
            copy_far(stage, landed[0].at[area], sem, sums.tile_recv.at[tile], sums.across).start()

    r.hook, r.tile_out = hook, tile_out
    layer_body(r, 0, groups, window, True, True)

    for index, source in enumerate((r.small, second_small)):
        for row in range(source.shape[1] // LANES):
            sums.small[index, row : row + 1, :] = source[:, row * LANES : (row + 1) * LANES]
        row = source.shape[1] // LANES
        sums.small[index, row : row + 1, :] = r.router_grad[...]
        sums.small[index, row + 1 : row + 2, :] = extra[...]
        left = sums.small.shape[1] - row - 2
        sums.small[index, row + 2 :, :] = jnp.zeros((left, LANES), F32)
    sums.small_begin()
    sums.show()

    for turn, now in enumerate(range(early[0], max(sums.end, early[0] + sums.bits + 1))):
        if now < sums.end:
            sums.moment(now)
        if turn <= sums.bits:
            sums.small_turn(turn)
    sums.close()


def layer_body(r, layer, groups, window, full, is_router):
    hook = r.hook if is_router else lambda: None
    rows, width = r.x.shape
    hidden = r.own[2].shape[2]
    core = lax.axis_index("section")
    pairs = width // 128

    kept = {0: 0, 1: 1, 2: 2, 3: 3} if not is_router else {0: 0, 1: 1}

    def weight(which, source):
        return pltpu.make_async_copy(source[which].at[0], r.weights[which], r.w_sem.at[which])

    def up_tile(source, k, slot):
        span = pl.ds(pl.multiple_of(k * STEP, STEP), STEP)
        return pltpu.make_async_copy(source[2].at[0, :, span], r.up_tile.at[slot], r.tile_sem.at[0, slot])

    def down_tile(source, k, slot):
        span = pl.ds(pl.multiple_of(k * STEP, STEP), STEP)
        return pltpu.make_async_copy(source[3].at[0, span, :], r.down_tile.at[slot], r.tile_sem.at[1, slot])

    def start_tiles(k, slot):
        for near, source in ((core == layer, r.own), (core != layer, r.far)):

            @pl.when(near)
            def _():
                up_tile(source, k, slot).start()
                down_tile(source, k, slot).start()

    for near, source in ((core == layer, r.own), (core != layer, r.far)):

        @pl.when(near)
        def _():
            for which in kept:
                weight(which, source).start()

    if is_router:
        start_tiles(0, 0)
        start_tiles(1, 1)

    def vec(start, count=width):
        return r.vec[:, start : start + count]

    g1, g2, b1, bq, bv, bo, b2 = (vec(k * width) for k in range(7))
    bu_at, bd_at = 7 * width, 7 * width + hidden

    def row_loop(step, init=0):
        def at(k, carry):
            return step(pl.ds(pl.multiple_of(k * ROW_TILE, ROW_TILE), ROW_TILE), carry)

        return lax.fori_loop(0, rows // ROW_TILE, at, init)

    def norm_step(source, gain, bias, target):
        def step(here, carry):
            normal, _ = norm_stats(source[here, :].astype(F32))
            target[here, :] = (normal * gain + bias).astype(BF16)
            return carry

        return step

    def tiles(step):
        for k in range(width // STEP):
            step(slice(k * STEP, (k + 1) * STEP))

    def show(source, target):
        def step(span):
            target[:, span] = dot(r.unsort[...], source[:, span]).astype(BF16)

        tiles(step)

    def spread(routed, others, target, shown):
        def step(span):
            value = dot(r.unpick[...], routed[:, span]) + others[:, span].astype(F32) * r.skipped[...]
            if target is not None:
                target[:, span] = value.astype(BF16)
            shown[:, span] = dot(r.unsort[...], value.astype(BF16)).astype(BF16)

        tiles(step)

    row_loop(norm_step(r.x, g1, b1, r.n1))
    if full and is_router:

        def route_step(span):
            r.dout[:, span] = dot(r.pick[...], r.all_dout[:, span]).astype(BF16)

        tiles(route_step)
    if full:

        def delta_step(here, carry):
            low = (r.dout[here, :].astype(F32) * r.scale[here, :]).astype(BF16)
            r.dmlp[here, :] = low
            return carry + fold(low.astype(F32))

        dbd = row_loop(delta_step, jnp.zeros((8, width), F32))
        r.small[:, bd_at:] = jnp.sum(dbd, axis=0, keepdims=True)

    for k, (start, low, high) in enumerate(groups):
        col = r.col_code[start : start + window, :]
        row = r.row_code[:, start : start + window]
        place = lax.broadcasted_iota(jnp.int32, (window, 1), 0) + start
        col = jnp.where((place >= low) & (place < high), col, -1)
        r.mask[k] = jnp.where(col == row, 0.0, NEGATIVE)

    weight(0, r.own).wait()
    for k in range(3 * width // STEP):
        span = slice(k * STEP, (k + 1) * STEP)
        value = dot(r.n1[...], r.weights[0][:, span])
        if k < width // STEP:
            value = (value + bq[:, span]).astype(BF16).astype(F32) * 0.125
        elif k >= 2 * width // STEP:
            value = value + bv[:, k * STEP - 2 * width : (k + 1) * STEP - 2 * width]
        r.qkv[:, span] = value.astype(BF16)

    hook()
    lane = lax.broadcasted_iota(jnp.int32, (1, 128), 1)

    def halves(block):
        zero = jnp.zeros_like(block)
        return jnp.where(lane < 64, block, zero), jnp.where(lane < 64, zero, block)

    r.mix[...] = jnp.zeros_like(r.mix)

    def lanes(pair, part):
        return pl.ds(pl.multiple_of(pair * 128 + part * width, 128), 128)

    def attend(pair, carry):
        for k, (start, low, high) in enumerate(groups):
            here = slice(start, start + window)
            q, key, v = (r.qkv[here, lanes(pair, part)] for part in range(3))
            vt = v.T
            place = lax.broadcasted_iota(jnp.int32, (1, window), 1) + start
            valid = (place >= low) & (place < high)
            parts = []
            for half, own_key in enumerate(halves(key)):
                scores = dot(own_key, q, NT) + r.mask[k]
                power = jnp.exp(scores - jnp.max(scores, axis=0, keepdims=True))
                total = jnp.sum(power, axis=0, keepdims=True)
                prob = (power * jnp.where(valid, 1.0 / total, 0.0)).astype(BF16)
                if full:
                    r.probs[(pair * 2 + half) * len(groups) + k] = prob
                parts.append(dot(vt[half * 64 : half * 64 + 64], prob))
            mixed = jnp.concatenate(parts, axis=0).T.astype(BF16)
            r.mix[here, lanes(pair, 0)] = r.mix[here, lanes(pair, 0)] + mixed
        return carry

    lax.fori_loop(0, pairs, attend, 0)

    weight(1, r.own).wait()
    for k in range(width // STEP):
        span = slice(k * STEP, (k + 1) * STEP)
        value = dot(r.mix[...], r.weights[1][:, span]) + bo[:, span]
        r.between[:, span] = r.x[:, span].astype(F32) + value
    row_loop(norm_step(r.between, g2, b2, r.n2))
    if full:
        r.n1t[...] = r.n1[...].T
        r.n2t[...] = r.n2[...].T
        r.mixt[...] = r.mix[...].T
    hook()

    if not is_router:
        weight(2, r.own).wait()
        weight(3, r.own).wait()

    def tile_out(stage, row, column, shape, sem, tile):
        target = r.grads.at[pl.ds(row, shape[0]), pl.ds(column, shape[1])]
        pltpu.make_async_copy(stage, target, sem).start()

    tile_out = r.tile_out if is_router else tile_out

    def down_out(k, slot):
        tile_out(
            r.down_stage.at[slot], pl.multiple_of(k * STEP, STEP), 0, (STEP, width), r.down_sem.at[slot], k
        )

    def side_out(block, k, slot):
        row = pl.multiple_of((block + k // 3) * width, width)
        column = pl.multiple_of(k % 3 * STEP, STEP)
        tile = k + {4: 12, 8: 24, 9: 27}[block]
        tile_out(r.up_stage.at[slot], row, column, (width, STEP), r.up_sem.at[slot], tile)

    def down_free(slot):
        target = r.grads.at[pl.ds(0, STEP), pl.ds(0, width)]
        pltpu.make_async_copy(r.down_stage.at[slot], target, r.down_sem.at[slot]).wait()

    def side_free(slot):
        target = r.grads.at[pl.ds(0, width), pl.ds(0, STEP)]
        pltpu.make_async_copy(r.up_stage.at[slot], target, r.up_sem.at[slot]).wait()

    def hidden_step(k, carry):
        at = pl.multiple_of(k * STEP, STEP)
        span = pl.ds(at, STEP)
        slot = lax.rem(k, 2)
        if is_router:
            up_tile(r.own, k, slot).wait()
            down_tile(r.own, k, slot).wait()
            w_up, w_down = r.up_tile[slot], r.down_tile[slot]
        else:
            w_up, w_down = r.weights[2][:, span], r.weights[3][span, :]
        pre = dot(r.n2[...], w_up) + r.vec[:, pl.ds(at + bu_at, STEP)]
        cdf, bell = gelu_parts(pre)
        act = (pre * cdf).astype(BF16)
        if not is_router:
            r.act[:, span] = act
        if full:

            @pl.when(k >= 2)
            def _():
                down_free(slot)
                side_free(slot)

            slope = cdf + pre * bell * 0.3989422804014327
            dact = dot(r.dmlp[...], w_down, NT)
            dpre = (dact * slope).astype(BF16)
            if is_router:
                r.dn[...] = r.dn[...] + dot(dpre, w_up, NT)
            else:
                r.dpre[:, span] = dpre
            r.small[:, pl.ds(at + bu_at, STEP)] = jnp.sum(dpre.astype(F32), axis=0, keepdims=True)
            r.down_stage[slot] = dot(act, r.dmlp[...], TN).astype(BF16)
            down_out(k, slot)
            r.up_stage[slot] = dot(r.n2t[...], dpre).astype(BF16)
            side_out(4, k, slot)
        if is_router:

            @pl.when(k + 2 < hidden // STEP)
            def _():
                start_tiles(k + 2, slot)

        return carry

    steps = hidden // STEP
    if is_router:
        r.dn[...] = jnp.zeros_like(r.dn)
        for part in range(2):
            lax.fori_loop(part * steps // 2, (part + 1) * steps // 2, hidden_step, 0)
            if part == 1:
                down_free(0)
                down_free(1)
            hook()
    else:
        lax.fori_loop(0, steps, hidden_step, 0)
    if not (full and is_router):
        for k in range(width // STEP):
            span = slice(k * STEP, (k + 1) * STEP)
            value = dot(r.act[...], r.weights[3][:, span]) + vec(bd_at)[:, span]
            source = r.x[:, span].astype(F32)
            value = r.between[:, span] - source + value
            if not full:
                r.delta[:, span] = value
            r.y[:, span] = (source + r.scale[...] * value).astype(BF16)
    if not full:
        spread(r.y, r.all_x, r.all_y, r.shown_y)
        return
    if not is_router:
        show(r.y, r.shown_y)

    if not is_router:
        for k in range(width // STEP):
            span = slice(k * STEP, (k + 1) * STEP)
            r.dn[:, span] = dot(r.dpre[...], r.weights[2][span, :], NT)

    def norm_back(source, gain, here):
        normal, recip = norm_stats(source[here, :].astype(F32))
        grad = r.dn[here, :]
        hat = grad * gain
        back = recip * (
            hat - jnp.mean(hat, axis=-1, keepdims=True) - normal * jnp.mean(hat * normal, axis=-1, keepdims=True)
        )
        return back, fold(grad * normal), fold(grad)

    def second_back(here, carry):
        back, dg, db = norm_back(r.between, g2, here)
        r.between[here, :] = back
        total = (r.dout[here, :].astype(F32) * r.scale[here, :] + back).astype(BF16)
        r.datt[here, :] = total
        return carry[0] + dg, carry[1] + db, carry[2] + fold(total.astype(F32))

    zero = jnp.zeros((8, width), F32)
    dg2, db2, dbo = row_loop(second_back, (zero, zero, zero))
    r.small[:, width : 2 * width] = jnp.sum(dg2, axis=0, keepdims=True)
    r.small[:, 6 * width : 7 * width] = jnp.sum(db2, axis=0, keepdims=True)
    r.small[:, 5 * width : 6 * width] = jnp.sum(dbo, axis=0, keepdims=True)

    for k in range(width // STEP):
        span = slice(k * STEP, (k + 1) * STEP)
        r.dmix[:, span] = dot(r.datt[...], r.weights[1][span, :], NT).astype(BF16)
        slot = k % 2
        side_free(slot)
        r.up_stage[slot] = dot(r.mixt[...], r.datt[:, span]).astype(BF16)
        side_out(8, k, slot)

    r.dqkv[...] = jnp.zeros_like(r.dqkv)

    def attend_back(pair, carry):
        for k, (start, low, high) in enumerate(groups):
            here = slice(start, start + window)
            q, key, v = (r.qkv[here, lanes(pair, part)] for part in range(3))
            dm = r.dmix[here, lanes(pair, 0)]
            key_t = key.T
            dq, dk, dv = [], None, None
            for half, (own_q, own_v, own_dm) in enumerate(zip(halves(q), halves(v), halves(dm))):
                prob = r.probs[(pair * 2 + half) * len(groups) + k]
                wide = prob.astype(F32)
                dprob = dot(own_v, dm, NT)
                product = wide * dprob
                ds = (product - wide * jnp.sum(product, axis=0, keepdims=True)).astype(BF16)
                dq.append(dot(key_t[half * 64 : half * 64 + 64], ds))
                one, two = dot(ds, own_q), dot(prob, own_dm)
                dk, dv = (one, two) if dk is None else (dk + one, dv + two)
            dq = jnp.concatenate(dq, axis=0).T * 0.125
            for part, value in enumerate((dq, dk, dv)):
                spot = lanes(pair, part)
                r.dqkv[here, spot] = r.dqkv[here, spot] + value.astype(BF16)
        return carry

    lax.fori_loop(0, pairs, attend_back, 0)
    hook()

    for k in range(3 * width // STEP):
        span = slice(k * STEP, (k + 1) * STEP)
        block = r.dqkv[:, span]
        if not width <= k * STEP < 2 * width:
            at = 3 * width + k * STEP - (width if k * STEP >= width else 0)
            r.small[:, at : at + STEP] = jnp.sum(block.astype(F32), axis=0, keepdims=True)
        slot = (k + 1) % 2
        side_free(slot)
        r.up_stage[slot] = dot(r.n1t[...], block).astype(BF16)
        side_out(9, k, slot)
    side_free(0)
    side_free(1)
    hook()

    for k in range(width // STEP):
        span = slice(k * STEP, (k + 1) * STEP)
        r.dn[:, span] = dot(r.dqkv[...], r.weights[0][span, :], NT)

    def first_back(here, carry):
        back, dg, db = norm_back(r.x, g1, here)
        dout = r.dout[here, :].astype(F32)
        total = dout + r.between[here, :] + back
        sums = [carry[0] + dg, carry[1] + db]
        if is_router:
            slope = jnp.sum(dout * r.delta[here, :], axis=1, keepdims=True) * r.factor[here, :]
            total = total + slope * r.router[...]
            sums.append(carry[2] + fold(slope * r.x[here, :].astype(F32)))
        r.du[here, :] = total.astype(BF16)
        return tuple(sums)

    sums = row_loop(first_back, (zero,) * (3 if is_router else 2))
    r.small[:, :width] = jnp.sum(sums[0], axis=0, keepdims=True)
    r.small[:, 2 * width : 3 * width] = jnp.sum(sums[1], axis=0, keepdims=True)
    if is_router:
        r.router_grad[...] = jnp.sum(sums[2], axis=0, keepdims=True)
        spread(r.du, r.all_dout, None, r.shown_du)
    else:
        show(r.du, r.shown_du)
    if not is_router:
        down_free(0)
        down_free(1)


def front_scratch(rows, width, hidden, groups, window, full, kept):
    sizes = [(width, 3 * width), (width, width), (width, hidden), (hidden, width)][:kept]
    held = [pltpu.VMEM(size, BF16) for size in sizes]
    held += [pltpu.SemaphoreType.DMA((4,))]
    held += [pltpu.VMEM((rows, width), BF16), pltpu.VMEM((rows, 3 * width), BF16)]
    held += [pltpu.VMEM((HEADS * len(groups) if full else 1, window, window), BF16)]
    held += [pltpu.VMEM((len(groups), window, window), F32), pltpu.VMEM((rows, width), BF16)]
    return held + [pltpu.VMEM((rows, width), F32), pltpu.VMEM((rows, width), BF16)]


def back_scratch(rows, width, hidden):
    held = [pltpu.VMEM((width, rows), BF16)] * 3 + [pltpu.VMEM((rows, width), BF16)]
    held += [pltpu.VMEM((rows, hidden), BF16), pltpu.VMEM((rows, width), F32)]
    held += [pltpu.VMEM((rows, width), BF16)] * 2 + [pltpu.VMEM((rows, 3 * width), BF16)]
    held += [pltpu.VMEM((2, STEP, width), BF16), pltpu.VMEM((2, width, STEP), BF16)]
    return held + [pltpu.SemaphoreType.DMA((2,))] * 2


def run_layer(layer, groups, window, x, code, vec, scale, own, far, rows_of, all_x=None, back=None):
    rows, width = x.shape
    hidden = own[2].shape[2]
    full = back is not None
    inside = pl.BlockSpec(memory_space=pltpu.VMEM)
    anywhere = pl.BlockSpec(memory_space=pl.ANY)
    unsort, pick, unpick, skipped = rows_of
    args = [x, code[:, None], code[None, :], vec, scale[:, None], *own, *far, unsort]
    every = unsort.shape[0]
    if full:
        args += [back]
        outs = [((every, width), BF16), ((1, vec.shape[1]), F32), ((GRAD_ROWS, LANES), BF16)]
        outs += [((rows, width), BF16)] * 2
    else:
        args += [all_x, unpick, skipped]
        outs = [((every, width), BF16), ((every, width), BF16), ((rows, width), F32)]
    in_specs = [inside] * 5 + [anywhere] * 8 + [inside] * (len(args) - 13)
    out_specs = [anywhere if full and k == 2 else inside for k in range(len(outs))]
    scratch = front_scratch(rows, width, hidden, groups, window, full, 4)
    scratch += [pltpu.VMEM((rows, hidden), BF16)]
    if full:
        scratch += back_scratch(rows, width, hidden)
    scratch += [pltpu.VMEM((rows, width), BF16)]
    flops = rows * width * (3 * width + width + 2 * hidden) * (6 if full else 2)
    return pl.pallas_call(
        functools.partial(layer_kernel, layer, groups, window, full),
        out_shape=[jax.ShapeDtypeStruct(*one) for one in outs],
        in_specs=in_specs,
        out_specs=out_specs,
        scratch_shapes=scratch,
        compiler_params=pltpu.CompilerParams(vmem_limit_bytes=60 * 1024 * 1024),
        cost_estimate=pl.CostEstimate(flops=flops, bytes_accessed=3 * 10**7, transcendentals=0),
        name="back" if full else "forward",
    )(*args)


def run_fused(axis_of, groups, window, x, code, vec, scale, own, far, rows_of, back, router, second, second_small, extra, shown):
    rows, width = x.shape
    hidden = own[2].shape[2]
    chunks = sum_plan(axis_of)
    inside = pl.BlockSpec(memory_space=pltpu.VMEM)
    anywhere = pl.BlockSpec(memory_space=pl.ANY)
    unsort, pick, unpick, skipped = rows_of
    delta, factor, router_row = router
    every = unsort.shape[0]
    args = [x, code[:, None], code[None, :], vec, scale[:, None], *own, *far, unsort]
    args += [back, pick, unpick, skipped, delta, factor[:, None], router_row]
    args += [second, second_small, extra, *shown]
    small_rows = -(-(vec.shape[1] // LANES + 2) // 8) * 8
    outs = [((GRAD_ROWS, LANES), BF16)] * 5
    outs += [((small_rows, LANES), F32)] + [((2, every, width), BF16)] * 2
    scratch = front_scratch(rows, width, hidden, groups, window, True, 2)
    scratch += back_scratch(rows, width, hidden)
    scratch += [pltpu.VMEM((rows, width), BF16)] * 2 + [pltpu.VMEM((every, width), BF16)]
    scratch += [pltpu.VMEM((1, vec.shape[1]), F32), pltpu.VMEM((1, width), F32)]
    scratch += [pltpu.VMEM((2, width, STEP), BF16), pltpu.VMEM((2, STEP, width), BF16)]
    scratch += [pltpu.SemaphoreType.DMA((2, 2))]
    scratch += Sums.scratch(chunks, small_rows)
    *sums, _, _, _, small, acts, grads = pl.pallas_call(
        functools.partial(fused_kernel, groups, window, chunks),
        out_shape=[jax.ShapeDtypeStruct(*one) for one in outs],
        in_specs=[inside] * 5 + [anywhere] * 8 + [inside] * 8 + [anywhere] + [inside] * 2 + [anywhere] * 3,
        out_specs=[anywhere] * 5 + [inside] + [anywhere] * 2,
        scratch_shapes=scratch,
        compiler_params=pltpu.CompilerParams(
            collective_id=0, has_side_effects=True, vmem_limit_bytes=64 * 1024 * 1024
        ),
        cost_estimate=pl.CostEstimate(flops=10**10, bytes_accessed=6 * 10**8, transcendentals=0),
        name="fused",
    )(*args)
    return sums, small, (acts, grads)


def row_plan(crop_lengths, chosen):
    rows = chosen.shape[0]
    ends = jnp.cumsum(crop_lengths)
    starts = ends - crop_lengths
    is_long = crop_lengths == LONG
    long_before = jnp.cumsum(is_long.astype(jnp.int32)) - is_long
    short = jnp.where(is_long, 0, crop_lengths)
    short_before = jnp.cumsum(short) - short
    base = jnp.where(is_long, long_before * LONG, 2 * LONG + short_before)
    at = jnp.arange(rows, dtype=jnp.int32)
    inside = (at[:, None] >= starts[None]) & (at[:, None] < ends[None])
    target = at + jnp.sum(jnp.where(inside, (base - starts)[None], 0), axis=1)
    order = target[None, :] == at[:, None]
    code = jnp.sum((at[:, None] >= base[None]).astype(jnp.int32), axis=1)
    chosen_in = jnp.sum(jnp.where(order, chosen[None, :], 0), axis=1)
    rank = jnp.sum(jnp.where(at[:, None] > at[None, :], chosen_in[None, :], 0), axis=1)
    slot = jnp.arange(rows // 2, dtype=jnp.int32)
    pick = (rank[None, :] == slot[:, None]) & (chosen_in[None, :] == 1)
    routed_code = jnp.sum(jnp.where(pick, code[None, :], 0), axis=1)
    unsort = target[:, None] == at[None, :]
    at_slot = at[None, : rows // 2]
    unpick = (rank[:, None] == at_slot) & (chosen_in[:, None] == 1)
    skipped = (1 - chosen_in)[:, None].astype(F32)
    return order.astype(BF16), code, routed_code, (unsort.astype(BF16), pick.astype(BF16), unpick.astype(BF16), skipped)


def body(axis_of, tokens, lengths, route_mask, router_weight, gains, biases, w_qkv, w_out, w_up, w_down, cotangent):
    section = lax.axis_index("section")
    micro, rows, width = tokens.shape
    own = (w_qkv, w_out, w_up, w_down)
    far = tuple(other_core(value) for value in own)
    own_vec = jnp.concatenate([gains, biases], axis=1)
    far_vec = other_core(own_vec)
    vecs = [jnp.where(section == layer, own_vec, far_vec) for layer in range(2)]
    router_f = router_weight.astype(F32)

    def pick_micro(array):
        return lax.dynamic_index_in_dim(array, section, 0, False)

    crop_lengths, chosen = pick_micro(lengths)[0], pick_micro(route_mask)
    order, code, routed_code, rows_of = row_plan(crop_lengths, chosen)
    x = dot(order, pick_micro(tokens)).astype(BF16)
    cot = dot(order, pick_micro(cotangent)).astype(BF16)
    routed = dot(rows_of[1], x).astype(BF16)
    inputs_one = routed.astype(F32)
    held = (routed_code > 0).astype(F32)
    gate = jax.nn.sigmoid(jnp.sum(inputs_one * router_f[None, :], axis=1))
    scale_one = held * gate
    half = LONG // 2
    groups_one = [(0, 0, half), (96, half, 2 * half), (192, 2 * half, rows // 2)]
    groups_two = [(0, 0, LONG), (192, LONG, 2 * LONG), (384, 2 * LONG, rows)]

    y1, shown_y1, delta_one = run_layer(
        0, groups_one, 128, routed, routed_code, vecs[0], scale_one, own, far, rows_of, all_x=x
    )
    ones = jnp.ones((rows,), F32)
    shown_du2, small_two, grads_two, dout, shown_y2 = run_layer(
        1, groups_two, 256, y1, code, vecs[1], ones, own, far, rows_of, back=cot
    )
    factor = held * gate * (1.0 - gate)
    micro_ids = jnp.arange(micro)
    here = (micro_ids == section).astype(F32)
    counts = here * jnp.sum(route_mask.astype(F32), axis=1)
    extra = jnp.concatenate([here * jnp.sum(scale_one), counts])
    extra = jnp.pad(extra, (0, width - extra.shape[0]))[None]
    factor = held * gate * (1.0 - gate)
    sums, small, (activations, input_grads) = run_fused(
        axis_of, groups_one, 128, routed, routed_code, vecs[0], scale_one, own, far, rows_of, dout,
        (delta_one, factor, router_f[None, :]), grads_two, small_two, extra, (shown_y1, shown_y2, shown_du2),
    )
    small = small.reshape(-1)
    span = vecs[0].shape[1]
    tail = small[span:]
    grads = cast_sums(sums, [value.shape for value in own])

    return (
        activations[None],
        input_grads[None],
        *grads,
        small[: 2 * width][None],
        small[2 * width : span][None],
        tail[:width],
        tail[width : width + micro] / tail[width + micro : width + 2 * micro],
    )


def solution(mesh):
    in_specs = (
        P(None, "dp", None),
        P(None, "dp", None),
        P(None, "dp"),
        P(),
        P("section", None),
        P("section", None),
        P("section", None, None),
        P("section", None, None),
        P("section", None, None),
        P("section", None, None),
        P(None, "dp", None),
    )
    out_specs = (
        P("section", None, "dp", None),
        P("section", None, "dp", None),
        P("section", None, None),
        P("section", None, None),
        P("section", None, None),
        P("section", None, None),
        P("section", None),
        P("section", None),
        P(),
        P(),
    )
    step = functools.partial(body, axis_bits(mesh))
    return jax.shard_map(step, mesh=mesh, in_specs=in_specs, out_specs=out_specs, check_vma=False)
```

```python
import functools

import jax
import jax.numpy as jnp
from jax import lax
from jax.experimental import pallas as pl
from jax.experimental.pallas import tpu as pltpu
from jax.sharding import PartitionSpec as P

HEADS = 12
HEAD = 64
LONG = 197
F32 = jnp.float32
BF16 = jnp.bfloat16
NT = (((1,), (1,)), ((), ()))
TN = (((0,), (0,)), ((), ()))
NN = (((1,), (0,)), ((), ()))


LANES = 768
TILE = 16
GRAD_ROWS = 12 * LANES


def axis_bits(mesh):
    line = mesh.devices[0]
    bits = len(line).bit_length() - 1
    try:
        spots = [tuple(device.coords) for device in line]
    except AttributeError:
        return [0] * bits
    return [
        next((w for w in range(3) if spots[1 << b][w] != spots[0][w]), 0) for b in range(bits)
    ]


HALVINGS = 4
GROUPS = 6
SLOTS = 4


GROUP_PLAN = (
    ((512, 2013), (512, 1203), (512, 132)),
    ((512, 2013), (512, 1320), (512, 123)),
    ((512, 2013), (512, 1023), (512, 123)),
    ((768, 123), (512, 1203), (256, 2013)),
    ((512, 2013), (512, 1203), (512, 123)),
    ((512, 2310), (512, 1032), (512, 123)),
)
GROUP_STARTS = (0, 1, 2, 4, 5, 6)


def sum_plan(axis_of):
    lists = {}
    for bit, axis in enumerate(axis_of):
        lists.setdefault(axis, []).append(bit)
    lists = sorted(lists.values(), key=len)
    while len(lists) < 3:
        lists.append([])
    roles = [lists[0][:1], lists[1][:1], lists[2][:1], lists[2][1:2]]
    plan = []
    for group in GROUP_PLAN:
        chunks, start = [], 0
        for size, code in group:
            order = [bit for place in (1000, 100, 10, 1) for bit in roles[code // place % 10]]
            order += [bit for bit in range(len(axis_of)) if bit not in order]
            chunks.append((start, size, order))
            start += size
        plan.append(chunks)
    return plan


def add_rows(into, into_start, source, start, other, other_start, count):
    tile = next(t for t in (64, 32, 16) if count % t == 0)

    def step(k, carry):
        target, here, there = (
            pl.ds(pl.multiple_of(first + k * tile, TILE), tile) for first in (into_start, start, other_start)
        )
        into[target, :] = source[here, :] + other[there, :]
        return carry

    lax.fori_loop(0, count // tile, step, 0)


class Names:
    pass


def copy_far(source, target, one, two, friend):
    return pltpu.make_async_remote_copy(
        src_ref=source,
        dst_ref=target,
        send_sem=one,
        recv_sem=two,
        device_id=friend,
        device_id_type=pl.DeviceIdType.MESH,
    )


def at_core(core, index, step):
    pl.when(core == index)(step)


GRAD_TILES = 36
GROUP_ROWS = GRAD_ROWS // GROUPS


class Sums:
    def __init__(self, chunks, starts, given):
        self.chunks, self.starts = chunks, starts
        self.shards = set()
        self.bits = bits = len(chunks[0][0][2])
        self.halvings = min(bits, HALVINGS)
        self.acc, self.mate = next(given), next(given)
        self.got = [next(given) for _ in range(bits)]
        self.small_got, self.small = next(given), next(given)
        self.load_sem, self.mate_sem, self.swap_send, self.swap_recv, self.shard_sem = (next(given) for _ in range(5))
        self.send, self.recv, self.back_send, self.back_recv = (next(given) for _ in range(4))
        self.small_send, self.small_recv = (next(given) for _ in range(2))
        self.shown_sem, self.shown_send, self.shown_recv = (next(given) for _ in range(3))
        self.tile_recv, self.give_send, self.give_recv = (next(given) for _ in range(3))
        self.core = lax.axis_index("section")
        self.me = lax.axis_index("dp")
        self.across = (1 - self.core, self.me)
        self.end = starts[-1] + bits + self.halvings + 1

    @staticmethod
    def scratch(chunks, small_rows):
        bits = len(chunks[0][0][2])
        count = sum(len(group) for group in chunks)
        rows = SLOTS * GROUP_ROWS
        held = [pltpu.VMEM((rows, LANES), BF16), pltpu.VMEM((GROUP_ROWS, LANES), BF16)]
        held += [pltpu.VMEM((rows >> min(depth + 1, HALVINGS), LANES), BF16) for depth in range(bits)]
        held += [pltpu.VMEM((bits + 1, small_rows, LANES), F32), pltpu.VMEM((2, small_rows, LANES), F32)]
        held += [pltpu.SemaphoreType.DMA((count,))] * 5
        held += [pltpu.SemaphoreType.DMA((count, bits))] * 4
        held += [pltpu.SemaphoreType.DMA((bits + 1,))] * 2
        held += [pltpu.SemaphoreType.DMA((2,))] * 3
        held += [pltpu.SemaphoreType.DMA((GRAD_TILES,))]
        return held + [pltpu.SemaphoreType.DMA((GROUPS,))] * 2

    def bit_at(self, bit):
        return lax.rem(self.me // (1 << bit), 2)

    def partner(self, bit):
        return (self.core, self.me + (1 - 2 * self.bit_at(bit)) * (1 << bit))

    def open(self):
        friends = [self.across] + [self.partner(bit) for bit in range(self.bits)]
        barrier = pltpu.get_barrier_semaphore()
        for friend in friends:
            pl.semaphore_signal(barrier, inc=1, device_id=friend, device_id_type=pl.DeviceIdType.MESH)
        pl.semaphore_wait(barrier, len(friends))

    @staticmethod
    def layer_of(j):
        return 1 if j < GROUPS // 2 else 0

    def base(self, j, core):
        return (2 * (j % (GROUPS // 2)) + core) * GROUP_ROWS

    def rows_at(self, j, core, c):
        start, size, _ = self.chunks[j][c]
        return pl.ds(pl.multiple_of(self.base(j, core) + start, TILE), size)

    def index(self, j, c):
        return sum(len(group) for group in self.chunks[:j]) + c

    def swap(self, j, c):
        rows, k = self.rows_at(j, 1 - self.core, c), self.index(j, c)
        return copy_far(
            self.grads[1].at[rows, :], self.landed[1].at[rows, :], self.swap_send.at[k], self.swap_recv.at[k],
            self.across,
        )

    def load(self, j, c):
        start, size, _ = self.chunks[j][c]
        target = self.acc.at[pl.ds(j % SLOTS * GROUP_ROWS + start, size), :]
        source = self.grads[self.layer_of(j)].at[self.rows_at(j, self.core, c), :]
        return pltpu.make_async_copy(source, target, self.load_sem.at[self.index(j, c)])

    def load_mate(self, j, c):
        source = self.landed[self.layer_of(j)].at[self.rows_at(j, self.core, c), :]
        start, size, _ = self.chunks[j][c]
        target = self.mate.at[pl.ds(start, size), :]
        return pltpu.make_async_copy(source, target, self.mate_sem.at[self.index(j, c)])

    def span(self, j, c, depth):
        start, size, order = self.chunks[j][c]
        for bit in order[: min(depth, self.halvings)]:
            size //= 2
            start = start + self.bit_at(bit) * size
        return start, size

    def in_acc(self, j, start, size):
        return pl.ds(pl.multiple_of(j % SLOTS * GROUP_ROWS + start, TILE), size)

    def got_at(self, j, c, depth):
        return (j % SLOTS * GROUP_ROWS + self.chunks[j][c][0]) >> min(depth + 1, HALVINGS)

    def down(self, j, c, depth):
        bit = self.chunks[j][c][2][depth]
        start, size = self.span(j, c, depth)
        if depth < self.halvings:
            size //= 2
            start = start + (1 - self.bit_at(bit)) * size
        k = self.index(j, c)
        return copy_far(
            self.acc.at[self.in_acc(j, start, size), :],
            self.got[depth].at[pl.ds(self.got_at(j, c, depth), size), :],
            self.send.at[k, depth],
            self.recv.at[k, depth],
            self.partner(bit),
        )

    def shard(self, j, c):
        start, size = self.span(j, c, self.halvings)
        there = pl.ds(pl.multiple_of(self.base(j, self.core) + start, TILE), size)
        target = self.full[self.layer_of(j)].at[there, :]
        return pltpu.make_async_copy(
            self.acc.at[self.in_acc(j, start, size), :], target, self.shard_sem.at[self.index(j, c)]
        )

    def up(self, j, c, depth):
        bit = self.chunks[j][c][2][depth]
        start, size = self.span(j, c, depth + 1)
        full = self.full[self.layer_of(j)]
        target = full.at[pl.ds(pl.multiple_of(self.base(j, self.core) + start, TILE), size), :]
        source = self.acc.at[self.in_acc(j, start, size), :] if depth == self.halvings - 1 else target
        k = self.index(j, c)
        return copy_far(source, target, self.back_send.at[k, depth], self.back_recv.at[k, depth], self.partner(bit))

    def give(self, j, core):
        full = self.full[self.layer_of(j)]
        rows = pl.ds(self.base(j, core), GROUP_ROWS)
        return copy_far(full.at[rows, :], full.at[rows, :], self.give_send.at[j], self.give_recv.at[j], self.across)

    def each(self, j):
        return range(len(self.chunks[j]))

    def start_swaps(self, j):
        for c in self.each(j):
            self.swap(j, c).start()

    def emptied(self, j):
        for c in self.each(j):
            for depth in range(self.halvings):
                self.down(j, c, depth).wait_send()
            self.up(j, c, self.halvings - 1).wait_send()
            self.shard_done(j, c)

    def shard_done(self, j, c):
        if (j, c) not in self.shards:
            self.shard(j, c).wait()
            self.shards.add((j, c))

    def prepare(self, j):
        if j >= SLOTS:
            self.emptied(j - SLOTS)
        for c in self.each(j):
            self.load(j, c).start()
        if self.layer_of(j) == 0:
            for tile in range(6):
                area = self.landed[0].at[pl.ds(0, LANES), pl.ds(0, STEP)]
                sem = self.tile_recv.at[(j - GROUPS // 2) * 12 + self.core * 6 + tile]
                copy_far(area, area, sem, sem, self.across).wait_recv()
        for c in self.each(j):
            if self.layer_of(j) == 1:
                self.swap(j, c).wait_recv()
            self.load_mate(j, c).start()

    def moment(self, now):
        bits, halvings = self.bits, self.halvings
        for j, start in enumerate(self.starts):
            if start == now:
                for c in self.each(j):
                    self.load(j, c).wait()
                    self.load_mate(j, c).wait()
                    first, size, _ = self.chunks[j][c]
                    at = j % SLOTS * GROUP_ROWS + first
                    add_rows(self.acc, at, self.acc, at, self.mate, first, size)
                    self.down(j, c, 0).start()
            if self.layer_of(j) == 1 and start == now + 2:
                self.start_swaps(j)
        for j, begun in enumerate(self.starts):
            stage = now - begun
            if not 0 < stage <= bits + halvings:
                continue
            for c in self.each(j):
                if stage <= bits:
                    depth = stage - 1
                    if depth < halvings:
                        self.down(j, c, depth).wait_recv()
                    else:
                        self.down(j, c, depth).wait()
                    first, size = self.span(j, c, stage)
                    at = j % SLOTS * GROUP_ROWS + first
                    add_rows(self.acc, at, self.acc, at, self.got[depth], self.got_at(j, c, depth), size)
                    if stage < bits:
                        self.down(j, c, stage).start()
                    else:
                        self.up(j, c, halvings - 1).start()
                        self.shard(j, c).start()
                else:
                    depth = bits + halvings - stage
                    self.up(j, c, depth).wait_recv()
                    if depth == halvings - 1:
                        self.shard_done(j, c)
                    if depth > 0:
                        self.up(j, c, depth - 1).start()
            if stage == bits + halvings:
                core = 1 - self.layer_of(j)
                at_core(self.core, core, lambda j=j, core=core: self.give(j, core).start())
        for j, start in enumerate(self.starts):
            if start == now + 1:
                self.prepare(j)

    def small_step(self, k):
        friend = self.across if k == 0 else self.partner(k - 1)
        return copy_far(
            self.small_out, self.small_got.at[k], self.small_send.at[k], self.small_recv.at[k], friend
        )

    def small_begin(self):
        for layer in range(2):

            def step(layer=layer):
                self.small_out[...] = self.small[layer]
                copy_far(
                    self.small.at[1 - layer], self.small_got.at[0], self.small_send.at[0], self.small_recv.at[0],
                    self.across,
                ).start()

            at_core(self.core, layer, step)

    def small_turn(self, k):
        self.small_step(k).wait()
        self.small_out[...] = self.small_out[...] + self.small_got[k]
        if k < self.bits:
            self.small_step(k + 1).start()

    def shown_keep(self, layer, k):
        return pltpu.make_async_copy(self.shown[2 * k + layer], self.shown_out[k].at[self.core], self.shown_sem.at[k])

    def shown_give(self, layer, k):
        return copy_far(
            self.shown[2 * k + 1 - layer], self.shown_out[k].at[self.core], self.shown_send.at[k],
            self.shown_recv.at[k], self.across,
        )

    def show(self):
        for layer in range(2):

            def step(layer=layer):
                for k in range(2):
                    self.shown_keep(layer, k).start()
                    self.shown_give(layer, k).start()

            at_core(self.core, layer, step)

    def close(self):
        for k in range(2):
            self.shown_keep(0, k).wait()
            self.shown_give(0, k).wait()
        for j in range(GROUPS):
            layer = self.layer_of(j)
            at_core(self.core, layer, lambda j=j: self.give(j, 1 - self.layer_of(j)).wait_recv())
            at_core(self.core, 1 - layer, lambda j=j: self.give(j, 1 - self.layer_of(j)).wait_send())
            if j >= GROUPS - SLOTS:
                self.emptied(j)
            for c in self.each(j):
                if layer == 1:
                    self.swap(j, c).wait_send()
                for depth in range(self.halvings - 1):
                    self.up(j, c, depth).wait_send()


def cast_kernel(first, second, qkv, out, up, down, low, high, in_sem, out_sem):
    rows = low.shape[1]
    per = LANES // rows
    slots = low.shape[0]
    count = 12 * per

    core = lax.axis_index("section")

    def take(k, source=first):
        return pltpu.make_async_copy(source.at[pl.ds(k * rows, rows), :], low.at[k % slots], in_sem.at[k % slots])

    def give(k):
        block, part = divmod(k, per)
        if block < 4:
            target = down.at[0, pl.ds(k * rows, rows), :]
        elif block < 8:
            target = up.at[0, pl.ds(part * rows, rows), pl.ds((block - 4) * LANES, LANES)]
        elif block < 9:
            target = out.at[0, pl.ds(part * rows, rows), :]
        else:
            target = qkv.at[0, pl.ds(part * rows, rows), pl.ds((block - 9) * LANES, LANES)]
        return pltpu.make_async_copy(high.at[k % slots], target, out_sem.at[k % slots])

    def fetch(k):
        at_core(core, 0, lambda: take(k).start())
        at_core(core, 1, lambda: take(k, second).start())

    for k in range(slots):
        fetch(k)
    for k in range(count):
        take(k).wait()
        if k >= slots:
            give(k - slots).wait()
        high[k % slots] = low[k % slots].astype(F32)
        give(k).start()
        if k + slots < count:
            fetch(k + slots)
    for k in range(count - slots, count):
        give(k).wait()


def cast_sums(sums, shapes):
    anywhere = pl.BlockSpec(memory_space=pl.ANY)
    return pl.pallas_call(
        cast_kernel,
        out_shape=[jax.ShapeDtypeStruct(shape, F32) for shape in shapes],
        in_specs=[anywhere] * 2,
        out_specs=[anywhere] * 4,
        scratch_shapes=[
            pltpu.VMEM((6, 256, LANES), BF16),
            pltpu.VMEM((6, 256, LANES), F32),
            pltpu.SemaphoreType.DMA((6,)),
            pltpu.SemaphoreType.DMA((6,)),
        ],
        compiler_params=pltpu.CompilerParams(vmem_limit_bytes=60 * 1024 * 1024),
        cost_estimate=pl.CostEstimate(flops=0, bytes_accessed=42 * 10**6, transcendentals=0),
        name="cast",
    )(*sums)


STEP = 256
ROW_TILE = 64
NEGATIVE = -1e30


def dot(left, right, dims=NN):
    return lax.dot_general(left, right, dims, preferred_element_type=F32)


def gelu_parts(pre):
    bell = jnp.exp(pre * pre * -0.5)
    t = pl.reciprocal(1.0 + jnp.abs(pre) * (0.3275911 * 0.7071067811865476))
    poly = t * (0.1274147960 + t * (-0.142248368 + t * (0.710706871 + t * (-0.7265760135 + t * 0.5307027145))))
    tail = poly * bell
    return jnp.where(pre >= 0.0, 1.0 - tail, tail), bell


def norm_stats(values):
    centred = values - jnp.mean(values, axis=-1, keepdims=True)
    recip = lax.rsqrt(jnp.mean(centred * centred, axis=-1, keepdims=True) + 1e-06)
    return centred * recip, recip


def fold(tile):
    return jnp.sum(tile.reshape(tile.shape[0] // 8, 8, tile.shape[1]), axis=0)


def front_names(r, given):
    r.weights = [next(given) for _ in range(4)]
    r.w_sem, r.n1, r.qkv, r.probs, r.mask, r.mix, r.between, r.n2, r.act = (next(given) for _ in range(9))
    r.pre = [next(given) for _ in range(2)]
    r.act_part = [next(given) for _ in range(2)]


def back_names(r, given):
    r.n1t, r.n2t, r.mixt, r.dmlp, r.dpre, r.dn, r.datt, r.dmix, r.dqkv = (next(given) for _ in range(9))
    r.dpre_part = [next(given) for _ in range(2)]
    r.down_stage, r.up_stage, r.down_sem, r.up_sem = (next(given) for _ in range(4))


def use_weights(r, layer):
    core = lax.axis_index("section")

    def weight(which, source):
        return pltpu.make_async_copy(source[which].at[0], r.weights[which], r.w_sem.at[which])

    for near, source in ((core == layer, r.own), (core != layer, r.far)):

        @pl.when(near)
        def _():
            for which in range(4):
                weight(which, source).start()

    r.ready = lambda which: weight(which, r.own).wait()


def layer_kernel(groups, window, *refs):
    r = Names()
    given = iter(refs)
    r.x, r.col_code, r.row_code, r.vec = (next(given) for _ in range(4))
    r.own = [next(given) for _ in range(4)]
    r.far = [next(given) for _ in range(4)]
    r.unsort, r.dout = (next(given) for _ in range(2))
    r.shown_du, r.small, r.grads, r.du, r.shown_y = (next(given) for _ in range(5))
    front_names(r, given)
    back_names(r, given)
    r.y, r.scale = None, None
    r.y = next(given)
    use_weights(r, 1)
    layer_body(r, groups, window, True, False)


def start_kernel(groups, window, *refs):
    r = Names()
    given = iter(refs)
    lengths, route_mask, tokens, cotangent, router, own_vec = (next(given) for _ in range(6))
    own = [next(given) for _ in range(4)]
    far = [next(given) for _ in range(4)]
    vecs = [next(given) for _ in range(2)]
    r.all_y, r.shown_y, r.delta, cot, r.x = (next(given) for _ in range(5))
    col_codes = [next(given) for _ in range(2)]
    row_codes = [next(given) for _ in range(2)]
    r.unsort, pick, r.unpick, r.skipped, r.scale, factor, extra = (next(given) for _ in range(7))
    front_names(r, given)
    r.y, r.all_x, order, raw, far_vec, raw_sem = (next(given) for _ in range(6))
    far_send, far_recv, vec_sem = (next(given) for _ in range(3))
    core = lax.axis_index("section")
    across = (1 - core, lax.axis_index("dp"))
    rows, width = r.all_x.shape
    half = rows // 2

    def fetch(k, source):
        return pltpu.make_async_copy(source.at[core], raw.at[k], raw_sem.at[k])

    fetch(0, tokens).start()
    fetch(1, cotangent).start()
    barrier = pltpu.get_barrier_semaphore()
    pl.semaphore_signal(barrier, inc=1, device_id=across, device_id_type=pl.DeviceIdType.MESH)
    pl.semaphore_wait(barrier, 1)

    def lend(which):
        return copy_far(own[which], far[which], far_send.at[which], far_recv.at[which], across)

    lend_vec = copy_far(own_vec, far_vec, vec_sem.at[0], vec_sem.at[1], across)
    lend_vec.start()
    lend(0).start()

    def weight(which, source):
        return pltpu.make_async_copy(source[which].at[0], r.weights[which], r.w_sem.at[which])

    def take_own():
        for which in range(4):
            weight(which, own).start()

    at_core(core, 0, take_own)

    def ready(which):
        def arrive():
            lend(which).wait_recv()
            weight(which, far).start()

        at_core(core, 1, arrive)
        weight(which, own).wait()

    r.ready = ready

    starts, bases, total, longs, short = [], [], 0, 0, 0
    count = lengths.shape[2]
    sizes = [lengths[core, 0, c] for c in range(count)]
    for size in sizes:
        is_long = size == LONG
        starts.append(total)
        bases.append(jnp.where(is_long, longs * LONG, 2 * LONG + short))
        total = total + size
        longs = longs + jnp.where(is_long, 1, 0)
        short = short + jnp.where(is_long, 0, size)

    def place(shape, dim):
        return lax.broadcasted_iota(jnp.int32, shape, dim)

    def target(at):
        moved = at
        for start, size, base in zip(starts, sizes, bases):
            moved = moved + jnp.where((at >= start) & (at < start + size), base - start, 0)
        return moved

    def code_of(at):
        return sum(jnp.where(at >= base, 1, 0) for base in bases)

    row_at, col_at = place((1, rows), 1), place((rows, 1), 0)

    def one_hot(left, right):
        return jnp.where(left == right, 1.0, 0.0).astype(BF16)

    goes_row, goes_col = target(row_at), target(col_at)
    row_codes[1][...] = code_of(row_at)
    col_codes[1][...] = code_of(col_at)
    for start in range(0, rows, 128):
        here = slice(start, start + 128)
        order[here, :] = one_hot(col_at[here], goes_row)
        r.unsort[here, :] = one_hot(goes_col[here], row_at)
    lend(1).start()
    lend(2).start()
    lend(3).start()
    for k, (source, moved) in enumerate(((tokens, r.all_x), (cotangent, cot))):
        fetch(k, source).wait()
        for part in range(width // STEP):
            span = slice(part * STEP, (part + 1) * STEP)
            moved[:, span] = dot(order[...], raw[k, :, span]).astype(BF16)

    mask = jnp.where(route_mask[pl.ds(core, 1), :] == 1, 1.0, 0.0)
    masks = jnp.broadcast_to(mask, (8, rows)).astype(BF16)
    chosen_row = dot(masks, r.unsort[...])
    chosen_col = dot(order[...], masks, NT)
    earlier = jnp.where(place((rows, rows), 0) < place((rows, rows), 1), 1.0, 0.0).astype(BF16)
    rank_row = dot(chosen_row.astype(BF16), earlier)[:1]
    later = jnp.where(place((rows, rows), 0) > place((rows, rows), 1), 1.0, 0.0).astype(BF16)
    rank_col = dot(later, chosen_col.astype(BF16))[:, :1]
    chosen_row, chosen_col = chosen_row[:1], chosen_col[:, :1]
    r.skipped[...] = 1.0 - chosen_col
    key_row = jnp.where(chosen_row > 0.5, rank_row, -1.0)
    key_col = jnp.where(chosen_col > 0.5, rank_col, -1.0)
    pick[...] = one_hot(place((half, 1), 0).astype(F32), key_row)
    r.unpick[...] = one_hot(key_col, place((1, half), 1).astype(F32))
    names_row = jnp.broadcast_to(code_of(row_at).astype(F32), (8, rows)).astype(BF16)
    routed_row = dot(names_row, r.unpick[...])[:1]
    routed_col = dot(pick[...], names_row, NT)[:, :1]
    row_codes[0][...] = routed_row.astype(jnp.int32)
    col_codes[0][...] = routed_col.astype(jnp.int32)
    for part in range(width // STEP):
        span = slice(part * STEP, (part + 1) * STEP)
        r.x[:, span] = dot(pick[...], r.all_x[:, span]).astype(BF16)
    logit = jnp.sum(r.x[...].astype(F32) * router[...], axis=1, keepdims=True)
    gate = 1.0 / (1.0 + jnp.exp(-logit))
    held = jnp.where(routed_col > 0.5, 1.0, 0.0)
    r.scale[...] = held * gate
    factor[...] = held * gate * (1.0 - gate)
    gates, counts = jnp.sum(held * gate, axis=0, keepdims=True), jnp.sum(mask, axis=1, keepdims=True)
    lane = place((1, width), 1)
    micro = tokens.shape[0]
    extra[...] = jnp.where(lane == core, gates, jnp.where(lane == core + micro, counts, 0.0))

    lend_vec.wait()
    for layer in range(2):
        vecs[layer][...] = jnp.where(core == layer, own_vec[...], far_vec[...])
    r.vec, r.col_code, r.row_code, r.own = vecs[0], col_codes[0], row_codes[0], own
    layer_body(r, groups, window, False, True)
    for which in range(4):
        lend(which).wait_send()
        at_core(core, 0, lambda which=which: lend(which).wait_recv())


def fused_kernel(groups, window, chunks, *refs):
    r = Names()
    given = iter(refs)
    r.x, r.col_code, r.row_code, r.vec, r.scale = (next(given) for _ in range(5))
    r.own = [next(given) for _ in range(4)]
    r.far = [next(given) for _ in range(4)]
    r.unsort = next(given)
    r.all_dout, r.pick, r.unpick, r.skipped, r.delta, r.factor, r.router = (next(given) for _ in range(7))
    second, second_small, extra = (next(given) for _ in range(3))
    shown = [next(given) for _ in range(3)]
    full = [next(given) for _ in range(2)]
    landed = [next(given) for _ in range(2)]
    first, small_out = (next(given) for _ in range(2))
    shown_out = [next(given) for _ in range(2)]
    front_names(r, given)
    back_names(r, given)
    r.dout, r.du, r.shown_du, r.small, r.router_grad = (next(given) for _ in range(5))
    sums = Sums(chunks, GROUP_STARTS, given)
    sums.grads, sums.landed, sums.full, sums.small_out = (first, second), landed, full, small_out
    sums.shown, sums.shown_out = (shown[0], shown[1], r.shown_du, shown[2]), shown_out
    r.grads = first
    core = sums.core
    use_weights(r, 0)
    sums.open()
    sums.start_swaps(0)
    sums.start_swaps(1)
    sums.prepare(0)
    early = [0]

    def hook():
        sums.moment(early[0])
        early[0] += 1

    def tile_out(stage, row, column, shape, sem, tile):
        area = (pl.ds(row, shape[0]), pl.ds(column, shape[1]))
        owner = lax.rem(tile // 6, 2)

        @pl.when(core == owner)
        def _():
            pltpu.make_async_copy(stage, first.at[area], sem).start()

        @pl.when(core != owner)
        def _():
            copy_far(stage, landed[0].at[area], sem, sums.tile_recv.at[tile], sums.across).start()

    r.hook, r.tile_out = hook, tile_out
    layer_body(r, groups, window, True, True)

    for index, source in enumerate((r.small, second_small)):
        for row in range(source.shape[1] // LANES):
            sums.small[index, row : row + 1, :] = source[:, row * LANES : (row + 1) * LANES]
        row = source.shape[1] // LANES
        sums.small[index, row : row + 1, :] = r.router_grad[...]
        sums.small[index, row + 1 : row + 2, :] = extra[...]
        left = sums.small.shape[1] - row - 2
        sums.small[index, row + 2 :, :] = jnp.zeros((left, LANES), F32)
    sums.small_begin()
    sums.show()

    for turn, now in enumerate(range(early[0], max(sums.end, early[0] + sums.bits + 1))):
        if now < sums.end:
            sums.moment(now)
        if turn <= sums.bits:
            sums.small_turn(turn)
    sums.close()


def layer_body(r, groups, window, full, is_router):
    hook = r.hook if full and is_router else lambda: None
    rows, width = r.x.shape
    hidden = r.own[2].shape[2]
    pairs = width // 128

    def vec(start, count=width):
        return r.vec[:, start : start + count]

    g1, g2, b1, bq, bv, bo, b2 = (vec(k * width) for k in range(7))
    bu_at, bd_at = 7 * width, 7 * width + hidden

    def row_loop(step, init=0):
        def at(k, carry):
            return step(pl.ds(pl.multiple_of(k * ROW_TILE, ROW_TILE), ROW_TILE), carry)

        return lax.fori_loop(0, rows // ROW_TILE, at, init)

    def norm_step(source, gain, bias, target):
        def step(here, carry):
            normal, _ = norm_stats(source[here, :].astype(F32))
            target[here, :] = (normal * gain + bias).astype(BF16)
            return carry

        return step

    def tiles(step):
        for k in range(width // STEP):
            step(slice(k * STEP, (k + 1) * STEP))

    def show(source, target):
        def step(span):
            target[:, span] = dot(r.unsort[...], source[:, span]).astype(BF16)

        tiles(step)

    def spread(routed, others, target, shown):
        def step(span):
            value = dot(r.unpick[...], routed[:, span]) + others[:, span].astype(F32) * r.skipped[...]
            if target is not None:
                target[:, span] = value.astype(BF16)
            shown[:, span] = dot(r.unsort[...], value.astype(BF16)).astype(BF16)

        tiles(step)

    row_loop(norm_step(r.x, g1, b1, r.n1))
    if full and is_router:

        def route_step(span):
            r.dout[:, span] = dot(r.pick[...], r.all_dout[:, span]).astype(BF16)

        tiles(route_step)
    if full:

        def delta_step(here, carry):
            low = (r.dout[here, :].astype(F32) * r.scale[here, :]).astype(BF16) if is_router else r.dout[here, :]
            r.dmlp[here, :] = low
            return carry + fold(low.astype(F32))

        dbd = row_loop(delta_step, jnp.zeros((8, width), F32))
        r.small[:, bd_at:] = jnp.sum(dbd, axis=0, keepdims=True)

    for k, (start, low, high) in enumerate(groups):
        col = r.col_code[start : start + window, :]
        row = r.row_code[:, start : start + window]
        place = lax.broadcasted_iota(jnp.int32, (window, 1), 0) + start
        col = jnp.where((place >= low) & (place < high), col, -1)
        r.mask[k] = jnp.where(col == row, 0.0, NEGATIVE)

    r.ready(0)
    for k in range(3 * width // STEP):
        span = slice(k * STEP, (k + 1) * STEP)
        value = dot(r.n1[...], r.weights[0][:, span])
        if k < width // STEP:
            value = (value + bq[:, span]).astype(BF16).astype(F32) * 0.125
        elif k >= 2 * width // STEP:
            value = value + bv[:, k * STEP - 2 * width : (k + 1) * STEP - 2 * width]
        r.qkv[:, span] = value.astype(BF16)

    hook()
    lane = lax.broadcasted_iota(jnp.int32, (1, 128), 1)

    def halves(block):
        zero = jnp.zeros_like(block)
        return jnp.where(lane < 64, block, zero), jnp.where(lane < 64, zero, block)

    r.mix[...] = jnp.zeros_like(r.mix)

    def lanes(pair, part):
        return pl.ds(pl.multiple_of(pair * 128 + part * width, 128), 128)

    def attend(pair, carry):
        for k, (start, low, high) in enumerate(groups):
            here = slice(start, start + window)
            q, key, v = (r.qkv[here, lanes(pair, part)] for part in range(3))
            vt = v.T
            place = lax.broadcasted_iota(jnp.int32, (1, window), 1) + start
            valid = (place >= low) & (place < high)
            parts = []
            for half, own_key in enumerate(halves(key)):
                scores = dot(own_key, q, NT) + r.mask[k]
                power = jnp.exp(scores - jnp.max(scores, axis=0, keepdims=True))
                total = jnp.sum(power, axis=0, keepdims=True)
                prob = (power * jnp.where(valid, 1.0 / total, 0.0)).astype(BF16)
                if full:
                    r.probs[(pair * 2 + half) * len(groups) + k] = prob
                parts.append(dot(vt[half * 64 : half * 64 + 64], prob))
            mixed = jnp.concatenate(parts, axis=0).T.astype(BF16)
            r.mix[here, lanes(pair, 0)] = r.mix[here, lanes(pair, 0)] + mixed
        return carry

    lax.fori_loop(0, pairs, attend, 0)

    r.ready(1)
    for k in range(width // STEP):
        span = slice(k * STEP, (k + 1) * STEP)
        value = dot(r.mix[...], r.weights[1][:, span]) + bo[:, span]
        r.between[:, span] = r.x[:, span].astype(F32) + value
    row_loop(norm_step(r.between, g2, b2, r.n2))
    if full:
        r.n1t[...] = r.n1[...].T
        r.n2t[...] = r.n2[...].T
        r.mixt[...] = r.mix[...].T
    hook()

    r.ready(2)
    if full:
        r.ready(3)

    def tile_out(stage, row, column, shape, sem, tile):
        target = r.grads.at[pl.ds(row, shape[0]), pl.ds(column, shape[1])]
        pltpu.make_async_copy(stage, target, sem).start()

    tile_out = r.tile_out if full and is_router else tile_out

    def down_out(k, slot):
        tile_out(
            r.down_stage.at[slot], pl.multiple_of(k * STEP, STEP), 0, (STEP, width), r.down_sem.at[slot], k
        )

    def side_out(block, k, slot):
        row = pl.multiple_of((block + k // 3) * width, width)
        column = pl.multiple_of(k % 3 * STEP, STEP)
        tile = k + {4: 12, 8: 24, 9: 27}[block]
        tile_out(r.up_stage.at[slot], row, column, (width, STEP), r.up_sem.at[slot], tile)

    def down_free(slot):
        target = r.grads.at[pl.ds(0, STEP), pl.ds(0, width)]
        pltpu.make_async_copy(r.down_stage.at[slot], target, r.down_sem.at[slot]).wait()

    def side_free(slot):
        target = r.grads.at[pl.ds(0, width), pl.ds(0, STEP)]
        pltpu.make_async_copy(r.up_stage.at[slot], target, r.up_sem.at[slot]).wait()

    steps = hidden // STEP

    def part_at(k):
        return pl.multiple_of(k * STEP, STEP)

    def ahead(k, side):
        at = part_at(k)
        r.pre[side][...] = dot(r.n2[...], r.weights[2][:, pl.ds(at, STEP)]) + r.vec[:, pl.ds(at + bu_at, STEP)]

    def middle(k, side):
        at = part_at(k)
        span = pl.ds(at, STEP)
        pre = r.pre[side][...]
        cdf, bell = gelu_parts(pre)
        act = (pre * cdf).astype(BF16)
        if not (full and is_router):
            r.act[:, span] = act
        if full:
            r.act_part[side][...] = act
            slope = cdf + pre * bell * 0.3989422804014327
            dact = dot(r.dmlp[...], r.weights[3][span, :], NT)
            dpre = (dact * slope).astype(BF16)
            r.dpre[:, span] = dpre
            r.dpre_part[side][...] = dpre
            r.small[:, pl.ds(at + bu_at, STEP)] = jnp.sum(dpre.astype(F32), axis=0, keepdims=True)

    def weigh(side):
        r.down_stage[side] = dot(r.act_part[side][...], r.dmlp[...], TN).astype(BF16)
        r.up_stage[side] = dot(r.n2t[...], r.dpre_part[side][...]).astype(BF16)

    def send_out(k, side):
        down_out(k, side)
        side_out(4, k, side)

    def two_steps(kk, first=False):
        even = kk * 2
        if full and not first:

            @pl.when(kk >= 2)
            def _():
                down_free(1)
                side_free(1)

            down_free(0)
            side_free(0)
        middle(even, 0)
        ahead(even + 1, 1)
        if full and not first:
            weigh(1)
        middle(even + 1, 1)
        ahead(jnp.minimum(even + 2, steps - 1), 0)
        if full:
            weigh(0)
            if not first:
                send_out(even - 1, 1)
            send_out(even, 0)

    def more_steps(kk, carry):
        two_steps(kk)
        return carry

    ahead(0, 0)
    two_steps(0, True)
    if full and is_router:
        lax.fori_loop(1, steps // 4, more_steps, 0)
        hook()
        lax.fori_loop(steps // 4, steps // 2, more_steps, 0)
    else:
        lax.fori_loop(1, steps // 2, more_steps, 0)
    if full:
        down_free(1)
        side_free(1)
        weigh(1)
        send_out(steps - 1, 1)
    if full and is_router:
        down_free(0)
        down_free(1)
        hook()
    if not full:
        r.ready(3)
    if not (full and is_router):
        for k in range(width // STEP):
            span = slice(k * STEP, (k + 1) * STEP)
            value = dot(r.act[...], r.weights[3][:, span]) + vec(bd_at)[:, span]
            source = r.x[:, span].astype(F32)
            value = r.between[:, span] - source + value
            if not full:
                r.delta[:, span] = value
            r.y[:, span] = (source + (r.scale[...] * value if is_router else value)).astype(BF16)
    if not full:
        spread(r.y, r.all_x, r.all_y, r.shown_y)
        return
    if not is_router:
        show(r.y, r.shown_y)

    for k in range(width // STEP):
        span = slice(k * STEP, (k + 1) * STEP)
        r.dn[:, span] = dot(r.dpre[...], r.weights[2][span, :], NT)

    def norm_back(source, gain, here):
        normal, recip = norm_stats(source[here, :].astype(F32))
        grad = r.dn[here, :]
        hat = grad * gain
        back = recip * (
            hat - jnp.mean(hat, axis=-1, keepdims=True) - normal * jnp.mean(hat * normal, axis=-1, keepdims=True)
        )
        return back, fold(grad * normal), fold(grad)

    def second_back(here, carry):
        back, dg, db = norm_back(r.between, g2, here)
        r.between[here, :] = back
        delta = r.dout[here, :].astype(F32)
        total = ((delta * r.scale[here, :] if is_router else delta) + back).astype(BF16)
        r.datt[here, :] = total
        return carry[0] + dg, carry[1] + db, carry[2] + fold(total.astype(F32))

    zero = jnp.zeros((8, width), F32)
    dg2, db2, dbo = row_loop(second_back, (zero, zero, zero))
    r.small[:, width : 2 * width] = jnp.sum(dg2, axis=0, keepdims=True)
    r.small[:, 6 * width : 7 * width] = jnp.sum(db2, axis=0, keepdims=True)
    r.small[:, 5 * width : 6 * width] = jnp.sum(dbo, axis=0, keepdims=True)

    for k in range(width // STEP):
        span = slice(k * STEP, (k + 1) * STEP)
        r.dmix[:, span] = dot(r.datt[...], r.weights[1][span, :], NT).astype(BF16)
        slot = k % 2
        side_free(slot)
        r.up_stage[slot] = dot(r.mixt[...], r.datt[:, span]).astype(BF16)
        side_out(8, k, slot)

    r.dqkv[...] = jnp.zeros_like(r.dqkv)

    def attend_back(pair, carry):
        for k, (start, low, high) in enumerate(groups):
            here = slice(start, start + window)
            q, key, v = (r.qkv[here, lanes(pair, part)] for part in range(3))
            dm = r.dmix[here, lanes(pair, 0)]
            key_t = key.T
            dq, dk, dv = [], None, None
            for half, (own_q, own_v, own_dm) in enumerate(zip(halves(q), halves(v), halves(dm))):
                prob = r.probs[(pair * 2 + half) * len(groups) + k]
                wide = prob.astype(F32)
                dprob = dot(own_v, dm, NT)
                product = wide * dprob
                ds = (product - wide * jnp.sum(product, axis=0, keepdims=True)).astype(BF16)
                dq.append(dot(key_t[half * 64 : half * 64 + 64], ds))
                one, two = dot(ds, own_q), dot(prob, own_dm)
                dk, dv = (one, two) if dk is None else (dk + one, dv + two)
            dq = jnp.concatenate(dq, axis=0).T * 0.125
            for part, value in enumerate((dq, dk, dv)):
                spot = lanes(pair, part)
                r.dqkv[here, spot] = r.dqkv[here, spot] + value.astype(BF16)
        return carry

    lax.fori_loop(0, pairs, attend_back, 0)
    hook()

    for k in range(3 * width // STEP):
        span = slice(k * STEP, (k + 1) * STEP)
        block = r.dqkv[:, span]
        if not width <= k * STEP < 2 * width:
            at = 3 * width + k * STEP - (width if k * STEP >= width else 0)
            r.small[:, at : at + STEP] = jnp.sum(block.astype(F32), axis=0, keepdims=True)
        slot = (k + 1) % 2
        side_free(slot)
        r.up_stage[slot] = dot(r.n1t[...], block).astype(BF16)
        side_out(9, k, slot)
    side_free(0)
    side_free(1)
    hook()

    for k in range(width // STEP):
        span = slice(k * STEP, (k + 1) * STEP)
        r.dn[:, span] = dot(r.dqkv[...], r.weights[0][span, :], NT)

    def first_back(here, carry):
        back, dg, db = norm_back(r.x, g1, here)
        dout = r.dout[here, :].astype(F32)
        total = dout + r.between[here, :] + back
        sums = [carry[0] + dg, carry[1] + db]
        if is_router:
            slope = jnp.sum(dout * r.delta[here, :], axis=1, keepdims=True) * r.factor[here, :]
            total = total + slope * r.router[...]
            sums.append(carry[2] + fold(slope * r.x[here, :].astype(F32)))
        r.du[here, :] = total.astype(BF16)
        return tuple(sums)

    sums = row_loop(first_back, (zero,) * (3 if is_router else 2))
    r.small[:, :width] = jnp.sum(sums[0], axis=0, keepdims=True)
    r.small[:, 2 * width : 3 * width] = jnp.sum(sums[1], axis=0, keepdims=True)
    if is_router:
        r.router_grad[...] = jnp.sum(sums[2], axis=0, keepdims=True)
        spread(r.du, r.all_dout, None, r.shown_du)
    else:
        show(r.du, r.shown_du)
    if not is_router:
        down_free(0)
        down_free(1)


def front_scratch(rows, width, hidden, groups, window, full, keep_act):
    sizes = [(width, 3 * width), (width, width), (width, hidden), (hidden, width)]
    held = [pltpu.VMEM(size, BF16) for size in sizes]
    held += [pltpu.SemaphoreType.DMA((4,))]
    held += [pltpu.VMEM((rows, width), BF16), pltpu.VMEM((rows, 3 * width), BF16)]
    held += [pltpu.VMEM((HEADS * len(groups) if full else 1, window, window), BF16)]
    held += [pltpu.VMEM((len(groups), window, window), F32), pltpu.VMEM((rows, width), BF16)]
    held += [pltpu.VMEM((rows, width), F32), pltpu.VMEM((rows, width), BF16)]
    held += [pltpu.VMEM((rows, hidden) if keep_act else (TILE, LANES), BF16)]
    return held + [pltpu.VMEM((rows, STEP), F32)] * 2 + [pltpu.VMEM((rows, STEP), BF16)] * 2


def back_scratch(rows, width, hidden):
    held = [pltpu.VMEM((width, rows), BF16)] * 3 + [pltpu.VMEM((rows, width), BF16)]
    held += [pltpu.VMEM((rows, hidden), BF16), pltpu.VMEM((rows, width), F32)]
    held += [pltpu.VMEM((rows, width), BF16)] * 2 + [pltpu.VMEM((rows, 3 * width), BF16)]
    held += [pltpu.VMEM((rows, STEP), BF16)] * 2
    held += [pltpu.VMEM((2, STEP, width), BF16), pltpu.VMEM((2, width, STEP), BF16)]
    return held + [pltpu.SemaphoreType.DMA((2,))] * 2


def run_start(groups, window, lengths, route_mask, tokens, cotangent, router_row, own_vec, own):
    _, rows, width = tokens.shape
    half, hidden = rows // 2, own[2].shape[2]
    inside = pl.BlockSpec(memory_space=pltpu.VMEM)
    anywhere = pl.BlockSpec(memory_space=pl.ANY)
    outs = [(value.shape, BF16) for value in own] + [(own_vec.shape, F32)] * 2
    outs += [((rows, width), BF16)] * 2 + [((half, width), F32), ((rows, width), BF16), ((half, width), BF16)]
    outs += [((half, 1), jnp.int32), ((rows, 1), jnp.int32), ((1, half), jnp.int32), ((1, rows), jnp.int32)]
    outs += [((rows, rows), BF16), ((half, rows), BF16), ((rows, half), BF16), ((rows, 1), F32)]
    outs += [((half, 1), F32)] * 2 + [((1, width), F32)]
    scratch = front_scratch(half, width, hidden, groups, window, False, True)
    scratch += [pltpu.VMEM((half, width), BF16), pltpu.VMEM((rows, width), BF16), pltpu.VMEM((rows, rows), BF16)]
    scratch += [pltpu.VMEM((2, rows, width), BF16), pltpu.VMEM(own_vec.shape, F32), pltpu.SemaphoreType.DMA((2,))]
    scratch += [pltpu.SemaphoreType.DMA((4,))] * 2 + [pltpu.SemaphoreType.DMA((2,))]
    return pl.pallas_call(
        functools.partial(start_kernel, groups, window),
        out_shape=[jax.ShapeDtypeStruct(*one) for one in outs],
        in_specs=[pl.BlockSpec(memory_space=pltpu.SMEM), inside] + [anywhere] * 2 + [inside] * 2 + [anywhere] * 4,
        out_specs=[anywhere] * 4 + [inside] * (len(outs) - 4),
        scratch_shapes=scratch,
        compiler_params=pltpu.CompilerParams(
            collective_id=1, has_side_effects=True, vmem_limit_bytes=60 * 1024 * 1024
        ),
        cost_estimate=pl.CostEstimate(flops=5 * 10**9, bytes_accessed=6 * 10**7, transcendentals=0),
        name="start",
    )(lengths, route_mask, tokens, cotangent, router_row, own_vec, *own)


def run_layer(groups, window, x, col_code, row_code, vec, own, far, unsort, back):
    rows, width = x.shape
    hidden = own[2].shape[2]
    inside = pl.BlockSpec(memory_space=pltpu.VMEM)
    anywhere = pl.BlockSpec(memory_space=pl.ANY)
    args = [x, col_code, row_code, vec, *own, *far, unsort, back]
    outs = [((rows, width), BF16), ((1, vec.shape[1]), F32), ((GRAD_ROWS, LANES), BF16)]
    outs += [((rows, width), BF16)] * 2
    scratch = front_scratch(rows, width, hidden, groups, window, True, True)
    scratch += back_scratch(rows, width, hidden) + [pltpu.VMEM((rows, width), BF16)]
    flops = rows * width * (3 * width + width + 2 * hidden) * 6
    return pl.pallas_call(
        functools.partial(layer_kernel, groups, window),
        out_shape=[jax.ShapeDtypeStruct(*one) for one in outs],
        in_specs=[inside] * 4 + [anywhere] * 8 + [inside] * 2,
        out_specs=[inside] * 2 + [anywhere] + [inside] * 2,
        scratch_shapes=scratch,
        compiler_params=pltpu.CompilerParams(vmem_limit_bytes=62 * 1024 * 1024),
        cost_estimate=pl.CostEstimate(flops=flops, bytes_accessed=3 * 10**7, transcendentals=0),
        name="layer",
    )(*args)


def run_fused(axis_of, groups, window, x, col_code, row_code, vec, scale, own, far, rows_of, back, router, second, second_small, extra, shown):
    rows, width = x.shape
    hidden = own[2].shape[2]
    chunks = sum_plan(axis_of)
    inside = pl.BlockSpec(memory_space=pltpu.VMEM)
    anywhere = pl.BlockSpec(memory_space=pl.ANY)
    unsort, pick, unpick, skipped = rows_of
    delta, factor, router_row = router
    every = unsort.shape[0]
    args = [x, col_code, row_code, vec, scale, *own, *far, unsort]
    args += [back, pick, unpick, skipped, delta, factor, router_row]
    args += [second, second_small, extra, *shown]
    small_rows = -(-(vec.shape[1] // LANES + 2) // 8) * 8
    outs = [((GRAD_ROWS, LANES), BF16)] * 5
    outs += [((small_rows, LANES), F32)] + [((2, every, width), BF16)] * 2
    scratch = front_scratch(rows, width, hidden, groups, window, True, False)
    scratch += back_scratch(rows, width, hidden)
    scratch += [pltpu.VMEM((rows, width), BF16)] * 2 + [pltpu.VMEM((every, width), BF16)]
    scratch += [pltpu.VMEM((1, vec.shape[1]), F32), pltpu.VMEM((1, width), F32)]
    scratch += Sums.scratch(chunks, small_rows)
    *sums, _, _, _, small, acts, grads = pl.pallas_call(
        functools.partial(fused_kernel, groups, window, chunks),
        out_shape=[jax.ShapeDtypeStruct(*one) for one in outs],
        in_specs=[inside] * 5 + [anywhere] * 8 + [inside] * 8 + [anywhere] + [inside] * 2 + [anywhere] * 3,
        out_specs=[anywhere] * 5 + [inside] + [anywhere] * 2,
        scratch_shapes=scratch,
        compiler_params=pltpu.CompilerParams(
            collective_id=0, has_side_effects=True, vmem_limit_bytes=64 * 1024 * 1024
        ),
        cost_estimate=pl.CostEstimate(flops=10**10, bytes_accessed=6 * 10**8, transcendentals=0),
        name="fused",
    )(*args)
    return sums, small, (acts, grads)


def body(axis_of, tokens, lengths, route_mask, router_weight, gains, biases, w_qkv, w_out, w_up, w_down, cotangent):
    micro, rows, width = tokens.shape
    own = (w_qkv, w_out, w_up, w_down)
    own_vec = jnp.concatenate([gains, biases], axis=1)
    router_row = router_weight.astype(F32)[None, :]
    half = LONG // 2
    groups_one = ((0, 0, half), (96, half, 2 * half), (192, 2 * half, rows // 2))
    groups_two = ((0, 0, LONG), (192, LONG, 2 * LONG), (384, 2 * LONG, rows))
    made = run_start(groups_one, 128, lengths, route_mask, tokens, cotangent, router_row, own_vec, own)
    far, (vec_one, vec_two), (y1, shown_y1, delta_one, cot, routed) = made[:4], made[4:6], made[6:11]
    col_one, col_two, row_one, row_two, *others = made[11:]
    unsort, pick, unpick, skipped, scale, factor, extra = others
    shown_du2, small_two, grads_two, dout, shown_y2 = run_layer(
        groups_two, 256, y1, col_two, row_two, vec_two, own, far, unsort, cot
    )
    sums, small, (activations, input_grads) = run_fused(
        axis_of, groups_one, 128, routed, col_one, row_one, vec_one, scale, own, far,
        (unsort, pick, unpick, skipped), dout, (delta_one, factor, router_row), grads_two, small_two, extra,
        (shown_y1, shown_y2, shown_du2),
    )
    small = small.reshape(-1)
    span = own_vec.shape[1]
    tail = small[span:]
    grads = cast_sums(sums, [value.shape for value in own])

    return (
        activations[None],
        input_grads[None],
        *grads,
        small[: 2 * width][None],
        small[2 * width : span][None],
        tail[:width],
        tail[width : width + micro] / tail[width + micro : width + 2 * micro],
    )


def solution(mesh):
    in_specs = (
        P(None, "dp", None),
        P(None, "dp", None),
        P(None, "dp"),
        P(),
        P("section", None),
        P("section", None),
        P("section", None, None),
        P("section", None, None),
        P("section", None, None),
        P("section", None, None),
        P(None, "dp", None),
    )
    out_specs = (
        P("section", None, "dp", None),
        P("section", None, "dp", None),
        P("section", None, None),
        P("section", None, None),
        P("section", None, None),
        P("section", None, None),
        P("section", None),
        P("section", None),
        P(),
        P(),
    )
    step = functools.partial(body, axis_bits(mesh))
    return jax.shard_map(step, mesh=mesh, in_specs=in_specs, out_specs=out_specs, check_vma=False)
```

```python
import functools

import jax
import jax.numpy as jnp
from jax import lax
from jax.experimental import pallas as pl
from jax.experimental.pallas import tpu as pltpu
from jax.sharding import PartitionSpec as P

HEADS = 12
HEAD = 64
LONG = 197
F32 = jnp.float32
BF16 = jnp.bfloat16
NT = (((1,), (1,)), ((), ()))
TN = (((0,), (0,)), ((), ()))
NN = (((1,), (0,)), ((), ()))


LANES = 768
TILE = 16
GRAD_ROWS = 12 * LANES


def axis_bits(mesh):
    line = mesh.devices[0]
    bits = len(line).bit_length() - 1
    try:
        spots = [tuple(device.coords) for device in line]
    except AttributeError:
        return [0] * bits
    return [
        next((w for w in range(3) if spots[1 << b][w] != spots[0][w]), 0) for b in range(bits)
    ]


HALVINGS = 4
GROUPS = 6
SLOTS = 4


GROUP_PLAN = (
    ((768, 123), (512, 1023), (256, 1032)),
    ((768, 123), (512, 1023), (256, 1320)),
    ((768, 132), (768, 1023)),
    ((512, 1230), (512, 123), (512, 2013)),
    ((768, 1023), (768, 132)),
    ((512, 2103), (512, 213), (512, 1023)),
)
GROUP_STARTS = (0, 1, 3, 4, 5, 7)


def sum_plan(axis_of):
    lists = {}
    for bit, axis in enumerate(axis_of):
        lists.setdefault(axis, []).append(bit)
    lists = sorted(lists.values(), key=len)
    while len(lists) < 3:
        lists.append([])
    roles = [lists[0][:1], lists[1][:1], lists[2][:1], lists[2][1:2]]
    plan = []
    for group in GROUP_PLAN:
        chunks, start = [], 0
        for size, code in group:
            order = [bit for place in (1000, 100, 10, 1) for bit in roles[code // place % 10]]
            order += [bit for bit in range(len(axis_of)) if bit not in order]
            chunks.append((start, size, order))
            start += size
        plan.append(chunks)
    return plan


def add_rows(into, into_start, source, start, other, other_start, count):
    tile = next(t for t in (64, 32, 16) if count % t == 0)

    def step(k, carry):
        target, here, there = (
            pl.ds(pl.multiple_of(first + k * tile, TILE), tile) for first in (into_start, start, other_start)
        )
        into[target, :] = source[here, :] + other[there, :]
        return carry

    lax.fori_loop(0, count // tile, step, 0)


class Names:
    pass


def copy_far(source, target, one, two, friend):
    return pltpu.make_async_remote_copy(
        src_ref=source,
        dst_ref=target,
        send_sem=one,
        recv_sem=two,
        device_id=friend,
        device_id_type=pl.DeviceIdType.MESH,
    )


def at_core(core, index, step):
    pl.when(core == index)(step)


GRAD_TILES = 36
GROUP_ROWS = GRAD_ROWS // GROUPS


class Sums:
    def __init__(self, chunks, starts, given):
        self.chunks, self.starts = chunks, starts
        self.shards = set()
        self.bits = bits = len(chunks[0][0][2])
        self.halvings = min(bits, HALVINGS)
        self.acc, self.mate = next(given), next(given)
        self.got = [next(given) for _ in range(bits)]
        self.small_got, self.small = next(given), next(given)
        self.load_sem, self.mate_sem, self.swap_send, self.swap_recv, self.shard_sem = (next(given) for _ in range(5))
        self.send, self.recv, self.back_send, self.back_recv = (next(given) for _ in range(4))
        self.small_send, self.small_recv = (next(given) for _ in range(2))
        self.shown_sem, self.shown_send, self.shown_recv = (next(given) for _ in range(3))
        self.tile_recv, self.give_send, self.give_recv = (next(given) for _ in range(3))
        self.core = lax.axis_index("section")
        self.me = lax.axis_index("dp")
        self.across = (1 - self.core, self.me)
        self.end = starts[-1] + bits + self.halvings + 1

    @staticmethod
    def scratch(chunks, small_rows):
        bits = len(chunks[0][0][2])
        count = sum(len(group) for group in chunks)
        rows = SLOTS * GROUP_ROWS
        held = [pltpu.VMEM((rows, LANES), BF16), pltpu.VMEM((GROUP_ROWS, LANES), BF16)]
        held += [pltpu.VMEM((rows >> min(depth + 1, HALVINGS), LANES), BF16) for depth in range(bits)]
        held += [pltpu.VMEM((bits + 1, small_rows, LANES), F32), pltpu.VMEM((2, small_rows, LANES), F32)]
        held += [pltpu.SemaphoreType.DMA((count,))] * 5
        held += [pltpu.SemaphoreType.DMA((count, bits))] * 4
        held += [pltpu.SemaphoreType.DMA((bits + 1,))] * 2
        held += [pltpu.SemaphoreType.DMA((2,))] * 3
        held += [pltpu.SemaphoreType.DMA((GRAD_TILES,))]
        return held + [pltpu.SemaphoreType.DMA((GROUPS,))] * 2

    def bit_at(self, bit):
        return lax.rem(self.me // (1 << bit), 2)

    def partner(self, bit):
        return (self.core, self.me + (1 - 2 * self.bit_at(bit)) * (1 << bit))

    def open(self):
        friends = [self.across] + [self.partner(bit) for bit in range(self.bits)]
        barrier = pltpu.get_barrier_semaphore()
        for friend in friends:
            pl.semaphore_signal(barrier, inc=1, device_id=friend, device_id_type=pl.DeviceIdType.MESH)
        pl.semaphore_wait(barrier, len(friends))

    @staticmethod
    def layer_of(j):
        return 1 if j < GROUPS // 2 else 0

    def base(self, j, core):
        return (2 * (j % (GROUPS // 2)) + core) * GROUP_ROWS

    def rows_at(self, j, core, c):
        start, size, _ = self.chunks[j][c]
        return pl.ds(pl.multiple_of(self.base(j, core) + start, TILE), size)

    def index(self, j, c):
        return sum(len(group) for group in self.chunks[:j]) + c

    def swap(self, j, c):
        rows, k = self.rows_at(j, 1 - self.core, c), self.index(j, c)
        return copy_far(
            self.grads[1].at[rows, :], self.landed[1].at[rows, :], self.swap_send.at[k], self.swap_recv.at[k],
            self.across,
        )

    def load(self, j, c):
        start, size, _ = self.chunks[j][c]
        target = self.acc.at[pl.ds(j % SLOTS * GROUP_ROWS + start, size), :]
        source = self.grads[self.layer_of(j)].at[self.rows_at(j, self.core, c), :]
        return pltpu.make_async_copy(source, target, self.load_sem.at[self.index(j, c)])

    def load_mate(self, j, c):
        source = self.landed[self.layer_of(j)].at[self.rows_at(j, self.core, c), :]
        start, size, _ = self.chunks[j][c]
        target = self.mate.at[pl.ds(start, size), :]
        return pltpu.make_async_copy(source, target, self.mate_sem.at[self.index(j, c)])

    def span(self, j, c, depth):
        start, size, order = self.chunks[j][c]
        for bit in order[: min(depth, self.halvings)]:
            size //= 2
            start = start + self.bit_at(bit) * size
        return start, size

    def in_acc(self, j, start, size):
        return pl.ds(pl.multiple_of(j % SLOTS * GROUP_ROWS + start, TILE), size)

    def got_at(self, j, c, depth):
        return (j % SLOTS * GROUP_ROWS + self.chunks[j][c][0]) >> min(depth + 1, HALVINGS)

    def down(self, j, c, depth):
        bit = self.chunks[j][c][2][depth]
        start, size = self.span(j, c, depth)
        if depth < self.halvings:
            size //= 2
            start = start + (1 - self.bit_at(bit)) * size
        k = self.index(j, c)
        return copy_far(
            self.acc.at[self.in_acc(j, start, size), :],
            self.got[depth].at[pl.ds(self.got_at(j, c, depth), size), :],
            self.send.at[k, depth],
            self.recv.at[k, depth],
            self.partner(bit),
        )

    def shard(self, j, c):
        start, size = self.span(j, c, self.halvings)
        there = pl.ds(pl.multiple_of(self.base(j, self.core) + start, TILE), size)
        target = self.full[self.layer_of(j)].at[there, :]
        return pltpu.make_async_copy(
            self.acc.at[self.in_acc(j, start, size), :], target, self.shard_sem.at[self.index(j, c)]
        )

    def up(self, j, c, depth):
        bit = self.chunks[j][c][2][depth]
        start, size = self.span(j, c, depth + 1)
        full = self.full[self.layer_of(j)]
        target = full.at[pl.ds(pl.multiple_of(self.base(j, self.core) + start, TILE), size), :]
        source = self.acc.at[self.in_acc(j, start, size), :] if depth == self.halvings - 1 else target
        k = self.index(j, c)
        return copy_far(source, target, self.back_send.at[k, depth], self.back_recv.at[k, depth], self.partner(bit))

    def give(self, j, core):
        full = self.full[self.layer_of(j)]
        rows = pl.ds(self.base(j, core), GROUP_ROWS)
        return copy_far(full.at[rows, :], full.at[rows, :], self.give_send.at[j], self.give_recv.at[j], self.across)

    def each(self, j):
        return range(len(self.chunks[j]))

    def start_swaps(self, j):
        for c in self.each(j):
            self.swap(j, c).start()

    def emptied(self, j):
        for c in self.each(j):
            for depth in range(self.halvings):
                self.down(j, c, depth).wait_send()
            self.up(j, c, self.halvings - 1).wait_send()
            self.shard_done(j, c)

    def shard_done(self, j, c):
        if (j, c) not in self.shards:
            self.shard(j, c).wait()
            self.shards.add((j, c))

    def prepare(self, j):
        if j >= SLOTS:
            self.emptied(j - SLOTS)
        for c in self.each(j):
            self.load(j, c).start()
        if self.layer_of(j) == 0:
            for tile in range(6):
                area = self.landed[0].at[pl.ds(0, LANES), pl.ds(0, STEP)]
                sem = self.tile_recv.at[(j - GROUPS // 2) * 12 + self.core * 6 + tile]
                copy_far(area, area, sem, sem, self.across).wait_recv()
        for c in self.each(j):
            if self.layer_of(j) == 1:
                self.swap(j, c).wait_recv()
            self.load_mate(j, c).start()

    def moment(self, now):
        bits, halvings = self.bits, self.halvings
        for j, start in enumerate(self.starts):
            if start == now:
                for c in self.each(j):
                    self.load(j, c).wait()
                    self.load_mate(j, c).wait()
                    first, size, _ = self.chunks[j][c]
                    at = j % SLOTS * GROUP_ROWS + first
                    add_rows(self.acc, at, self.acc, at, self.mate, first, size)
                    self.down(j, c, 0).start()
            if self.layer_of(j) == 1 and start == now + 2:
                self.start_swaps(j)
        for j, begun in enumerate(self.starts):
            stage = now - begun
            if not 0 < stage <= bits + halvings:
                continue
            for c in self.each(j):
                if stage <= bits:
                    depth = stage - 1
                    if depth < halvings:
                        self.down(j, c, depth).wait_recv()
                    else:
                        self.down(j, c, depth).wait()
                    first, size = self.span(j, c, stage)
                    at = j % SLOTS * GROUP_ROWS + first
                    add_rows(self.acc, at, self.acc, at, self.got[depth], self.got_at(j, c, depth), size)
                    if stage < bits:
                        self.down(j, c, stage).start()
                    else:
                        self.up(j, c, halvings - 1).start()
                        self.shard(j, c).start()
                else:
                    depth = bits + halvings - stage
                    self.up(j, c, depth).wait_recv()
                    if depth == halvings - 1:
                        self.shard_done(j, c)
                    if depth > 0:
                        self.up(j, c, depth - 1).start()
            if stage == bits + halvings:
                core = 1 - self.layer_of(j)
                at_core(self.core, core, lambda j=j, core=core: self.give(j, core).start())
        for j, start in enumerate(self.starts):
            if start == now + 1:
                self.prepare(j)

    def small_step(self, k):
        friend = self.across if k == 0 else self.partner(k - 1)
        return copy_far(
            self.small_out, self.small_got.at[k], self.small_send.at[k], self.small_recv.at[k], friend
        )

    def small_begin(self):
        for layer in range(2):

            def step(layer=layer):
                self.small_out[...] = self.small[layer]
                copy_far(
                    self.small.at[1 - layer], self.small_got.at[0], self.small_send.at[0], self.small_recv.at[0],
                    self.across,
                ).start()

            at_core(self.core, layer, step)

    def small_turn(self, k):
        self.small_step(k).wait()
        self.small_out[...] = self.small_out[...] + self.small_got[k]
        if k < self.bits:
            self.small_step(k + 1).start()

    def shown_keep(self, layer, k):
        return pltpu.make_async_copy(self.shown[2 * k + layer], self.shown_out[k].at[self.core], self.shown_sem.at[k])

    def shown_give(self, layer, k):
        return copy_far(
            self.shown[2 * k + 1 - layer], self.shown_out[k].at[self.core], self.shown_send.at[k],
            self.shown_recv.at[k], self.across,
        )

    def show(self):
        for layer in range(2):

            def step(layer=layer):
                for k in range(2):
                    self.shown_keep(layer, k).start()
                    self.shown_give(layer, k).start()

            at_core(self.core, layer, step)

    def close(self):
        for k in range(2):
            self.shown_keep(0, k).wait()
            self.shown_give(0, k).wait()
        for j in range(GROUPS):
            layer = self.layer_of(j)
            at_core(self.core, layer, lambda j=j: self.give(j, 1 - self.layer_of(j)).wait_recv())
            at_core(self.core, 1 - layer, lambda j=j: self.give(j, 1 - self.layer_of(j)).wait_send())
            if j >= GROUPS - SLOTS:
                self.emptied(j)
            for c in self.each(j):
                if layer == 1:
                    self.swap(j, c).wait_send()
                for depth in range(self.halvings - 1):
                    self.up(j, c, depth).wait_send()


def cast_kernel(first, second, qkv, out, up, down, low, high, in_sem, out_sem):
    rows = low.shape[1]
    per = LANES // rows
    slots = low.shape[0]
    count = 12 * per

    core = lax.axis_index("section")

    def take(k, source=first):
        return pltpu.make_async_copy(source.at[pl.ds(k * rows, rows), :], low.at[k % slots], in_sem.at[k % slots])

    def give(k):
        block, part = divmod(k, per)
        if block < 4:
            target = down.at[0, pl.ds(k * rows, rows), :]
        elif block < 8:
            target = up.at[0, pl.ds(part * rows, rows), pl.ds((block - 4) * LANES, LANES)]
        elif block < 9:
            target = out.at[0, pl.ds(part * rows, rows), :]
        else:
            target = qkv.at[0, pl.ds(part * rows, rows), pl.ds((block - 9) * LANES, LANES)]
        return pltpu.make_async_copy(high.at[k % slots], target, out_sem.at[k % slots])

    def fetch(k):
        at_core(core, 0, lambda: take(k).start())
        at_core(core, 1, lambda: take(k, second).start())

    for k in range(slots):
        fetch(k)
    for k in range(count):
        take(k).wait()
        if k >= slots:
            give(k - slots).wait()
        high[k % slots] = low[k % slots].astype(F32)
        give(k).start()
        if k + slots < count:
            fetch(k + slots)
    for k in range(count - slots, count):
        give(k).wait()


def cast_sums(sums, shapes):
    anywhere = pl.BlockSpec(memory_space=pl.ANY)
    return pl.pallas_call(
        cast_kernel,
        out_shape=[jax.ShapeDtypeStruct(shape, F32) for shape in shapes],
        in_specs=[anywhere] * 2,
        out_specs=[anywhere] * 4,
        scratch_shapes=[
            pltpu.VMEM((6, 256, LANES), BF16),
            pltpu.VMEM((6, 256, LANES), F32),
            pltpu.SemaphoreType.DMA((6,)),
            pltpu.SemaphoreType.DMA((6,)),
        ],
        compiler_params=pltpu.CompilerParams(vmem_limit_bytes=60 * 1024 * 1024),
        cost_estimate=pl.CostEstimate(flops=0, bytes_accessed=42 * 10**6, transcendentals=0),
        name="cast",
    )(*sums)


STEP = 256
NEGATIVE = -1e30


def dot(left, right, dims=NN):
    return lax.dot_general(left, right, dims, preferred_element_type=F32)


def gelu_parts(pre):
    bell = jnp.exp(pre * pre * -0.5)
    t = pl.reciprocal(1.0 + jnp.abs(pre) * (0.3275911 * 0.7071067811865476))
    poly = t * (0.1274147960 + t * (-0.142248368 + t * (0.710706871 + t * (-0.7265760135 + t * 0.5307027145))))
    tail = poly * bell
    return jnp.where(pre >= 0.0, 1.0 - tail, tail), bell


def norm_stats(values):
    centred = values - jnp.mean(values, axis=-1, keepdims=True)
    recip = lax.rsqrt(jnp.mean(centred * centred, axis=-1, keepdims=True) + 1e-06)
    return centred * recip, recip


def fold(tile):
    return jnp.sum(tile.reshape(tile.shape[0] // 8, 8, tile.shape[1]), axis=0)


def front_names(r, given):
    r.weights = [next(given) for _ in range(4)]
    r.w_sem, r.n1, r.qkv, r.probs, r.mask, r.mix, r.between, r.n2, r.act = (next(given) for _ in range(9))
    r.pre = [next(given) for _ in range(2)]
    r.act_part = [next(given) for _ in range(2)]


def back_names(r, given):
    r.n1t, r.n2t, r.mixt, r.dmlp, r.dpre, r.dn, r.datt, r.dmix, r.dqkv = (next(given) for _ in range(9))
    r.dpre_part = [next(given) for _ in range(2)]
    r.down_stage, r.up_stage, r.down_sem, r.up_sem = (next(given) for _ in range(4))


def use_weights(r, layer):
    core = lax.axis_index("section")

    def weight(which, source):
        return pltpu.make_async_copy(source[which].at[0], r.weights[which], r.w_sem.at[which])

    for near, source in ((core == layer, r.own), (core != layer, r.far)):

        @pl.when(near)
        def _():
            for which in range(4):
                weight(which, source).start()

    r.ready = lambda which: weight(which, r.own).wait()


def layer_kernel(groups, window, *refs):
    r = Names()
    given = iter(refs)
    r.x, r.col_code, r.row_code, r.vec = (next(given) for _ in range(4))
    r.own = [next(given) for _ in range(4)]
    r.far = [next(given) for _ in range(4)]
    r.unsort, r.dout = (next(given) for _ in range(2))
    r.shown_du, r.small, r.grads, r.du, r.shown_y = (next(given) for _ in range(5))
    front_names(r, given)
    back_names(r, given)
    r.y, r.scale = None, None
    r.y = next(given)
    use_weights(r, 1)
    layer_body(r, groups, window, True, False)


def start_kernel(groups, window, *refs):
    r = Names()
    given = iter(refs)
    lengths, route_mask, tokens, cotangent, router, own_vec = (next(given) for _ in range(6))
    own = [next(given) for _ in range(4)]
    far = [next(given) for _ in range(4)]
    vecs = [next(given) for _ in range(2)]
    r.all_y, r.shown_y, r.delta, cot, r.x = (next(given) for _ in range(5))
    col_codes = [next(given) for _ in range(2)]
    row_codes = [next(given) for _ in range(2)]
    r.unsort, pick, r.unpick, r.skipped, r.scale, factor, extra = (next(given) for _ in range(7))
    front_names(r, given)
    r.y, r.all_x, order, raw, far_vec, raw_sem = (next(given) for _ in range(6))
    far_send, far_recv, vec_sem = (next(given) for _ in range(3))
    core = lax.axis_index("section")
    across = (1 - core, lax.axis_index("dp"))
    rows, width = r.all_x.shape
    half = rows // 2

    def fetch(k, source):
        return pltpu.make_async_copy(source.at[core], raw.at[k], raw_sem.at[k])

    fetch(0, tokens).start()
    fetch(1, cotangent).start()
    barrier = pltpu.get_barrier_semaphore()
    pl.semaphore_signal(barrier, inc=1, device_id=across, device_id_type=pl.DeviceIdType.MESH)
    pl.semaphore_wait(barrier, 1)

    def lend(which):
        return copy_far(own[which], far[which], far_send.at[which], far_recv.at[which], across)

    lend_vec = copy_far(own_vec, far_vec, vec_sem.at[0], vec_sem.at[1], across)
    lend_vec.start()
    lend(0).start()

    def weight(which, source):
        return pltpu.make_async_copy(source[which].at[0], r.weights[which], r.w_sem.at[which])

    def take_own():
        for which in range(4):
            weight(which, own).start()

    at_core(core, 0, take_own)

    def ready(which):
        def arrive():
            lend(which).wait_recv()
            weight(which, far).start()

        at_core(core, 1, arrive)
        weight(which, own).wait()

    r.ready = ready

    starts, bases, total, longs, short = [], [], 0, 0, 0
    count = lengths.shape[2]
    sizes = [lengths[core, 0, c] for c in range(count)]
    for size in sizes:
        is_long = size == LONG
        starts.append(total)
        bases.append(jnp.where(is_long, longs * LONG, 2 * LONG + short))
        total = total + size
        longs = longs + jnp.where(is_long, 1, 0)
        short = short + jnp.where(is_long, 0, size)

    def place(shape, dim):
        return lax.broadcasted_iota(jnp.int32, shape, dim)

    def target(at):
        moved = at
        for start, size, base in zip(starts, sizes, bases):
            moved = moved + jnp.where((at >= start) & (at < start + size), base - start, 0)
        return moved

    def code_of(at):
        return sum(jnp.where(at >= base, 1, 0) for base in bases)

    row_at, col_at = place((1, rows), 1), place((rows, 1), 0)

    def one_hot(left, right):
        return jnp.where(left == right, 1.0, 0.0).astype(BF16)

    goes_row, goes_col = target(row_at), target(col_at)
    row_codes[1][...] = code_of(row_at)
    col_codes[1][...] = code_of(col_at)
    for start in range(0, rows, 128):
        here = slice(start, start + 128)
        order[here, :] = one_hot(col_at[here], goes_row)
        r.unsort[here, :] = one_hot(goes_col[here], row_at)
    lend(1).start()
    lend(2).start()
    lend(3).start()
    for k, (source, moved) in enumerate(((tokens, r.all_x), (cotangent, cot))):
        fetch(k, source).wait()
        for part in range(width // STEP):
            span = slice(part * STEP, (part + 1) * STEP)
            moved[:, span] = dot(order[...], raw[k, :, span]).astype(BF16)

    mask = jnp.where(route_mask[pl.ds(core, 1), :] == 1, 1.0, 0.0)
    masks = jnp.broadcast_to(mask, (8, rows)).astype(BF16)
    chosen_row = dot(masks, r.unsort[...])
    chosen_col = dot(order[...], masks, NT)
    earlier = jnp.where(place((rows, rows), 0) < place((rows, rows), 1), 1.0, 0.0).astype(BF16)
    rank_row = dot(chosen_row.astype(BF16), earlier)[:1]
    later = jnp.where(place((rows, rows), 0) > place((rows, rows), 1), 1.0, 0.0).astype(BF16)
    rank_col = dot(later, chosen_col.astype(BF16))[:, :1]
    chosen_row, chosen_col = chosen_row[:1], chosen_col[:, :1]
    r.skipped[...] = 1.0 - chosen_col
    key_row = jnp.where(chosen_row > 0.5, rank_row, -1.0)
    key_col = jnp.where(chosen_col > 0.5, rank_col, -1.0)
    pick[...] = one_hot(place((half, 1), 0).astype(F32), key_row)
    r.unpick[...] = one_hot(key_col, place((1, half), 1).astype(F32))
    names_row = jnp.broadcast_to(code_of(row_at).astype(F32), (8, rows)).astype(BF16)
    routed_row = dot(names_row, r.unpick[...])[:1]
    routed_col = dot(pick[...], names_row, NT)[:, :1]
    row_codes[0][...] = routed_row.astype(jnp.int32)
    col_codes[0][...] = routed_col.astype(jnp.int32)
    for part in range(width // STEP):
        span = slice(part * STEP, (part + 1) * STEP)
        r.x[:, span] = dot(pick[...], r.all_x[:, span]).astype(BF16)
    logit = jnp.sum(r.x[...].astype(F32) * router[...], axis=1, keepdims=True)
    gate = 1.0 / (1.0 + jnp.exp(-logit))
    held = jnp.where(routed_col > 0.5, 1.0, 0.0)
    r.scale[...] = held * gate
    factor[...] = held * gate * (1.0 - gate)
    gates, counts = jnp.sum(held * gate, axis=0, keepdims=True), jnp.sum(mask, axis=1, keepdims=True)
    lane = place((1, width), 1)
    micro = tokens.shape[0]
    extra[...] = jnp.where(lane == core, gates, jnp.where(lane == core + micro, counts, 0.0))

    lend_vec.wait()
    for layer in range(2):
        vecs[layer][...] = jnp.where(core == layer, own_vec[...], far_vec[...])
    r.vec, r.col_code, r.row_code, r.own = vecs[0], col_codes[0], row_codes[0], own
    layer_body(r, groups, window, False, True)
    for which in range(4):
        lend(which).wait_send()
        at_core(core, 0, lambda which=which: lend(which).wait_recv())


def fused_kernel(groups, window, chunks, *refs):
    r = Names()
    given = iter(refs)
    r.x, r.col_code, r.row_code, r.vec, r.scale = (next(given) for _ in range(5))
    r.own = [next(given) for _ in range(4)]
    r.far = [next(given) for _ in range(4)]
    r.unsort = next(given)
    r.all_dout, r.pick, r.unpick, r.skipped, r.delta, r.factor, r.router = (next(given) for _ in range(7))
    second, second_small, extra = (next(given) for _ in range(3))
    shown = [next(given) for _ in range(3)]
    full = [next(given) for _ in range(2)]
    landed = [next(given) for _ in range(2)]
    first, small_out = (next(given) for _ in range(2))
    shown_out = [next(given) for _ in range(2)]
    front_names(r, given)
    back_names(r, given)
    r.dout, r.du, r.shown_du, r.small, r.router_grad = (next(given) for _ in range(5))
    sums = Sums(chunks, GROUP_STARTS, given)
    sums.grads, sums.landed, sums.full, sums.small_out = (first, second), landed, full, small_out
    sums.shown, sums.shown_out = (shown[0], shown[1], r.shown_du, shown[2]), shown_out
    r.grads = first
    core = sums.core
    use_weights(r, 0)
    sums.open()
    sums.start_swaps(0)
    sums.start_swaps(1)
    sums.prepare(0)
    early = [0]

    def hook():
        sums.moment(early[0])
        early[0] += 1

    def tile_out(stage, row, column, shape, sem, tile):
        area = (pl.ds(row, shape[0]), pl.ds(column, shape[1]))
        owner = lax.rem(tile // 6, 2)

        @pl.when(core == owner)
        def _():
            pltpu.make_async_copy(stage, first.at[area], sem).start()

        @pl.when(core != owner)
        def _():
            copy_far(stage, landed[0].at[area], sem, sums.tile_recv.at[tile], sums.across).start()

    r.hook, r.tile_out = hook, tile_out
    layer_body(r, groups, window, True, True)

    for index, source in enumerate((r.small, second_small)):
        for row in range(source.shape[1] // LANES):
            sums.small[index, row : row + 1, :] = source[:, row * LANES : (row + 1) * LANES]
        row = source.shape[1] // LANES
        sums.small[index, row : row + 1, :] = r.router_grad[...]
        sums.small[index, row + 1 : row + 2, :] = extra[...]
        left = sums.small.shape[1] - row - 2
        sums.small[index, row + 2 :, :] = jnp.zeros((left, LANES), F32)
    sums.small_begin()
    sums.show()

    for turn, now in enumerate(range(early[0], max(sums.end, early[0] + sums.bits + 1))):
        if now < sums.end:
            sums.moment(now)
        if turn <= sums.bits:
            sums.small_turn(turn)
    sums.close()


def layer_body(r, groups, window, full, is_router):
    hook = r.hook if full and is_router else lambda: None
    rows, width = r.x.shape
    hidden = r.own[2].shape[2]
    pairs = width // 128
    row_tile = rows // 5

    def vec(start, count=width):
        return r.vec[:, start : start + count]

    g1, g2, b1, bq, bv, bo, b2 = (vec(k * width) for k in range(7))
    bu_at, bd_at = 7 * width, 7 * width + hidden

    def row_loop(step, init=0):
        def at(k, carry):
            return step(pl.ds(pl.multiple_of(k * row_tile, row_tile), row_tile), carry)

        return lax.fori_loop(0, rows // row_tile, at, init)

    def norm_step(source, gain, bias, target):
        def step(here, carry):
            normal, _ = norm_stats(source[here, :].astype(F32))
            target[here, :] = (normal * gain + bias).astype(BF16)
            return carry

        return step

    def tiles(step):
        for k in range(width // STEP):
            step(slice(k * STEP, (k + 1) * STEP))

    def show(source, target):
        def step(span):
            target[:, span] = dot(r.unsort[...], source[:, span]).astype(BF16)

        tiles(step)

    def spread(routed, others, target, shown):
        def step(span):
            value = dot(r.unpick[...], routed[:, span]) + others[:, span].astype(F32) * r.skipped[...]
            if target is not None:
                target[:, span] = value.astype(BF16)
            shown[:, span] = dot(r.unsort[...], value.astype(BF16)).astype(BF16)

        tiles(step)

    row_loop(norm_step(r.x, g1, b1, r.n1))
    if full and is_router:

        def route_step(span):
            r.dout[:, span] = dot(r.pick[...], r.all_dout[:, span]).astype(BF16)

        tiles(route_step)
    if full:

        def delta_step(here, carry):
            low = (r.dout[here, :].astype(F32) * r.scale[here, :]).astype(BF16) if is_router else r.dout[here, :]
            r.dmlp[here, :] = low
            return carry + fold(low.astype(F32))

        dbd = row_loop(delta_step, jnp.zeros((8, width), F32))
        r.small[:, bd_at:] = jnp.sum(dbd, axis=0, keepdims=True)

    for k, (start, low, high) in enumerate(groups):
        col = r.col_code[start : start + window, :]
        row = r.row_code[:, start : start + window]
        place = lax.broadcasted_iota(jnp.int32, (window, 1), 0) + start
        col = jnp.where((place >= low) & (place < high), col, -1)
        r.mask[k] = jnp.where(col == row, 0.0, NEGATIVE)

    r.ready(0)
    for k in range(3 * width // STEP):
        span = slice(k * STEP, (k + 1) * STEP)
        value = dot(r.n1[...], r.weights[0][:, span])
        if k < width // STEP:
            value = (value + bq[:, span]).astype(BF16).astype(F32) * 0.125
        elif k >= 2 * width // STEP:
            value = value + bv[:, k * STEP - 2 * width : (k + 1) * STEP - 2 * width]
        r.qkv[:, span] = value.astype(BF16)

    hook()
    lane = lax.broadcasted_iota(jnp.int32, (1, 128), 1)

    def halves(block):
        zero = jnp.zeros_like(block)
        return jnp.concatenate([jnp.where(lane < 64, block, zero), jnp.where(lane < 64, zero, block)], axis=0)

    high_half = lax.broadcasted_iota(jnp.int32, (128, 1), 0) >= 64

    def own_half(both):
        return jnp.where(high_half, both[:, window:], both[:, :window]).T

    r.mix[...] = jnp.zeros_like(r.mix)

    def lanes(pair, part):
        return pl.ds(pl.multiple_of(pair * 128 + part * width, 128), 128)

    spots = [slice(start, start + window) for start, _, _ in groups]
    count = len(groups)

    def qkv_at(pair, part):
        return [r.qkv[here, lanes(pair, part)] for here in spots]

    def attend(pair, carry):
        q, key, v = (qkv_at(pair, part) for part in range(3))
        scores = [dot(key[k], halves(q[k]), NT) for k in range(count)]
        probs = []
        for k, (start, low, high) in enumerate(groups):
            mask = r.mask[k]
            masked = scores[k] + jnp.concatenate([mask, mask], axis=1)
            place = lax.broadcasted_iota(jnp.int32, (1, window), 1) + start
            valid = (place >= low) & (place < high)
            valid = jnp.concatenate([valid, valid], axis=1)
            power = jnp.exp(masked - jnp.max(masked, axis=0, keepdims=True))
            total = jnp.sum(power, axis=0, keepdims=True)
            prob = (power * jnp.where(valid, 1.0 / total, 0.0)).astype(BF16)
            if full:
                r.probs[pair * count + k] = prob
            probs.append(prob)
        mixed = [dot(v[k].T, probs[k]) for k in range(count)]
        for k, here in enumerate(spots):
            r.mix[here, lanes(pair, 0)] = r.mix[here, lanes(pair, 0)] + own_half(mixed[k]).astype(BF16)
        return carry

    lax.fori_loop(0, pairs, attend, 0)

    r.ready(1)
    for k in range(width // STEP):
        span = slice(k * STEP, (k + 1) * STEP)
        value = dot(r.mix[...], r.weights[1][:, span]) + bo[:, span]
        r.between[:, span] = r.x[:, span].astype(F32) + value
    row_loop(norm_step(r.between, g2, b2, r.n2))
    if full:
        r.n1t[...] = r.n1[...].T
        r.n2t[...] = r.n2[...].T
        r.mixt[...] = r.mix[...].T
    hook()

    r.ready(2)
    if full:
        r.ready(3)

    def tile_out(stage, row, column, shape, sem, tile):
        target = r.grads.at[pl.ds(row, shape[0]), pl.ds(column, shape[1])]
        pltpu.make_async_copy(stage, target, sem).start()

    tile_out = r.tile_out if full and is_router else tile_out

    def down_out(k, slot):
        tile_out(
            r.down_stage.at[slot], pl.multiple_of(k * STEP, STEP), 0, (STEP, width), r.down_sem.at[slot], k
        )

    def side_out(block, k, slot):
        row = pl.multiple_of((block + k // 3) * width, width)
        column = pl.multiple_of(k % 3 * STEP, STEP)
        tile = k + {4: 12, 8: 24, 9: 27}[block]
        tile_out(r.up_stage.at[slot], row, column, (width, STEP), r.up_sem.at[slot], tile)

    def down_free(slot):
        target = r.grads.at[pl.ds(0, STEP), pl.ds(0, width)]
        pltpu.make_async_copy(r.down_stage.at[slot], target, r.down_sem.at[slot]).wait()

    def side_free(slot):
        target = r.grads.at[pl.ds(0, width), pl.ds(0, STEP)]
        pltpu.make_async_copy(r.up_stage.at[slot], target, r.up_sem.at[slot]).wait()

    steps = hidden // STEP

    def part_at(k):
        return pl.multiple_of(k * STEP, STEP)

    def ahead(k, side):
        at = part_at(k)
        r.pre[side][...] = dot(r.n2[...], r.weights[2][:, pl.ds(at, STEP)]) + r.vec[:, pl.ds(at + bu_at, STEP)]

    def middle(k, side):
        at = part_at(k)
        span = pl.ds(at, STEP)
        pre = r.pre[side][...]
        cdf, bell = gelu_parts(pre)
        act = (pre * cdf).astype(BF16)
        if not (full and is_router):
            r.act[:, span] = act
        if full:
            r.act_part[side][...] = act
            slope = cdf + pre * bell * 0.3989422804014327
            dact = dot(r.dmlp[...], r.weights[3][span, :], NT)
            dpre = (dact * slope).astype(BF16)
            r.dpre[:, span] = dpre
            r.dpre_part[side][...] = dpre
            r.small[:, pl.ds(at + bu_at, STEP)] = jnp.sum(dpre.astype(F32), axis=0, keepdims=True)

    def weigh(side):
        r.down_stage[side] = dot(r.act_part[side][...], r.dmlp[...], TN).astype(BF16)
        r.up_stage[side] = dot(r.n2t[...], r.dpre_part[side][...]).astype(BF16)

    def send_out(k, side):
        down_out(k, side)
        side_out(4, k, side)

    def two_steps(kk, first=False):
        even = kk * 2
        if full and not first:

            @pl.when(kk >= 2)
            def _():
                down_free(1)
                side_free(1)

            down_free(0)
            side_free(0)
        middle(even, 0)
        ahead(even + 1, 1)
        if full and not first:
            weigh(1)
        middle(even + 1, 1)
        ahead(jnp.minimum(even + 2, steps - 1), 0)
        if full:
            weigh(0)
            if not first:
                send_out(even - 1, 1)
            send_out(even, 0)

    def more_steps(kk, carry):
        two_steps(kk)
        return carry

    ahead(0, 0)
    two_steps(0, True)
    if full and is_router:
        lax.fori_loop(1, steps // 4, more_steps, 0)
        hook()
        lax.fori_loop(steps // 4, steps // 2, more_steps, 0)
    else:
        lax.fori_loop(1, steps // 2, more_steps, 0)
    if full:
        down_free(1)
        side_free(1)
        weigh(1)
        send_out(steps - 1, 1)
    if full and is_router:
        down_free(0)
        down_free(1)
        hook()
    if not full:
        r.ready(3)
    if not (full and is_router):
        for k in range(width // STEP):
            span = slice(k * STEP, (k + 1) * STEP)
            value = dot(r.act[...], r.weights[3][:, span]) + vec(bd_at)[:, span]
            source = r.x[:, span].astype(F32)
            value = r.between[:, span] - source + value
            if not full:
                r.delta[:, span] = value
            r.y[:, span] = (source + (r.scale[...] * value if is_router else value)).astype(BF16)
    if not full:
        spread(r.y, r.all_x, r.all_y, r.shown_y)
        return
    if not is_router:
        show(r.y, r.shown_y)

    for k in range(width // STEP):
        span = slice(k * STEP, (k + 1) * STEP)
        r.dn[:, span] = dot(r.dpre[...], r.weights[2][span, :], NT)

    def norm_back(source, gain, here):
        normal, recip = norm_stats(source[here, :].astype(F32))
        grad = r.dn[here, :]
        hat = grad * gain
        back = recip * (
            hat - jnp.mean(hat, axis=-1, keepdims=True) - normal * jnp.mean(hat * normal, axis=-1, keepdims=True)
        )
        return back, fold(grad * normal), fold(grad)

    def second_back(here, carry):
        back, dg, db = norm_back(r.between, g2, here)
        r.between[here, :] = back
        delta = r.dout[here, :].astype(F32)
        total = ((delta * r.scale[here, :] if is_router else delta) + back).astype(BF16)
        r.datt[here, :] = total
        return carry[0] + dg, carry[1] + db, carry[2] + fold(total.astype(F32))

    zero = jnp.zeros((8, width), F32)
    dg2, db2, dbo = row_loop(second_back, (zero, zero, zero))
    r.small[:, width : 2 * width] = jnp.sum(dg2, axis=0, keepdims=True)
    r.small[:, 6 * width : 7 * width] = jnp.sum(db2, axis=0, keepdims=True)
    r.small[:, 5 * width : 6 * width] = jnp.sum(dbo, axis=0, keepdims=True)

    for k in range(width // STEP):
        span = slice(k * STEP, (k + 1) * STEP)
        r.dmix[:, span] = dot(r.datt[...], r.weights[1][span, :], NT).astype(BF16)
        slot = k % 2
        side_free(slot)
        r.up_stage[slot] = dot(r.mixt[...], r.datt[:, span]).astype(BF16)
        side_out(8, k, slot)

    r.dqkv[...] = jnp.zeros_like(r.dqkv)

    def attend_back(pair, carry):
        q, key, v = (qkv_at(pair, part) for part in range(3))
        dm = [halves(r.dmix[here, lanes(pair, 0)]) for here in spots]
        dprobs = [dot(v[k], dm[k], NT) for k in range(count)]
        dv = [dot(r.probs[pair * count + k], dm[k]) for k in range(count)]
        ds = []
        for k in range(count):
            wide = r.probs[pair * count + k].astype(F32)
            product = wide * dprobs[k]
            ds.append((product - wide * jnp.sum(product, axis=0, keepdims=True)).astype(BF16))
        dk = [dot(ds[k], halves(q[k])) for k in range(count)]
        dq = [dot(key[k].T, ds[k]) for k in range(count)]
        for k, here in enumerate(spots):
            for part, value in enumerate((own_half(dq[k]) * 0.125, dk[k], dv[k])):
                spot = lanes(pair, part)
                r.dqkv[here, spot] = r.dqkv[here, spot] + value.astype(BF16)
        return carry

    lax.fori_loop(0, pairs, attend_back, 0)
    hook()

    for k in range(3 * width // STEP):
        span = slice(k * STEP, (k + 1) * STEP)
        block = r.dqkv[:, span]
        if not width <= k * STEP < 2 * width:
            at = 3 * width + k * STEP - (width if k * STEP >= width else 0)
            r.small[:, at : at + STEP] = jnp.sum(block.astype(F32), axis=0, keepdims=True)
        slot = (k + 1) % 2
        side_free(slot)
        r.up_stage[slot] = dot(r.n1t[...], block).astype(BF16)
        side_out(9, k, slot)
    side_free(0)
    side_free(1)
    hook()

    for k in range(width // STEP):
        span = slice(k * STEP, (k + 1) * STEP)
        r.dn[:, span] = dot(r.dqkv[...], r.weights[0][span, :], NT)

    def first_back(here, carry):
        back, dg, db = norm_back(r.x, g1, here)
        dout = r.dout[here, :].astype(F32)
        total = dout + r.between[here, :] + back
        sums = [carry[0] + dg, carry[1] + db]
        if is_router:
            slope = jnp.sum(dout * r.delta[here, :], axis=1, keepdims=True) * r.factor[here, :]
            total = total + slope * r.router[...]
            sums.append(carry[2] + fold(slope * r.x[here, :].astype(F32)))
        r.du[here, :] = total.astype(BF16)
        return tuple(sums)

    sums = row_loop(first_back, (zero,) * (3 if is_router else 2))
    r.small[:, :width] = jnp.sum(sums[0], axis=0, keepdims=True)
    r.small[:, 2 * width : 3 * width] = jnp.sum(sums[1], axis=0, keepdims=True)
    if is_router:
        r.router_grad[...] = jnp.sum(sums[2], axis=0, keepdims=True)
        spread(r.du, r.all_dout, None, r.shown_du)
    else:
        show(r.du, r.shown_du)
    if not is_router:
        down_free(0)
        down_free(1)


def front_scratch(rows, width, hidden, groups, window, full, keep_act):
    sizes = [(width, 3 * width), (width, width), (width, hidden), (hidden, width)]
    held = [pltpu.VMEM(size, BF16) for size in sizes]
    held += [pltpu.SemaphoreType.DMA((4,))]
    held += [pltpu.VMEM((rows, width), BF16), pltpu.VMEM((rows, 3 * width), BF16)]
    held += [pltpu.VMEM((HEADS // 2 * len(groups) if full else 1, window, 2 * window), BF16)]
    held += [pltpu.VMEM((len(groups), window, window), F32), pltpu.VMEM((rows, width), BF16)]
    held += [pltpu.VMEM((rows, width), F32), pltpu.VMEM((rows, width), BF16)]
    held += [pltpu.VMEM((rows, hidden) if keep_act else (TILE, LANES), BF16)]
    return held + [pltpu.VMEM((rows, STEP), F32)] * 2 + [pltpu.VMEM((rows, STEP), BF16)] * 2


def back_scratch(rows, width, hidden):
    held = [pltpu.VMEM((width, rows), BF16)] * 3 + [pltpu.VMEM((rows, width), BF16)]
    held += [pltpu.VMEM((rows, hidden), BF16), pltpu.VMEM((rows, width), F32)]
    held += [pltpu.VMEM((rows, width), BF16)] * 2 + [pltpu.VMEM((rows, 3 * width), BF16)]
    held += [pltpu.VMEM((rows, STEP), BF16)] * 2
    held += [pltpu.VMEM((2, STEP, width), BF16), pltpu.VMEM((2, width, STEP), BF16)]
    return held + [pltpu.SemaphoreType.DMA((2,))] * 2


def run_start(groups, window, lengths, route_mask, tokens, cotangent, router_row, own_vec, own):
    _, rows, width = tokens.shape
    half, hidden = rows // 2, own[2].shape[2]
    inside = pl.BlockSpec(memory_space=pltpu.VMEM)
    anywhere = pl.BlockSpec(memory_space=pl.ANY)
    outs = [(value.shape, BF16) for value in own] + [(own_vec.shape, F32)] * 2
    outs += [((rows, width), BF16)] * 2 + [((half, width), F32), ((rows, width), BF16), ((half, width), BF16)]
    outs += [((half, 1), jnp.int32), ((rows, 1), jnp.int32), ((1, half), jnp.int32), ((1, rows), jnp.int32)]
    outs += [((rows, rows), BF16), ((half, rows), BF16), ((rows, half), BF16), ((rows, 1), F32)]
    outs += [((half, 1), F32)] * 2 + [((1, width), F32)]
    scratch = front_scratch(half, width, hidden, groups, window, False, True)
    scratch += [pltpu.VMEM((half, width), BF16), pltpu.VMEM((rows, width), BF16), pltpu.VMEM((rows, rows), BF16)]
    scratch += [pltpu.VMEM((2, rows, width), BF16), pltpu.VMEM(own_vec.shape, F32), pltpu.SemaphoreType.DMA((2,))]
    scratch += [pltpu.SemaphoreType.DMA((4,))] * 2 + [pltpu.SemaphoreType.DMA((2,))]
    return pl.pallas_call(
        functools.partial(start_kernel, groups, window),
        out_shape=[jax.ShapeDtypeStruct(*one) for one in outs],
        in_specs=[pl.BlockSpec(memory_space=pltpu.SMEM), inside] + [anywhere] * 2 + [inside] * 2 + [anywhere] * 4,
        out_specs=[anywhere] * 4 + [inside] * (len(outs) - 4),
        scratch_shapes=scratch,
        compiler_params=pltpu.CompilerParams(
            collective_id=1, has_side_effects=True, vmem_limit_bytes=60 * 1024 * 1024
        ),
        cost_estimate=pl.CostEstimate(flops=5 * 10**9, bytes_accessed=6 * 10**7, transcendentals=0),
        name="start",
    )(lengths, route_mask, tokens, cotangent, router_row, own_vec, *own)


def run_layer(groups, window, x, col_code, row_code, vec, own, far, unsort, back):
    rows, width = x.shape
    hidden = own[2].shape[2]
    inside = pl.BlockSpec(memory_space=pltpu.VMEM)
    anywhere = pl.BlockSpec(memory_space=pl.ANY)
    args = [x, col_code, row_code, vec, *own, *far, unsort, back]
    outs = [((rows, width), BF16), ((1, vec.shape[1]), F32), ((GRAD_ROWS, LANES), BF16)]
    outs += [((rows, width), BF16)] * 2
    scratch = front_scratch(rows, width, hidden, groups, window, True, True)
    scratch += back_scratch(rows, width, hidden) + [pltpu.VMEM((rows, width), BF16)]
    flops = rows * width * (3 * width + width + 2 * hidden) * 6
    return pl.pallas_call(
        functools.partial(layer_kernel, groups, window),
        out_shape=[jax.ShapeDtypeStruct(*one) for one in outs],
        in_specs=[inside] * 4 + [anywhere] * 8 + [inside] * 2,
        out_specs=[inside] * 2 + [anywhere] + [inside] * 2,
        scratch_shapes=scratch,
        compiler_params=pltpu.CompilerParams(vmem_limit_bytes=62 * 1024 * 1024),
        cost_estimate=pl.CostEstimate(flops=flops, bytes_accessed=3 * 10**7, transcendentals=0),
        name="layer",
    )(*args)


def run_fused(axis_of, groups, window, x, col_code, row_code, vec, scale, own, far, rows_of, back, router, second, second_small, extra, shown):
    rows, width = x.shape
    hidden = own[2].shape[2]
    chunks = sum_plan(axis_of)
    inside = pl.BlockSpec(memory_space=pltpu.VMEM)
    anywhere = pl.BlockSpec(memory_space=pl.ANY)
    unsort, pick, unpick, skipped = rows_of
    delta, factor, router_row = router
    every = unsort.shape[0]
    args = [x, col_code, row_code, vec, scale, *own, *far, unsort]
    args += [back, pick, unpick, skipped, delta, factor, router_row]
    args += [second, second_small, extra, *shown]
    small_rows = -(-(vec.shape[1] // LANES + 2) // 8) * 8
    outs = [((GRAD_ROWS, LANES), BF16)] * 5
    outs += [((small_rows, LANES), F32)] + [((2, every, width), BF16)] * 2
    scratch = front_scratch(rows, width, hidden, groups, window, True, False)
    scratch += back_scratch(rows, width, hidden)
    scratch += [pltpu.VMEM((rows, width), BF16)] * 2 + [pltpu.VMEM((every, width), BF16)]
    scratch += [pltpu.VMEM((1, vec.shape[1]), F32), pltpu.VMEM((1, width), F32)]
    scratch += Sums.scratch(chunks, small_rows)
    *sums, _, _, _, small, acts, grads = pl.pallas_call(
        functools.partial(fused_kernel, groups, window, chunks),
        out_shape=[jax.ShapeDtypeStruct(*one) for one in outs],
        in_specs=[inside] * 5 + [anywhere] * 8 + [inside] * 8 + [anywhere] + [inside] * 2 + [anywhere] * 3,
        out_specs=[anywhere] * 5 + [inside] + [anywhere] * 2,
        scratch_shapes=scratch,
        compiler_params=pltpu.CompilerParams(
            collective_id=0, has_side_effects=True, vmem_limit_bytes=64 * 1024 * 1024
        ),
        cost_estimate=pl.CostEstimate(flops=10**10, bytes_accessed=6 * 10**8, transcendentals=0),
        name="fused",
    )(*args)
    return sums, small, (acts, grads)


def body(axis_of, tokens, lengths, route_mask, router_weight, gains, biases, w_qkv, w_out, w_up, w_down, cotangent):
    micro, rows, width = tokens.shape
    own = (w_qkv, w_out, w_up, w_down)
    own_vec = jnp.concatenate([gains, biases], axis=1)
    router_row = router_weight.astype(F32)[None, :]
    half = LONG // 2
    groups_one = ((0, 0, half), (96, half, 2 * half), (192, 2 * half, rows // 2))
    groups_two = ((0, 0, LONG), (192, LONG, 2 * LONG), (384, 2 * LONG, rows))
    made = run_start(groups_one, 128, lengths, route_mask, tokens, cotangent, router_row, own_vec, own)
    far, (vec_one, vec_two), (y1, shown_y1, delta_one, cot, routed) = made[:4], made[4:6], made[6:11]
    col_one, col_two, row_one, row_two, *others = made[11:]
    unsort, pick, unpick, skipped, scale, factor, extra = others
    shown_du2, small_two, grads_two, dout, shown_y2 = run_layer(
        groups_two, 256, y1, col_two, row_two, vec_two, own, far, unsort, cot
    )
    sums, small, (activations, input_grads) = run_fused(
        axis_of, groups_one, 128, routed, col_one, row_one, vec_one, scale, own, far,
        (unsort, pick, unpick, skipped), dout, (delta_one, factor, router_row), grads_two, small_two, extra,
        (shown_y1, shown_y2, shown_du2),
    )
    small = small.reshape(-1)
    span = own_vec.shape[1]
    tail = small[span:]
    grads = cast_sums(sums, [value.shape for value in own])

    return (
        activations[None],
        input_grads[None],
        *grads,
        small[: 2 * width][None],
        small[2 * width : span][None],
        tail[:width],
        tail[width : width + micro] / tail[width + micro : width + 2 * micro],
    )


def solution(mesh):
    in_specs = (
        P(None, "dp", None),
        P(None, "dp", None),
        P(None, "dp"),
        P(),
        P("section", None),
        P("section", None),
        P("section", None, None),
        P("section", None, None),
        P("section", None, None),
        P("section", None, None),
        P(None, "dp", None),
    )
    out_specs = (
        P("section", None, "dp", None),
        P("section", None, "dp", None),
        P("section", None, None),
        P("section", None, None),
        P("section", None, None),
        P("section", None, None),
        P("section", None),
        P("section", None),
        P(),
        P(),
    )
    step = functools.partial(body, axis_bits(mesh))
    return jax.shard_map(step, mesh=mesh, in_specs=in_specs, out_specs=out_specs, check_vma=False)
```

```python
import functools

import jax
import jax.numpy as jnp
from jax import lax
from jax.experimental import pallas as pl
from jax.experimental.pallas import tpu as pltpu
from jax.sharding import PartitionSpec as P

HEADS = 12
HEAD = 64
LONG = 197
F32 = jnp.float32
BF16 = jnp.bfloat16
NT = (((1,), (1,)), ((), ()))
TN = (((0,), (0,)), ((), ()))
NN = (((1,), (0,)), ((), ()))


LANES = 768
TILE = 16
GRAD_ROWS = 12 * LANES


def axis_bits(mesh):
    line = mesh.devices[0]
    bits = len(line).bit_length() - 1
    try:
        spots = [tuple(device.coords) for device in line]
    except AttributeError:
        return [0] * bits
    return [
        next((w for w in range(3) if spots[1 << b][w] != spots[0][w]), 0) for b in range(bits)
    ]


HALVINGS = 4
GROUPS = 6
SLOTS = 4


GROUP_PLAN = (
    ((768, 123), (512, 1023), (256, 1032)),
    ((768, 123), (512, 1023), (256, 1320)),
    ((768, 132), (768, 1023)),
    ((512, 1230), (512, 123), (512, 2013)),
    ((768, 1023), (768, 132)),
    ((512, 2103), (512, 213), (512, 1023)),
)
GROUP_STARTS = (0, 1, 3, 4, 5, 7)


def sum_plan(axis_of):
    lists = {}
    for bit, axis in enumerate(axis_of):
        lists.setdefault(axis, []).append(bit)
    lists = sorted(lists.values(), key=len)
    while len(lists) < 3:
        lists.append([])
    roles = [lists[0][:1], lists[1][:1], lists[2][:1], lists[2][1:2]]
    plan = []
    for group in GROUP_PLAN:
        chunks, start = [], 0
        for size, code in group:
            order = [bit for place in (1000, 100, 10, 1) for bit in roles[code // place % 10]]
            order += [bit for bit in range(len(axis_of)) if bit not in order]
            chunks.append((start, size, order))
            start += size
        plan.append(chunks)
    return plan


def add_rows(into, into_start, source, start, other, other_start, count):
    tile = next(t for t in (64, 32, 16) if count % t == 0)

    def step(k, carry):
        target, here, there = (
            pl.ds(pl.multiple_of(first + k * tile, TILE), tile) for first in (into_start, start, other_start)
        )
        into[target, :] = source[here, :] + other[there, :]
        return carry

    lax.fori_loop(0, count // tile, step, 0)


class Names:
    pass


def copy_far(source, target, one, two, friend):
    return pltpu.make_async_remote_copy(
        src_ref=source,
        dst_ref=target,
        send_sem=one,
        recv_sem=two,
        device_id=friend,
        device_id_type=pl.DeviceIdType.MESH,
    )


def at_core(core, index, step):
    pl.when(core == index)(step)


GRAD_TILES = 36
GROUP_ROWS = GRAD_ROWS // GROUPS


class Sums:
    def __init__(self, chunks, starts, given):
        self.chunks, self.starts = chunks, starts
        self.bits = bits = len(chunks[0][0][2])
        self.halvings = min(bits, HALVINGS)
        self.acc, self.mate = next(given), next(given)
        self.got = [next(given) for _ in range(bits)]
        self.small_got, self.small = next(given), next(given)
        self.load_sem, self.mate_sem, self.swap_send, self.swap_recv = (next(given) for _ in range(4))
        self.send, self.recv, self.back_send, self.back_recv = (next(given) for _ in range(4))
        self.small_send, self.small_recv = (next(given) for _ in range(2))
        self.shown_sem, self.shown_send, self.shown_recv = (next(given) for _ in range(3))
        self.tile_recv, self.give_send, self.give_recv, self.put_sem, self.ready = (next(given) for _ in range(5))
        self.core = lax.axis_index("section")
        self.me = lax.axis_index("dp")
        self.across = (1 - self.core, self.me)
        self.end = starts[-1] + bits + self.halvings + 1

    @staticmethod
    def scratch(chunks, small_rows):
        bits = len(chunks[0][0][2])
        count = sum(len(group) for group in chunks)
        rows = SLOTS * GROUP_ROWS
        held = [pltpu.VMEM((GRAD_ROWS, LANES), BF16), pltpu.VMEM((GROUP_ROWS, LANES), BF16)]
        held += [pltpu.VMEM((rows >> min(depth + 1, HALVINGS), LANES), BF16) for depth in range(bits)]
        held += [pltpu.VMEM((bits + 1, small_rows, LANES), F32), pltpu.VMEM((2, small_rows, LANES), F32)]
        held += [pltpu.SemaphoreType.DMA((count,))] * 4
        held += [pltpu.SemaphoreType.DMA((count, bits))] * 4
        held += [pltpu.SemaphoreType.DMA((bits + 1,))] * 2
        held += [pltpu.SemaphoreType.DMA((2,))] * 3
        held += [pltpu.SemaphoreType.DMA((GRAD_TILES,))]
        held += [pltpu.SemaphoreType.DMA((GROUPS,))] * 3
        return held + [pltpu.SemaphoreType.REGULAR((count, min(bits, HALVINGS)))]

    def bit_at(self, bit):
        return lax.rem(self.me // (1 << bit), 2)

    def partner(self, bit):
        return (self.core, self.me + (1 - 2 * self.bit_at(bit)) * (1 << bit))

    def open(self):
        friends = [self.across] + [self.partner(bit) for bit in range(self.bits)]
        barrier = pltpu.get_barrier_semaphore()
        for friend in friends:
            pl.semaphore_signal(barrier, inc=1, device_id=friend, device_id_type=pl.DeviceIdType.MESH)
        pl.semaphore_wait(barrier, len(friends))

    @staticmethod
    def layer_of(j):
        return 1 if j < GROUPS // 2 else 0

    def base(self, j, core):
        return (2 * (j % (GROUPS // 2)) + core) * GROUP_ROWS

    def rows_at(self, j, core, c):
        start, size, _ = self.chunks[j][c]
        return pl.ds(pl.multiple_of(self.base(j, core) + start, TILE), size)

    def index(self, j, c):
        return sum(len(group) for group in self.chunks[:j]) + c

    def swap(self, j, c):
        rows, k = self.rows_at(j, 1 - self.core, c), self.index(j, c)
        return copy_far(
            self.grads[1].at[rows, :], self.landed[1].at[rows, :], self.swap_send.at[k], self.swap_recv.at[k],
            self.across,
        )

    def load(self, j, c):
        start, size, _ = self.chunks[j][c]
        target = self.acc.at[pl.ds(j * GROUP_ROWS + start, size), :]
        source = self.grads[self.layer_of(j)].at[self.rows_at(j, self.core, c), :]
        return pltpu.make_async_copy(source, target, self.load_sem.at[self.index(j, c)])

    def load_mate(self, j, c):
        source = self.landed[self.layer_of(j)].at[self.rows_at(j, self.core, c), :]
        start, size, _ = self.chunks[j][c]
        target = self.mate.at[pl.ds(start, size), :]
        return pltpu.make_async_copy(source, target, self.mate_sem.at[self.index(j, c)])

    def span(self, j, c, depth):
        start, size, order = self.chunks[j][c]
        for bit in order[: min(depth, self.halvings)]:
            size //= 2
            start = start + self.bit_at(bit) * size
        return start, size

    def in_acc(self, j, start, size):
        return pl.ds(pl.multiple_of(j * GROUP_ROWS + start, TILE), size)

    def got_at(self, j, c, depth):
        return (j % SLOTS * GROUP_ROWS + self.chunks[j][c][0]) >> min(depth + 1, HALVINGS)

    def down(self, j, c, depth):
        bit = self.chunks[j][c][2][depth]
        start, size = self.span(j, c, depth)
        if depth < self.halvings:
            size //= 2
            start = start + (1 - self.bit_at(bit)) * size
        k = self.index(j, c)
        return copy_far(
            self.acc.at[self.in_acc(j, start, size), :],
            self.got[depth].at[pl.ds(self.got_at(j, c, depth), size), :],
            self.send.at[k, depth],
            self.recv.at[k, depth],
            self.partner(bit),
        )

    def up(self, j, c, depth):
        bit = self.chunks[j][c][2][depth]
        start, size = self.span(j, c, depth + 1)
        here = self.acc.at[self.in_acc(j, start, size), :]
        k = self.index(j, c)
        return copy_far(here, here, self.back_send.at[k, depth], self.back_recv.at[k, depth], self.partner(bit))

    def left(self, j, c, depth):
        self.down(j, c, depth).wait_send()
        partner = self.partner(self.chunks[j][c][2][depth])
        pl.semaphore_signal(
            self.ready.at[self.index(j, c), depth], inc=1, device_id=partner, device_id_type=pl.DeviceIdType.MESH
        )

    def raise_up(self, j, c, depth):
        pl.semaphore_wait(self.ready.at[self.index(j, c), depth], 1)
        self.up(j, c, depth).start()

    def give(self, j, core):
        rows = pl.ds(self.base(j, core), GROUP_ROWS)
        source = self.acc.at[pl.ds(j * GROUP_ROWS, GROUP_ROWS), :]
        target = self.full[self.layer_of(j)].at[rows, :]
        return copy_far(source, target, self.give_send.at[j], self.give_recv.at[j], self.across)

    def put(self, j, core):
        rows = pl.ds(self.base(j, core), GROUP_ROWS)
        source = self.acc.at[pl.ds(j * GROUP_ROWS, GROUP_ROWS), :]
        return pltpu.make_async_copy(source, self.full[self.layer_of(j)].at[rows, :], self.put_sem.at[j])

    def each(self, j):
        return range(len(self.chunks[j]))

    def start_swaps(self, j):
        for c in self.each(j):
            self.swap(j, c).start()

    def prepare(self, j):
        for c in self.each(j):
            self.load(j, c).start()
        if self.layer_of(j) == 0:
            for tile in range(6):
                area = self.landed[0].at[pl.ds(0, LANES), pl.ds(0, STEP)]
                sem = self.tile_recv.at[(j - GROUPS // 2) * 12 + self.core * 6 + tile]
                copy_far(area, area, sem, sem, self.across).wait_recv()
        for c in self.each(j):
            if self.layer_of(j) == 1:
                self.swap(j, c).wait_recv()
            self.load_mate(j, c).start()

    def moment(self, now):
        bits, halvings = self.bits, self.halvings
        for j, start in enumerate(self.starts):
            if start == now:
                for c in self.each(j):
                    self.load(j, c).wait()
                    self.load_mate(j, c).wait()
                    first, size, _ = self.chunks[j][c]
                    at = j * GROUP_ROWS + first
                    add_rows(self.acc, at, self.acc, at, self.mate, first, size)
                    self.down(j, c, 0).start()
            if self.layer_of(j) == 1 and start == now + 2:
                self.start_swaps(j)
        for j, begun in enumerate(self.starts):
            stage = now - begun
            if not 0 < stage <= bits + halvings:
                continue
            for c in self.each(j):
                if stage <= bits:
                    depth = stage - 1
                    if depth < halvings:
                        self.down(j, c, depth).wait_recv()
                        self.left(j, c, depth)
                    else:
                        self.down(j, c, depth).wait()
                    first, size = self.span(j, c, stage)
                    at = j * GROUP_ROWS + first
                    add_rows(self.acc, at, self.acc, at, self.got[depth], self.got_at(j, c, depth), size)
                    if stage < bits:
                        self.down(j, c, stage).start()
                    else:
                        self.raise_up(j, c, halvings - 1)
                else:
                    depth = bits + halvings - stage
                    self.up(j, c, depth).wait_recv()
                    if depth > 0:
                        self.raise_up(j, c, depth - 1)
            if stage == bits + halvings:
                layer = self.layer_of(j)
                at_core(self.core, layer, lambda j=j, layer=layer: self.put(j, layer).start())
                at_core(self.core, 1 - layer, lambda j=j, layer=layer: self.give(j, 1 - layer).start())
        for j, start in enumerate(self.starts):
            if start == now + 1:
                self.prepare(j)

    def small_step(self, k):
        friend = self.across if k == 0 else self.partner(k - 1)
        return copy_far(
            self.small_out, self.small_got.at[k], self.small_send.at[k], self.small_recv.at[k], friend
        )

    def small_begin(self):
        for layer in range(2):

            def step(layer=layer):
                self.small_out[...] = self.small[layer]
                copy_far(
                    self.small.at[1 - layer], self.small_got.at[0], self.small_send.at[0], self.small_recv.at[0],
                    self.across,
                ).start()

            at_core(self.core, layer, step)

    def small_turn(self, k):
        self.small_step(k).wait()
        self.small_out[...] = self.small_out[...] + self.small_got[k]
        if k < self.bits:
            self.small_step(k + 1).start()

    def shown_keep(self, layer, k):
        return pltpu.make_async_copy(self.shown[2 * k + layer], self.shown_out[k].at[self.core], self.shown_sem.at[k])

    def shown_give(self, layer, k):
        return copy_far(
            self.shown[2 * k + 1 - layer], self.shown_out[k].at[self.core], self.shown_send.at[k],
            self.shown_recv.at[k], self.across,
        )

    def show(self):
        for layer in range(2):

            def step(layer=layer):
                for k in range(2):
                    self.shown_keep(layer, k).start()
                    self.shown_give(layer, k).start()

            at_core(self.core, layer, step)

    def close(self):
        for k in range(2):
            self.shown_keep(0, k).wait()
            self.shown_give(0, k).wait()
        for j in range(GROUPS):
            layer = self.layer_of(j)

            def kept(j=j, layer=layer):
                self.put(j, layer).wait()
                self.give(j, 1 - layer).wait_recv()

            at_core(self.core, layer, kept)
            at_core(self.core, 1 - layer, lambda j=j, layer=layer: self.give(j, 1 - layer).wait_send())
            for c in self.each(j):
                if layer == 1:
                    self.swap(j, c).wait_send()
                for depth in range(self.halvings):
                    self.up(j, c, depth).wait_send()


def cast_kernel(first, second, small, acts, slopes, qkv, out, up, down, *refs):
    gains, biases, router, means, acts_out, slopes_out, low, high, in_sem, out_sem, copy_sem = refs
    rows = low.shape[1]
    per = LANES // rows
    slots = low.shape[0]
    count = 12 * per
    core = lax.axis_index("section")
    passed = [
        pltpu.make_async_copy(source, target.at[0], copy_sem.at[k])
        for k, (source, target) in enumerate(((acts, acts_out), (slopes, slopes_out)))
    ]

    def take(k, source=first):
        return pltpu.make_async_copy(source.at[pl.ds(k * rows, rows), :], low.at[k % slots], in_sem.at[k % slots])

    def give(k):
        block, part = divmod(k, per)
        if block < 4:
            target = down.at[0, pl.ds(k * rows, rows), :]
        elif block < 8:
            target = up.at[0, pl.ds(part * rows, rows), pl.ds((block - 4) * LANES, LANES)]
        elif block < 9:
            target = out.at[0, pl.ds(part * rows, rows), :]
        else:
            target = qkv.at[0, pl.ds(part * rows, rows), pl.ds((block - 9) * LANES, LANES)]
        return pltpu.make_async_copy(high.at[k % slots], target, out_sem.at[k % slots])

    def fetch(k):
        at_core(core, 0, lambda: take(k).start())
        at_core(core, 1, lambda: take(k, second).start())

    for k in range(slots):
        fetch(k)
    for copy in passed:
        copy.start()
    held = gains.shape[1] // LANES
    for row in range(held):
        gains[:, row * LANES : (row + 1) * LANES] = small[row : row + 1, :]
    for row in range(biases.shape[1] // LANES):
        biases[:, row * LANES : (row + 1) * LANES] = small[held + row : held + row + 1, :]
    row = held + biases.shape[1] // LANES
    router[...] = small[row : row + 1, :]
    micro = means.shape[1]
    means[...] = small[row + 1 : row + 2, :micro] / small[row + 1 : row + 2, micro : 2 * micro]
    for k in range(count):
        take(k).wait()
        if k >= slots:
            give(k - slots).wait()
        high[k % slots] = low[k % slots].astype(F32)
        give(k).start()
        if k + slots < count:
            fetch(k + slots)
    for k in range(count - slots, count):
        give(k).wait()
    for copy in passed:
        copy.wait()


def cast_sums(sums, small, acts, slopes, shapes, micro):
    anywhere = pl.BlockSpec(memory_space=pl.ANY)
    inside = pl.BlockSpec(memory_space=pltpu.VMEM)
    outs = [(shape, F32) for shape in shapes] + [((1, LANES), F32), ((1, micro), F32)]
    outs += [((1, *value.shape), BF16) for value in (acts, slopes)]
    return pl.pallas_call(
        cast_kernel,
        out_shape=[jax.ShapeDtypeStruct(*one) for one in outs],
        in_specs=[anywhere] * 2 + [inside] + [anywhere] * 2,
        out_specs=[anywhere] * 4 + [inside] * 4 + [anywhere] * 2,
        scratch_shapes=[
            pltpu.VMEM((4, LANES, LANES), BF16),
            pltpu.VMEM((4, LANES, LANES), F32),
            pltpu.SemaphoreType.DMA((4,)),
            pltpu.SemaphoreType.DMA((4,)),
            pltpu.SemaphoreType.DMA((2,)),
        ],
        compiler_params=pltpu.CompilerParams(vmem_limit_bytes=60 * 1024 * 1024),
        cost_estimate=pl.CostEstimate(flops=0, bytes_accessed=50 * 10**6, transcendentals=0),
        name="cast",
    )(*sums, small, acts, slopes)


STEP = 256
NEGATIVE = -1e30


def dot(left, right, dims=NN):
    return lax.dot_general(left, right, dims, preferred_element_type=F32)


def gelu_parts(pre):
    bell = jnp.exp(pre * pre * -0.5)
    t = pl.reciprocal(1.0 + jnp.abs(pre) * (0.3275911 * 0.7071067811865476))
    poly = t * (0.1274147960 + t * (-0.142248368 + t * (0.710706871 + t * (-0.7265760135 + t * 0.5307027145))))
    tail = poly * bell
    return jnp.where(pre >= 0.0, 1.0 - tail, tail), bell


def norm_stats(values):
    centred = values - jnp.mean(values, axis=-1, keepdims=True)
    recip = lax.rsqrt(jnp.mean(centred * centred, axis=-1, keepdims=True) + 1e-06)
    return centred * recip, recip


def fold(tile):
    return jnp.sum(tile.reshape(tile.shape[0] // 8, 8, tile.shape[1]), axis=0)


def front_names(r, given):
    r.weights = [next(given) for _ in range(4)]
    r.w_sem, r.n1, r.qkv, r.probs, r.mask, r.mix, r.between, r.n2, r.act = (next(given) for _ in range(9))
    r.pre = [next(given) for _ in range(2)]
    r.act_part = [next(given) for _ in range(2)]


def back_names(r, given):
    r.n1t, r.n2t, r.mixt, r.dmlp, r.dpre, r.dn, r.datt, r.dmix, r.dqkv = (next(given) for _ in range(9))
    r.dpre_part = [next(given) for _ in range(2)]
    r.down_stage, r.up_stage, r.down_sem, r.up_sem = (next(given) for _ in range(4))


def use_weights(r, layer):
    core = lax.axis_index("section")

    def weight(which, source):
        return pltpu.make_async_copy(source[which].at[0], r.weights[which], r.w_sem.at[which])

    for near, source in ((core == layer, r.own), (core != layer, r.far)):

        @pl.when(near)
        def _():
            for which in range(4):
                weight(which, source).start()

    r.ready = lambda which: weight(which, r.own).wait()


def layer_kernel(groups, window, *refs):
    r = Names()
    given = iter(refs)
    r.x, r.col_code, r.row_code, r.vec = (next(given) for _ in range(4))
    r.own = [next(given) for _ in range(4)]
    r.far = [next(given) for _ in range(4)]
    r.unsort, r.dout = (next(given) for _ in range(2))
    r.shown_du, r.small, r.grads, r.du, r.shown_y = (next(given) for _ in range(5))
    front_names(r, given)
    back_names(r, given)
    r.y, r.scale = None, None
    r.y = next(given)
    use_weights(r, 1)
    layer_body(r, groups, window, True, False)


def start_kernel(groups, window, *refs):
    r = Names()
    given = iter(refs)
    lengths, route_mask, tokens, cotangent, router, own_vec = (next(given) for _ in range(6))
    own = [next(given) for _ in range(4)]
    far = [next(given) for _ in range(4)]
    vecs = [next(given) for _ in range(2)]
    r.all_y, r.shown_y, r.delta, cot, r.x = (next(given) for _ in range(5))
    col_codes = [next(given) for _ in range(2)]
    row_codes = [next(given) for _ in range(2)]
    r.unsort, pick, r.unpick, r.skipped, r.scale, factor, extra = (next(given) for _ in range(7))
    front_names(r, given)
    r.y, r.all_x, order, raw, far_vec, raw_sem = (next(given) for _ in range(6))
    far_send, far_recv, vec_sem = (next(given) for _ in range(3))
    core = lax.axis_index("section")
    across = (1 - core, lax.axis_index("dp"))
    rows, width = r.all_x.shape
    half = rows // 2

    def fetch(k, source):
        return pltpu.make_async_copy(source.at[core], raw.at[k], raw_sem.at[k])

    fetch(0, tokens).start()
    fetch(1, cotangent).start()
    barrier = pltpu.get_barrier_semaphore()
    pl.semaphore_signal(barrier, inc=1, device_id=across, device_id_type=pl.DeviceIdType.MESH)
    pl.semaphore_wait(barrier, 1)

    def lend(which):
        return copy_far(own[which], far[which], far_send.at[which], far_recv.at[which], across)

    lend_vec = copy_far(own_vec, far_vec, vec_sem.at[0], vec_sem.at[1], across)
    lend_vec.start()
    lend(0).start()

    def weight(which, source):
        return pltpu.make_async_copy(source[which].at[0], r.weights[which], r.w_sem.at[which])

    def take_own():
        for which in range(4):
            weight(which, own).start()

    at_core(core, 0, take_own)

    def ready(which):
        def arrive():
            lend(which).wait_recv()
            weight(which, far).start()

        at_core(core, 1, arrive)
        weight(which, own).wait()

    r.ready = ready

    starts, bases, total, longs, short = [], [], 0, 0, 0
    count = lengths.shape[2]
    sizes = [lengths[core, 0, c] for c in range(count)]
    for size in sizes:
        is_long = size == LONG
        starts.append(total)
        bases.append(jnp.where(is_long, longs * LONG, 2 * LONG + short))
        total = total + size
        longs = longs + jnp.where(is_long, 1, 0)
        short = short + jnp.where(is_long, 0, size)

    def place(shape, dim):
        return lax.broadcasted_iota(jnp.int32, shape, dim)

    def target(at):
        moved = at
        for start, size, base in zip(starts, sizes, bases):
            moved = moved + jnp.where((at >= start) & (at < start + size), base - start, 0)
        return moved

    def code_of(at):
        return sum(jnp.where(at >= base, 1, 0) for base in bases)

    row_at, col_at = place((1, rows), 1), place((rows, 1), 0)

    def one_hot(left, right):
        return jnp.where(left == right, 1.0, 0.0).astype(BF16)

    goes_row, goes_col = target(row_at), target(col_at)
    row_codes[1][...] = code_of(row_at)
    col_codes[1][...] = code_of(col_at)
    for start in range(0, rows, 128):
        here = slice(start, start + 128)
        order[here, :] = one_hot(col_at[here], goes_row)
        r.unsort[here, :] = one_hot(goes_col[here], row_at)
    lend(1).start()
    lend(2).start()
    lend(3).start()
    for k, (source, moved) in enumerate(((tokens, r.all_x), (cotangent, cot))):
        fetch(k, source).wait()
        for part in range(width // STEP):
            span = slice(part * STEP, (part + 1) * STEP)
            moved[:, span] = dot(order[...], raw[k, :, span]).astype(BF16)

    mask = jnp.where(route_mask[pl.ds(core, 1), :] == 1, 1.0, 0.0)
    masks = jnp.broadcast_to(mask, (8, rows)).astype(BF16)
    chosen_row = dot(masks, r.unsort[...])
    chosen_col = dot(order[...], masks, NT)
    earlier = jnp.where(place((rows, rows), 0) < place((rows, rows), 1), 1.0, 0.0).astype(BF16)
    rank_row = dot(chosen_row.astype(BF16), earlier)[:1]
    later = jnp.where(place((rows, rows), 0) > place((rows, rows), 1), 1.0, 0.0).astype(BF16)
    rank_col = dot(later, chosen_col.astype(BF16))[:, :1]
    chosen_row, chosen_col = chosen_row[:1], chosen_col[:, :1]
    r.skipped[...] = 1.0 - chosen_col
    key_row = jnp.where(chosen_row > 0.5, rank_row, -1.0)
    key_col = jnp.where(chosen_col > 0.5, rank_col, -1.0)
    pick[...] = one_hot(place((half, 1), 0).astype(F32), key_row)
    r.unpick[...] = one_hot(key_col, place((1, half), 1).astype(F32))
    names_row = jnp.broadcast_to(code_of(row_at).astype(F32), (8, rows)).astype(BF16)
    routed_row = dot(names_row, r.unpick[...])[:1]
    routed_col = dot(pick[...], names_row, NT)[:, :1]
    row_codes[0][...] = routed_row.astype(jnp.int32)
    col_codes[0][...] = routed_col.astype(jnp.int32)
    for part in range(width // STEP):
        span = slice(part * STEP, (part + 1) * STEP)
        r.x[:, span] = dot(pick[...], r.all_x[:, span]).astype(BF16)
    logit = jnp.sum(r.x[...].astype(F32) * router[...], axis=1, keepdims=True)
    gate = 1.0 / (1.0 + jnp.exp(-logit))
    held = jnp.where(routed_col > 0.5, 1.0, 0.0)
    r.scale[...] = held * gate
    factor[...] = held * gate * (1.0 - gate)
    gates, counts = jnp.sum(held * gate, axis=0, keepdims=True), jnp.sum(mask, axis=1, keepdims=True)
    lane = place((1, width), 1)
    micro = tokens.shape[0]
    extra[...] = jnp.where(lane == core, gates, jnp.where(lane == core + micro, counts, 0.0))

    lend_vec.wait()
    for layer in range(2):
        vecs[layer][...] = jnp.where(core == layer, own_vec[...], far_vec[...])
    r.vec, r.col_code, r.row_code, r.own = vecs[0], col_codes[0], row_codes[0], own
    layer_body(r, groups, window, False, True)
    for which in range(4):
        lend(which).wait_send()
        at_core(core, 0, lambda which=which: lend(which).wait_recv())


def fused_kernel(groups, window, chunks, *refs):
    r = Names()
    given = iter(refs)
    r.x, r.col_code, r.row_code, r.vec, r.scale = (next(given) for _ in range(5))
    r.own = [next(given) for _ in range(4)]
    r.far = [next(given) for _ in range(4)]
    r.unsort = next(given)
    r.all_dout, r.pick, r.unpick, r.skipped, r.delta, r.factor, r.router = (next(given) for _ in range(7))
    second, second_small, extra = (next(given) for _ in range(3))
    shown = [next(given) for _ in range(3)]
    full = [next(given) for _ in range(2)]
    landed = [next(given) for _ in range(2)]
    first, small_out = (next(given) for _ in range(2))
    shown_out = [next(given) for _ in range(2)]
    front_names(r, given)
    back_names(r, given)
    r.dout, r.du, r.shown_du, r.small, r.router_grad = (next(given) for _ in range(5))
    sums = Sums(chunks, GROUP_STARTS, given)
    sums.grads, sums.landed, sums.full, sums.small_out = (first, second), landed, full, small_out
    sums.shown, sums.shown_out = (shown[0], shown[1], r.shown_du, shown[2]), shown_out
    r.grads = first
    core = sums.core
    use_weights(r, 0)
    sums.open()
    sums.start_swaps(0)
    sums.start_swaps(1)
    sums.prepare(0)
    early = [0]

    def hook():
        sums.moment(early[0])
        early[0] += 1

    def tile_out(stage, row, column, shape, sem, tile):
        area = (pl.ds(row, shape[0]), pl.ds(column, shape[1]))
        owner = lax.rem(tile // 6, 2)

        @pl.when(core == owner)
        def _():
            pltpu.make_async_copy(stage, first.at[area], sem).start()

        @pl.when(core != owner)
        def _():
            copy_far(stage, landed[0].at[area], sem, sums.tile_recv.at[tile], sums.across).start()

    r.hook, r.tile_out = hook, tile_out
    layer_body(r, groups, window, True, True)

    for index, source in enumerate((r.small, second_small)):
        for row in range(source.shape[1] // LANES):
            sums.small[index, row : row + 1, :] = source[:, row * LANES : (row + 1) * LANES]
        row = source.shape[1] // LANES
        sums.small[index, row : row + 1, :] = r.router_grad[...]
        sums.small[index, row + 1 : row + 2, :] = extra[...]
        left = sums.small.shape[1] - row - 2
        sums.small[index, row + 2 :, :] = jnp.zeros((left, LANES), F32)
    sums.small_begin()
    sums.show()

    for turn, now in enumerate(range(early[0], max(sums.end, early[0] + sums.bits + 1))):
        if now < sums.end:
            sums.moment(now)
        if turn <= sums.bits:
            sums.small_turn(turn)
    sums.close()


def layer_body(r, groups, window, full, is_router):
    hook = r.hook if full and is_router else lambda: None
    rows, width = r.x.shape
    hidden = r.own[2].shape[2]
    pairs = width // 128
    row_tile = rows // 5

    def vec(start, count=width):
        return r.vec[:, start : start + count]

    g1, g2, b1, bq, bv, bo, b2 = (vec(k * width) for k in range(7))
    bu_at, bd_at = 7 * width, 7 * width + hidden

    def row_loop(step, init=0):
        def at(k, carry):
            return step(pl.ds(pl.multiple_of(k * row_tile, row_tile), row_tile), carry)

        return lax.fori_loop(0, rows // row_tile, at, init)

    def norm_step(source, gain, bias, target):
        def step(here, carry):
            normal, _ = norm_stats(source[here, :].astype(F32))
            target[here, :] = (normal * gain + bias).astype(BF16)
            return carry

        return step

    def tiles(step):
        for k in range(width // STEP):
            step(slice(k * STEP, (k + 1) * STEP))

    def show(source, target):
        def step(span):
            target[:, span] = dot(r.unsort[...], source[:, span]).astype(BF16)

        tiles(step)

    def spread(routed, others, target, shown):
        def step(span):
            value = dot(r.unpick[...], routed[:, span]) + others[:, span].astype(F32) * r.skipped[...]
            if target is not None:
                target[:, span] = value.astype(BF16)
            shown[:, span] = dot(r.unsort[...], value.astype(BF16)).astype(BF16)

        tiles(step)

    row_loop(norm_step(r.x, g1, b1, r.n1))
    if full and is_router:

        def route_step(span):
            r.dout[:, span] = dot(r.pick[...], r.all_dout[:, span]).astype(BF16)

        tiles(route_step)
    if full:

        def delta_step(here, carry):
            low = (r.dout[here, :].astype(F32) * r.scale[here, :]).astype(BF16) if is_router else r.dout[here, :]
            r.dmlp[here, :] = low
            return carry + fold(low.astype(F32))

        dbd = row_loop(delta_step, jnp.zeros((8, width), F32))
        r.small[:, bd_at:] = jnp.sum(dbd, axis=0, keepdims=True)

    for k, (start, low, high) in enumerate(groups):
        col = r.col_code[start : start + window, :]
        row = r.row_code[:, start : start + window]
        place = lax.broadcasted_iota(jnp.int32, (window, 1), 0) + start
        col = jnp.where((place >= low) & (place < high), col, -1)
        r.mask[k] = jnp.where(col == row, 0.0, NEGATIVE)

    r.ready(0)
    for k in range(3 * width // STEP):
        span = slice(k * STEP, (k + 1) * STEP)
        value = dot(r.n1[...], r.weights[0][:, span])
        if k < width // STEP:
            value = (value + bq[:, span]).astype(BF16).astype(F32) * 0.125
        elif k >= 2 * width // STEP:
            value = value + bv[:, k * STEP - 2 * width : (k + 1) * STEP - 2 * width]
        r.qkv[:, span] = value.astype(BF16)

    hook()
    lane = lax.broadcasted_iota(jnp.int32, (1, 128), 1)

    def halves(block):
        zero = jnp.zeros_like(block)
        return jnp.concatenate([jnp.where(lane < 64, block, zero), jnp.where(lane < 64, zero, block)], axis=0)

    high_half = lax.broadcasted_iota(jnp.int32, (128, 1), 0) >= 64

    def own_half(both):
        return jnp.where(high_half, both[:, window:], both[:, :window]).T

    r.mix[...] = jnp.zeros_like(r.mix)

    def lanes(pair, part):
        return pl.ds(pl.multiple_of(pair * 128 + part * width, 128), 128)

    spots = [slice(start, start + window) for start, _, _ in groups]
    count = len(groups)

    def qkv_at(pair, part):
        return [r.qkv[here, lanes(pair, part)] for here in spots]

    def attend(pair, carry):
        q, key, v = (qkv_at(pair, part) for part in range(3))
        scores = [dot(key[k], halves(q[k]), NT) for k in range(count)]
        probs = []
        for k, (start, low, high) in enumerate(groups):
            mask = r.mask[k]
            masked = scores[k] + jnp.concatenate([mask, mask], axis=1)
            place = lax.broadcasted_iota(jnp.int32, (1, window), 1) + start
            valid = (place >= low) & (place < high)
            valid = jnp.concatenate([valid, valid], axis=1)
            power = jnp.exp(masked - jnp.max(masked, axis=0, keepdims=True))
            total = jnp.sum(power, axis=0, keepdims=True)
            prob = (power * jnp.where(valid, 1.0 / total, 0.0)).astype(BF16)
            if full:
                r.probs[pair * count + k] = prob
            probs.append(prob)
        mixed = [dot(v[k].T, probs[k]) for k in range(count)]
        for k, here in enumerate(spots):
            r.mix[here, lanes(pair, 0)] = r.mix[here, lanes(pair, 0)] + own_half(mixed[k]).astype(BF16)
        return carry

    lax.fori_loop(0, pairs, attend, 0)

    r.ready(1)
    for k in range(width // STEP):
        span = slice(k * STEP, (k + 1) * STEP)
        value = dot(r.mix[...], r.weights[1][:, span]) + bo[:, span]
        r.between[:, span] = r.x[:, span].astype(F32) + value
    row_loop(norm_step(r.between, g2, b2, r.n2))
    if full:
        r.n1t[...] = r.n1[...].T
        r.n2t[...] = r.n2[...].T
        r.mixt[...] = r.mix[...].T
    hook()

    r.ready(2)
    if full:
        r.ready(3)

    def tile_out(stage, row, column, shape, sem, tile):
        target = r.grads.at[pl.ds(row, shape[0]), pl.ds(column, shape[1])]
        pltpu.make_async_copy(stage, target, sem).start()

    tile_out = r.tile_out if full and is_router else tile_out

    def down_out(k, slot):
        tile_out(
            r.down_stage.at[slot], pl.multiple_of(k * STEP, STEP), 0, (STEP, width), r.down_sem.at[slot], k
        )

    def side_out(block, k, slot):
        row = pl.multiple_of((block + k // 3) * width, width)
        column = pl.multiple_of(k % 3 * STEP, STEP)
        tile = k + {4: 12, 8: 24, 9: 27}[block]
        tile_out(r.up_stage.at[slot], row, column, (width, STEP), r.up_sem.at[slot], tile)

    def down_free(slot):
        target = r.grads.at[pl.ds(0, STEP), pl.ds(0, width)]
        pltpu.make_async_copy(r.down_stage.at[slot], target, r.down_sem.at[slot]).wait()

    def side_free(slot):
        target = r.grads.at[pl.ds(0, width), pl.ds(0, STEP)]
        pltpu.make_async_copy(r.up_stage.at[slot], target, r.up_sem.at[slot]).wait()

    steps = hidden // STEP

    def part_at(k):
        return pl.multiple_of(k * STEP, STEP)

    def ahead(k, side):
        at = part_at(k)
        r.pre[side][...] = dot(r.n2[...], r.weights[2][:, pl.ds(at, STEP)]) + r.vec[:, pl.ds(at + bu_at, STEP)]

    def middle(k, side):
        at = part_at(k)
        span = pl.ds(at, STEP)
        pre = r.pre[side][...]
        cdf, bell = gelu_parts(pre)
        act = (pre * cdf).astype(BF16)
        if not (full and is_router):
            r.act[:, span] = act
        if full:
            r.act_part[side][...] = act
            slope = cdf + pre * bell * 0.3989422804014327
            dact = dot(r.dmlp[...], r.weights[3][span, :], NT)
            dpre = (dact * slope).astype(BF16)
            r.dpre[:, span] = dpre
            r.dpre_part[side][...] = dpre
            r.small[:, pl.ds(at + bu_at, STEP)] = jnp.sum(dpre.astype(F32), axis=0, keepdims=True)

    def weigh(side):
        r.down_stage[side] = dot(r.act_part[side][...], r.dmlp[...], TN).astype(BF16)
        r.up_stage[side] = dot(r.n2t[...], r.dpre_part[side][...]).astype(BF16)

    def send_out(k, side):
        down_out(k, side)
        side_out(4, k, side)

    def two_steps(kk, first=False):
        even = kk * 2
        if full and not first:

            @pl.when(kk >= 2)
            def _():
                down_free(1)
                side_free(1)

            down_free(0)
            side_free(0)
        middle(even, 0)
        ahead(even + 1, 1)
        if full and not first:
            weigh(1)
        middle(even + 1, 1)
        ahead(jnp.minimum(even + 2, steps - 1), 0)
        if full:
            weigh(0)
            if not first:
                send_out(even - 1, 1)
            send_out(even, 0)

    def more_steps(kk, carry):
        two_steps(kk)
        return carry

    ahead(0, 0)
    two_steps(0, True)
    if full and is_router:
        lax.fori_loop(1, steps // 4, more_steps, 0)
        hook()
        lax.fori_loop(steps // 4, steps // 2, more_steps, 0)
    else:
        lax.fori_loop(1, steps // 2, more_steps, 0)
    if full:
        down_free(1)
        side_free(1)
        weigh(1)
        send_out(steps - 1, 1)
    if full and is_router:
        down_free(0)
        down_free(1)
        hook()
    if not full:
        r.ready(3)
    if not (full and is_router):
        for k in range(width // STEP):
            span = slice(k * STEP, (k + 1) * STEP)
            value = dot(r.act[...], r.weights[3][:, span]) + vec(bd_at)[:, span]
            source = r.x[:, span].astype(F32)
            value = r.between[:, span] - source + value
            if not full:
                r.delta[:, span] = value
            r.y[:, span] = (source + (r.scale[...] * value if is_router else value)).astype(BF16)
    if not full:
        spread(r.y, r.all_x, r.all_y, r.shown_y)
        return
    if not is_router:
        show(r.y, r.shown_y)

    for k in range(width // STEP):
        span = slice(k * STEP, (k + 1) * STEP)
        r.dn[:, span] = dot(r.dpre[...], r.weights[2][span, :], NT)

    def norm_back(source, gain, here):
        normal, recip = norm_stats(source[here, :].astype(F32))
        grad = r.dn[here, :]
        hat = grad * gain
        back = recip * (
            hat - jnp.mean(hat, axis=-1, keepdims=True) - normal * jnp.mean(hat * normal, axis=-1, keepdims=True)
        )
        return back, fold(grad * normal), fold(grad)

    def second_back(here, carry):
        back, dg, db = norm_back(r.between, g2, here)
        r.between[here, :] = back
        delta = r.dout[here, :].astype(F32)
        total = ((delta * r.scale[here, :] if is_router else delta) + back).astype(BF16)
        r.datt[here, :] = total
        return carry[0] + dg, carry[1] + db, carry[2] + fold(total.astype(F32))

    zero = jnp.zeros((8, width), F32)
    dg2, db2, dbo = row_loop(second_back, (zero, zero, zero))
    r.small[:, width : 2 * width] = jnp.sum(dg2, axis=0, keepdims=True)
    r.small[:, 6 * width : 7 * width] = jnp.sum(db2, axis=0, keepdims=True)
    r.small[:, 5 * width : 6 * width] = jnp.sum(dbo, axis=0, keepdims=True)

    for k in range(width // STEP):
        span = slice(k * STEP, (k + 1) * STEP)
        r.dmix[:, span] = dot(r.datt[...], r.weights[1][span, :], NT).astype(BF16)
        slot = k % 2
        side_free(slot)
        r.up_stage[slot] = dot(r.mixt[...], r.datt[:, span]).astype(BF16)
        side_out(8, k, slot)

    r.dqkv[...] = jnp.zeros_like(r.dqkv)

    def attend_back(pair, carry):
        q, key, v = (qkv_at(pair, part) for part in range(3))
        dm = [halves(r.dmix[here, lanes(pair, 0)]) for here in spots]
        dprobs = [dot(v[k], dm[k], NT) for k in range(count)]
        dv = [dot(r.probs[pair * count + k], dm[k]) for k in range(count)]
        ds = []
        for k in range(count):
            wide = r.probs[pair * count + k].astype(F32)
            product = wide * dprobs[k]
            ds.append((product - wide * jnp.sum(product, axis=0, keepdims=True)).astype(BF16))
        dk = [dot(ds[k], halves(q[k])) for k in range(count)]
        dq = [dot(key[k].T, ds[k]) for k in range(count)]
        for k, here in enumerate(spots):
            for part, value in enumerate((own_half(dq[k]) * 0.125, dk[k], dv[k])):
                spot = lanes(pair, part)
                r.dqkv[here, spot] = r.dqkv[here, spot] + value.astype(BF16)
        return carry

    lax.fori_loop(0, pairs, attend_back, 0)
    hook()

    for k in range(3 * width // STEP):
        span = slice(k * STEP, (k + 1) * STEP)
        block = r.dqkv[:, span]
        if not width <= k * STEP < 2 * width:
            at = 3 * width + k * STEP - (width if k * STEP >= width else 0)
            r.small[:, at : at + STEP] = jnp.sum(block.astype(F32), axis=0, keepdims=True)
        slot = (k + 1) % 2
        side_free(slot)
        r.up_stage[slot] = dot(r.n1t[...], block).astype(BF16)
        side_out(9, k, slot)
    side_free(0)
    side_free(1)
    hook()

    for k in range(width // STEP):
        span = slice(k * STEP, (k + 1) * STEP)
        r.dn[:, span] = dot(r.dqkv[...], r.weights[0][span, :], NT)

    def first_back(here, carry):
        back, dg, db = norm_back(r.x, g1, here)
        dout = r.dout[here, :].astype(F32)
        total = dout + r.between[here, :] + back
        sums = [carry[0] + dg, carry[1] + db]
        if is_router:
            slope = jnp.sum(dout * r.delta[here, :], axis=1, keepdims=True) * r.factor[here, :]
            total = total + slope * r.router[...]
            sums.append(carry[2] + fold(slope * r.x[here, :].astype(F32)))
        r.du[here, :] = total.astype(BF16)
        return tuple(sums)

    sums = row_loop(first_back, (zero,) * (3 if is_router else 2))
    r.small[:, :width] = jnp.sum(sums[0], axis=0, keepdims=True)
    r.small[:, 2 * width : 3 * width] = jnp.sum(sums[1], axis=0, keepdims=True)
    if is_router:
        r.router_grad[...] = jnp.sum(sums[2], axis=0, keepdims=True)
        spread(r.du, r.all_dout, None, r.shown_du)
    else:
        show(r.du, r.shown_du)
    if not is_router:
        down_free(0)
        down_free(1)


def front_scratch(rows, width, hidden, groups, window, full, keep_act):
    sizes = [(width, 3 * width), (width, width), (width, hidden), (hidden, width)]
    held = [pltpu.VMEM(size, BF16) for size in sizes]
    held += [pltpu.SemaphoreType.DMA((4,))]
    held += [pltpu.VMEM((rows, width), BF16), pltpu.VMEM((rows, 3 * width), BF16)]
    held += [pltpu.VMEM((HEADS // 2 * len(groups) if full else 1, window, 2 * window), BF16)]
    held += [pltpu.VMEM((len(groups), window, window), F32), pltpu.VMEM((rows, width), BF16)]
    held += [pltpu.VMEM((rows, width), F32), pltpu.VMEM((rows, width), BF16)]
    held += [pltpu.VMEM((rows, hidden) if keep_act else (TILE, LANES), BF16)]
    return held + [pltpu.VMEM((rows, STEP), F32)] * 2 + [pltpu.VMEM((rows, STEP), BF16)] * 2


def back_scratch(rows, width, hidden):
    held = [pltpu.VMEM((width, rows), BF16)] * 3 + [pltpu.VMEM((rows, width), BF16)]
    held += [pltpu.VMEM((rows, hidden), BF16), pltpu.VMEM((rows, width), F32)]
    held += [pltpu.VMEM((rows, width), BF16)] * 2 + [pltpu.VMEM((rows, 3 * width), BF16)]
    held += [pltpu.VMEM((rows, STEP), BF16)] * 2
    held += [pltpu.VMEM((2, STEP, width), BF16), pltpu.VMEM((2, width, STEP), BF16)]
    return held + [pltpu.SemaphoreType.DMA((2,))] * 2


def run_start(groups, window, lengths, route_mask, tokens, cotangent, router_row, own_vec, own):
    _, rows, width = tokens.shape
    half, hidden = rows // 2, own[2].shape[2]
    inside = pl.BlockSpec(memory_space=pltpu.VMEM)
    anywhere = pl.BlockSpec(memory_space=pl.ANY)
    outs = [(value.shape, BF16) for value in own] + [(own_vec.shape, F32)] * 2
    outs += [((rows, width), BF16)] * 2 + [((half, width), F32), ((rows, width), BF16), ((half, width), BF16)]
    outs += [((half, 1), jnp.int32), ((rows, 1), jnp.int32), ((1, half), jnp.int32), ((1, rows), jnp.int32)]
    outs += [((rows, rows), BF16), ((half, rows), BF16), ((rows, half), BF16), ((rows, 1), F32)]
    outs += [((half, 1), F32)] * 2 + [((1, width), F32)]
    scratch = front_scratch(half, width, hidden, groups, window, False, True)
    scratch += [pltpu.VMEM((half, width), BF16), pltpu.VMEM((rows, width), BF16), pltpu.VMEM((rows, rows), BF16)]
    scratch += [pltpu.VMEM((2, rows, width), BF16), pltpu.VMEM(own_vec.shape, F32), pltpu.SemaphoreType.DMA((2,))]
    scratch += [pltpu.SemaphoreType.DMA((4,))] * 2 + [pltpu.SemaphoreType.DMA((2,))]
    return pl.pallas_call(
        functools.partial(start_kernel, groups, window),
        out_shape=[jax.ShapeDtypeStruct(*one) for one in outs],
        in_specs=[pl.BlockSpec(memory_space=pltpu.SMEM), inside] + [anywhere] * 2 + [inside] * 2 + [anywhere] * 4,
        out_specs=[anywhere] * 4 + [inside] * (len(outs) - 4),
        scratch_shapes=scratch,
        compiler_params=pltpu.CompilerParams(
            collective_id=1, has_side_effects=True, vmem_limit_bytes=60 * 1024 * 1024
        ),
        cost_estimate=pl.CostEstimate(flops=5 * 10**9, bytes_accessed=6 * 10**7, transcendentals=0),
        name="start",
    )(lengths, route_mask, tokens, cotangent, router_row, own_vec, *own)


def run_layer(groups, window, x, col_code, row_code, vec, own, far, unsort, back):
    rows, width = x.shape
    hidden = own[2].shape[2]
    inside = pl.BlockSpec(memory_space=pltpu.VMEM)
    anywhere = pl.BlockSpec(memory_space=pl.ANY)
    args = [x, col_code, row_code, vec, *own, *far, unsort, back]
    outs = [((rows, width), BF16), ((1, vec.shape[1]), F32), ((GRAD_ROWS, LANES), BF16)]
    outs += [((rows, width), BF16)] * 2
    scratch = front_scratch(rows, width, hidden, groups, window, True, True)
    scratch += back_scratch(rows, width, hidden) + [pltpu.VMEM((rows, width), BF16)]
    flops = rows * width * (3 * width + width + 2 * hidden) * 6
    return pl.pallas_call(
        functools.partial(layer_kernel, groups, window),
        out_shape=[jax.ShapeDtypeStruct(*one) for one in outs],
        in_specs=[inside] * 4 + [anywhere] * 8 + [inside] * 2,
        out_specs=[inside] * 2 + [anywhere] + [inside] * 2,
        scratch_shapes=scratch,
        compiler_params=pltpu.CompilerParams(vmem_limit_bytes=62 * 1024 * 1024),
        cost_estimate=pl.CostEstimate(flops=flops, bytes_accessed=3 * 10**7, transcendentals=0),
        name="layer",
    )(*args)


def run_fused(axis_of, groups, window, x, col_code, row_code, vec, scale, own, far, rows_of, back, router, second, second_small, extra, shown):
    rows, width = x.shape
    hidden = own[2].shape[2]
    chunks = sum_plan(axis_of)
    inside = pl.BlockSpec(memory_space=pltpu.VMEM)
    anywhere = pl.BlockSpec(memory_space=pl.ANY)
    unsort, pick, unpick, skipped = rows_of
    delta, factor, router_row = router
    every = unsort.shape[0]
    args = [x, col_code, row_code, vec, scale, *own, *far, unsort]
    args += [back, pick, unpick, skipped, delta, factor, router_row]
    args += [second, second_small, extra, *shown]
    small_rows = -(-(vec.shape[1] // LANES + 2) // 8) * 8
    outs = [((GRAD_ROWS, LANES), BF16)] * 5
    outs += [((small_rows, LANES), F32)] + [((2, every, width), BF16)] * 2
    scratch = front_scratch(rows, width, hidden, groups, window, True, False)
    scratch += back_scratch(rows, width, hidden)
    scratch += [pltpu.VMEM((rows, width), BF16)] * 2 + [pltpu.VMEM((every, width), BF16)]
    scratch += [pltpu.VMEM((1, vec.shape[1]), F32), pltpu.VMEM((1, width), F32)]
    scratch += Sums.scratch(chunks, small_rows)
    *sums, _, _, _, small, acts, grads = pl.pallas_call(
        functools.partial(fused_kernel, groups, window, chunks),
        out_shape=[jax.ShapeDtypeStruct(*one) for one in outs],
        in_specs=[inside] * 5 + [anywhere] * 8 + [inside] * 8 + [anywhere] + [inside] * 2 + [anywhere] * 3,
        out_specs=[anywhere] * 5 + [inside] + [anywhere] * 2,
        scratch_shapes=scratch,
        compiler_params=pltpu.CompilerParams(
            collective_id=0, has_side_effects=True, vmem_limit_bytes=64 * 1024 * 1024
        ),
        cost_estimate=pl.CostEstimate(flops=10**10, bytes_accessed=6 * 10**8, transcendentals=0),
        name="fused",
    )(*args)
    return sums, small, (acts, grads)


def body(axis_of, tokens, lengths, route_mask, router_weight, gains, biases, w_qkv, w_out, w_up, w_down, cotangent):
    micro, rows, width = tokens.shape
    own = (w_qkv, w_out, w_up, w_down)
    own_vec = jnp.concatenate([gains, biases], axis=1)
    router_row = router_weight.astype(F32)[None, :]
    half = LONG // 2
    groups_one = ((0, 0, half), (96, half, 2 * half), (192, 2 * half, rows // 2))
    groups_two = ((0, 0, LONG), (192, LONG, 2 * LONG), (384, 2 * LONG, rows))
    made = run_start(groups_one, 128, lengths, route_mask, tokens, cotangent, router_row, own_vec, own)
    far, (vec_one, vec_two), (y1, shown_y1, delta_one, cot, routed) = made[:4], made[4:6], made[6:11]
    col_one, col_two, row_one, row_two, *others = made[11:]
    unsort, pick, unpick, skipped, scale, factor, extra = others
    shown_du2, small_two, grads_two, dout, shown_y2 = run_layer(
        groups_two, 256, y1, col_two, row_two, vec_two, own, far, unsort, cot
    )
    sums, small, (activations, input_grads) = run_fused(
        axis_of, groups_one, 128, routed, col_one, row_one, vec_one, scale, own, far,
        (unsort, pick, unpick, skipped), dout, (delta_one, factor, router_row), grads_two, small_two, extra,
        (shown_y1, shown_y2, shown_du2),
    )
    *grads, router_grad, means, activations, input_grads = cast_sums(
        sums, small, activations, input_grads,
        [value.shape for value in (*own, gains, biases)], micro,
    )
    return (activations, input_grads, *grads, router_grad[0], means[0])


def solution(mesh):
    in_specs = (
        P(None, "dp", None),
        P(None, "dp", None),
        P(None, "dp"),
        P(),
        P("section", None),
        P("section", None),
        P("section", None, None),
        P("section", None, None),
        P("section", None, None),
        P("section", None, None),
        P(None, "dp", None),
    )
    out_specs = (
        P("section", None, "dp", None),
        P("section", None, "dp", None),
        P("section", None, None),
        P("section", None, None),
        P("section", None, None),
        P("section", None, None),
        P("section", None),
        P("section", None),
        P(),
        P(),
    )
    step = functools.partial(body, axis_bits(mesh))
    return jax.shard_map(step, mesh=mesh, in_specs=in_specs, out_specs=out_specs, check_vma=False)
```

```python
import functools

import jax
import jax.numpy as jnp
from jax import lax
from jax.experimental import pallas as pl
from jax.experimental.pallas import tpu as pltpu
from jax.sharding import PartitionSpec as P

HEADS = 12
HEAD = 64
LONG = 197
F32 = jnp.float32
BF16 = jnp.bfloat16
NT = (((1,), (1,)), ((), ()))
TN = (((0,), (0,)), ((), ()))
NN = (((1,), (0,)), ((), ()))


LANES = 768
TILE = 16
GRAD_ROWS = 12 * LANES


def axis_bits(mesh):
    line = mesh.devices[0]
    bits = len(line).bit_length() - 1
    try:
        spots = [tuple(device.coords) for device in line]
    except AttributeError:
        return [0] * bits
    return [
        next((w for w in range(3) if spots[1 << b][w] != spots[0][w]), 0) for b in range(bits)
    ]


HALVINGS = 4
GROUPS = 6
SLOTS = 4


GROUP_PLAN = (
    ((768, 123), (512, 1023), (256, 1032)),
    ((768, 123), (512, 1023), (256, 1320)),
    ((768, 132), (768, 1023)),
    ((512, 1230), (512, 123), (512, 2013)),
    ((768, 1023), (768, 132)),
    ((512, 2103), (512, 213), (512, 1023)),
)
GROUP_STARTS = (0, 1, 3, 4, 5, 7)


def sum_plan(axis_of):
    lists = {}
    for bit, axis in enumerate(axis_of):
        lists.setdefault(axis, []).append(bit)
    lists = sorted(lists.values(), key=len)
    while len(lists) < 3:
        lists.append([])
    roles = [lists[0][:1], lists[1][:1], lists[2][:1], lists[2][1:2]]
    plan = []
    for group in GROUP_PLAN:
        chunks, start = [], 0
        for size, code in group:
            order = [bit for place in (1000, 100, 10, 1) for bit in roles[code // place % 10]]
            order += [bit for bit in range(len(axis_of)) if bit not in order]
            chunks.append((start, size, order))
            start += size
        plan.append(chunks)
    return plan


def add_rows(into, into_start, source, start, other, other_start, count):
    tile = next(t for t in (64, 32, 16) if count % t == 0)

    def step(k, carry):
        target, here, there = (
            pl.ds(pl.multiple_of(first + k * tile, TILE), tile) for first in (into_start, start, other_start)
        )
        into[target, :] = source[here, :] + other[there, :]
        return carry

    lax.fori_loop(0, count // tile, step, 0)


class Names:
    pass


def copy_far(source, target, one, two, friend):
    return pltpu.make_async_remote_copy(
        src_ref=source,
        dst_ref=target,
        send_sem=one,
        recv_sem=two,
        device_id=friend,
        device_id_type=pl.DeviceIdType.MESH,
    )


def at_core(core, index, step):
    pl.when(core == index)(step)


GRAD_TILES = 36
GROUP_ROWS = GRAD_ROWS // GROUPS


class Sums:
    def __init__(self, chunks, starts, given):
        self.chunks, self.starts = chunks, starts
        self.bits = bits = len(chunks[0][0][2])
        self.halvings = min(bits, HALVINGS)
        self.acc, self.mate = next(given), next(given)
        self.got = [next(given) for _ in range(bits)]
        self.small_got, self.small = next(given), next(given)
        self.load_sem, self.mate_sem, self.swap_send, self.swap_recv = (next(given) for _ in range(4))
        self.send, self.recv, self.back_send, self.back_recv = (next(given) for _ in range(4))
        self.small_send, self.small_recv = (next(given) for _ in range(2))
        self.shown_sem, self.shown_send, self.shown_recv = (next(given) for _ in range(3))
        self.tile_recv, self.give_send, self.give_recv, self.put_sem, self.ready = (next(given) for _ in range(5))
        self.core = lax.axis_index("section")
        self.me = lax.axis_index("dp")
        self.across = (1 - self.core, self.me)
        self.end = starts[-1] + bits + self.halvings + 1

    @staticmethod
    def scratch(chunks, small_rows):
        bits = len(chunks[0][0][2])
        count = sum(len(group) for group in chunks)
        rows = SLOTS * GROUP_ROWS
        held = [pltpu.VMEM((GRAD_ROWS, LANES), BF16), pltpu.VMEM((GROUP_ROWS, LANES), BF16)]
        held += [pltpu.VMEM((rows >> min(depth + 1, HALVINGS), LANES), BF16) for depth in range(bits)]
        held += [pltpu.VMEM((bits + 1, small_rows, LANES), F32), pltpu.VMEM((2, small_rows, LANES), F32)]
        held += [pltpu.SemaphoreType.DMA((count,))] * 4
        held += [pltpu.SemaphoreType.DMA((count, bits))] * 4
        held += [pltpu.SemaphoreType.DMA((bits + 1,))] * 2
        held += [pltpu.SemaphoreType.DMA((2,))] * 3
        held += [pltpu.SemaphoreType.DMA((GRAD_TILES,))]
        held += [pltpu.SemaphoreType.DMA((GROUPS,))] * 3
        return held + [pltpu.SemaphoreType.REGULAR((count, min(bits, HALVINGS)))]

    def bit_at(self, bit):
        return lax.rem(self.me // (1 << bit), 2)

    def partner(self, bit):
        return (self.core, self.me + (1 - 2 * self.bit_at(bit)) * (1 << bit))

    def open(self):
        friends = [self.across] + [self.partner(bit) for bit in range(self.bits)]
        barrier = pltpu.get_barrier_semaphore()
        for friend in friends:
            pl.semaphore_signal(barrier, inc=1, device_id=friend, device_id_type=pl.DeviceIdType.MESH)
        pl.semaphore_wait(barrier, len(friends))

    @staticmethod
    def layer_of(j):
        return 1 if j < GROUPS // 2 else 0

    def base(self, j, core):
        return (2 * (j % (GROUPS // 2)) + core) * GROUP_ROWS

    def rows_at(self, j, core, c):
        start, size, _ = self.chunks[j][c]
        return pl.ds(pl.multiple_of(self.base(j, core) + start, TILE), size)

    def index(self, j, c):
        return sum(len(group) for group in self.chunks[:j]) + c

    def swap(self, j, c):
        rows, k = self.rows_at(j, 1 - self.core, c), self.index(j, c)
        return copy_far(
            self.grads[1].at[rows, :], self.landed[1].at[rows, :], self.swap_send.at[k], self.swap_recv.at[k],
            self.across,
        )

    def load(self, j, c):
        start, size, _ = self.chunks[j][c]
        target = self.acc.at[pl.ds(j * GROUP_ROWS + start, size), :]
        source = self.grads[self.layer_of(j)].at[self.rows_at(j, self.core, c), :]
        return pltpu.make_async_copy(source, target, self.load_sem.at[self.index(j, c)])

    def load_mate(self, j, c):
        source = self.landed[self.layer_of(j)].at[self.rows_at(j, self.core, c), :]
        start, size, _ = self.chunks[j][c]
        target = self.mate.at[pl.ds(start, size), :]
        return pltpu.make_async_copy(source, target, self.mate_sem.at[self.index(j, c)])

    def span(self, j, c, depth):
        start, size, order = self.chunks[j][c]
        for bit in order[: min(depth, self.halvings)]:
            size //= 2
            start = start + self.bit_at(bit) * size
        return start, size

    def in_acc(self, j, start, size):
        return pl.ds(pl.multiple_of(j * GROUP_ROWS + start, TILE), size)

    def got_at(self, j, c, depth):
        return (j % SLOTS * GROUP_ROWS + self.chunks[j][c][0]) >> min(depth + 1, HALVINGS)

    def down(self, j, c, depth):
        bit = self.chunks[j][c][2][depth]
        start, size = self.span(j, c, depth)
        if depth < self.halvings:
            size //= 2
            start = start + (1 - self.bit_at(bit)) * size
        k = self.index(j, c)
        return copy_far(
            self.acc.at[self.in_acc(j, start, size), :],
            self.got[depth].at[pl.ds(self.got_at(j, c, depth), size), :],
            self.send.at[k, depth],
            self.recv.at[k, depth],
            self.partner(bit),
        )

    def up(self, j, c, depth):
        bit = self.chunks[j][c][2][depth]
        start, size = self.span(j, c, depth + 1)
        here = self.acc.at[self.in_acc(j, start, size), :]
        k = self.index(j, c)
        return copy_far(here, here, self.back_send.at[k, depth], self.back_recv.at[k, depth], self.partner(bit))

    def left(self, j, c, depth):
        self.down(j, c, depth).wait_send()
        partner = self.partner(self.chunks[j][c][2][depth])
        pl.semaphore_signal(
            self.ready.at[self.index(j, c), depth], inc=1, device_id=partner, device_id_type=pl.DeviceIdType.MESH
        )

    def raise_up(self, j, c, depth):
        pl.semaphore_wait(self.ready.at[self.index(j, c), depth], 1)
        self.up(j, c, depth).start()

    def give(self, j, core):
        rows = pl.ds(self.base(j, core), GROUP_ROWS)
        source = self.acc.at[pl.ds(j * GROUP_ROWS, GROUP_ROWS), :]
        target = self.full[self.layer_of(j)].at[rows, :]
        return copy_far(source, target, self.give_send.at[j], self.give_recv.at[j], self.across)

    def put(self, j, core):
        rows = pl.ds(self.base(j, core), GROUP_ROWS)
        source = self.acc.at[pl.ds(j * GROUP_ROWS, GROUP_ROWS), :]
        return pltpu.make_async_copy(source, self.full[self.layer_of(j)].at[rows, :], self.put_sem.at[j])

    def each(self, j):
        return range(len(self.chunks[j]))

    def start_swaps(self, j):
        for c in self.each(j):
            self.swap(j, c).start()

    def prepare(self, j):
        for c in self.each(j):
            self.load(j, c).start()
        if self.layer_of(j) == 0:
            for tile in range(6):
                area = self.landed[0].at[pl.ds(0, LANES), pl.ds(0, STEP)]
                sem = self.tile_recv.at[(j - GROUPS // 2) * 12 + self.core * 6 + tile]
                copy_far(area, area, sem, sem, self.across).wait_recv()
        for c in self.each(j):
            if self.layer_of(j) == 1:
                self.swap(j, c).wait_recv()
            self.load_mate(j, c).start()

    def moment(self, now):
        bits, halvings = self.bits, self.halvings
        for j, start in enumerate(self.starts):
            if start == now:
                for c in self.each(j):
                    self.load(j, c).wait()
                    self.load_mate(j, c).wait()
                    first, size, _ = self.chunks[j][c]
                    at = j * GROUP_ROWS + first
                    add_rows(self.acc, at, self.acc, at, self.mate, first, size)
                    self.down(j, c, 0).start()
            if self.layer_of(j) == 1 and start == now + 2:
                self.start_swaps(j)
        for j, begun in enumerate(self.starts):
            stage = now - begun
            if not 0 < stage <= bits + halvings:
                continue
            for c in self.each(j):
                if stage <= bits:
                    depth = stage - 1
                    if depth < halvings:
                        self.down(j, c, depth).wait_recv()
                        self.left(j, c, depth)
                    else:
                        self.down(j, c, depth).wait()
                    first, size = self.span(j, c, stage)
                    at = j * GROUP_ROWS + first
                    add_rows(self.acc, at, self.acc, at, self.got[depth], self.got_at(j, c, depth), size)
                    if stage < bits:
                        self.down(j, c, stage).start()
                    else:
                        self.raise_up(j, c, halvings - 1)
                else:
                    depth = bits + halvings - stage
                    self.up(j, c, depth).wait_recv()
                    if depth > 0:
                        self.raise_up(j, c, depth - 1)
            if stage == bits + halvings:
                layer = self.layer_of(j)
                at_core(self.core, layer, lambda j=j, layer=layer: self.put(j, layer).start())
                at_core(self.core, 1 - layer, lambda j=j, layer=layer: self.give(j, 1 - layer).start())
        for j, start in enumerate(self.starts):
            if start == now + 1:
                self.prepare(j)

    def small_step(self, k):
        friend = self.across if k == 0 else self.partner(k - 1)
        return copy_far(
            self.small_out, self.small_got.at[k], self.small_send.at[k], self.small_recv.at[k], friend
        )

    def small_begin(self):
        for layer in range(2):

            def step(layer=layer):
                self.small_out[...] = self.small[layer]
                copy_far(
                    self.small.at[1 - layer], self.small_got.at[0], self.small_send.at[0], self.small_recv.at[0],
                    self.across,
                ).start()

            at_core(self.core, layer, step)

    def small_turn(self, k):
        self.small_step(k).wait()
        self.small_out[...] = self.small_out[...] + self.small_got[k]
        if k < self.bits:
            self.small_step(k + 1).start()

    def shown_keep(self, layer, k):
        return pltpu.make_async_copy(self.shown[2 * k + layer], self.shown_out[k].at[self.core], self.shown_sem.at[k])

    def shown_give(self, layer, k):
        return copy_far(
            self.shown[2 * k + 1 - layer], self.shown_out[k].at[self.core], self.shown_send.at[k],
            self.shown_recv.at[k], self.across,
        )

    def show(self):
        for layer in range(2):

            def step(layer=layer):
                for k in range(2):
                    self.shown_keep(layer, k).start()
                    self.shown_give(layer, k).start()

            at_core(self.core, layer, step)

    def close(self):
        for k in range(2):
            self.shown_keep(0, k).wait()
            self.shown_give(0, k).wait()
        for j in range(GROUPS):
            layer = self.layer_of(j)

            def kept(j=j, layer=layer):
                self.put(j, layer).wait()
                self.give(j, 1 - layer).wait_recv()

            at_core(self.core, layer, kept)
            at_core(self.core, 1 - layer, lambda j=j, layer=layer: self.give(j, 1 - layer).wait_send())
            for c in self.each(j):
                if layer == 1:
                    self.swap(j, c).wait_send()
                for depth in range(self.halvings):
                    self.up(j, c, depth).wait_send()


def cast_kernel(first, second, small, acts, slopes, qkv, out, up, down, *refs):
    gains, biases, router, means, acts_out, slopes_out, low, high, bounce, in_sem, out_sem, copy_sem = refs
    rows = low.shape[1]
    per = LANES // rows
    slots = low.shape[0]
    count = 12 * per
    core = lax.axis_index("section")
    passed = [
        (
            pltpu.make_async_copy(source, bounce.at[k], copy_sem.at[k]),
            pltpu.make_async_copy(bounce.at[k], target.at[0], copy_sem.at[k]),
        )
        for k, (source, target) in enumerate(((acts, acts_out), (slopes, slopes_out)))
    ]

    def take(k, source=first):
        return pltpu.make_async_copy(source.at[pl.ds(k * rows, rows), :], low.at[k % slots], in_sem.at[k % slots])

    def give(k):
        block, part = divmod(k, per)
        if block < 4:
            target = down.at[0, pl.ds(k * rows, rows), :]
        elif block < 8:
            target = up.at[0, pl.ds(part * rows, rows), pl.ds((block - 4) * LANES, LANES)]
        elif block < 9:
            target = out.at[0, pl.ds(part * rows, rows), :]
        else:
            target = qkv.at[0, pl.ds(part * rows, rows), pl.ds((block - 9) * LANES, LANES)]
        return pltpu.make_async_copy(high.at[k % slots], target, out_sem.at[k % slots])

    def fetch(k):
        at_core(core, 0, lambda: take(k).start())
        at_core(core, 1, lambda: take(k, second).start())

    for k in range(slots):
        fetch(k)
    for copy, _ in passed:
        copy.start()
    held = gains.shape[1] // LANES
    for row in range(held):
        gains[:, row * LANES : (row + 1) * LANES] = small[row : row + 1, :]
    for row in range(biases.shape[1] // LANES):
        biases[:, row * LANES : (row + 1) * LANES] = small[held + row : held + row + 1, :]
    row = held + biases.shape[1] // LANES
    router[...] = small[row : row + 1, :]
    micro = means.shape[1]
    means[...] = small[row + 1 : row + 2, :micro] / small[row + 1 : row + 2, micro : 2 * micro]
    for k in range(count):
        take(k).wait()
        if k >= slots:
            give(k - slots).wait()
        high[k % slots] = low[k % slots].astype(F32)
        give(k).start()
        if k + slots < count:
            fetch(k + slots)
        if k < 2:
            passed[k][0].wait()
            passed[k][1].start()
    for k in range(count - slots, count):
        give(k).wait()
    for _, copy in passed:
        copy.wait()


def cast_sums(sums, small, acts, slopes, shapes, micro):
    anywhere = pl.BlockSpec(memory_space=pl.ANY)
    inside = pl.BlockSpec(memory_space=pltpu.VMEM)
    outs = [(shape, F32) for shape in shapes] + [((1, LANES), F32), ((1, micro), F32)]
    outs += [((1, *value.shape), BF16) for value in (acts, slopes)]
    return pl.pallas_call(
        cast_kernel,
        out_shape=[jax.ShapeDtypeStruct(*one) for one in outs],
        in_specs=[anywhere] * 2 + [inside] + [anywhere] * 2,
        out_specs=[anywhere] * 4 + [inside] * 4 + [anywhere] * 2,
        scratch_shapes=[
            pltpu.VMEM((4, LANES, LANES), BF16),
            pltpu.VMEM((4, LANES, LANES), F32),
            pltpu.VMEM((2, *acts.shape), BF16),
            pltpu.SemaphoreType.DMA((4,)),
            pltpu.SemaphoreType.DMA((4,)),
            pltpu.SemaphoreType.DMA((2,)),
        ],
        compiler_params=pltpu.CompilerParams(vmem_limit_bytes=60 * 1024 * 1024),
        cost_estimate=pl.CostEstimate(flops=0, bytes_accessed=50 * 10**6, transcendentals=0),
        name="cast",
    )(*sums, small, acts, slopes)


STEP = 256
NEGATIVE = -1e30


def dot(left, right, dims=NN):
    return lax.dot_general(left, right, dims, preferred_element_type=F32)


def gelu_parts(pre):
    bell = jnp.exp(pre * pre * -0.5)
    t = pl.reciprocal(1.0 + jnp.abs(pre) * (0.3275911 * 0.7071067811865476))
    poly = t * (0.1274147960 + t * (-0.142248368 + t * (0.710706871 + t * (-0.7265760135 + t * 0.5307027145))))
    tail = poly * bell
    return jnp.where(pre >= 0.0, 1.0 - tail, tail), bell


def norm_stats(values):
    centred = values - jnp.mean(values, axis=-1, keepdims=True)
    recip = lax.rsqrt(jnp.mean(centred * centred, axis=-1, keepdims=True) + 1e-06)
    return centred * recip, recip


def fold(tile):
    return jnp.sum(tile.reshape(tile.shape[0] // 8, 8, tile.shape[1]), axis=0)


def front_names(r, given):
    r.weights = [next(given) for _ in range(4)]
    r.w_sem, r.n1, r.qkv, r.probs, r.mask, r.mix, r.between, r.n2, r.act = (next(given) for _ in range(9))
    r.pre = [next(given) for _ in range(2)]
    r.act_part = [next(given) for _ in range(2)]


def back_names(r, given):
    r.n1t, r.n2t, r.mixt, r.dmlp, r.dpre, r.dn, r.dqkv = (next(given) for _ in range(7))
    r.datt, r.dmix = r.n1, r.mix
    r.dpre_part = [next(given) for _ in range(2)]
    r.down_stage, r.up_stage, r.down_sem, r.up_sem = (next(given) for _ in range(4))


def use_weights(r, layer):
    core = lax.axis_index("section")

    def weight(which, source):
        return pltpu.make_async_copy(source[which].at[0], r.weights[which], r.w_sem.at[which])

    for near, source in ((core == layer, r.own), (core != layer, r.far)):

        @pl.when(near)
        def _():
            for which in range(4):
                weight(which, source).start()

    r.ready = lambda which: weight(which, r.own).wait()


def layer_kernel(groups, window, *refs):
    r = Names()
    given = iter(refs)
    r.x, r.col_code, r.row_code, r.vec = (next(given) for _ in range(4))
    r.own = [next(given) for _ in range(4)]
    r.far = [next(given) for _ in range(4)]
    r.unsort, r.dout = (next(given) for _ in range(2))
    r.shown_du, r.small, r.grads, r.du, r.shown_y = (next(given) for _ in range(5))
    front_names(r, given)
    back_names(r, given)
    r.y, r.scale = None, None
    r.y = next(given)
    use_weights(r, 1)
    layer_body(r, groups, window, True, False)


def start_kernel(groups, window, *refs):
    r = Names()
    given = iter(refs)
    lengths, route_mask, tokens, cotangent, router, own_vec = (next(given) for _ in range(6))
    own = [next(given) for _ in range(4)]
    far = [next(given) for _ in range(4)]
    vecs = [next(given) for _ in range(2)]
    r.all_y, r.shown_y, r.delta, cot, r.x = (next(given) for _ in range(5))
    col_codes = [next(given) for _ in range(2)]
    row_codes = [next(given) for _ in range(2)]
    r.unsort, pick, r.unpick, r.skipped, r.scale, factor, extra = (next(given) for _ in range(7))
    front_names(r, given)
    r.y, r.all_x, order, raw, far_vec, raw_sem = (next(given) for _ in range(6))
    far_send, far_recv, vec_sem = (next(given) for _ in range(3))
    core = lax.axis_index("section")
    across = (1 - core, lax.axis_index("dp"))
    rows, width = r.all_x.shape
    half = rows // 2

    def fetch(k, source):
        return pltpu.make_async_copy(source.at[core], raw.at[k], raw_sem.at[k])

    fetch(0, tokens).start()
    fetch(1, cotangent).start()
    barrier = pltpu.get_barrier_semaphore()
    pl.semaphore_signal(barrier, inc=1, device_id=across, device_id_type=pl.DeviceIdType.MESH)
    pl.semaphore_wait(barrier, 1)

    def lend(which):
        return copy_far(own[which], far[which], far_send.at[which], far_recv.at[which], across)

    lend_vec = copy_far(own_vec, far_vec, vec_sem.at[0], vec_sem.at[1], across)
    lend_vec.start()
    lend(0).start()

    def weight(which, source):
        return pltpu.make_async_copy(source[which].at[0], r.weights[which], r.w_sem.at[which])

    def take_own():
        for which in range(4):
            weight(which, own).start()

    at_core(core, 0, take_own)

    def ready(which):
        def arrive():
            lend(which).wait_recv()
            weight(which, far).start()

        at_core(core, 1, arrive)
        weight(which, own).wait()

    r.ready = ready

    starts, bases, total, longs, short = [], [], 0, 0, 0
    count = lengths.shape[2]
    sizes = [lengths[core, 0, c] for c in range(count)]
    for size in sizes:
        is_long = size == LONG
        starts.append(total)
        bases.append(jnp.where(is_long, longs * LONG, 2 * LONG + short))
        total = total + size
        longs = longs + jnp.where(is_long, 1, 0)
        short = short + jnp.where(is_long, 0, size)

    def place(shape, dim):
        return lax.broadcasted_iota(jnp.int32, shape, dim)

    def target(at):
        moved = at
        for start, size, base in zip(starts, sizes, bases):
            moved = moved + jnp.where((at >= start) & (at < start + size), base - start, 0)
        return moved

    def code_of(at):
        return sum(jnp.where(at >= base, 1, 0) for base in bases)

    row_at, col_at = place((1, rows), 1), place((rows, 1), 0)

    def one_hot(left, right):
        return jnp.where(left == right, 1.0, 0.0).astype(BF16)

    goes_row, goes_col = target(row_at), target(col_at)
    row_codes[1][...] = code_of(row_at)
    col_codes[1][...] = code_of(col_at)
    for start in range(0, rows, 128):
        here = slice(start, start + 128)
        order[here, :] = one_hot(col_at[here], goes_row)
        r.unsort[here, :] = one_hot(goes_col[here], row_at)
    lend(1).start()
    lend(2).start()
    lend(3).start()
    for k, (source, moved) in enumerate(((tokens, r.all_x), (cotangent, cot))):
        fetch(k, source).wait()
        moved[...] = dot(order[...], raw[k]).astype(BF16)

    mask = jnp.where(route_mask[pl.ds(core, 1), :] == 1, 1.0, 0.0)
    masks = jnp.broadcast_to(mask, (8, rows)).astype(BF16)
    chosen_row = dot(masks, r.unsort[...])
    chosen_col = dot(order[...], masks, NT)
    earlier = jnp.where(place((rows, rows), 0) < place((rows, rows), 1), 1.0, 0.0).astype(BF16)
    rank_row = dot(chosen_row.astype(BF16), earlier)[:1]
    later = jnp.where(place((rows, rows), 0) > place((rows, rows), 1), 1.0, 0.0).astype(BF16)
    rank_col = dot(later, chosen_col.astype(BF16))[:, :1]
    chosen_row, chosen_col = chosen_row[:1], chosen_col[:, :1]
    r.skipped[...] = 1.0 - chosen_col
    key_row = jnp.where(chosen_row > 0.5, rank_row, -1.0)
    key_col = jnp.where(chosen_col > 0.5, rank_col, -1.0)
    pick[...] = one_hot(place((half, 1), 0).astype(F32), key_row)
    r.unpick[...] = one_hot(key_col, place((1, half), 1).astype(F32))
    names_row = jnp.broadcast_to(code_of(row_at).astype(F32), (8, rows)).astype(BF16)
    routed_row = dot(names_row, r.unpick[...])[:1]
    routed_col = dot(pick[...], names_row, NT)[:, :1]
    row_codes[0][...] = routed_row.astype(jnp.int32)
    col_codes[0][...] = routed_col.astype(jnp.int32)
    r.x[...] = dot(pick[...], r.all_x[...]).astype(BF16)
    logit = jnp.sum(r.x[...].astype(F32) * router[...], axis=1, keepdims=True)
    gate = 1.0 / (1.0 + jnp.exp(-logit))
    held = jnp.where(routed_col > 0.5, 1.0, 0.0)
    r.scale[...] = held * gate
    factor[...] = held * gate * (1.0 - gate)
    gates, counts = jnp.sum(held * gate, axis=0, keepdims=True), jnp.sum(mask, axis=1, keepdims=True)
    lane = place((1, width), 1)
    micro = tokens.shape[0]
    extra[...] = jnp.where(lane == core, gates, jnp.where(lane == core + micro, counts, 0.0))

    lend_vec.wait()
    for layer in range(2):
        vecs[layer][...] = jnp.where(core == layer, own_vec[...], far_vec[...])
    r.vec, r.col_code, r.row_code, r.own = vecs[0], col_codes[0], row_codes[0], own
    layer_body(r, groups, window, False, True)
    for which in range(4):
        lend(which).wait_send()
        at_core(core, 0, lambda which=which: lend(which).wait_recv())


def fused_kernel(groups, window, chunks, *refs):
    r = Names()
    given = iter(refs)
    r.x, r.col_code, r.row_code, r.vec, r.scale = (next(given) for _ in range(5))
    r.own = [next(given) for _ in range(4)]
    r.far = [next(given) for _ in range(4)]
    r.unsort = next(given)
    r.all_dout, r.pick, r.unpick, r.skipped, r.delta, r.factor, r.router = (next(given) for _ in range(7))
    second, second_small, extra = (next(given) for _ in range(3))
    shown = [next(given) for _ in range(3)]
    full = [next(given) for _ in range(2)]
    landed = [next(given) for _ in range(2)]
    first, small_out = (next(given) for _ in range(2))
    shown_out = [next(given) for _ in range(2)]
    front_names(r, given)
    back_names(r, given)
    r.dout, r.du, r.shown_du, r.small, r.router_grad = (next(given) for _ in range(5))
    sums = Sums(chunks, GROUP_STARTS, given)
    sums.grads, sums.landed, sums.full, sums.small_out = (first, second), landed, full, small_out
    sums.shown, sums.shown_out = (shown[0], shown[1], r.shown_du, shown[2]), shown_out
    r.grads = first
    core = sums.core
    use_weights(r, 0)
    sums.open()
    sums.start_swaps(0)
    sums.start_swaps(1)
    sums.prepare(0)
    early = [0]

    def hook():
        sums.moment(early[0])
        early[0] += 1

    def tile_out(stage, row, column, shape, sem, tile):
        area = (pl.ds(row, shape[0]), pl.ds(column, shape[1]))
        owner = lax.rem(tile // 6, 2)

        @pl.when(core == owner)
        def _():
            pltpu.make_async_copy(stage, first.at[area], sem).start()

        @pl.when(core != owner)
        def _():
            copy_far(stage, landed[0].at[area], sem, sums.tile_recv.at[tile], sums.across).start()

    r.hook, r.tile_out = hook, tile_out
    layer_body(r, groups, window, True, True)

    for index, source in enumerate((r.small, second_small)):
        for row in range(source.shape[1] // LANES):
            sums.small[index, row : row + 1, :] = source[:, row * LANES : (row + 1) * LANES]
        row = source.shape[1] // LANES
        sums.small[index, row : row + 1, :] = r.router_grad[...]
        sums.small[index, row + 1 : row + 2, :] = extra[...]
        left = sums.small.shape[1] - row - 2
        sums.small[index, row + 2 :, :] = jnp.zeros((left, LANES), F32)
    sums.small_begin()
    sums.show()

    for turn, now in enumerate(range(early[0], max(sums.end, early[0] + sums.bits + 1))):
        if now < sums.end:
            sums.moment(now)
        if turn <= sums.bits:
            sums.small_turn(turn)
    sums.close()


def layer_body(r, groups, window, full, is_router):
    hook = r.hook if full and is_router else lambda: None
    rows, width = r.x.shape
    hidden = r.own[2].shape[2]
    pairs = width // 128
    row_tile = rows // 5

    def vec(start, count=width):
        return r.vec[:, start : start + count]

    g1, g2, b1, bq, bv, bo, b2 = (vec(k * width) for k in range(7))
    bu_at, bd_at = 7 * width, 7 * width + hidden

    def row_loop(step, init=0):
        def at(k, carry):
            return step(pl.ds(pl.multiple_of(k * row_tile, row_tile), row_tile), carry)

        return lax.fori_loop(0, rows // row_tile, at, init)

    def norm_step(source, gain, bias, target):
        def step(here, carry):
            normal, _ = norm_stats(source[here, :].astype(F32))
            target[here, :] = (normal * gain + bias).astype(BF16)
            return carry

        return step

    def tiles(step):
        step(slice(0, width))

    def show(source, target):
        def step(span):
            target[:, span] = dot(r.unsort[...], source[:, span]).astype(BF16)

        tiles(step)

    def spread(routed, others, target, shown):
        def step(span):
            value = dot(r.unpick[...], routed[:, span]) + others[:, span].astype(F32) * r.skipped[...]
            if target is not None:
                target[:, span] = value.astype(BF16)
            shown[:, span] = dot(r.unsort[...], value.astype(BF16)).astype(BF16)

        tiles(step)

    row_loop(norm_step(r.x, g1, b1, r.n1))
    if full and is_router:

        def route_step(span):
            r.dout[:, span] = dot(r.pick[...], r.all_dout[:, span]).astype(BF16)

        tiles(route_step)
    if full:

        def delta_step(here, carry):
            low = (r.dout[here, :].astype(F32) * r.scale[here, :]).astype(BF16) if is_router else r.dout[here, :]
            r.dmlp[here, :] = low
            return carry + fold(low.astype(F32))

        dbd = row_loop(delta_step, jnp.zeros((8, width), F32))
        r.small[:, bd_at:] = jnp.sum(dbd, axis=0, keepdims=True)

    for k, (start, low, high) in enumerate(groups):
        col = r.col_code[start : start + window, :]
        row = r.row_code[:, start : start + window]
        place = lax.broadcasted_iota(jnp.int32, (window, 1), 0) + start
        col = jnp.where((place >= low) & (place < high), col, -1)
        r.mask[k] = jnp.where(col == row, 0.0, NEGATIVE)

    r.ready(0)
    for part in range(3):
        span = slice(part * width, (part + 1) * width)
        value = dot(r.n1[...], r.weights[0][:, span])
        if part == 0:
            value = (value + bq).astype(BF16).astype(F32) * 0.125
        elif part == 2:
            value = value + bv
        r.qkv[:, span] = value.astype(BF16)

    hook()
    lane = lax.broadcasted_iota(jnp.int32, (1, 128), 1)

    def halves(block):
        zero = jnp.zeros_like(block)
        return jnp.concatenate([jnp.where(lane < 64, block, zero), jnp.where(lane < 64, zero, block)], axis=0)

    high_half = lax.broadcasted_iota(jnp.int32, (128, 1), 0) >= 64

    def own_half(both):
        return jnp.where(high_half, both[:, window:], both[:, :window]).T

    r.mix[...] = jnp.zeros_like(r.mix)

    def lanes(pair, part):
        return pl.ds(pl.multiple_of(pair * 128 + part * width, 128), 128)

    spots = [slice(start, start + window) for start, _, _ in groups]
    count = len(groups)

    def qkv_at(pair, part):
        return [r.qkv[here, lanes(pair, part)] for here in spots]

    def attend(pair, carry):
        q, key, v = (qkv_at(pair, part) for part in range(3))
        scores = [dot(key[k], halves(q[k]), NT) for k in range(count)]
        probs = []
        for k, (start, low, high) in enumerate(groups):
            mask = r.mask[k]
            masked = scores[k] + jnp.concatenate([mask, mask], axis=1)
            place = lax.broadcasted_iota(jnp.int32, (1, window), 1) + start
            valid = (place >= low) & (place < high)
            valid = jnp.concatenate([valid, valid], axis=1)
            power = jnp.exp(masked - jnp.max(masked, axis=0, keepdims=True))
            total = jnp.sum(power, axis=0, keepdims=True)
            prob = (power * jnp.where(valid, 1.0 / total, 0.0)).astype(BF16)
            if full:
                r.probs[pair * count + k] = prob
            probs.append(prob)
        mixed = [dot(v[k].T, probs[k]) for k in range(count)]
        for k, here in enumerate(spots):
            r.mix[here, lanes(pair, 0)] = r.mix[here, lanes(pair, 0)] + own_half(mixed[k]).astype(BF16)
        return carry

    lax.fori_loop(0, pairs, attend, 0)

    r.ready(1)
    r.between[...] = r.x[...].astype(F32) + (dot(r.mix[...], r.weights[1][...]) + bo)
    row_loop(norm_step(r.between, g2, b2, r.n2))
    if full:
        r.n1t[...] = r.n1[...].T
        r.n2t[...] = r.n2[...].T
        r.mixt[...] = r.mix[...].T
    hook()

    r.ready(2)
    if full:
        r.ready(3)

    def tile_out(stage, row, column, shape, sem, tile):
        target = r.grads.at[pl.ds(row, shape[0]), pl.ds(column, shape[1])]
        pltpu.make_async_copy(stage, target, sem).start()

    tile_out = r.tile_out if full and is_router else tile_out

    def down_out(k, slot):
        tile_out(
            r.down_stage.at[slot], pl.multiple_of(k * STEP, STEP), 0, (STEP, width), r.down_sem.at[slot], k
        )

    def side_out(block, k, slot):
        row = pl.multiple_of((block + k // 3) * width, width)
        column = pl.multiple_of(k % 3 * STEP, STEP)
        tile = k + {4: 12, 8: 24, 9: 27}[block]
        tile_out(r.up_stage.at[slot], row, column, (width, STEP), r.up_sem.at[slot], tile)

    def down_free(slot):
        target = r.grads.at[pl.ds(0, STEP), pl.ds(0, width)]
        pltpu.make_async_copy(r.down_stage.at[slot], target, r.down_sem.at[slot]).wait()

    def side_free(slot):
        target = r.grads.at[pl.ds(0, width), pl.ds(0, STEP)]
        pltpu.make_async_copy(r.up_stage.at[slot], target, r.up_sem.at[slot]).wait()

    steps = hidden // STEP

    def part_at(k):
        return pl.multiple_of(k * STEP, STEP)

    def ahead(k, side):
        at = part_at(k)
        r.pre[side][...] = dot(r.n2[...], r.weights[2][:, pl.ds(at, STEP)]) + r.vec[:, pl.ds(at + bu_at, STEP)]

    def middle(k, side):
        at = part_at(k)
        span = pl.ds(at, STEP)
        pre = r.pre[side][...]
        cdf, bell = gelu_parts(pre)
        act = (pre * cdf).astype(BF16)
        if not (full and is_router):
            r.act[:, span] = act
        if full:
            r.act_part[side][...] = act
            slope = cdf + pre * bell * 0.3989422804014327
            dact = dot(r.dmlp[...], r.weights[3][span, :], NT)
            dpre = (dact * slope).astype(BF16)
            r.dpre[:, span] = dpre
            r.dpre_part[side][...] = dpre
            r.small[:, pl.ds(at + bu_at, STEP)] = jnp.sum(dpre.astype(F32), axis=0, keepdims=True)

    def weigh(side):
        r.down_stage[side] = dot(r.act_part[side][...], r.dmlp[...], TN).astype(BF16)
        r.up_stage[side] = dot(r.n2t[...], r.dpre_part[side][...]).astype(BF16)

    def send_out(k, side):
        down_out(k, side)
        side_out(4, k, side)

    def two_steps(kk, first=False):
        even = kk * 2
        if full and not first:

            @pl.when(kk >= 2)
            def _():
                down_free(1)
                side_free(1)

            down_free(0)
            side_free(0)
        middle(even, 0)
        ahead(even + 1, 1)
        if full and not first:
            weigh(1)
        middle(even + 1, 1)
        ahead(jnp.minimum(even + 2, steps - 1), 0)
        if full:
            weigh(0)
            if not first:
                send_out(even - 1, 1)
            send_out(even, 0)

    def more_steps(kk, carry):
        two_steps(kk)
        return carry

    ahead(0, 0)
    two_steps(0, True)
    if full and is_router:
        lax.fori_loop(1, steps // 4, more_steps, 0)
        hook()
        lax.fori_loop(steps // 4, steps // 2, more_steps, 0)
    else:
        lax.fori_loop(1, steps // 2, more_steps, 0)
    if full:
        down_free(1)
        side_free(1)
        weigh(1)
        send_out(steps - 1, 1)
    if full and is_router:
        down_free(0)
        down_free(1)
        hook()
    if not full:
        r.ready(3)
    if not (full and is_router):
        value = dot(r.act[...], r.weights[3][...]) + vec(bd_at)
        source = r.x[...].astype(F32)
        value = r.between[...] - source + value
        if not full:
            r.delta[...] = value
        r.y[...] = (source + (r.scale[...] * value if is_router else value)).astype(BF16)
    if not full:
        spread(r.y, r.all_x, r.all_y, r.shown_y)
        return
    if not is_router:
        show(r.y, r.shown_y)

    r.dn[...] = dot(r.dpre[...], r.weights[2][...], NT)

    def norm_back(source, gain, here):
        normal, recip = norm_stats(source[here, :].astype(F32))
        grad = r.dn[here, :]
        hat = grad * gain
        back = recip * (
            hat - jnp.mean(hat, axis=-1, keepdims=True) - normal * jnp.mean(hat * normal, axis=-1, keepdims=True)
        )
        return back, fold(grad * normal), fold(grad)

    def second_back(here, carry):
        back, dg, db = norm_back(r.between, g2, here)
        r.between[here, :] = back
        delta = r.dout[here, :].astype(F32)
        total = ((delta * r.scale[here, :] if is_router else delta) + back).astype(BF16)
        r.datt[here, :] = total
        return carry[0] + dg, carry[1] + db, carry[2] + fold(total.astype(F32))

    zero = jnp.zeros((8, width), F32)
    dg2, db2, dbo = row_loop(second_back, (zero, zero, zero))
    r.small[:, width : 2 * width] = jnp.sum(dg2, axis=0, keepdims=True)
    r.small[:, 6 * width : 7 * width] = jnp.sum(db2, axis=0, keepdims=True)
    r.small[:, 5 * width : 6 * width] = jnp.sum(dbo, axis=0, keepdims=True)

    r.dmix[...] = dot(r.datt[...], r.weights[1][...], NT).astype(BF16)
    for k in range(width // STEP):
        span = slice(k * STEP, (k + 1) * STEP)
        slot = k % 2
        side_free(slot)
        r.up_stage[slot] = dot(r.mixt[...], r.datt[:, span]).astype(BF16)
        side_out(8, k, slot)

    r.dqkv[...] = jnp.zeros_like(r.dqkv)

    def attend_back(pair, carry):
        q, key, v = (qkv_at(pair, part) for part in range(3))
        dm = [halves(r.dmix[here, lanes(pair, 0)]) for here in spots]
        dprobs = [dot(v[k], dm[k], NT) for k in range(count)]
        dv = [dot(r.probs[pair * count + k], dm[k]) for k in range(count)]
        ds = []
        for k in range(count):
            wide = r.probs[pair * count + k].astype(F32)
            product = wide * dprobs[k]
            ds.append((product - wide * jnp.sum(product, axis=0, keepdims=True)).astype(BF16))
        dk = [dot(ds[k], halves(q[k])) for k in range(count)]
        dq = [dot(key[k].T, ds[k]) for k in range(count)]
        for k, here in enumerate(spots):
            for part, value in enumerate((own_half(dq[k]) * 0.125, dk[k], dv[k])):
                spot = lanes(pair, part)
                r.dqkv[here, spot] = r.dqkv[here, spot] + value.astype(BF16)
        return carry

    lax.fori_loop(0, pairs, attend_back, 0)
    hook()

    for k in range(3 * width // STEP):
        span = slice(k * STEP, (k + 1) * STEP)
        block = r.dqkv[:, span]
        if not width <= k * STEP < 2 * width:
            at = 3 * width + k * STEP - (width if k * STEP >= width else 0)
            r.small[:, at : at + STEP] = jnp.sum(block.astype(F32), axis=0, keepdims=True)
        slot = (k + 1) % 2
        side_free(slot)
        r.up_stage[slot] = dot(r.n1t[...], block).astype(BF16)
        side_out(9, k, slot)
    side_free(0)
    side_free(1)
    hook()

    r.dn[...] = dot(r.dqkv[...], r.weights[0][...], NT)

    def first_back(here, carry):
        back, dg, db = norm_back(r.x, g1, here)
        dout = r.dout[here, :].astype(F32)
        total = dout + r.between[here, :] + back
        sums = [carry[0] + dg, carry[1] + db]
        if is_router:
            slope = jnp.sum(dout * r.delta[here, :], axis=1, keepdims=True) * r.factor[here, :]
            total = total + slope * r.router[...]
            sums.append(carry[2] + fold(slope * r.x[here, :].astype(F32)))
        r.du[here, :] = total.astype(BF16)
        return tuple(sums)

    sums = row_loop(first_back, (zero,) * (3 if is_router else 2))
    r.small[:, :width] = jnp.sum(sums[0], axis=0, keepdims=True)
    r.small[:, 2 * width : 3 * width] = jnp.sum(sums[1], axis=0, keepdims=True)
    if is_router:
        r.router_grad[...] = jnp.sum(sums[2], axis=0, keepdims=True)
        spread(r.du, r.all_dout, None, r.shown_du)
    else:
        show(r.du, r.shown_du)
    if not is_router:
        down_free(0)
        down_free(1)


def front_scratch(rows, width, hidden, groups, window, full, keep_act):
    sizes = [(width, 3 * width), (width, width), (width, hidden), (hidden, width)]
    held = [pltpu.VMEM(size, BF16) for size in sizes]
    held += [pltpu.SemaphoreType.DMA((4,))]
    held += [pltpu.VMEM((rows, width), BF16), pltpu.VMEM((rows, 3 * width), BF16)]
    held += [pltpu.VMEM((HEADS // 2 * len(groups) if full else 1, window, 2 * window), BF16)]
    held += [pltpu.VMEM((len(groups), window, window), F32), pltpu.VMEM((rows, width), BF16)]
    held += [pltpu.VMEM((rows, width), F32), pltpu.VMEM((rows, width), BF16)]
    held += [pltpu.VMEM((rows, hidden) if keep_act else (TILE, LANES), BF16)]
    return held + [pltpu.VMEM((rows, STEP), F32)] * 2 + [pltpu.VMEM((rows, STEP), BF16)] * 2


def back_scratch(rows, width, hidden):
    held = [pltpu.VMEM((width, rows), BF16)] * 3 + [pltpu.VMEM((rows, width), BF16)]
    held += [pltpu.VMEM((rows, hidden), BF16), pltpu.VMEM((rows, width), F32)]
    held += [pltpu.VMEM((rows, 3 * width), BF16)] + [pltpu.VMEM((rows, STEP), BF16)] * 2
    held += [pltpu.VMEM((2, STEP, width), BF16), pltpu.VMEM((2, width, STEP), BF16)]
    return held + [pltpu.SemaphoreType.DMA((2,))] * 2


def run_start(groups, window, lengths, route_mask, tokens, cotangent, router_row, own_vec, own):
    _, rows, width = tokens.shape
    half, hidden = rows // 2, own[2].shape[2]
    inside = pl.BlockSpec(memory_space=pltpu.VMEM)
    anywhere = pl.BlockSpec(memory_space=pl.ANY)
    outs = [(value.shape, BF16) for value in own] + [(own_vec.shape, F32)] * 2
    outs += [((rows, width), BF16)] * 2 + [((half, width), F32), ((rows, width), BF16), ((half, width), BF16)]
    outs += [((half, 1), jnp.int32), ((rows, 1), jnp.int32), ((1, half), jnp.int32), ((1, rows), jnp.int32)]
    outs += [((rows, rows), BF16), ((half, rows), BF16), ((rows, half), BF16), ((rows, 1), F32)]
    outs += [((half, 1), F32)] * 2 + [((1, width), F32)]
    scratch = front_scratch(half, width, hidden, groups, window, False, True)
    scratch += [pltpu.VMEM((half, width), BF16), pltpu.VMEM((rows, width), BF16), pltpu.VMEM((rows, rows), BF16)]
    scratch += [pltpu.VMEM((2, rows, width), BF16), pltpu.VMEM(own_vec.shape, F32), pltpu.SemaphoreType.DMA((2,))]
    scratch += [pltpu.SemaphoreType.DMA((4,))] * 2 + [pltpu.SemaphoreType.DMA((2,))]
    return pl.pallas_call(
        functools.partial(start_kernel, groups, window),
        out_shape=[jax.ShapeDtypeStruct(*one) for one in outs],
        in_specs=[pl.BlockSpec(memory_space=pltpu.SMEM), inside] + [anywhere] * 2 + [inside] * 2 + [anywhere] * 4,
        out_specs=[anywhere] * 4 + [inside] * (len(outs) - 4),
        scratch_shapes=scratch,
        compiler_params=pltpu.CompilerParams(
            collective_id=1, has_side_effects=True, vmem_limit_bytes=60 * 1024 * 1024
        ),
        cost_estimate=pl.CostEstimate(flops=5 * 10**9, bytes_accessed=6 * 10**7, transcendentals=0),
        name="start",
    )(lengths, route_mask, tokens, cotangent, router_row, own_vec, *own)


def run_layer(groups, window, x, col_code, row_code, vec, own, far, unsort, back):
    rows, width = x.shape
    hidden = own[2].shape[2]
    inside = pl.BlockSpec(memory_space=pltpu.VMEM)
    anywhere = pl.BlockSpec(memory_space=pl.ANY)
    args = [x, col_code, row_code, vec, *own, *far, unsort, back]
    outs = [((rows, width), BF16), ((1, vec.shape[1]), F32), ((GRAD_ROWS, LANES), BF16)]
    outs += [((rows, width), BF16)] * 2
    scratch = front_scratch(rows, width, hidden, groups, window, True, True)
    scratch += back_scratch(rows, width, hidden) + [pltpu.VMEM((rows, width), BF16)]
    flops = rows * width * (3 * width + width + 2 * hidden) * 6
    return pl.pallas_call(
        functools.partial(layer_kernel, groups, window),
        out_shape=[jax.ShapeDtypeStruct(*one) for one in outs],
        in_specs=[inside] * 4 + [anywhere] * 8 + [inside] * 2,
        out_specs=[inside] * 2 + [anywhere] + [inside] * 2,
        scratch_shapes=scratch,
        compiler_params=pltpu.CompilerParams(vmem_limit_bytes=62 * 1024 * 1024),
        cost_estimate=pl.CostEstimate(flops=flops, bytes_accessed=3 * 10**7, transcendentals=0),
        name="layer",
    )(*args)


def run_fused(axis_of, groups, window, x, col_code, row_code, vec, scale, own, far, rows_of, back, router, second, second_small, extra, shown):
    rows, width = x.shape
    hidden = own[2].shape[2]
    chunks = sum_plan(axis_of)
    inside = pl.BlockSpec(memory_space=pltpu.VMEM)
    anywhere = pl.BlockSpec(memory_space=pl.ANY)
    unsort, pick, unpick, skipped = rows_of
    delta, factor, router_row = router
    every = unsort.shape[0]
    args = [x, col_code, row_code, vec, scale, *own, *far, unsort]
    args += [back, pick, unpick, skipped, delta, factor, router_row]
    args += [second, second_small, extra, *shown]
    small_rows = -(-(vec.shape[1] // LANES + 2) // 8) * 8
    outs = [((GRAD_ROWS, LANES), BF16)] * 5
    outs += [((small_rows, LANES), F32)] + [((2, every, width), BF16)] * 2
    scratch = front_scratch(rows, width, hidden, groups, window, True, False)
    scratch += back_scratch(rows, width, hidden)
    scratch += [pltpu.VMEM((rows, width), BF16)] * 2 + [pltpu.VMEM((every, width), BF16)]
    scratch += [pltpu.VMEM((1, vec.shape[1]), F32), pltpu.VMEM((1, width), F32)]
    scratch += Sums.scratch(chunks, small_rows)
    *sums, _, _, _, small, acts, grads = pl.pallas_call(
        functools.partial(fused_kernel, groups, window, chunks),
        out_shape=[jax.ShapeDtypeStruct(*one) for one in outs],
        in_specs=[inside] * 5 + [anywhere] * 8 + [inside] * 8 + [anywhere] + [inside] * 2 + [anywhere] * 3,
        out_specs=[anywhere] * 5 + [inside] + [anywhere] * 2,
        scratch_shapes=scratch,
        compiler_params=pltpu.CompilerParams(
            collective_id=0, has_side_effects=True, vmem_limit_bytes=64 * 1024 * 1024
        ),
        cost_estimate=pl.CostEstimate(flops=10**10, bytes_accessed=6 * 10**8, transcendentals=0),
        name="fused",
    )(*args)
    return sums, small, (acts, grads)


def body(axis_of, tokens, lengths, route_mask, router_weight, gains, biases, w_qkv, w_out, w_up, w_down, cotangent):
    micro, rows, width = tokens.shape
    own = (w_qkv, w_out, w_up, w_down)
    own_vec = jnp.concatenate([gains, biases], axis=1)
    router_row = router_weight.astype(F32)[None, :]
    half = LONG // 2
    groups_one = ((0, 0, half), (96, half, 2 * half), (192, 2 * half, rows // 2))
    groups_two = ((0, 0, LONG), (192, LONG, 2 * LONG), (384, 2 * LONG, rows))
    made = run_start(groups_one, 128, lengths, route_mask, tokens, cotangent, router_row, own_vec, own)
    far, (vec_one, vec_two), (y1, shown_y1, delta_one, cot, routed) = made[:4], made[4:6], made[6:11]
    col_one, col_two, row_one, row_two, *others = made[11:]
    unsort, pick, unpick, skipped, scale, factor, extra = others
    shown_du2, small_two, grads_two, dout, shown_y2 = run_layer(
        groups_two, 256, y1, col_two, row_two, vec_two, own, far, unsort, cot
    )
    sums, small, (activations, input_grads) = run_fused(
        axis_of, groups_one, 128, routed, col_one, row_one, vec_one, scale, own, far,
        (unsort, pick, unpick, skipped), dout, (delta_one, factor, router_row), grads_two, small_two, extra,
        (shown_y1, shown_y2, shown_du2),
    )
    *grads, router_grad, means, activations, input_grads = cast_sums(
        sums, small, activations, input_grads,
        [value.shape for value in (*own, gains, biases)], micro,
    )
    return (activations, input_grads, *grads, router_grad[0], means[0])


def solution(mesh):
    in_specs = (
        P(None, "dp", None),
        P(None, "dp", None),
        P(None, "dp"),
        P(),
        P("section", None),
        P("section", None),
        P("section", None, None),
        P("section", None, None),
        P("section", None, None),
        P("section", None, None),
        P(None, "dp", None),
    )
    out_specs = (
        P("section", None, "dp", None),
        P("section", None, "dp", None),
        P("section", None, None),
        P("section", None, None),
        P("section", None, None),
        P("section", None, None),
        P("section", None),
        P("section", None),
        P(),
        P(),
    )
    step = functools.partial(body, axis_bits(mesh))
    return jax.shard_map(step, mesh=mesh, in_specs=in_specs, out_specs=out_specs, check_vma=False)
```

```python
import functools

import jax
import jax.numpy as jnp
from jax import lax
from jax.experimental import pallas as pl
from jax.experimental.pallas import tpu as pltpu
from jax.sharding import PartitionSpec as P

HEADS = 12
HEAD = 64
LONG = 197
F32 = jnp.float32
BF16 = jnp.bfloat16
NT = (((1,), (1,)), ((), ()))
TN = (((0,), (0,)), ((), ()))
NN = (((1,), (0,)), ((), ()))


LANES = 768
TILE = 16
GRAD_ROWS = 12 * LANES


def axis_bits(mesh):
    line = mesh.devices[0]
    bits = len(line).bit_length() - 1
    try:
        spots = [tuple(device.coords) for device in line]
    except AttributeError:
        return [0] * bits
    return [
        next((w for w in range(3) if spots[1 << b][w] != spots[0][w]), 0) for b in range(bits)
    ]


HALVINGS = 4
GROUPS = 6
SLOTS = 4


GROUP_PLAN = (
    ((768, 1023), (768, 132)),
    ((768, 123), (512, 1023), (256, 1203)),
    ((768, 123), (768, 1032)),
    ((512, 2103), (512, 123), (512, 1032)),
    ((768, 1023), (512, 2103), (256, 132)),
    ((512, 2013), (512, 132), (512, 1203)),
)
REDUCED = ((0, 3), (2, 1))
GROUP_STARTS = (0, 1, 2, 4, 5, 7)


def sum_plan(axis_of):
    lists = {}
    for bit, axis in enumerate(axis_of):
        lists.setdefault(axis, []).append(bit)
    lists = sorted(lists.values(), key=len)
    while len(lists) < 3:
        lists.append([])
    roles = [lists[0][:1], lists[1][:1], lists[2][:1], lists[2][1:2]]
    plan = []
    for group in GROUP_PLAN:
        chunks, start = [], 0
        for size, code in group:
            order = [bit for place in (1000, 100, 10, 1) for bit in roles[code // place % 10]]
            order += [bit for bit in range(len(axis_of)) if bit not in order]
            chunks.append((start, size, order))
            start += size
        plan.append(chunks)
    return plan


def add_rows(into, into_start, source, start, other, other_start, count):
    tile = next(t for t in (64, 32, 16) if count % t == 0)

    def step(k, carry):
        target, here, there = (
            pl.ds(pl.multiple_of(first + k * tile, TILE), tile) for first in (into_start, start, other_start)
        )
        into[target, :] = source[here, :] + other[there, :]
        return carry

    lax.fori_loop(0, count // tile, step, 0)


class Names:
    pass


def copy_far(source, target, one, two, friend):
    return pltpu.make_async_remote_copy(
        src_ref=source,
        dst_ref=target,
        send_sem=one,
        recv_sem=two,
        device_id=friend,
        device_id_type=pl.DeviceIdType.MESH,
    )


def at_core(core, index, step):
    pl.when(core == index)(step)


GRAD_TILES = 36
GROUP_ROWS = GRAD_ROWS // GROUPS


class Sums:
    def __init__(self, chunks, jobs, tiles, given, whole):
        self.chunks, self.jobs, self.tiles = chunks, jobs, tiles
        self.bits = bits = len(chunks[0][0][2])
        self.halvings = min(bits, HALVINGS)
        self.acc, self.mate = next(given), next(given)
        self.got = [next(given) for _ in range(bits)]
        self.load_sem, self.mate_sem = (next(given) for _ in range(2))
        self.send, self.recv, self.back_send, self.back_recv = (next(given) for _ in range(4))
        self.tile_recv, self.ready = (next(given) for _ in range(2))
        if whole:
            self.small_got, self.small = next(given), next(given)
            self.small_send, self.small_recv = (next(given) for _ in range(2))
            self.shown_sem, self.shown_send, self.shown_recv = (next(given) for _ in range(3))
            self.give_send, self.give_recv, self.put_sem = (next(given) for _ in range(3))
        self.core = lax.axis_index("section")
        self.me = lax.axis_index("dp")
        self.across = (1 - self.core, self.me)
        self.end = max(start + last - first + 1 for start, first, last in jobs.values())
        self.now = 0

    @staticmethod
    def scratch(chunks, held_groups, small_rows):
        bits = len(chunks[0][0][2])
        count = sum(len(group) for group in chunks)
        rows = min(held_groups, SLOTS) * GROUP_ROWS
        held = [pltpu.VMEM((held_groups * GROUP_ROWS, LANES), BF16), pltpu.VMEM((GROUP_ROWS, LANES), BF16)]
        held += [pltpu.VMEM((rows >> min(depth + 1, HALVINGS), LANES), BF16) for depth in range(bits)]
        held += [pltpu.SemaphoreType.DMA((count,))] * 2
        held += [pltpu.SemaphoreType.DMA((count, bits))] * 4
        held += [pltpu.SemaphoreType.DMA((GRAD_TILES,))]
        held += [pltpu.SemaphoreType.REGULAR((count, min(bits, HALVINGS)))]
        if small_rows:
            held += [pltpu.VMEM((bits + 1, small_rows, LANES), F32), pltpu.VMEM((2, small_rows, LANES), F32)]
            held += [pltpu.SemaphoreType.DMA((bits + 1,))] * 2
            held += [pltpu.SemaphoreType.DMA((2,))] * 3
            held += [pltpu.SemaphoreType.DMA((GROUPS,))] * 3
        return held

    def bit_at(self, bit):
        return lax.rem(self.me // (1 << bit), 2)

    def partner(self, bit):
        return (self.core, self.me + (1 - 2 * self.bit_at(bit)) * (1 << bit))

    def open(self):
        friends = [self.across] + [self.partner(bit) for bit in range(self.bits)]
        barrier = pltpu.get_barrier_semaphore()
        for friend in friends:
            pl.semaphore_signal(barrier, inc=1, device_id=friend, device_id_type=pl.DeviceIdType.MESH)
        pl.semaphore_wait(barrier, len(friends))

    @staticmethod
    def layer_of(j):
        return 1 if j < GROUPS // 2 else 0

    def base(self, j, core):
        return (2 * (j % (GROUPS // 2)) + core) * GROUP_ROWS

    def rows_at(self, j, core, c):
        start, size, _ = self.chunks[j][c]
        return pl.ds(pl.multiple_of(self.base(j, core) + start, TILE), size)

    def index(self, j, c):
        return sum(len(group) for group in self.chunks[:j]) + c

    def load(self, j, c):
        start, size, _ = self.chunks[j][c]
        target = self.acc.at[pl.ds(j * GROUP_ROWS + start, size), :]
        source = self.grads[self.layer_of(j)].at[self.rows_at(j, self.core, c), :]
        return pltpu.make_async_copy(source, target, self.load_sem.at[self.index(j, c)])

    def load_mate(self, j, c):
        source = self.landed[self.layer_of(j)].at[self.rows_at(j, self.core, c), :]
        start, size, _ = self.chunks[j][c]
        target = self.mate.at[pl.ds(start, size), :]
        return pltpu.make_async_copy(source, target, self.mate_sem.at[self.index(j, c)])

    def span(self, j, c, depth):
        start, size, order = self.chunks[j][c]
        for bit in order[: min(depth, self.halvings)]:
            size //= 2
            start = start + self.bit_at(bit) * size
        return start, size

    def in_acc(self, j, start, size):
        return pl.ds(pl.multiple_of(j * GROUP_ROWS + start, TILE), size)

    def got_at(self, j, c, depth):
        return (j % SLOTS * GROUP_ROWS + self.chunks[j][c][0]) >> min(depth + 1, HALVINGS)

    def down(self, j, c, depth):
        bit = self.chunks[j][c][2][depth]
        start, size = self.span(j, c, depth)
        if depth < self.halvings:
            size //= 2
            start = start + (1 - self.bit_at(bit)) * size
        k = self.index(j, c)
        return copy_far(
            self.acc.at[self.in_acc(j, start, size), :],
            self.got[depth].at[pl.ds(self.got_at(j, c, depth), size), :],
            self.send.at[k, depth],
            self.recv.at[k, depth],
            self.partner(bit),
        )

    def up(self, j, c, depth):
        bit = self.chunks[j][c][2][depth]
        start, size = self.span(j, c, depth + 1)
        here = self.acc.at[self.in_acc(j, start, size), :]
        k = self.index(j, c)
        return copy_far(here, here, self.back_send.at[k, depth], self.back_recv.at[k, depth], self.partner(bit))

    def left(self, j, c, depth):
        self.down(j, c, depth).wait_send()
        if self.jobs[j][2] > self.bits:
            partner = self.partner(self.chunks[j][c][2][depth])
            pl.semaphore_signal(
                self.ready.at[self.index(j, c), depth], inc=1, device_id=partner, device_id_type=pl.DeviceIdType.MESH
            )

    def raise_up(self, j, c, depth):
        if depth >= self.jobs[j][1]:
            pl.semaphore_wait(self.ready.at[self.index(j, c), depth], 1)
        self.up(j, c, depth).start()

    def carried(self, j, c, keep):
        start, size = self.span(j, c, REDUCED[j][1])
        here = self.in_acc(j, start, size)
        pair = (self.acc.at[here, :], self.carry.at[here, :])
        return pltpu.make_async_copy(*(pair if keep else pair[::-1]), self.load_sem.at[self.index(j, c)])

    def wait_tiles(self, layer, first):
        for tile in range(6):
            area = self.landed[layer].at[pl.ds(0, LANES), pl.ds(0, STEP)]
            sem = self.tile_recv.at[first + self.core * 6 + tile]
            copy_far(area, area, sem, sem, self.across).wait_recv()

    def tile_out(self, layer, stage, row, column, shape, sem, tile):
        area = (pl.ds(row, shape[0]), pl.ds(column, shape[1]))
        owner = lax.rem(tile // 6, 2)

        @pl.when(self.core == owner)
        def _():
            pltpu.make_async_copy(stage, self.grads[layer].at[area], sem).start()

        @pl.when(self.core != owner)
        def _():
            copy_far(stage, self.landed[layer].at[area], sem, self.tile_recv.at[tile], self.across).start()

    def give(self, j, core):
        rows = pl.ds(self.base(j, core), GROUP_ROWS)
        source = self.acc.at[pl.ds(j * GROUP_ROWS, GROUP_ROWS), :]
        target = self.full[self.layer_of(j)].at[rows, :]
        return copy_far(source, target, self.give_send.at[j], self.give_recv.at[j], self.across)

    def put(self, j, core):
        rows = pl.ds(self.base(j, core), GROUP_ROWS)
        source = self.acc.at[pl.ds(j * GROUP_ROWS, GROUP_ROWS), :]
        return pltpu.make_async_copy(source, self.full[self.layer_of(j)].at[rows, :], self.put_sem.at[j])

    def each(self, j):
        return range(len(self.chunks[j]))

    def prepare(self, j):
        for c in self.each(j):
            self.load(j, c).start()
        if j in self.tiles:
            self.wait_tiles(self.layer_of(j), self.tiles[j])
        for c in self.each(j):
            self.load_mate(j, c).start()

    def moment(self):
        now, self.now = self.now, self.now + 1
        bits, halvings = self.bits, self.halvings
        order = sorted(self.jobs, key=lambda j: self.jobs[j][:2] != (now, 0))
        for j in order:
            start, first_stage, last_stage = self.jobs[j]
            stage = now - start + first_stage
            if not first_stage <= stage <= last_stage:
                continue
            for c in self.each(j):
                if stage == 0:
                    self.load(j, c).wait()
                    self.load_mate(j, c).wait()
                    first, size, _ = self.chunks[j][c]
                    at = j * GROUP_ROWS + first
                    add_rows(self.acc, at, self.acc, at, self.mate, first, size)
                    self.down(j, c, 0).start()
                elif stage == first_stage:
                    self.carried(j, c, False).wait()
                    self.down(j, c, stage).start()
                elif stage <= bits:
                    depth = stage - 1
                    if depth < halvings:
                        self.down(j, c, depth).wait_recv()
                        self.left(j, c, depth)
                    else:
                        self.down(j, c, depth).wait()
                    first, size = self.span(j, c, stage)
                    at = j * GROUP_ROWS + first
                    add_rows(self.acc, at, self.acc, at, self.got[depth], self.got_at(j, c, depth), size)
                    if stage < min(bits, last_stage):
                        self.down(j, c, stage).start()
                    elif stage < last_stage:
                        self.raise_up(j, c, halvings - 1)
                else:
                    depth = bits + halvings - stage
                    self.up(j, c, depth).wait_recv()
                    if depth > 0:
                        self.raise_up(j, c, depth - 1)
            if stage == bits + halvings:
                layer = self.layer_of(j)
                at_core(self.core, layer, lambda j=j, layer=layer: self.put(j, layer).start())
                at_core(self.core, 1 - layer, lambda j=j, layer=layer: self.give(j, 1 - layer).start())
        for j, (start, first_stage, _) in self.jobs.items():
            if start == now + 1 and first_stage == 0:
                self.prepare(j)

    def small_step(self, k):
        friend = self.across if k == 0 else self.partner(k - 1)
        return copy_far(
            self.small_out, self.small_got.at[k], self.small_send.at[k], self.small_recv.at[k], friend
        )

    def small_begin(self):
        for layer in range(2):

            def step(layer=layer):
                self.small_out[...] = self.small[layer]
                copy_far(
                    self.small.at[1 - layer], self.small_got.at[0], self.small_send.at[0], self.small_recv.at[0],
                    self.across,
                ).start()

            at_core(self.core, layer, step)

    def small_turn(self, k):
        self.small_step(k).wait()
        self.small_out[...] = self.small_out[...] + self.small_got[k]
        if k < self.bits:
            self.small_step(k + 1).start()

    def shown_keep(self, layer, k):
        return pltpu.make_async_copy(self.shown[2 * k + layer], self.shown_out[k].at[self.core], self.shown_sem.at[k])

    def shown_give(self, layer, k):
        return copy_far(
            self.shown[2 * k + 1 - layer], self.shown_out[k].at[self.core], self.shown_send.at[k],
            self.shown_recv.at[k], self.across,
        )

    def show(self):
        for layer in range(2):

            def step(layer=layer):
                for k in range(2):
                    self.shown_keep(layer, k).start()
                    self.shown_give(layer, k).start()

            at_core(self.core, layer, step)

    def close(self):
        for k in range(2):
            self.shown_keep(0, k).wait()
            self.shown_give(0, k).wait()
        for j in range(GROUPS):
            layer = self.layer_of(j)

            def kept(j=j, layer=layer):
                self.put(j, layer).wait()
                self.give(j, 1 - layer).wait_recv()

            at_core(self.core, layer, kept)
            at_core(self.core, 1 - layer, lambda j=j, layer=layer: self.give(j, 1 - layer).wait_send())
            for c in self.each(j):
                for depth in range(self.halvings):
                    self.up(j, c, depth).wait_send()


def cast_kernel(first, second, small, acts, slopes, qkv, out, up, down, *refs):
    gains, biases, router, means, acts_out, slopes_out, low, high, bounce, in_sem, out_sem, copy_sem = refs
    rows = low.shape[1]
    per = LANES // rows
    slots = low.shape[0]
    count = 12 * per
    core = lax.axis_index("section")
    passed = [
        (
            pltpu.make_async_copy(source, bounce.at[k], copy_sem.at[k]),
            pltpu.make_async_copy(bounce.at[k], target.at[0], copy_sem.at[k]),
        )
        for k, (source, target) in enumerate(((acts, acts_out), (slopes, slopes_out)))
    ]

    def take(k, source=first):
        return pltpu.make_async_copy(source.at[pl.ds(k * rows, rows), :], low.at[k % slots], in_sem.at[k % slots])

    def give(k):
        block, part = divmod(k, per)
        if block < 4:
            target = down.at[0, pl.ds(k * rows, rows), :]
        elif block < 8:
            target = up.at[0, pl.ds(part * rows, rows), pl.ds((block - 4) * LANES, LANES)]
        elif block < 9:
            target = out.at[0, pl.ds(part * rows, rows), :]
        else:
            target = qkv.at[0, pl.ds(part * rows, rows), pl.ds((block - 9) * LANES, LANES)]
        return pltpu.make_async_copy(high.at[k % slots], target, out_sem.at[k % slots])

    def fetch(k):
        at_core(core, 0, lambda: take(k).start())
        at_core(core, 1, lambda: take(k, second).start())

    for k in range(slots):
        fetch(k)
    for copy, _ in passed:
        copy.start()
    held = gains.shape[1] // LANES
    for row in range(held):
        gains[:, row * LANES : (row + 1) * LANES] = small[row : row + 1, :]
    for row in range(biases.shape[1] // LANES):
        biases[:, row * LANES : (row + 1) * LANES] = small[held + row : held + row + 1, :]
    row = held + biases.shape[1] // LANES
    router[...] = small[row : row + 1, :]
    micro = means.shape[1]
    means[...] = small[row + 1 : row + 2, :micro] / small[row + 1 : row + 2, micro : 2 * micro]
    for k in range(count):
        take(k).wait()
        if k >= slots:
            give(k - slots).wait()
        high[k % slots] = low[k % slots].astype(F32)
        give(k).start()
        if k + slots < count:
            fetch(k + slots)
        if k < 2:
            passed[k][0].wait()
            passed[k][1].start()
    for k in range(count - slots, count):
        give(k).wait()
    for _, copy in passed:
        copy.wait()


def cast_sums(sums, small, acts, slopes, shapes, micro):
    anywhere = pl.BlockSpec(memory_space=pl.ANY)
    inside = pl.BlockSpec(memory_space=pltpu.VMEM)
    outs = [(shape, F32) for shape in shapes] + [((1, LANES), F32), ((1, micro), F32)]
    outs += [((1, *value.shape), BF16) for value in (acts, slopes)]
    return pl.pallas_call(
        cast_kernel,
        out_shape=[jax.ShapeDtypeStruct(*one) for one in outs],
        in_specs=[anywhere] * 2 + [inside] + [anywhere] * 2,
        out_specs=[anywhere] * 4 + [inside] * 4 + [anywhere] * 2,
        scratch_shapes=[
            pltpu.VMEM((4, LANES, LANES), BF16),
            pltpu.VMEM((4, LANES, LANES), F32),
            pltpu.VMEM((2, *acts.shape), BF16),
            pltpu.SemaphoreType.DMA((4,)),
            pltpu.SemaphoreType.DMA((4,)),
            pltpu.SemaphoreType.DMA((2,)),
        ],
        compiler_params=pltpu.CompilerParams(vmem_limit_bytes=60 * 1024 * 1024),
        cost_estimate=pl.CostEstimate(flops=0, bytes_accessed=50 * 10**6, transcendentals=0),
        name="cast",
    )(*sums, small, acts, slopes)


STEP = 256
NEGATIVE = -1e30


def dot(left, right, dims=NN):
    return lax.dot_general(left, right, dims, preferred_element_type=F32)


def gelu_parts(pre):
    bell = jnp.exp(pre * pre * -0.5)
    t = pl.reciprocal(1.0 + jnp.abs(pre) * (0.3275911 * 0.7071067811865476))
    poly = t * (0.1274147960 + t * (-0.142248368 + t * (0.710706871 + t * (-0.7265760135 + t * 0.5307027145))))
    tail = poly * bell
    return jnp.where(pre >= 0.0, 1.0 - tail, tail), bell


def norm_stats(values):
    centred = values - jnp.mean(values, axis=-1, keepdims=True)
    recip = lax.rsqrt(jnp.mean(centred * centred, axis=-1, keepdims=True) + 1e-06)
    return centred * recip, recip


def fold(tile):
    return jnp.sum(tile.reshape(tile.shape[0] // 8, 8, tile.shape[1]), axis=0)


def front_names(r, given, full):
    r.weights = [next(given) for _ in range(4)]
    r.w_sem, r.n1, r.qkv, r.probs, r.mask, r.mix, r.between, r.n2, r.act = (next(given) for _ in range(9))
    if not full:
        r.pre = [next(given) for _ in range(2)]
    r.act_part = [next(given) for _ in range(2)]


def back_names(r, given, scaled):
    r.n1t, r.n2t = (next(given) for _ in range(2))
    r.mixt = r.n2t
    r.dmlp = next(given) if scaled else r.dout
    r.dpre, r.dn = (next(given) for _ in range(2))
    r.pre = [r.dn.at[:, pl.ds(side * STEP, STEP)] for side in range(2)]
    r.dqkv = r.dpre.at[:, pl.ds(0, 3 * LANES)]
    r.datt, r.dmix = r.n1, r.mix
    r.dpre_part = [next(given) for _ in range(2)]
    r.down_stage, r.up_stage, r.down_sem, r.up_sem = (next(given) for _ in range(4))


def use_weights(r, layer):
    core = lax.axis_index("section")

    def weight(which, source):
        return pltpu.make_async_copy(source[which].at[0], r.weights[which], r.w_sem.at[which])

    for near, source in ((core == layer, r.own), (core != layer, r.far)):

        @pl.when(near)
        def _():
            for which in range(4):
                weight(which, source).start()

    r.ready = lambda which: weight(which, r.own).wait()


def layer_kernel(groups, window, chunks, *refs):
    r = Names()
    given = iter(refs)
    r.x, r.col_code, r.row_code, r.vec = (next(given) for _ in range(4))
    r.own = [next(given) for _ in range(4)]
    r.far = [next(given) for _ in range(4)]
    r.unsort, r.dout = (next(given) for _ in range(2))
    r.shown_du, r.small, r.grads, r.du, r.shown_y, landed, carry = (next(given) for _ in range(7))
    front_names(r, given, True)
    back_names(r, given, False)
    r.y, r.shown_sem = r.n2, next(given)
    jobs = {j: (start, 0, stage) for j, (start, stage) in enumerate(REDUCED)}
    sums = Sums(chunks, jobs, {0: 0, 1: 12}, given, False)
    sums.grads, sums.landed, sums.carry = (None, r.grads), (None, landed), carry
    use_weights(r, 1)
    sums.open()
    r.tile_out = functools.partial(sums.tile_out, 1)
    r.hooks = {at: sums.moment for at in (4, 7, 8)}
    r.hooks[3] = lambda: sums.prepare(0)
    layer_body(r, groups, window, True, False)
    while sums.now < sums.end:
        sums.moment()
    for j in jobs:
        for c in sums.each(j):
            sums.carried(j, c, True).start()
    sums.wait_tiles(1, 24)
    for j in jobs:
        for c in sums.each(j):
            sums.carried(j, c, True).wait()


def start_kernel(groups, window, *refs):
    r = Names()
    given = iter(refs)
    lengths, route_mask, tokens, cotangent, router, own_vec = (next(given) for _ in range(6))
    own = [next(given) for _ in range(4)]
    far = [next(given) for _ in range(4)]
    vecs = [next(given) for _ in range(2)]
    r.all_y, r.shown_y, r.delta, cot, r.x = (next(given) for _ in range(5))
    col_codes = [next(given) for _ in range(2)]
    row_codes = [next(given) for _ in range(2)]
    r.unsort, pick, r.unpick, r.skipped, r.scale, factor, extra = (next(given) for _ in range(7))
    front_names(r, given, False)
    r.y, r.all_x, order, raw, far_vec, raw_sem = (next(given) for _ in range(6))
    far_send, far_recv, vec_sem = (next(given) for _ in range(3))
    core = lax.axis_index("section")
    across = (1 - core, lax.axis_index("dp"))
    rows, width = r.all_x.shape
    half = rows // 2

    def fetch(k, source):
        return pltpu.make_async_copy(source.at[core], raw.at[k], raw_sem.at[k])

    fetch(0, tokens).start()
    fetch(1, cotangent).start()
    barrier = pltpu.get_barrier_semaphore()
    pl.semaphore_signal(barrier, inc=1, device_id=across, device_id_type=pl.DeviceIdType.MESH)
    pl.semaphore_wait(barrier, 1)

    def lend(which):
        return copy_far(own[which], far[which], far_send.at[which], far_recv.at[which], across)

    lend_vec = copy_far(own_vec, far_vec, vec_sem.at[0], vec_sem.at[1], across)
    lend_vec.start()
    lend(0).start()

    def weight(which, source):
        return pltpu.make_async_copy(source[which].at[0], r.weights[which], r.w_sem.at[which])

    def take_own():
        for which in range(4):
            weight(which, own).start()

    at_core(core, 0, take_own)

    def ready(which):
        def arrive():
            lend(which).wait_recv()
            weight(which, far).start()

        at_core(core, 1, arrive)
        weight(which, own).wait()

    r.ready = ready

    starts, bases, total, longs, short = [], [], 0, 0, 0
    count = lengths.shape[2]
    sizes = [lengths[core, 0, c] for c in range(count)]
    for size in sizes:
        is_long = size == LONG
        starts.append(total)
        bases.append(jnp.where(is_long, longs * LONG, 2 * LONG + short))
        total = total + size
        longs = longs + jnp.where(is_long, 1, 0)
        short = short + jnp.where(is_long, 0, size)

    def place(shape, dim):
        return lax.broadcasted_iota(jnp.int32, shape, dim)

    def target(at):
        moved = at
        for start, size, base in zip(starts, sizes, bases):
            moved = moved + jnp.where((at >= start) & (at < start + size), base - start, 0)
        return moved

    def code_of(at):
        return sum(jnp.where(at >= base, 1, 0) for base in bases)

    row_at, col_at = place((1, rows), 1), place((rows, 1), 0)

    def one_hot(left, right):
        return jnp.where(left == right, 1.0, 0.0).astype(BF16)

    goes_row, goes_col = target(row_at), target(col_at)
    row_codes[1][...] = code_of(row_at)
    col_codes[1][...] = code_of(col_at)
    for start in range(0, rows, 128):
        here = slice(start, start + 128)
        order[here, :] = one_hot(col_at[here], goes_row)
        r.unsort[here, :] = one_hot(goes_col[here], row_at)
    lend(1).start()
    lend(2).start()
    lend(3).start()
    for k, (source, moved) in enumerate(((tokens, r.all_x), (cotangent, cot))):
        fetch(k, source).wait()
        moved[...] = dot(order[...], raw[k]).astype(BF16)

    mask = jnp.where(route_mask[pl.ds(core, 1), :] == 1, 1.0, 0.0)
    masks = jnp.broadcast_to(mask, (8, rows)).astype(BF16)
    chosen_row = dot(masks, r.unsort[...])
    chosen_col = dot(order[...], masks, NT)
    earlier = jnp.where(place((rows, rows), 0) < place((rows, rows), 1), 1.0, 0.0).astype(BF16)
    rank_row = dot(chosen_row.astype(BF16), earlier)[:1]
    later = jnp.where(place((rows, rows), 0) > place((rows, rows), 1), 1.0, 0.0).astype(BF16)
    rank_col = dot(later, chosen_col.astype(BF16))[:, :1]
    chosen_row, chosen_col = chosen_row[:1], chosen_col[:, :1]
    r.skipped[...] = 1.0 - chosen_col
    key_row = jnp.where(chosen_row > 0.5, rank_row, -1.0)
    key_col = jnp.where(chosen_col > 0.5, rank_col, -1.0)
    pick[...] = one_hot(place((half, 1), 0).astype(F32), key_row)
    r.unpick[...] = one_hot(key_col, place((1, half), 1).astype(F32))
    names_row = jnp.broadcast_to(code_of(row_at).astype(F32), (8, rows)).astype(BF16)
    routed_row = dot(names_row, r.unpick[...])[:1]
    routed_col = dot(pick[...], names_row, NT)[:, :1]
    row_codes[0][...] = routed_row.astype(jnp.int32)
    col_codes[0][...] = routed_col.astype(jnp.int32)
    r.x[...] = dot(pick[...], r.all_x[...]).astype(BF16)
    logit = jnp.sum(r.x[...].astype(F32) * router[...], axis=1, keepdims=True)
    gate = 1.0 / (1.0 + jnp.exp(-logit))
    held = jnp.where(routed_col > 0.5, 1.0, 0.0)
    r.scale[...] = held * gate
    factor[...] = held * gate * (1.0 - gate)
    gates, counts = jnp.sum(held * gate, axis=0, keepdims=True), jnp.sum(mask, axis=1, keepdims=True)
    lane = place((1, width), 1)
    micro = tokens.shape[0]
    extra[...] = jnp.where(lane == core, gates, jnp.where(lane == core + micro, counts, 0.0))

    lend_vec.wait()
    for layer in range(2):
        vecs[layer][...] = jnp.where(core == layer, own_vec[...], far_vec[...])
    r.vec, r.col_code, r.row_code, r.own = vecs[0], col_codes[0], row_codes[0], own
    r.hooks = {}
    layer_body(r, groups, window, False, True)
    for which in range(4):
        lend(which).wait_send()
        at_core(core, 0, lambda which=which: lend(which).wait_recv())


def fused_kernel(groups, window, chunks, *refs):
    r = Names()
    given = iter(refs)
    r.x, r.col_code, r.row_code, r.vec, r.scale = (next(given) for _ in range(5))
    r.own = [next(given) for _ in range(4)]
    r.far = [next(given) for _ in range(4)]
    r.unsort = next(given)
    r.all_dout, r.pick, r.unpick, r.skipped, r.delta, r.factor, r.router = (next(given) for _ in range(7))
    second, second_landed, carry, second_small, extra = (next(given) for _ in range(5))
    shown = [next(given) for _ in range(3)]
    full = [next(given) for _ in range(2)]
    first_landed, first, small_out = (next(given) for _ in range(3))
    shown_out = [next(given) for _ in range(2)]
    front_names(r, given, True)
    back_names(r, given, True)
    r.dout, r.du, r.shown_du, r.small, r.router_grad = (next(given) for _ in range(5))
    bits = len(chunks[0][0][2])
    last = bits + min(bits, HALVINGS)
    reduced = len(REDUCED)
    jobs = {j: (start, REDUCED[j][1] if j < reduced else 0, last) for j, start in enumerate(GROUP_STARTS)}
    sums = Sums(chunks, jobs, {3: 0, 4: 12, 5: 24}, given, True)
    sums.grads, sums.landed, sums.full = (first, second), (first_landed, second_landed), full
    sums.carry, sums.small_out = carry, small_out
    sums.shown, sums.shown_out = (shown[0], shown[1], r.shown_du, shown[2]), shown_out
    r.grads = first
    use_weights(r, 0)
    sums.open()
    for j in range(reduced):
        for c in sums.each(j):
            sums.carried(j, c, False).start()
    for j, (start, first_stage, _) in jobs.items():
        if start == 0 and first_stage == 0:
            sums.prepare(j)
    r.tile_out = functools.partial(sums.tile_out, 0)
    r.hooks = {at: sums.moment for at in (0, 1, 2, 3, 8, 9)}
    layer_body(r, groups, window, True, True)

    for index, source in enumerate((r.small, second_small)):
        for row in range(source.shape[1] // LANES):
            sums.small[index, row : row + 1, :] = source[:, row * LANES : (row + 1) * LANES]
        row = source.shape[1] // LANES
        sums.small[index, row : row + 1, :] = r.router_grad[...]
        sums.small[index, row + 1 : row + 2, :] = extra[...]
        left = sums.small.shape[1] - row - 2
        sums.small[index, row + 2 :, :] = jnp.zeros((left, LANES), F32)
    sums.small_begin()
    sums.show()

    for turn in range(max(sums.end - sums.now, sums.bits + 1)):
        if sums.now < sums.end:
            sums.moment()
        if turn <= sums.bits:
            sums.small_turn(turn)
    sums.close()


def layer_body(r, groups, window, full, is_router):
    def hook(at):
        if at in r.hooks:
            r.hooks[at]()

    rows, width = r.x.shape
    hidden = r.own[2].shape[2]
    pairs = width // 128
    row_tile = rows // 5

    def vec(start, count=width):
        return r.vec[:, start : start + count]

    g1, g2, b1, bq, bv, bo, b2 = (vec(k * width) for k in range(7))
    bu_at, bd_at = 7 * width, 7 * width + hidden

    def row_loop(step, init=0):
        def at(k, carry):
            return step(pl.ds(pl.multiple_of(k * row_tile, row_tile), row_tile), carry)

        return lax.fori_loop(0, rows // row_tile, at, init)

    def norm_step(source, gain, bias, target):
        def step(here, carry):
            normal, _ = norm_stats(source[here, :].astype(F32))
            target[here, :] = (normal * gain + bias).astype(BF16)
            return carry

        return step

    def tiles(step):
        for k in range(width // STEP):
            step(slice(k * STEP, (k + 1) * STEP))

    def show(source, target):
        def step(span):
            target[:, span] = dot(r.unsort[...], source[:, span]).astype(BF16)

        tiles(step)

    def spread(routed, others, target, shown):
        def step(span):
            value = dot(r.unpick[...], routed[:, span]) + others[:, span].astype(F32) * r.skipped[...]
            if target is not None:
                target[:, span] = value.astype(BF16)
            shown[:, span] = dot(r.unsort[...], value.astype(BF16)).astype(BF16)

        tiles(step)

    row_loop(norm_step(r.x, g1, b1, r.n1))
    if full and is_router:

        def route_step(span):
            r.dout[:, span] = dot(r.pick[...], r.all_dout[:, span]).astype(BF16)

        tiles(route_step)
    if full:

        def delta_step(here, carry):
            low = r.dout[here, :]
            if is_router:
                low = (low.astype(F32) * r.scale[here, :]).astype(BF16)
                r.dmlp[here, :] = low
            return carry + fold(low.astype(F32))

        dbd = row_loop(delta_step, jnp.zeros((8, width), F32))
        r.small[:, bd_at:] = jnp.sum(dbd, axis=0, keepdims=True)

    for k, (start, low, high) in enumerate(groups):
        col = r.col_code[start : start + window, :]
        row = r.row_code[:, start : start + window]
        place = lax.broadcasted_iota(jnp.int32, (window, 1), 0) + start
        col = jnp.where((place >= low) & (place < high), col, -1)
        r.mask[k] = jnp.where(col == row, 0.0, NEGATIVE)

    r.ready(0)
    for k in range(3 * width // STEP):
        span = slice(k * STEP, (k + 1) * STEP)
        value = dot(r.n1[...], r.weights[0][:, span])
        if k < width // STEP:
            value = (value + bq[:, span]).astype(BF16).astype(F32) * 0.125
        elif k >= 2 * width // STEP:
            value = value + bv[:, k * STEP - 2 * width : (k + 1) * STEP - 2 * width]
        r.qkv[:, span] = value.astype(BF16)

    hook(0)
    lane = lax.broadcasted_iota(jnp.int32, (1, 128), 1)

    def halves(block):
        zero = jnp.zeros_like(block)
        return jnp.concatenate([jnp.where(lane < 64, block, zero), jnp.where(lane < 64, zero, block)], axis=0)

    high_half = lax.broadcasted_iota(jnp.int32, (128, 1), 0) >= 64

    def own_half(both):
        return jnp.where(high_half, both[:, window:], both[:, :window]).T

    r.mix[...] = jnp.zeros_like(r.mix)

    def lanes(pair, part):
        return pl.ds(pl.multiple_of(pair * 128 + part * width, 128), 128)

    spots = [slice(start, start + window) for start, _, _ in groups]
    count = len(groups)

    def qkv_at(pair, part):
        return [r.qkv[here, lanes(pair, part)] for here in spots]

    def attend(pair, carry):
        q, key, v = (qkv_at(pair, part) for part in range(3))
        scores = [dot(key[k], halves(q[k]), NT) for k in range(count)]
        probs = []
        for k, (start, low, high) in enumerate(groups):
            mask = r.mask[k]
            masked = scores[k] + jnp.concatenate([mask, mask], axis=1)
            place = lax.broadcasted_iota(jnp.int32, (1, window), 1) + start
            valid = (place >= low) & (place < high)
            valid = jnp.concatenate([valid, valid], axis=1)
            power = jnp.exp(masked - jnp.max(masked, axis=0, keepdims=True))
            total = jnp.sum(power, axis=0, keepdims=True)
            prob = (power * jnp.where(valid, 1.0 / total, 0.0)).astype(BF16)
            if full:
                r.probs[pair * count + k] = prob
            probs.append(prob)
        mixed = [dot(v[k].T, probs[k]) for k in range(count)]
        for k, here in enumerate(spots):
            r.mix[here, lanes(pair, 0)] = r.mix[here, lanes(pair, 0)] + own_half(mixed[k]).astype(BF16)
        return carry

    lax.fori_loop(0, pairs, attend, 0)

    r.ready(1)
    for k in range(width // STEP):
        span = slice(k * STEP, (k + 1) * STEP)
        value = dot(r.mix[...], r.weights[1][:, span]) + bo[:, span]
        r.between[:, span] = r.x[:, span].astype(F32) + value
    row_loop(norm_step(r.between, g2, b2, r.n2))
    if full:
        r.n1t[...] = r.n1[...].T
        r.n2t[...] = r.n2[...].T
    hook(1)

    r.ready(2)
    if full:
        r.ready(3)

    def down_out(k, slot):
        r.tile_out(
            r.down_stage.at[slot], pl.multiple_of(k * STEP, STEP), 0, (STEP, width), r.down_sem.at[slot], k
        )

    def side_out(block, k, slot):
        row = pl.multiple_of((block + k // 3) * width, width)
        column = pl.multiple_of(k % 3 * STEP, STEP)
        tile = k + {4: 12, 8: 24, 9: 27}[block]
        r.tile_out(r.up_stage.at[slot], row, column, (width, STEP), r.up_sem.at[slot], tile)

    def down_free(slot):
        target = r.grads.at[pl.ds(0, STEP), pl.ds(0, width)]
        pltpu.make_async_copy(r.down_stage.at[slot], target, r.down_sem.at[slot]).wait()

    def side_free(slot):
        target = r.grads.at[pl.ds(0, width), pl.ds(0, STEP)]
        pltpu.make_async_copy(r.up_stage.at[slot], target, r.up_sem.at[slot]).wait()

    steps = hidden // STEP

    def part_at(k):
        return pl.multiple_of(k * STEP, STEP)

    def ahead(k, side):
        at = part_at(k)
        r.pre[side][...] = dot(r.n2[...], r.weights[2][:, pl.ds(at, STEP)]) + r.vec[:, pl.ds(at + bu_at, STEP)]

    def middle(k, side):
        at = part_at(k)
        span = pl.ds(at, STEP)
        pre = r.pre[side][...]
        cdf, bell = gelu_parts(pre)
        act = (pre * cdf).astype(BF16)
        if not (full and is_router):
            r.act[:, span] = act
        if full:
            r.act_part[side][...] = act
            slope = cdf + pre * bell * 0.3989422804014327
            dact = dot(r.dmlp[...], r.weights[3][span, :], NT)
            dpre = (dact * slope).astype(BF16)
            r.dpre[:, span] = dpre
            r.dpre_part[side][...] = dpre
            r.small[:, pl.ds(at + bu_at, STEP)] = jnp.sum(dpre.astype(F32), axis=0, keepdims=True)

    def weigh(side):
        r.down_stage[side] = dot(r.act_part[side][...], r.dmlp[...], TN).astype(BF16)
        r.up_stage[side] = dot(r.n2t[...], r.dpre_part[side][...]).astype(BF16)

    def send_out(k, side):
        down_out(k, side)
        side_out(4, k, side)

    def two_steps(kk, first=False):
        even = kk * 2
        if full and not first:

            @pl.when(kk >= 2)
            def _():
                down_free(1)
                side_free(1)

            down_free(0)
            side_free(0)
        middle(even, 0)
        ahead(even + 1, 1)
        if full and not first:
            weigh(1)
        middle(even + 1, 1)
        ahead(jnp.minimum(even + 2, steps - 1), 0)
        if full:
            weigh(0)
            if not first:
                send_out(even - 1, 1)
            send_out(even, 0)

    def more_steps(kk, carry):
        two_steps(kk)
        return carry

    ahead(0, 0)
    two_steps(0, True)
    if 2 in r.hooks:
        lax.fori_loop(1, steps // 4, more_steps, 0)
        hook(2)
        lax.fori_loop(steps // 4, steps // 2, more_steps, 0)
    else:
        lax.fori_loop(1, steps // 2, more_steps, 0)
    if full:
        down_free(1)
        side_free(1)
        weigh(1)
        send_out(steps - 1, 1)
        for side in range(2):
            down_free(side)
            side_free(side)
        hook(3)
    if not full:
        r.ready(3)
    if not (full and is_router):
        for k in range(width // STEP):
            span = slice(k * STEP, (k + 1) * STEP)
            value = dot(r.act[...], r.weights[3][:, span]) + vec(bd_at)[:, span]
            source = r.x[:, span].astype(F32)
            value = r.between[:, span] - source + value
            if not full:
                r.delta[:, span] = value
            r.y[:, span] = (source + (r.scale[...] * value if is_router else value)).astype(BF16)
    if not full:
        spread(r.y, r.all_x, r.all_y, r.shown_y)
        return
    if not is_router:
        show(r.y, r.shown_du)
        r.shown_copy = pltpu.make_async_copy(r.shown_du, r.shown_y, r.shown_sem.at[0])
        r.shown_copy.start()

    r.dn[...] = dot(r.dpre[...], r.weights[2][...], NT)
    hook(4)

    def norm_back(source, gain, here):
        normal, recip = norm_stats(source[here, :].astype(F32))
        grad = r.dn[here, :]
        hat = grad * gain
        back = recip * (
            hat - jnp.mean(hat, axis=-1, keepdims=True) - normal * jnp.mean(hat * normal, axis=-1, keepdims=True)
        )
        return back, fold(grad * normal), fold(grad)

    def second_back(here, carry):
        back, dg, db = norm_back(r.between, g2, here)
        r.between[here, :] = back
        delta = r.dout[here, :].astype(F32)
        total = ((delta * r.scale[here, :] if is_router else delta) + back).astype(BF16)
        r.datt[here, :] = total
        return carry[0] + dg, carry[1] + db, carry[2] + fold(total.astype(F32))

    zero = jnp.zeros((8, width), F32)
    dg2, db2, dbo = row_loop(second_back, (zero, zero, zero))
    r.small[:, width : 2 * width] = jnp.sum(dg2, axis=0, keepdims=True)
    r.small[:, 6 * width : 7 * width] = jnp.sum(db2, axis=0, keepdims=True)
    r.small[:, 5 * width : 6 * width] = jnp.sum(dbo, axis=0, keepdims=True)

    hook(5)
    r.mixt[...] = r.mix[...].T
    r.dmix[...] = dot(r.datt[...], r.weights[1][...], NT).astype(BF16)
    for k in range(width // STEP):
        span = slice(k * STEP, (k + 1) * STEP)
        slot = k % 2
        if k >= 2:
            side_free(slot)
        r.up_stage[slot] = dot(r.mixt[...], r.datt[:, span]).astype(BF16)
        side_out(8, k, slot)
    hook(6)

    r.dqkv[...] = jnp.zeros((rows, 3 * width), BF16)

    def attend_back(pair, carry):
        q, key, v = (qkv_at(pair, part) for part in range(3))
        dm = [halves(r.dmix[here, lanes(pair, 0)]) for here in spots]
        dprobs = [dot(v[k], dm[k], NT) for k in range(count)]
        dv = [dot(r.probs[pair * count + k], dm[k]) for k in range(count)]
        ds = []
        for k in range(count):
            wide = r.probs[pair * count + k].astype(F32)
            product = wide * dprobs[k]
            ds.append((product - wide * jnp.sum(product, axis=0, keepdims=True)).astype(BF16))
        dk = [dot(ds[k], halves(q[k])) for k in range(count)]
        dq = [dot(key[k].T, ds[k]) for k in range(count)]
        for k, here in enumerate(spots):
            for part, value in enumerate((own_half(dq[k]) * 0.125, dk[k], dv[k])):
                spot = lanes(pair, part)
                r.dqkv[here, spot] = r.dqkv[here, spot] + value.astype(BF16)
        return carry

    if 7 in r.hooks:
        lax.fori_loop(0, pairs // 2, attend_back, 0)
        hook(7)
        lax.fori_loop(pairs // 2, pairs, attend_back, 0)
    else:
        lax.fori_loop(0, pairs, attend_back, 0)
    hook(8)

    for k in range(3 * width // STEP):
        span = slice(k * STEP, (k + 1) * STEP)
        block = r.dqkv[:, span]
        if not width <= k * STEP < 2 * width:
            at = 3 * width + k * STEP - (width if k * STEP >= width else 0)
            r.small[:, at : at + STEP] = jnp.sum(block.astype(F32), axis=0, keepdims=True)
        slot = (k + 1) % 2
        side_free(slot)
        r.up_stage[slot] = dot(r.n1t[...], block).astype(BF16)
        side_out(9, k, slot)
    side_free(0)
    side_free(1)
    hook(9)

    r.dn[...] = dot(r.dqkv[...], r.weights[0][...], NT)

    def first_back(here, carry):
        back, dg, db = norm_back(r.x, g1, here)
        dout = r.dout[here, :].astype(F32)
        total = dout + r.between[here, :] + back
        sums = [carry[0] + dg, carry[1] + db]
        if is_router:
            slope = jnp.sum(dout * r.delta[here, :], axis=1, keepdims=True) * r.factor[here, :]
            total = total + slope * r.router[...]
            sums.append(carry[2] + fold(slope * r.x[here, :].astype(F32)))
        r.du[here, :] = total.astype(BF16)
        return tuple(sums)

    sums = row_loop(first_back, (zero,) * (3 if is_router else 2))
    r.small[:, :width] = jnp.sum(sums[0], axis=0, keepdims=True)
    r.small[:, 2 * width : 3 * width] = jnp.sum(sums[1], axis=0, keepdims=True)
    if is_router:
        r.router_grad[...] = jnp.sum(sums[2], axis=0, keepdims=True)
        spread(r.du, r.all_dout, None, r.shown_du)
    else:
        r.shown_copy.wait()
        show(r.du, r.shown_du)


def front_scratch(rows, width, hidden, groups, window, full, keep_act):
    sizes = [(width, 3 * width), (width, width), (width, hidden), (hidden, width)]
    held = [pltpu.VMEM(size, BF16) for size in sizes]
    held += [pltpu.SemaphoreType.DMA((4,))]
    held += [pltpu.VMEM((rows, width), BF16), pltpu.VMEM((rows, 3 * width), BF16)]
    held += [pltpu.VMEM((HEADS // 2 * len(groups) if full else 1, window, 2 * window), BF16)]
    held += [pltpu.VMEM((len(groups), window, window), F32), pltpu.VMEM((rows, width), BF16)]
    held += [pltpu.VMEM((rows, width), F32), pltpu.VMEM((rows, width), BF16)]
    held += [pltpu.VMEM((rows, hidden) if keep_act else (TILE, LANES), BF16)]
    held += [pltpu.VMEM((rows, STEP), F32)] * (0 if full else 2)
    return held + [pltpu.VMEM((rows, STEP), BF16)] * 2


def back_scratch(rows, width, hidden, scaled):
    held = [pltpu.VMEM((width, rows), BF16)] * 2 + [pltpu.VMEM((rows, width), BF16)] * int(scaled)
    held += [pltpu.VMEM((rows, hidden), BF16), pltpu.VMEM((rows, width), F32)]
    held += [pltpu.VMEM((rows, STEP), BF16)] * 2
    held += [pltpu.VMEM((2, STEP, width), BF16), pltpu.VMEM((2, width, STEP), BF16)]
    return held + [pltpu.SemaphoreType.DMA((2,))] * 2


def run_start(groups, window, lengths, route_mask, tokens, cotangent, router_row, own_vec, own):
    _, rows, width = tokens.shape
    half, hidden = rows // 2, own[2].shape[2]
    inside = pl.BlockSpec(memory_space=pltpu.VMEM)
    anywhere = pl.BlockSpec(memory_space=pl.ANY)
    outs = [(value.shape, BF16) for value in own] + [(own_vec.shape, F32)] * 2
    outs += [((rows, width), BF16)] * 2 + [((half, width), F32), ((rows, width), BF16), ((half, width), BF16)]
    outs += [((half, 1), jnp.int32), ((rows, 1), jnp.int32), ((1, half), jnp.int32), ((1, rows), jnp.int32)]
    outs += [((rows, rows), BF16), ((half, rows), BF16), ((rows, half), BF16), ((rows, 1), F32)]
    outs += [((half, 1), F32)] * 2 + [((1, width), F32)]
    scratch = front_scratch(half, width, hidden, groups, window, False, True)
    scratch += [pltpu.VMEM((half, width), BF16), pltpu.VMEM((rows, width), BF16), pltpu.VMEM((rows, rows), BF16)]
    scratch += [pltpu.VMEM((2, rows, width), BF16), pltpu.VMEM(own_vec.shape, F32), pltpu.SemaphoreType.DMA((2,))]
    scratch += [pltpu.SemaphoreType.DMA((4,))] * 2 + [pltpu.SemaphoreType.DMA((2,))]
    return pl.pallas_call(
        functools.partial(start_kernel, groups, window),
        out_shape=[jax.ShapeDtypeStruct(*one) for one in outs],
        in_specs=[pl.BlockSpec(memory_space=pltpu.SMEM), inside] + [anywhere] * 2 + [inside] * 2 + [anywhere] * 4,
        out_specs=[anywhere] * 4 + [inside] * (len(outs) - 4),
        scratch_shapes=scratch,
        compiler_params=pltpu.CompilerParams(
            collective_id=1, has_side_effects=True, vmem_limit_bytes=60 * 1024 * 1024
        ),
        cost_estimate=pl.CostEstimate(flops=5 * 10**9, bytes_accessed=6 * 10**7, transcendentals=0),
        name="start",
    )(lengths, route_mask, tokens, cotangent, router_row, own_vec, *own)


def run_layer(axis_of, groups, window, x, col_code, row_code, vec, own, far, unsort, back):
    chunks = sum_plan(axis_of)
    reduced = len(REDUCED)
    rows, width = x.shape
    hidden = own[2].shape[2]
    inside = pl.BlockSpec(memory_space=pltpu.VMEM)
    anywhere = pl.BlockSpec(memory_space=pl.ANY)
    args = [x, col_code, row_code, vec, *own, *far, unsort, back]
    outs = [((rows, width), BF16), ((1, vec.shape[1]), F32), ((GRAD_ROWS, LANES), BF16)]
    outs += [((rows, width), BF16)] * 2 + [((GRAD_ROWS, LANES), BF16), ((reduced * GROUP_ROWS, LANES), BF16)]
    scratch = front_scratch(rows, width, hidden, groups, window, True, True)
    scratch += back_scratch(rows, width, hidden, False) + [pltpu.SemaphoreType.DMA((1,))]
    scratch += Sums.scratch(chunks, reduced, 0)
    flops = rows * width * (3 * width + width + 2 * hidden) * 6
    return pl.pallas_call(
        functools.partial(layer_kernel, groups, window, chunks),
        out_shape=[jax.ShapeDtypeStruct(*one) for one in outs],
        in_specs=[inside] * 4 + [anywhere] * 8 + [inside] * 2,
        out_specs=[inside] * 2 + [anywhere] + [inside] + [anywhere] * 3,
        scratch_shapes=scratch,
        compiler_params=pltpu.CompilerParams(
            collective_id=2, has_side_effects=True, vmem_limit_bytes=64 * 1024 * 1024
        ),
        cost_estimate=pl.CostEstimate(flops=flops, bytes_accessed=3 * 10**7, transcendentals=0),
        name="layer",
    )(*args)


def run_fused(axis_of, groups, window, x, col_code, row_code, vec, scale, own, far, rows_of, back, router, second, extra, shown):
    rows, width = x.shape
    hidden = own[2].shape[2]
    chunks = sum_plan(axis_of)
    inside = pl.BlockSpec(memory_space=pltpu.VMEM)
    anywhere = pl.BlockSpec(memory_space=pl.ANY)
    unsort, pick, unpick, skipped = rows_of
    delta, factor, router_row = router
    every = unsort.shape[0]
    args = [x, col_code, row_code, vec, scale, *own, *far, unsort]
    args += [back, pick, unpick, skipped, delta, factor, router_row]
    args += [*second, extra, *shown]
    small_rows = -(-(vec.shape[1] // LANES + 2) // 8) * 8
    outs = [((GRAD_ROWS, LANES), BF16)] * 4
    outs += [((small_rows, LANES), F32)] + [((2, every, width), BF16)] * 2
    scratch = front_scratch(rows, width, hidden, groups, window, True, False)
    scratch += back_scratch(rows, width, hidden, True)
    scratch += [pltpu.VMEM((rows, width), BF16)] * 2 + [pltpu.VMEM((every, width), BF16)]
    scratch += [pltpu.VMEM((1, vec.shape[1]), F32), pltpu.VMEM((1, width), F32)]
    scratch += Sums.scratch(chunks, GROUPS, small_rows)
    *sums, _, _, small, acts, grads = pl.pallas_call(
        functools.partial(fused_kernel, groups, window, chunks),
        out_shape=[jax.ShapeDtypeStruct(*one) for one in outs],
        in_specs=[inside] * 5 + [anywhere] * 8 + [inside] * 8 + [anywhere] * 3 + [inside] * 2 + [anywhere] * 3,
        out_specs=[anywhere] * 4 + [inside] + [anywhere] * 2,
        scratch_shapes=scratch,
        compiler_params=pltpu.CompilerParams(
            collective_id=0, has_side_effects=True, vmem_limit_bytes=64 * 1024 * 1024
        ),
        cost_estimate=pl.CostEstimate(flops=10**10, bytes_accessed=6 * 10**8, transcendentals=0),
        name="fused",
    )(*args)
    return sums, small, (acts, grads)


def body(axis_of, tokens, lengths, route_mask, router_weight, gains, biases, w_qkv, w_out, w_up, w_down, cotangent):
    micro, rows, width = tokens.shape
    own = (w_qkv, w_out, w_up, w_down)
    own_vec = jnp.concatenate([gains, biases], axis=1)
    router_row = router_weight.astype(F32)[None, :]
    half = LONG // 2
    groups_one = ((0, 0, half), (96, half, 2 * half), (192, 2 * half, rows // 2))
    groups_two = ((0, 0, LONG), (192, LONG, 2 * LONG), (384, 2 * LONG, rows))
    made = run_start(groups_one, 128, lengths, route_mask, tokens, cotangent, router_row, own_vec, own)
    far, (vec_one, vec_two), (y1, shown_y1, delta_one, cot, routed) = made[:4], made[4:6], made[6:11]
    col_one, col_two, row_one, row_two, *others = made[11:]
    unsort, pick, unpick, skipped, scale, factor, extra = others
    shown_du2, small_two, grads_two, dout, shown_y2, landed_two, carry = run_layer(
        axis_of, groups_two, 256, y1, col_two, row_two, vec_two, own, far, unsort, cot
    )
    sums, small, (activations, input_grads) = run_fused(
        axis_of, groups_one, 128, routed, col_one, row_one, vec_one, scale, own, far,
        (unsort, pick, unpick, skipped), dout, (delta_one, factor, router_row),
        (grads_two, landed_two, carry, small_two), extra,
        (shown_y1, shown_y2, shown_du2),
    )
    *grads, router_grad, means, activations, input_grads = cast_sums(
        sums, small, activations, input_grads,
        [value.shape for value in (*own, gains, biases)], micro,
    )
    return (activations, input_grads, *grads, router_grad[0], means[0])


def solution(mesh):
    in_specs = (
        P(None, "dp", None),
        P(None, "dp", None),
        P(None, "dp"),
        P(),
        P("section", None),
        P("section", None),
        P("section", None, None),
        P("section", None, None),
        P("section", None, None),
        P("section", None, None),
        P(None, "dp", None),
    )
    out_specs = (
        P("section", None, "dp", None),
        P("section", None, "dp", None),
        P("section", None, None),
        P("section", None, None),
        P("section", None, None),
        P("section", None, None),
        P("section", None),
        P("section", None),
        P(),
        P(),
    )
    step = functools.partial(body, axis_bits(mesh))
    return jax.shard_map(step, mesh=mesh, in_specs=in_specs, out_specs=out_specs, check_vma=False)
```

```python
import functools

import jax
import jax.numpy as jnp
from jax import lax
from jax.experimental import pallas as pl
from jax.experimental.pallas import tpu as pltpu
from jax.sharding import PartitionSpec as P

HEADS = 12
HEAD = 64
LONG = 197
F32 = jnp.float32
BF16 = jnp.bfloat16
NT = (((1,), (1,)), ((), ()))
TN = (((0,), (0,)), ((), ()))
NN = (((1,), (0,)), ((), ()))


LANES = 768
TILE = 16
GRAD_ROWS = 12 * LANES


def axis_bits(mesh):
    line = mesh.devices[0]
    bits = len(line).bit_length() - 1
    try:
        spots = [tuple(device.coords) for device in line]
    except AttributeError:
        return [0] * bits
    return [
        next((w for w in range(3) if spots[1 << b][w] != spots[0][w]), 0) for b in range(bits)
    ]


HALVINGS = 4
GROUPS = 6
SLOTS = 4


GROUP_PLAN = (
    ((768, 1023), (768, 132)),
    ((768, 123), (512, 1023), (256, 1203)),
    ((768, 123), (768, 1032)),
    ((512, 2103), (512, 123), (512, 1032)),
    ((768, 1023), (512, 2103), (256, 132)),
    ((512, 2013), (512, 132), (512, 1203)),
)
REDUCED = ((0, 3), (2, 1))
GROUP_STARTS = (0, 1, 2, 4, 5, 7)


def sum_plan(axis_of):
    lists = {}
    for bit, axis in enumerate(axis_of):
        lists.setdefault(axis, []).append(bit)
    lists = sorted(lists.values(), key=len)
    while len(lists) < 3:
        lists.append([])
    roles = [lists[0][:1], lists[1][:1], lists[2][:1], lists[2][1:2]]
    plan = []
    for group in GROUP_PLAN:
        chunks, start = [], 0
        for size, code in group:
            order = [bit for place in (1000, 100, 10, 1) for bit in roles[code // place % 10]]
            order += [bit for bit in range(len(axis_of)) if bit not in order]
            chunks.append((start, size, order))
            start += size
        plan.append(chunks)
    return plan


def add_rows(into, into_start, source, start, other, other_start, count):
    tile = next(t for t in (64, 32, 16) if count % t == 0)

    def step(k, carry):
        target, here, there = (
            pl.ds(pl.multiple_of(first + k * tile, TILE), tile) for first in (into_start, start, other_start)
        )
        into[target, :] = source[here, :] + other[there, :]
        return carry

    lax.fori_loop(0, count // tile, step, 0)


class Names:
    pass


def copy_far(source, target, one, two, friend):
    return pltpu.make_async_remote_copy(
        src_ref=source,
        dst_ref=target,
        send_sem=one,
        recv_sem=two,
        device_id=friend,
        device_id_type=pl.DeviceIdType.MESH,
    )


def at_core(core, index, step):
    pl.when(core == index)(step)


GRAD_TILES = 36
GROUP_ROWS = GRAD_ROWS // GROUPS


class Sums:
    def __init__(self, chunks, jobs, tiles, given, whole):
        self.chunks, self.jobs, self.tiles = chunks, jobs, tiles
        self.bits = bits = len(chunks[0][0][2])
        self.halvings = min(bits, HALVINGS)
        self.acc, self.mate = next(given), next(given)
        self.got = [next(given) for _ in range(bits)]
        self.load_sem, self.mate_sem = (next(given) for _ in range(2))
        self.send, self.recv, self.back_send, self.back_recv = (next(given) for _ in range(4))
        self.tile_recv, self.ready = (next(given) for _ in range(2))
        if whole:
            self.small_got, self.small = next(given), next(given)
            self.small_send, self.small_recv = (next(given) for _ in range(2))
            self.shown_sem, self.shown_send, self.shown_recv = (next(given) for _ in range(3))
            self.give_send, self.give_recv, self.put_sem = (next(given) for _ in range(3))
        self.core = lax.axis_index("section")
        self.me = lax.axis_index("dp")
        self.across = (1 - self.core, self.me)
        self.end = max(start + last - first + 1 for start, first, last in jobs.values())
        self.now = 0

    @staticmethod
    def scratch(chunks, held_groups, small_rows):
        bits = len(chunks[0][0][2])
        count = sum(len(group) for group in chunks)
        rows = min(held_groups, SLOTS) * GROUP_ROWS
        held = [pltpu.VMEM((held_groups * GROUP_ROWS, LANES), BF16), pltpu.VMEM((GROUP_ROWS, LANES), BF16)]
        held += [pltpu.VMEM((rows >> min(depth + 1, HALVINGS), LANES), BF16) for depth in range(bits)]
        held += [pltpu.SemaphoreType.DMA((count,))] * 2
        held += [pltpu.SemaphoreType.DMA((count, bits))] * 4
        held += [pltpu.SemaphoreType.DMA((GRAD_TILES,))]
        held += [pltpu.SemaphoreType.REGULAR((count, min(bits, HALVINGS)))]
        if small_rows:
            held += [pltpu.VMEM((bits + 1, small_rows, LANES), F32), pltpu.VMEM((2, small_rows, LANES), F32)]
            held += [pltpu.SemaphoreType.DMA((bits + 1,))] * 2
            held += [pltpu.SemaphoreType.DMA((2,))] * 3
            held += [pltpu.SemaphoreType.DMA((GROUPS,))] * 3
        return held

    def bit_at(self, bit):
        return lax.rem(self.me // (1 << bit), 2)

    def partner(self, bit):
        return (self.core, self.me + (1 - 2 * self.bit_at(bit)) * (1 << bit))

    def open(self):
        friends = [self.across] + [self.partner(bit) for bit in range(self.bits)]
        barrier = pltpu.get_barrier_semaphore()
        for friend in friends:
            pl.semaphore_signal(barrier, inc=1, device_id=friend, device_id_type=pl.DeviceIdType.MESH)
        pl.semaphore_wait(barrier, len(friends))

    @staticmethod
    def layer_of(j):
        return 1 if j < GROUPS // 2 else 0

    def base(self, j, core):
        return (2 * (j % (GROUPS // 2)) + core) * GROUP_ROWS

    def rows_at(self, j, core, c):
        start, size, _ = self.chunks[j][c]
        return pl.ds(pl.multiple_of(self.base(j, core) + start, TILE), size)

    def index(self, j, c):
        return sum(len(group) for group in self.chunks[:j]) + c

    def load(self, j, c):
        start, size, _ = self.chunks[j][c]
        target = self.acc.at[pl.ds(j * GROUP_ROWS + start, size), :]
        source = self.grads[self.layer_of(j)].at[self.rows_at(j, self.core, c), :]
        return pltpu.make_async_copy(source, target, self.load_sem.at[self.index(j, c)])

    def load_mate(self, j, c):
        source = self.landed[self.layer_of(j)].at[self.rows_at(j, self.core, c), :]
        start, size, _ = self.chunks[j][c]
        target = self.mate.at[pl.ds(start, size), :]
        return pltpu.make_async_copy(source, target, self.mate_sem.at[self.index(j, c)])

    def span(self, j, c, depth):
        start, size, order = self.chunks[j][c]
        for bit in order[: min(depth, self.halvings)]:
            size //= 2
            start = start + self.bit_at(bit) * size
        return start, size

    def in_acc(self, j, start, size):
        return pl.ds(pl.multiple_of(j * GROUP_ROWS + start, TILE), size)

    def got_at(self, j, c, depth):
        return (j % SLOTS * GROUP_ROWS + self.chunks[j][c][0]) >> min(depth + 1, HALVINGS)

    def down(self, j, c, depth):
        bit = self.chunks[j][c][2][depth]
        start, size = self.span(j, c, depth)
        if depth < self.halvings:
            size //= 2
            start = start + (1 - self.bit_at(bit)) * size
        k = self.index(j, c)
        return copy_far(
            self.acc.at[self.in_acc(j, start, size), :],
            self.got[depth].at[pl.ds(self.got_at(j, c, depth), size), :],
            self.send.at[k, depth],
            self.recv.at[k, depth],
            self.partner(bit),
        )

    def up(self, j, c, depth):
        bit = self.chunks[j][c][2][depth]
        start, size = self.span(j, c, depth + 1)
        here = self.acc.at[self.in_acc(j, start, size), :]
        k = self.index(j, c)
        return copy_far(here, here, self.back_send.at[k, depth], self.back_recv.at[k, depth], self.partner(bit))

    def left(self, j, c, depth):
        self.down(j, c, depth).wait_send()
        if self.jobs[j][2] > self.bits:
            partner = self.partner(self.chunks[j][c][2][depth])
            pl.semaphore_signal(
                self.ready.at[self.index(j, c), depth], inc=1, device_id=partner, device_id_type=pl.DeviceIdType.MESH
            )

    def raise_up(self, j, c, depth):
        if depth >= self.jobs[j][1]:
            pl.semaphore_wait(self.ready.at[self.index(j, c), depth], 1)
        self.up(j, c, depth).start()

    def carried(self, j, c, keep):
        start, size = self.span(j, c, REDUCED[j][1])
        here = self.in_acc(j, start, size)
        pair = (self.acc.at[here, :], self.carry.at[here, :])
        return pltpu.make_async_copy(*(pair if keep else pair[::-1]), self.load_sem.at[self.index(j, c)])

    def wait_tiles(self, layer, first):
        for tile in range(6):
            area = self.landed[layer].at[pl.ds(0, LANES), pl.ds(0, STEP)]
            sem = self.tile_recv.at[first + self.core * 6 + tile]
            copy_far(area, area, sem, sem, self.across).wait_recv()

    def tile_out(self, layer, stage, row, column, shape, sem, tile):
        area = (pl.ds(row, shape[0]), pl.ds(column, shape[1]))
        owner = lax.rem(tile // 6, 2)

        @pl.when(self.core == owner)
        def _():
            pltpu.make_async_copy(stage, self.grads[layer].at[area], sem).start()

        @pl.when(self.core != owner)
        def _():
            copy_far(stage, self.landed[layer].at[area], sem, self.tile_recv.at[tile], self.across).start()

    def give(self, j, core):
        rows = pl.ds(self.base(j, core), GROUP_ROWS)
        source = self.acc.at[pl.ds(j * GROUP_ROWS, GROUP_ROWS), :]
        target = self.full[self.layer_of(j)].at[rows, :]
        return copy_far(source, target, self.give_send.at[j], self.give_recv.at[j], self.across)

    def put(self, j, core):
        rows = pl.ds(self.base(j, core), GROUP_ROWS)
        source = self.acc.at[pl.ds(j * GROUP_ROWS, GROUP_ROWS), :]
        return pltpu.make_async_copy(source, self.full[self.layer_of(j)].at[rows, :], self.put_sem.at[j])

    def each(self, j):
        return range(len(self.chunks[j]))

    def prepare(self, j):
        for c in self.each(j):
            self.load(j, c).start()
        if j in self.tiles:
            self.wait_tiles(self.layer_of(j), self.tiles[j])
        for c in self.each(j):
            self.load_mate(j, c).start()

    def moment(self):
        now, self.now = self.now, self.now + 1
        bits, halvings = self.bits, self.halvings
        order = sorted(self.jobs, key=lambda j: self.jobs[j][:2] != (now, 0))
        for j in order:
            start, first_stage, last_stage = self.jobs[j]
            stage = now - start + first_stage
            if not first_stage <= stage <= last_stage:
                continue
            for c in self.each(j):
                if stage == 0:
                    self.load(j, c).wait()
                    self.load_mate(j, c).wait()
                    first, size, _ = self.chunks[j][c]
                    at = j * GROUP_ROWS + first
                    add_rows(self.acc, at, self.acc, at, self.mate, first, size)
                    self.down(j, c, 0).start()
                elif stage == first_stage:
                    self.carried(j, c, False).wait()
                    self.down(j, c, stage).start()
                elif stage <= bits:
                    depth = stage - 1
                    if depth < halvings:
                        self.down(j, c, depth).wait_recv()
                        self.left(j, c, depth)
                    else:
                        self.down(j, c, depth).wait()
                    first, size = self.span(j, c, stage)
                    at = j * GROUP_ROWS + first
                    add_rows(self.acc, at, self.acc, at, self.got[depth], self.got_at(j, c, depth), size)
                    if stage < min(bits, last_stage):
                        self.down(j, c, stage).start()
                    elif stage < last_stage:
                        self.raise_up(j, c, halvings - 1)
                else:
                    depth = bits + halvings - stage
                    self.up(j, c, depth).wait_recv()
                    if depth > 0:
                        self.raise_up(j, c, depth - 1)
            if stage == bits + halvings:
                layer = self.layer_of(j)
                at_core(self.core, layer, lambda j=j, layer=layer: self.put(j, layer).start())
                at_core(self.core, 1 - layer, lambda j=j, layer=layer: self.give(j, 1 - layer).start())
        for j, (start, first_stage, _) in self.jobs.items():
            if start == now + 1 and first_stage == 0:
                self.prepare(j)

    def small_step(self, k):
        friend = self.across if k == 0 else self.partner(k - 1)
        return copy_far(
            self.small_out, self.small_got.at[k], self.small_send.at[k], self.small_recv.at[k], friend
        )

    def small_begin(self):
        for layer in range(2):

            def step(layer=layer):
                self.small_out[...] = self.small[layer]
                copy_far(
                    self.small.at[1 - layer], self.small_got.at[0], self.small_send.at[0], self.small_recv.at[0],
                    self.across,
                ).start()

            at_core(self.core, layer, step)

    def small_turn(self, k):
        self.small_step(k).wait()
        self.small_out[...] = self.small_out[...] + self.small_got[k]
        if k < self.bits:
            self.small_step(k + 1).start()

    def shown_keep(self, layer, k):
        return pltpu.make_async_copy(self.shown[2 * k + layer], self.shown_out[k].at[self.core], self.shown_sem.at[k])

    def shown_give(self, layer, k):
        return copy_far(
            self.shown[2 * k + 1 - layer], self.shown_out[k].at[self.core], self.shown_send.at[k],
            self.shown_recv.at[k], self.across,
        )

    def show(self):
        for layer in range(2):

            def step(layer=layer):
                for k in range(2):
                    self.shown_keep(layer, k).start()
                    self.shown_give(layer, k).start()

            at_core(self.core, layer, step)

    def close(self):
        for k in range(2):
            self.shown_keep(0, k).wait()
            self.shown_give(0, k).wait()
        for j in range(GROUPS):
            layer = self.layer_of(j)

            def kept(j=j, layer=layer):
                self.put(j, layer).wait()
                self.give(j, 1 - layer).wait_recv()

            at_core(self.core, layer, kept)
            at_core(self.core, 1 - layer, lambda j=j, layer=layer: self.give(j, 1 - layer).wait_send())
            for c in self.each(j):
                for depth in range(self.halvings):
                    self.up(j, c, depth).wait_send()


def cast_kernel(first, second, small, acts, slopes, qkv, out, up, down, *refs):
    gains, biases, router, means, acts_out, slopes_out, low, high, bounce, in_sem, out_sem, copy_sem = refs
    rows = low.shape[1]
    per = LANES // rows
    slots = low.shape[0]
    count = 12 * per
    core = lax.axis_index("section")
    passed = [
        (
            pltpu.make_async_copy(source, bounce.at[k], copy_sem.at[k]),
            pltpu.make_async_copy(bounce.at[k], target.at[0], copy_sem.at[k]),
        )
        for k, (source, target) in enumerate(((acts, acts_out), (slopes, slopes_out)))
    ]

    def take(k, source=first):
        return pltpu.make_async_copy(source.at[pl.ds(k * rows, rows), :], low.at[k % slots], in_sem.at[k % slots])

    def give(k):
        block, part = divmod(k, per)
        if block < 4:
            target = down.at[0, pl.ds(k * rows, rows), :]
        elif block < 8:
            target = up.at[0, pl.ds(part * rows, rows), pl.ds((block - 4) * LANES, LANES)]
        elif block < 9:
            target = out.at[0, pl.ds(part * rows, rows), :]
        else:
            target = qkv.at[0, pl.ds(part * rows, rows), pl.ds((block - 9) * LANES, LANES)]
        return pltpu.make_async_copy(high.at[k % slots], target, out_sem.at[k % slots])

    def fetch(k):
        at_core(core, 0, lambda: take(k).start())
        at_core(core, 1, lambda: take(k, second).start())

    for k in range(slots):
        fetch(k)
    for copy, _ in passed:
        copy.start()
    held = gains.shape[1] // LANES
    for row in range(held):
        gains[:, row * LANES : (row + 1) * LANES] = small[row : row + 1, :]
    for row in range(biases.shape[1] // LANES):
        biases[:, row * LANES : (row + 1) * LANES] = small[held + row : held + row + 1, :]
    row = held + biases.shape[1] // LANES
    router[...] = small[row : row + 1, :]
    micro = means.shape[1]
    means[...] = small[row + 1 : row + 2, :micro] / small[row + 1 : row + 2, micro : 2 * micro]
    for k in range(count):
        take(k).wait()
        if k >= slots:
            give(k - slots).wait()
        high[k % slots] = low[k % slots].astype(F32)
        give(k).start()
        if k + slots < count:
            fetch(k + slots)
        if k < 2:
            passed[k][0].wait()
            passed[k][1].start()
    for k in range(count - slots, count):
        give(k).wait()
    for _, copy in passed:
        copy.wait()


def cast_sums(sums, small, acts, slopes, shapes, micro):
    anywhere = pl.BlockSpec(memory_space=pl.ANY)
    inside = pl.BlockSpec(memory_space=pltpu.VMEM)
    outs = [(shape, F32) for shape in shapes] + [((1, LANES), F32), ((1, micro), F32)]
    outs += [((1, *value.shape), BF16) for value in (acts, slopes)]
    return pl.pallas_call(
        cast_kernel,
        out_shape=[jax.ShapeDtypeStruct(*one) for one in outs],
        in_specs=[anywhere] * 2 + [inside] + [anywhere] * 2,
        out_specs=[anywhere] * 4 + [inside] * 4 + [anywhere] * 2,
        scratch_shapes=[
            pltpu.VMEM((4, LANES, LANES), BF16),
            pltpu.VMEM((4, LANES, LANES), F32),
            pltpu.VMEM((2, *acts.shape), BF16),
            pltpu.SemaphoreType.DMA((4,)),
            pltpu.SemaphoreType.DMA((4,)),
            pltpu.SemaphoreType.DMA((2,)),
        ],
        compiler_params=pltpu.CompilerParams(vmem_limit_bytes=60 * 1024 * 1024),
        cost_estimate=pl.CostEstimate(flops=0, bytes_accessed=50 * 10**6, transcendentals=0),
        name="cast",
    )(*sums, small, acts, slopes)


STEP = 256
NEGATIVE = -1e30


def dot(left, right, dims=NN):
    return lax.dot_general(left, right, dims, preferred_element_type=F32)


def gelu_parts(pre):
    bell = jnp.exp(pre * pre * -0.5)
    t = pl.reciprocal(1.0 + jnp.abs(pre) * (0.3275911 * 0.7071067811865476))
    poly = t * (0.1274147960 + t * (-0.142248368 + t * (0.710706871 + t * (-0.7265760135 + t * 0.5307027145))))
    tail = poly * bell
    return jnp.where(pre >= 0.0, 1.0 - tail, tail), bell


def norm_stats(values):
    centred = values - jnp.mean(values, axis=-1, keepdims=True)
    recip = lax.rsqrt(jnp.mean(centred * centred, axis=-1, keepdims=True) + 1e-06)
    return centred * recip, recip


def fold(tile):
    return jnp.sum(tile.reshape(tile.shape[0] // 8, 8, tile.shape[1]), axis=0)


def front_names(r, given, full):
    r.weights = [next(given) for _ in range(4)]
    r.w_sem, r.n1, r.qkv, r.probs, r.mask, r.mix, r.between, r.n2, r.act = (next(given) for _ in range(9))
    if not full:
        r.pre = [next(given) for _ in range(2)]
    r.act_part = [next(given) for _ in range(2)]


def back_names(r, given, scaled):
    r.n1t, r.n2t = (next(given) for _ in range(2))
    r.mixt = r.n2t
    r.dmlp = next(given) if scaled else r.dout
    r.dpre, r.dn = (next(given) for _ in range(2))
    r.pre = [r.dn.at[:, pl.ds(side * STEP, STEP)] for side in range(2)]
    r.dqkv = r.dpre.at[:, pl.ds(0, 3 * LANES)]
    r.datt, r.dmix = r.n1, r.mix
    r.dpre_part = [next(given) for _ in range(2)]
    r.down_stage, r.up_stage, r.down_sem, r.up_sem = (next(given) for _ in range(4))


def use_weights(r, layer):
    core = lax.axis_index("section")

    def weight(which, source):
        return pltpu.make_async_copy(source[which].at[0], r.weights[which], r.w_sem.at[which])

    for near, source in ((core == layer, r.own), (core != layer, r.far)):

        @pl.when(near)
        def _():
            for which in range(4):
                weight(which, source).start()

    r.ready = lambda which: weight(which, r.own).wait()


def layer_kernel(groups, window, chunks, *refs):
    r = Names()
    given = iter(refs)
    r.x, r.col_code, r.row_code, r.vec = (next(given) for _ in range(4))
    r.own = [next(given) for _ in range(4)]
    r.far = [next(given) for _ in range(4)]
    r.unsort, r.dout = (next(given) for _ in range(2))
    r.shown_du, r.small, r.grads, r.du, r.shown_y, landed, carry = (next(given) for _ in range(7))
    front_names(r, given, True)
    back_names(r, given, False)
    r.y, r.shown_sem = r.n2, next(given)
    jobs = {j: (start, 0, stage) for j, (start, stage) in enumerate(REDUCED)}
    sums = Sums(chunks, jobs, {0: 0, 1: 12}, given, False)
    sums.grads, sums.landed, sums.carry = (None, r.grads), (None, landed), carry
    use_weights(r, 1)
    sums.open()
    r.tile_out = functools.partial(sums.tile_out, 1)
    r.hooks = {at: sums.moment for at in (4, 7, 8)}
    r.hooks[3] = lambda: sums.prepare(0)
    layer_body(r, groups, window, True, False)
    while sums.now < sums.end:
        sums.moment()
    for j in jobs:
        for c in sums.each(j):
            sums.carried(j, c, True).start()
    sums.wait_tiles(1, 24)
    for j in jobs:
        for c in sums.each(j):
            sums.carried(j, c, True).wait()


def start_kernel(groups, window, *refs):
    r = Names()
    given = iter(refs)
    lengths, route_mask, tokens, cotangent, router, own_vec = (next(given) for _ in range(6))
    own = [next(given) for _ in range(4)]
    far = [next(given) for _ in range(4)]
    vecs = [next(given) for _ in range(2)]
    r.all_y, r.shown_y, r.delta, cot, r.x = (next(given) for _ in range(5))
    col_codes = [next(given) for _ in range(2)]
    row_codes = [next(given) for _ in range(2)]
    r.unsort, pick, r.unpick, r.skipped, r.scale, factor, extra = (next(given) for _ in range(7))
    front_names(r, given, False)
    r.y, r.all_x, order, raw, far_vec, raw_sem = (next(given) for _ in range(6))
    far_send, far_recv, vec_sem = (next(given) for _ in range(3))
    core = lax.axis_index("section")
    across = (1 - core, lax.axis_index("dp"))
    rows, width = r.all_x.shape
    half = rows // 2

    def fetch(k, source):
        return pltpu.make_async_copy(source.at[core], raw.at[k], raw_sem.at[k])

    fetch(0, tokens).start()
    fetch(1, cotangent).start()
    barrier = pltpu.get_barrier_semaphore()
    pl.semaphore_signal(barrier, inc=1, device_id=across, device_id_type=pl.DeviceIdType.MESH)
    pl.semaphore_wait(barrier, 1)

    def lend(which):
        return copy_far(own[which], far[which], far_send.at[which], far_recv.at[which], across)

    lend_vec = copy_far(own_vec, far_vec, vec_sem.at[0], vec_sem.at[1], across)
    lend_vec.start()
    lend(0).start()

    def weight(which, source):
        return pltpu.make_async_copy(source[which].at[0], r.weights[which], r.w_sem.at[which])

    def take_own():
        for which in range(4):
            weight(which, own).start()

    at_core(core, 0, take_own)

    def ready(which):
        def arrive():
            lend(which).wait_recv()
            weight(which, far).start()

        at_core(core, 1, arrive)
        weight(which, own).wait()

    r.ready = ready

    starts, bases, total, longs, short = [], [], 0, 0, 0
    count = lengths.shape[2]
    sizes = [lengths[core, 0, c] for c in range(count)]
    for size in sizes:
        is_long = size == LONG
        starts.append(total)
        bases.append(jnp.where(is_long, longs * LONG, 2 * LONG + short))
        total = total + size
        longs = longs + jnp.where(is_long, 1, 0)
        short = short + jnp.where(is_long, 0, size)

    def place(shape, dim):
        return lax.broadcasted_iota(jnp.int32, shape, dim)

    def target(at):
        moved = at
        for start, size, base in zip(starts, sizes, bases):
            moved = moved + jnp.where((at >= start) & (at < start + size), base - start, 0)
        return moved

    def code_of(at):
        return sum(jnp.where(at >= base, 1, 0) for base in bases)

    row_at, col_at = place((1, rows), 1), place((rows, 1), 0)

    def one_hot(left, right):
        return jnp.where(left == right, 1.0, 0.0).astype(BF16)

    goes_row, goes_col = target(row_at), target(col_at)
    row_codes[1][...] = code_of(row_at)
    col_codes[1][...] = code_of(col_at)
    for start in range(0, rows, 128):
        here = slice(start, start + 128)
        order[here, :] = one_hot(col_at[here], goes_row)
        r.unsort[here, :] = one_hot(goes_col[here], row_at)
    lend(1).start()
    lend(2).start()
    lend(3).start()
    for k, (source, moved) in enumerate(((tokens, r.all_x), (cotangent, cot))):
        fetch(k, source).wait()
        moved[...] = dot(order[...], raw[k]).astype(BF16)

    mask = jnp.where(route_mask[pl.ds(core, 1), :] == 1, 1.0, 0.0)
    masks = jnp.broadcast_to(mask, (8, rows)).astype(BF16)
    chosen_row = dot(masks, r.unsort[...])
    chosen_col = dot(order[...], masks, NT)
    earlier = jnp.where(place((rows, rows), 0) < place((rows, rows), 1), 1.0, 0.0).astype(BF16)
    rank_row = dot(chosen_row.astype(BF16), earlier)[:1]
    later = jnp.where(place((rows, rows), 0) > place((rows, rows), 1), 1.0, 0.0).astype(BF16)
    rank_col = dot(later, chosen_col.astype(BF16))[:, :1]
    chosen_row, chosen_col = chosen_row[:1], chosen_col[:, :1]
    r.skipped[...] = 1.0 - chosen_col
    key_row = jnp.where(chosen_row > 0.5, rank_row, -1.0)
    key_col = jnp.where(chosen_col > 0.5, rank_col, -1.0)
    pick[...] = one_hot(place((half, 1), 0).astype(F32), key_row)
    r.unpick[...] = one_hot(key_col, place((1, half), 1).astype(F32))
    names_row = jnp.broadcast_to(code_of(row_at).astype(F32), (8, rows)).astype(BF16)
    routed_row = dot(names_row, r.unpick[...])[:1]
    routed_col = dot(pick[...], names_row, NT)[:, :1]
    row_codes[0][...] = routed_row.astype(jnp.int32)
    col_codes[0][...] = routed_col.astype(jnp.int32)
    r.x[...] = dot(pick[...], r.all_x[...]).astype(BF16)
    logit = jnp.sum(r.x[...].astype(F32) * router[...], axis=1, keepdims=True)
    gate = 1.0 / (1.0 + jnp.exp(-logit))
    held = jnp.where(routed_col > 0.5, 1.0, 0.0)
    r.scale[...] = held * gate
    factor[...] = held * gate * (1.0 - gate)
    gates, counts = jnp.sum(held * gate, axis=0, keepdims=True), jnp.sum(mask, axis=1, keepdims=True)
    lane = place((1, width), 1)
    micro = tokens.shape[0]
    extra[...] = jnp.where(lane == core, gates, jnp.where(lane == core + micro, counts, 0.0))

    lend_vec.wait()
    for layer in range(2):
        vecs[layer][...] = jnp.where(core == layer, own_vec[...], far_vec[...])
    r.vec, r.col_code, r.row_code, r.own = vecs[0], col_codes[0], row_codes[0], own
    r.hooks = {}
    layer_body(r, groups, window, False, True)
    for which in range(4):
        lend(which).wait_send()
        at_core(core, 0, lambda which=which: lend(which).wait_recv())


def fused_kernel(groups, window, chunks, *refs):
    r = Names()
    given = iter(refs)
    r.x, r.col_code, r.row_code, r.vec, r.scale = (next(given) for _ in range(5))
    r.own = [next(given) for _ in range(4)]
    r.far = [next(given) for _ in range(4)]
    r.unsort = next(given)
    r.all_dout, r.pick, r.unpick, r.skipped, r.delta, r.factor, r.router = (next(given) for _ in range(7))
    second, second_landed, carry, second_small, extra = (next(given) for _ in range(5))
    shown = [next(given) for _ in range(3)]
    full = [next(given) for _ in range(2)]
    first_landed, first, small_out = (next(given) for _ in range(3))
    shown_out = [next(given) for _ in range(2)]
    front_names(r, given, True)
    back_names(r, given, True)
    r.dout, r.du, r.shown_du, r.small, r.router_grad = (next(given) for _ in range(5))
    bits = len(chunks[0][0][2])
    last = bits + min(bits, HALVINGS)
    reduced = len(REDUCED)
    jobs = {j: (start, REDUCED[j][1] if j < reduced else 0, last) for j, start in enumerate(GROUP_STARTS)}
    sums = Sums(chunks, jobs, {3: 0, 4: 12, 5: 24}, given, True)
    sums.grads, sums.landed, sums.full = (first, second), (first_landed, second_landed), full
    sums.carry, sums.small_out = carry, small_out
    sums.shown, sums.shown_out = (shown[0], shown[1], r.shown_du, shown[2]), shown_out
    r.grads = first
    use_weights(r, 0)
    sums.open()
    for j in range(reduced):
        for c in sums.each(j):
            sums.carried(j, c, False).start()
    for j, (start, first_stage, _) in jobs.items():
        if start == 0 and first_stage == 0:
            sums.prepare(j)
    r.tile_out = functools.partial(sums.tile_out, 0)
    r.hooks = {at: sums.moment for at in (0, 1, 2, 3, 8, 9)}
    layer_body(r, groups, window, True, True)

    for index, source in enumerate((r.small, second_small)):
        for row in range(source.shape[1] // LANES):
            sums.small[index, row : row + 1, :] = source[:, row * LANES : (row + 1) * LANES]
        row = source.shape[1] // LANES
        sums.small[index, row : row + 1, :] = r.router_grad[...]
        sums.small[index, row + 1 : row + 2, :] = extra[...]
        left = sums.small.shape[1] - row - 2
        sums.small[index, row + 2 :, :] = jnp.zeros((left, LANES), F32)
    sums.small_begin()
    sums.show()

    for turn in range(max(sums.end - sums.now, sums.bits + 1)):
        if sums.now < sums.end:
            sums.moment()
        if turn <= sums.bits:
            sums.small_turn(turn)
    sums.close()


def layer_body(r, groups, window, full, is_router):
    def hook(at):
        if at in r.hooks:
            r.hooks[at]()

    rows, width = r.x.shape
    hidden = r.own[2].shape[2]
    pairs = width // 128
    row_tile = rows // 5

    def vec(start, count=width):
        return r.vec[:, start : start + count]

    g1, g2, b1, bq, bv, bo, b2 = (vec(k * width) for k in range(7))
    bu_at, bd_at = 7 * width, 7 * width + hidden

    def row_loop(step, init=0):
        def at(k, carry):
            return step(pl.ds(pl.multiple_of(k * row_tile, row_tile), row_tile), carry)

        return lax.fori_loop(0, rows // row_tile, at, init)

    def norm_step(source, gain, bias, target):
        def step(here, carry):
            normal, _ = norm_stats(source[here, :].astype(F32))
            target[here, :] = (normal * gain + bias).astype(BF16)
            return carry

        return step

    def tiles(step):
        for k in range(width // STEP):
            step(slice(k * STEP, (k + 1) * STEP))

    def show(source, target):
        def step(span):
            target[:, span] = dot(r.unsort[...], source[:, span]).astype(BF16)

        tiles(step)

    def spread(routed, others, target, shown):
        def step(span):
            value = dot(r.unpick[...], routed[:, span]) + others[:, span].astype(F32) * r.skipped[...]
            if target is not None:
                target[:, span] = value.astype(BF16)
            shown[:, span] = dot(r.unsort[...], value.astype(BF16)).astype(BF16)

        tiles(step)

    row_loop(norm_step(r.x, g1, b1, r.n1))
    if full and is_router:

        def route_step(span):
            r.dout[:, span] = dot(r.pick[...], r.all_dout[:, span]).astype(BF16)

        tiles(route_step)
    if full:

        def delta_step(here, carry):
            low = r.dout[here, :]
            if is_router:
                low = (low.astype(F32) * r.scale[here, :]).astype(BF16)
                r.dmlp[here, :] = low
            return carry + fold(low.astype(F32))

        dbd = row_loop(delta_step, jnp.zeros((8, width), F32))
        r.small[:, bd_at:] = jnp.sum(dbd, axis=0, keepdims=True)

    for k, (start, low, high) in enumerate(groups):
        col = r.col_code[start : start + window, :]
        row = r.row_code[:, start : start + window]
        place = lax.broadcasted_iota(jnp.int32, (window, 1), 0) + start
        col = jnp.where((place >= low) & (place < high), col, -1)
        r.mask[k] = jnp.where(col == row, 0.0, NEGATIVE)

    r.ready(0)
    for k in range(3 * width // STEP):
        span = slice(k * STEP, (k + 1) * STEP)
        value = dot(r.n1[...], r.weights[0][:, span])
        if k < width // STEP:
            value = (value + bq[:, span]).astype(BF16).astype(F32) * 0.125
        elif k >= 2 * width // STEP:
            value = value + bv[:, k * STEP - 2 * width : (k + 1) * STEP - 2 * width]
        r.qkv[:, span] = value.astype(BF16)

    hook(0)
    lane = lax.broadcasted_iota(jnp.int32, (1, 128), 1)

    def halves(block):
        zero = jnp.zeros_like(block)
        return jnp.concatenate([jnp.where(lane < 64, block, zero), jnp.where(lane < 64, zero, block)], axis=0)

    high_half = lax.broadcasted_iota(jnp.int32, (128, 1), 0) >= 64

    def own_half(both):
        return jnp.where(high_half, both[:, window:], both[:, :window]).T

    r.mix[...] = jnp.zeros_like(r.mix)

    def lanes(pair, part):
        return pl.ds(pl.multiple_of(pair * 128 + part * width, 128), 128)

    spots = [slice(start, start + window) for start, _, _ in groups]
    count = len(groups)

    def qkv_at(pair, part):
        return [r.qkv[here, lanes(pair, part)] for here in spots]

    def attend(pair, carry):
        q, key, v = (qkv_at(pair, part) for part in range(3))
        scores = [dot(key[k], halves(q[k]), NT) for k in range(count)]
        probs = []
        for k, (start, low, high) in enumerate(groups):
            mask = r.mask[k]
            masked = scores[k] + jnp.concatenate([mask, mask], axis=1)
            place = lax.broadcasted_iota(jnp.int32, (1, window), 1) + start
            valid = (place >= low) & (place < high)
            valid = jnp.concatenate([valid, valid], axis=1)
            power = jnp.exp(masked - jnp.max(masked, axis=0, keepdims=True))
            total = jnp.sum(power, axis=0, keepdims=True)
            prob = (power * jnp.where(valid, 1.0 / total, 0.0)).astype(BF16)
            if full:
                r.probs[pair * count + k] = prob
            probs.append(prob)
        mixed = [dot(v[k].T, probs[k]) for k in range(count)]
        for k, here in enumerate(spots):
            r.mix[here, lanes(pair, 0)] = r.mix[here, lanes(pair, 0)] + own_half(mixed[k]).astype(BF16)
        return carry

    lax.fori_loop(0, pairs, attend, 0)

    r.ready(1)
    for k in range(width // STEP):
        span = slice(k * STEP, (k + 1) * STEP)
        value = dot(r.mix[...], r.weights[1][:, span]) + bo[:, span]
        r.between[:, span] = r.x[:, span].astype(F32) + value
    row_loop(norm_step(r.between, g2, b2, r.n2))
    if full:
        r.n1t[...] = r.n1[...].T
        r.n2t[...] = r.n2[...].T
    hook(1)

    r.ready(2)
    if full:
        r.ready(3)

    def down_out(k, slot):
        r.tile_out(
            r.down_stage.at[slot], pl.multiple_of(k * STEP, STEP), 0, (STEP, width), r.down_sem.at[slot], k
        )

    def side_out(block, k, slot):
        row = pl.multiple_of((block + k // 3) * width, width)
        column = pl.multiple_of(k % 3 * STEP, STEP)
        tile = k + {4: 12, 8: 24, 9: 27}[block]
        r.tile_out(r.up_stage.at[slot], row, column, (width, STEP), r.up_sem.at[slot], tile)

    def down_free(slot):
        target = r.grads.at[pl.ds(0, STEP), pl.ds(0, width)]
        pltpu.make_async_copy(r.down_stage.at[slot], target, r.down_sem.at[slot]).wait()

    def side_free(slot):
        target = r.grads.at[pl.ds(0, width), pl.ds(0, STEP)]
        pltpu.make_async_copy(r.up_stage.at[slot], target, r.up_sem.at[slot]).wait()

    steps = hidden // STEP

    def part_at(k):
        return pl.multiple_of(k * STEP, STEP)

    def ahead(k, side):
        at = part_at(k)
        r.pre[side][...] = dot(r.n2[...], r.weights[2][:, pl.ds(at, STEP)]) + r.vec[:, pl.ds(at + bu_at, STEP)]

    def middle(k, side):
        at = part_at(k)
        span = pl.ds(at, STEP)
        pre = r.pre[side][...]
        cdf, bell = gelu_parts(pre)
        act = (pre * cdf).astype(BF16)
        if not (full and is_router):
            r.act[:, span] = act
        if full:
            r.act_part[side][...] = act
            slope = cdf + pre * bell * 0.3989422804014327
            dact = dot(r.dmlp[...], r.weights[3][span, :], NT)
            dpre = (dact * slope).astype(BF16)
            r.dpre[:, span] = dpre
            r.dpre_part[side][...] = dpre
            r.small[:, pl.ds(at + bu_at, STEP)] = jnp.sum(dpre.astype(F32), axis=0, keepdims=True)

    def weigh(side):
        r.down_stage[side] = dot(r.act_part[side][...], r.dmlp[...], TN).astype(BF16)
        r.up_stage[side] = dot(r.n2t[...], r.dpre_part[side][...]).astype(BF16)

    def send_out(k, side):
        down_out(k, side)
        side_out(4, k, side)

    def two_steps(kk, first=False):
        even, odd = kk, kk + steps // 2
        if full and not first:

            @pl.when(kk >= 2)
            def _():
                down_free(1)
                side_free(1)

            down_free(0)
            side_free(0)
        middle(even, 0)
        ahead(odd, 1)
        if full and not first:
            weigh(1)
        middle(odd, 1)
        ahead(jnp.minimum(even + 1, steps // 2 - 1), 0)
        if full:
            weigh(0)
            if not first:
                send_out(odd - 1, 1)
            send_out(even, 0)

    def more_steps(kk, carry):
        two_steps(kk)
        return carry

    ahead(0, 0)
    two_steps(0, True)
    if 2 in r.hooks:
        lax.fori_loop(1, steps // 4, more_steps, 0)
        hook(2)
        lax.fori_loop(steps // 4, steps // 2, more_steps, 0)
    else:
        lax.fori_loop(1, steps // 2, more_steps, 0)
    if full:
        down_free(1)
        side_free(1)
        weigh(1)
        send_out(steps - 1, 1)
        for side in range(2):
            down_free(side)
            side_free(side)
        hook(3)
    if not full:
        r.ready(3)
    if not (full and is_router):
        for k in range(width // STEP):
            span = slice(k * STEP, (k + 1) * STEP)
            value = dot(r.act[...], r.weights[3][:, span]) + vec(bd_at)[:, span]
            source = r.x[:, span].astype(F32)
            value = r.between[:, span] - source + value
            if not full:
                r.delta[:, span] = value
            r.y[:, span] = (source + (r.scale[...] * value if is_router else value)).astype(BF16)
    if not full:
        spread(r.y, r.all_x, r.all_y, r.shown_y)
        return
    if not is_router:
        show(r.y, r.shown_du)
        r.shown_copy = pltpu.make_async_copy(r.shown_du, r.shown_y, r.shown_sem.at[0])
        r.shown_copy.start()

    r.dn[...] = dot(r.dpre[...], r.weights[2][...], NT)
    hook(4)

    def norm_back(source, gain, here):
        normal, recip = norm_stats(source[here, :].astype(F32))
        grad = r.dn[here, :]
        hat = grad * gain
        back = recip * (
            hat - jnp.mean(hat, axis=-1, keepdims=True) - normal * jnp.mean(hat * normal, axis=-1, keepdims=True)
        )
        return back, fold(grad * normal), fold(grad)

    def second_back(here, carry):
        back, dg, db = norm_back(r.between, g2, here)
        r.between[here, :] = back
        delta = r.dout[here, :].astype(F32)
        total = ((delta * r.scale[here, :] if is_router else delta) + back).astype(BF16)
        r.datt[here, :] = total
        return carry[0] + dg, carry[1] + db, carry[2] + fold(total.astype(F32))

    zero = jnp.zeros((8, width), F32)
    dg2, db2, dbo = row_loop(second_back, (zero, zero, zero))
    r.small[:, width : 2 * width] = jnp.sum(dg2, axis=0, keepdims=True)
    r.small[:, 6 * width : 7 * width] = jnp.sum(db2, axis=0, keepdims=True)
    r.small[:, 5 * width : 6 * width] = jnp.sum(dbo, axis=0, keepdims=True)

    hook(5)
    r.mixt[...] = r.mix[...].T
    r.dmix[...] = dot(r.datt[...], r.weights[1][...], NT).astype(BF16)
    for k in range(width // STEP):
        span = slice(k * STEP, (k + 1) * STEP)
        slot = k % 2
        if k >= 2:
            side_free(slot)
        r.up_stage[slot] = dot(r.mixt[...], r.datt[:, span]).astype(BF16)
        side_out(8, k, slot)
    hook(6)

    r.dqkv[...] = jnp.zeros((rows, 3 * width), BF16)

    def attend_back(pair, carry):
        q, key, v = (qkv_at(pair, part) for part in range(3))
        dm = [halves(r.dmix[here, lanes(pair, 0)]) for here in spots]
        dprobs = [dot(v[k], dm[k], NT) for k in range(count)]
        dv = [dot(r.probs[pair * count + k], dm[k]) for k in range(count)]
        ds = []
        for k in range(count):
            wide = r.probs[pair * count + k].astype(F32)
            product = wide * dprobs[k]
            ds.append((product - wide * jnp.sum(product, axis=0, keepdims=True)).astype(BF16))
        dk = [dot(ds[k], halves(q[k])) for k in range(count)]
        dq = [dot(key[k].T, ds[k]) for k in range(count)]
        for k, here in enumerate(spots):
            for part, value in enumerate((own_half(dq[k]) * 0.125, dk[k], dv[k])):
                spot = lanes(pair, part)
                r.dqkv[here, spot] = r.dqkv[here, spot] + value.astype(BF16)
        return carry

    if 7 in r.hooks:
        lax.fori_loop(0, pairs // 2, attend_back, 0)
        hook(7)
        lax.fori_loop(pairs // 2, pairs, attend_back, 0)
    else:
        lax.fori_loop(0, pairs, attend_back, 0)
    hook(8)

    for k in range(3 * width // STEP):
        span = slice(k * STEP, (k + 1) * STEP)
        block = r.dqkv[:, span]
        if not width <= k * STEP < 2 * width:
            at = 3 * width + k * STEP - (width if k * STEP >= width else 0)
            r.small[:, at : at + STEP] = jnp.sum(block.astype(F32), axis=0, keepdims=True)
        slot = (k + 1) % 2
        side_free(slot)
        r.up_stage[slot] = dot(r.n1t[...], block).astype(BF16)
        side_out(9, k, slot)
    side_free(0)
    side_free(1)
    hook(9)

    r.dn[...] = dot(r.dqkv[...], r.weights[0][...], NT)

    def first_back(here, carry):
        back, dg, db = norm_back(r.x, g1, here)
        dout = r.dout[here, :].astype(F32)
        total = dout + r.between[here, :] + back
        sums = [carry[0] + dg, carry[1] + db]
        if is_router:
            slope = jnp.sum(dout * r.delta[here, :], axis=1, keepdims=True) * r.factor[here, :]
            total = total + slope * r.router[...]
            sums.append(carry[2] + fold(slope * r.x[here, :].astype(F32)))
        r.du[here, :] = total.astype(BF16)
        return tuple(sums)

    sums = row_loop(first_back, (zero,) * (3 if is_router else 2))
    r.small[:, :width] = jnp.sum(sums[0], axis=0, keepdims=True)
    r.small[:, 2 * width : 3 * width] = jnp.sum(sums[1], axis=0, keepdims=True)
    if is_router:
        r.router_grad[...] = jnp.sum(sums[2], axis=0, keepdims=True)
        spread(r.du, r.all_dout, None, r.shown_du)
    else:
        r.shown_copy.wait()
        show(r.du, r.shown_du)


def front_scratch(rows, width, hidden, groups, window, full, keep_act):
    sizes = [(width, 3 * width), (width, width), (width, hidden), (hidden, width)]
    held = [pltpu.VMEM(size, BF16) for size in sizes]
    held += [pltpu.SemaphoreType.DMA((4,))]
    held += [pltpu.VMEM((rows, width), BF16), pltpu.VMEM((rows, 3 * width), BF16)]
    held += [pltpu.VMEM((HEADS // 2 * len(groups) if full else 1, window, 2 * window), BF16)]
    held += [pltpu.VMEM((len(groups), window, window), F32), pltpu.VMEM((rows, width), BF16)]
    held += [pltpu.VMEM((rows, width), F32), pltpu.VMEM((rows, width), BF16)]
    held += [pltpu.VMEM((rows, hidden) if keep_act else (TILE, LANES), BF16)]
    held += [pltpu.VMEM((rows, STEP), F32)] * (0 if full else 2)
    return held + [pltpu.VMEM((rows, STEP), BF16)] * 2


def back_scratch(rows, width, hidden, scaled):
    held = [pltpu.VMEM((width, rows), BF16)] * 2 + [pltpu.VMEM((rows, width), BF16)] * int(scaled)
    held += [pltpu.VMEM((rows, hidden), BF16), pltpu.VMEM((rows, width), F32)]
    held += [pltpu.VMEM((rows, STEP), BF16)] * 2
    held += [pltpu.VMEM((2, STEP, width), BF16), pltpu.VMEM((2, width, STEP), BF16)]
    return held + [pltpu.SemaphoreType.DMA((2,))] * 2


def run_start(groups, window, lengths, route_mask, tokens, cotangent, router_row, own_vec, own):
    _, rows, width = tokens.shape
    half, hidden = rows // 2, own[2].shape[2]
    inside = pl.BlockSpec(memory_space=pltpu.VMEM)
    anywhere = pl.BlockSpec(memory_space=pl.ANY)
    outs = [(value.shape, BF16) for value in own] + [(own_vec.shape, F32)] * 2
    outs += [((rows, width), BF16)] * 2 + [((half, width), F32), ((rows, width), BF16), ((half, width), BF16)]
    outs += [((half, 1), jnp.int32), ((rows, 1), jnp.int32), ((1, half), jnp.int32), ((1, rows), jnp.int32)]
    outs += [((rows, rows), BF16), ((half, rows), BF16), ((rows, half), BF16), ((rows, 1), F32)]
    outs += [((half, 1), F32)] * 2 + [((1, width), F32)]
    scratch = front_scratch(half, width, hidden, groups, window, False, True)
    scratch += [pltpu.VMEM((half, width), BF16), pltpu.VMEM((rows, width), BF16), pltpu.VMEM((rows, rows), BF16)]
    scratch += [pltpu.VMEM((2, rows, width), BF16), pltpu.VMEM(own_vec.shape, F32), pltpu.SemaphoreType.DMA((2,))]
    scratch += [pltpu.SemaphoreType.DMA((4,))] * 2 + [pltpu.SemaphoreType.DMA((2,))]
    return pl.pallas_call(
        functools.partial(start_kernel, groups, window),
        out_shape=[jax.ShapeDtypeStruct(*one) for one in outs],
        in_specs=[pl.BlockSpec(memory_space=pltpu.SMEM), inside] + [anywhere] * 2 + [inside] * 2 + [anywhere] * 4,
        out_specs=[anywhere] * 4 + [inside] * (len(outs) - 4),
        scratch_shapes=scratch,
        compiler_params=pltpu.CompilerParams(
            collective_id=1, has_side_effects=True, vmem_limit_bytes=60 * 1024 * 1024
        ),
        cost_estimate=pl.CostEstimate(flops=5 * 10**9, bytes_accessed=6 * 10**7, transcendentals=0),
        name="start",
    )(lengths, route_mask, tokens, cotangent, router_row, own_vec, *own)


def run_layer(axis_of, groups, window, x, col_code, row_code, vec, own, far, unsort, back):
    chunks = sum_plan(axis_of)
    reduced = len(REDUCED)
    rows, width = x.shape
    hidden = own[2].shape[2]
    inside = pl.BlockSpec(memory_space=pltpu.VMEM)
    anywhere = pl.BlockSpec(memory_space=pl.ANY)
    args = [x, col_code, row_code, vec, *own, *far, unsort, back]
    outs = [((rows, width), BF16), ((1, vec.shape[1]), F32), ((GRAD_ROWS, LANES), BF16)]
    outs += [((rows, width), BF16)] * 2 + [((GRAD_ROWS, LANES), BF16), ((reduced * GROUP_ROWS, LANES), BF16)]
    scratch = front_scratch(rows, width, hidden, groups, window, True, True)
    scratch += back_scratch(rows, width, hidden, False) + [pltpu.SemaphoreType.DMA((1,))]
    scratch += Sums.scratch(chunks, reduced, 0)
    flops = rows * width * (3 * width + width + 2 * hidden) * 6
    return pl.pallas_call(
        functools.partial(layer_kernel, groups, window, chunks),
        out_shape=[jax.ShapeDtypeStruct(*one) for one in outs],
        in_specs=[inside] * 4 + [anywhere] * 8 + [inside] * 2,
        out_specs=[inside] * 2 + [anywhere] + [inside] + [anywhere] * 3,
        scratch_shapes=scratch,
        compiler_params=pltpu.CompilerParams(
            collective_id=2, has_side_effects=True, vmem_limit_bytes=64 * 1024 * 1024
        ),
        cost_estimate=pl.CostEstimate(flops=flops, bytes_accessed=3 * 10**7, transcendentals=0),
        name="layer",
    )(*args)


def run_fused(axis_of, groups, window, x, col_code, row_code, vec, scale, own, far, rows_of, back, router, second, extra, shown):
    rows, width = x.shape
    hidden = own[2].shape[2]
    chunks = sum_plan(axis_of)
    inside = pl.BlockSpec(memory_space=pltpu.VMEM)
    anywhere = pl.BlockSpec(memory_space=pl.ANY)
    unsort, pick, unpick, skipped = rows_of
    delta, factor, router_row = router
    every = unsort.shape[0]
    args = [x, col_code, row_code, vec, scale, *own, *far, unsort]
    args += [back, pick, unpick, skipped, delta, factor, router_row]
    args += [*second, extra, *shown]
    small_rows = -(-(vec.shape[1] // LANES + 2) // 8) * 8
    outs = [((GRAD_ROWS, LANES), BF16)] * 4
    outs += [((small_rows, LANES), F32)] + [((2, every, width), BF16)] * 2
    scratch = front_scratch(rows, width, hidden, groups, window, True, False)
    scratch += back_scratch(rows, width, hidden, True)
    scratch += [pltpu.VMEM((rows, width), BF16)] * 2 + [pltpu.VMEM((every, width), BF16)]
    scratch += [pltpu.VMEM((1, vec.shape[1]), F32), pltpu.VMEM((1, width), F32)]
    scratch += Sums.scratch(chunks, GROUPS, small_rows)
    *sums, _, _, small, acts, grads = pl.pallas_call(
        functools.partial(fused_kernel, groups, window, chunks),
        out_shape=[jax.ShapeDtypeStruct(*one) for one in outs],
        in_specs=[inside] * 5 + [anywhere] * 8 + [inside] * 8 + [anywhere] * 3 + [inside] * 2 + [anywhere] * 3,
        out_specs=[anywhere] * 4 + [inside] + [anywhere] * 2,
        scratch_shapes=scratch,
        compiler_params=pltpu.CompilerParams(
            collective_id=0, has_side_effects=True, vmem_limit_bytes=64 * 1024 * 1024
        ),
        cost_estimate=pl.CostEstimate(flops=10**10, bytes_accessed=6 * 10**8, transcendentals=0),
        name="fused",
    )(*args)
    return sums, small, (acts, grads)


def body(axis_of, tokens, lengths, route_mask, router_weight, gains, biases, w_qkv, w_out, w_up, w_down, cotangent):
    micro, rows, width = tokens.shape
    own = (w_qkv, w_out, w_up, w_down)
    own_vec = jnp.concatenate([gains, biases], axis=1)
    router_row = router_weight.astype(F32)[None, :]
    half = LONG // 2
    groups_one = ((0, 0, half), (96, half, 2 * half), (192, 2 * half, rows // 2))
    groups_two = ((0, 0, LONG), (192, LONG, 2 * LONG), (384, 2 * LONG, rows))
    made = run_start(groups_one, 128, lengths, route_mask, tokens, cotangent, router_row, own_vec, own)
    far, (vec_one, vec_two), (y1, shown_y1, delta_one, cot, routed) = made[:4], made[4:6], made[6:11]
    col_one, col_two, row_one, row_two, *others = made[11:]
    unsort, pick, unpick, skipped, scale, factor, extra = others
    shown_du2, small_two, grads_two, dout, shown_y2, landed_two, carry = run_layer(
        axis_of, groups_two, 256, y1, col_two, row_two, vec_two, own, far, unsort, cot
    )
    sums, small, (activations, input_grads) = run_fused(
        axis_of, groups_one, 128, routed, col_one, row_one, vec_one, scale, own, far,
        (unsort, pick, unpick, skipped), dout, (delta_one, factor, router_row),
        (grads_two, landed_two, carry, small_two), extra,
        (shown_y1, shown_y2, shown_du2),
    )
    *grads, router_grad, means, activations, input_grads = cast_sums(
        sums, small, activations, input_grads,
        [value.shape for value in (*own, gains, biases)], micro,
    )
    return (activations, input_grads, *grads, router_grad[0], means[0])


def solution(mesh):
    in_specs = (
        P(None, "dp", None),
        P(None, "dp", None),
        P(None, "dp"),
        P(),
        P("section", None),
        P("section", None),
        P("section", None, None),
        P("section", None, None),
        P("section", None, None),
        P("section", None, None),
        P(None, "dp", None),
    )
    out_specs = (
        P("section", None, "dp", None),
        P("section", None, "dp", None),
        P("section", None, None),
        P("section", None, None),
        P("section", None, None),
        P("section", None, None),
        P("section", None),
        P("section", None),
        P(),
        P(),
    )
    step = functools.partial(body, axis_bits(mesh))
    return jax.shard_map(step, mesh=mesh, in_specs=in_specs, out_specs=out_specs, check_vma=False)
```

```python
import functools

import jax
import jax.numpy as jnp
from jax import lax
from jax.experimental import pallas as pl
from jax.experimental.pallas import tpu as pltpu
from jax.sharding import PartitionSpec as P

HEADS = 12
HEAD = 64
LONG = 197
F32 = jnp.float32
BF16 = jnp.bfloat16
NT = (((1,), (1,)), ((), ()))
TN = (((0,), (0,)), ((), ()))
NN = (((1,), (0,)), ((), ()))


LANES = 768
TILE = 16
GRAD_ROWS = 12 * LANES


def axis_bits(mesh):
    line = mesh.devices[0]
    bits = len(line).bit_length() - 1
    try:
        spots = [tuple(device.coords) for device in line]
    except AttributeError:
        return [0] * bits
    return [
        next((w for w in range(3) if spots[1 << b][w] != spots[0][w]), 0) for b in range(bits)
    ]


HALVINGS = 4
GROUPS = 6
SLOTS = 4


GROUP_PLAN = (
    ((768, 1023), (768, 132)),
    ((768, 123), (512, 1023), (256, 1203)),
    ((768, 123), (768, 1032)),
    ((512, 2103), (512, 123), (512, 1032)),
    ((768, 1023), (512, 2103), (256, 132)),
    ((512, 2013), (512, 132), (512, 1203)),
)
REDUCED = ((0, 2),)
GROUP_STARTS = (0, 1, 2, 4, 5, 7)


def sum_plan(axis_of):
    lists = {}
    for bit, axis in enumerate(axis_of):
        lists.setdefault(axis, []).append(bit)
    lists = sorted(lists.values(), key=len)
    while len(lists) < 3:
        lists.append([])
    roles = [lists[0][:1], lists[1][:1], lists[2][:1], lists[2][1:2]]
    plan = []
    for group in GROUP_PLAN:
        chunks, start = [], 0
        for size, code in group:
            order = [bit for place in (1000, 100, 10, 1) for bit in roles[code // place % 10]]
            order += [bit for bit in range(len(axis_of)) if bit not in order]
            chunks.append((start, size, order))
            start += size
        plan.append(chunks)
    return plan


def add_rows(into, into_start, source, start, other, other_start, count):
    tile = next(t for t in (64, 32, 16) if count % t == 0)

    def step(k, carry):
        target, here, there = (
            pl.ds(pl.multiple_of(first + k * tile, TILE), tile) for first in (into_start, start, other_start)
        )
        into[target, :] = source[here, :] + other[there, :]
        return carry

    lax.fori_loop(0, count // tile, step, 0)


class Names:
    pass


def copy_far(source, target, one, two, friend):
    return pltpu.make_async_remote_copy(
        src_ref=source,
        dst_ref=target,
        send_sem=one,
        recv_sem=two,
        device_id=friend,
        device_id_type=pl.DeviceIdType.MESH,
    )


def at_core(core, index, step):
    pl.when(core == index)(step)


GRAD_TILES = 36
GROUP_ROWS = GRAD_ROWS // GROUPS


class Sums:
    def __init__(self, chunks, jobs, tiles, given, whole):
        self.chunks, self.jobs, self.tiles = chunks, jobs, tiles
        self.bits = bits = len(chunks[0][0][2])
        self.halvings = min(bits, HALVINGS)
        self.acc, self.mate = next(given), next(given)
        self.got = [next(given) for _ in range(bits)]
        self.load_sem, self.mate_sem = (next(given) for _ in range(2))
        self.send, self.recv, self.back_send, self.back_recv = (next(given) for _ in range(4))
        self.tile_recv, self.ready = (next(given) for _ in range(2))
        if whole:
            self.small_got, self.small = next(given), next(given)
            self.small_send, self.small_recv = (next(given) for _ in range(2))
            self.shown_sem, self.shown_send, self.shown_recv = (next(given) for _ in range(3))
            self.give_send, self.give_recv, self.put_sem = (next(given) for _ in range(3))
        self.core = lax.axis_index("section")
        self.me = lax.axis_index("dp")
        self.across = (1 - self.core, self.me)
        self.end = max(start + last - first + 1 for start, first, last in jobs.values())
        self.now = 0

    @staticmethod
    def scratch(chunks, held_groups, small_rows):
        bits = len(chunks[0][0][2])
        count = sum(len(group) for group in chunks)
        rows = min(held_groups, SLOTS) * GROUP_ROWS
        held = [pltpu.VMEM((held_groups * GROUP_ROWS, LANES), BF16), pltpu.VMEM((GROUP_ROWS, LANES), BF16)]
        held += [pltpu.VMEM((rows >> min(depth + 1, HALVINGS), LANES), BF16) for depth in range(bits)]
        held += [pltpu.SemaphoreType.DMA((count,))] * 2
        held += [pltpu.SemaphoreType.DMA((count, bits))] * 4
        held += [pltpu.SemaphoreType.DMA((GRAD_TILES,))]
        held += [pltpu.SemaphoreType.REGULAR((count, min(bits, HALVINGS)))]
        if small_rows:
            held += [pltpu.VMEM((bits + 1, small_rows, LANES), F32), pltpu.VMEM((2, small_rows, LANES), F32)]
            held += [pltpu.SemaphoreType.DMA((bits + 1,))] * 2
            held += [pltpu.SemaphoreType.DMA((2,))] * 3
            held += [pltpu.SemaphoreType.DMA((GROUPS,))] * 3
        return held

    def bit_at(self, bit):
        return lax.rem(self.me // (1 << bit), 2)

    def partner(self, bit):
        return (self.core, self.me + (1 - 2 * self.bit_at(bit)) * (1 << bit))

    def open(self):
        friends = [self.across] + [self.partner(bit) for bit in range(self.bits)]
        barrier = pltpu.get_barrier_semaphore()
        for friend in friends:
            pl.semaphore_signal(barrier, inc=1, device_id=friend, device_id_type=pl.DeviceIdType.MESH)
        pl.semaphore_wait(barrier, len(friends))

    @staticmethod
    def layer_of(j):
        return 1 if j < GROUPS // 2 else 0

    def base(self, j, core):
        return (2 * (j % (GROUPS // 2)) + core) * GROUP_ROWS

    def rows_at(self, j, core, c):
        start, size, _ = self.chunks[j][c]
        return pl.ds(pl.multiple_of(self.base(j, core) + start, TILE), size)

    def index(self, j, c):
        return sum(len(group) for group in self.chunks[:j]) + c

    def load(self, j, c):
        start, size, _ = self.chunks[j][c]
        target = self.acc.at[pl.ds(j * GROUP_ROWS + start, size), :]
        source = self.grads[self.layer_of(j)].at[self.rows_at(j, self.core, c), :]
        return pltpu.make_async_copy(source, target, self.load_sem.at[self.index(j, c)])

    def load_mate(self, j, c):
        source = self.landed[self.layer_of(j)].at[self.rows_at(j, self.core, c), :]
        start, size, _ = self.chunks[j][c]
        target = self.mate.at[pl.ds(start, size), :]
        return pltpu.make_async_copy(source, target, self.mate_sem.at[self.index(j, c)])

    def span(self, j, c, depth):
        start, size, order = self.chunks[j][c]
        for bit in order[: min(depth, self.halvings)]:
            size //= 2
            start = start + self.bit_at(bit) * size
        return start, size

    def in_acc(self, j, start, size):
        return pl.ds(pl.multiple_of(j * GROUP_ROWS + start, TILE), size)

    def got_at(self, j, c, depth):
        return (j % SLOTS * GROUP_ROWS + self.chunks[j][c][0]) >> min(depth + 1, HALVINGS)

    def down(self, j, c, depth):
        bit = self.chunks[j][c][2][depth]
        start, size = self.span(j, c, depth)
        if depth < self.halvings:
            size //= 2
            start = start + (1 - self.bit_at(bit)) * size
        k = self.index(j, c)
        return copy_far(
            self.acc.at[self.in_acc(j, start, size), :],
            self.got[depth].at[pl.ds(self.got_at(j, c, depth), size), :],
            self.send.at[k, depth],
            self.recv.at[k, depth],
            self.partner(bit),
        )

    def up(self, j, c, depth):
        bit = self.chunks[j][c][2][depth]
        start, size = self.span(j, c, depth + 1)
        here = self.acc.at[self.in_acc(j, start, size), :]
        k = self.index(j, c)
        return copy_far(here, here, self.back_send.at[k, depth], self.back_recv.at[k, depth], self.partner(bit))

    def left(self, j, c, depth):
        self.down(j, c, depth).wait_send()
        if self.jobs[j][2] > self.bits:
            partner = self.partner(self.chunks[j][c][2][depth])
            pl.semaphore_signal(
                self.ready.at[self.index(j, c), depth], inc=1, device_id=partner, device_id_type=pl.DeviceIdType.MESH
            )

    def raise_up(self, j, c, depth):
        if depth >= self.jobs[j][1]:
            pl.semaphore_wait(self.ready.at[self.index(j, c), depth], 1)
        self.up(j, c, depth).start()

    def carried(self, j, c, keep):
        start, size = self.span(j, c, REDUCED[j][1])
        here = self.in_acc(j, start, size)
        pair = (self.acc.at[here, :], self.carry.at[here, :])
        return pltpu.make_async_copy(*(pair if keep else pair[::-1]), self.load_sem.at[self.index(j, c)])

    def wait_tiles(self, layer, first):
        for tile in range(6):
            area = self.landed[layer].at[pl.ds(0, LANES), pl.ds(0, STEP)]
            sem = self.tile_recv.at[first + self.core * 6 + tile]
            copy_far(area, area, sem, sem, self.across).wait_recv()

    def tile_out(self, layer, stage, row, column, shape, sem, tile):
        area = (pl.ds(row, shape[0]), pl.ds(column, shape[1]))
        owner = lax.rem(tile // 6, 2)

        @pl.when(self.core == owner)
        def _():
            pltpu.make_async_copy(stage, self.grads[layer].at[area], sem).start()

        @pl.when(self.core != owner)
        def _():
            copy_far(stage, self.landed[layer].at[area], sem, self.tile_recv.at[tile], self.across).start()

    def give(self, j, core):
        rows = pl.ds(self.base(j, core), GROUP_ROWS)
        source = self.acc.at[pl.ds(j * GROUP_ROWS, GROUP_ROWS), :]
        target = self.full[self.layer_of(j)].at[rows, :]
        return copy_far(source, target, self.give_send.at[j], self.give_recv.at[j], self.across)

    def put(self, j, core):
        rows = pl.ds(self.base(j, core), GROUP_ROWS)
        source = self.acc.at[pl.ds(j * GROUP_ROWS, GROUP_ROWS), :]
        return pltpu.make_async_copy(source, self.full[self.layer_of(j)].at[rows, :], self.put_sem.at[j])

    def each(self, j):
        return range(len(self.chunks[j]))

    def prepare(self, j):
        for c in self.each(j):
            self.load(j, c).start()
        if j in self.tiles:
            self.wait_tiles(self.layer_of(j), self.tiles[j])
        for c in self.each(j):
            self.load_mate(j, c).start()

    def moment(self):
        now, self.now = self.now, self.now + 1
        bits, halvings = self.bits, self.halvings
        order = sorted(self.jobs, key=lambda j: self.jobs[j][:2] != (now, 0))
        for j in order:
            start, first_stage, last_stage = self.jobs[j]
            stage = now - start + first_stage
            if not first_stage <= stage <= last_stage:
                continue
            for c in self.each(j):
                if stage == 0:
                    self.load(j, c).wait()
                    self.load_mate(j, c).wait()
                    first, size, _ = self.chunks[j][c]
                    at = j * GROUP_ROWS + first
                    add_rows(self.acc, at, self.acc, at, self.mate, first, size)
                    self.down(j, c, 0).start()
                elif stage == first_stage:
                    self.carried(j, c, False).wait()
                    self.down(j, c, stage).start()
                elif stage <= bits:
                    depth = stage - 1
                    if depth < halvings:
                        self.down(j, c, depth).wait_recv()
                        self.left(j, c, depth)
                    else:
                        self.down(j, c, depth).wait()
                    first, size = self.span(j, c, stage)
                    at = j * GROUP_ROWS + first
                    add_rows(self.acc, at, self.acc, at, self.got[depth], self.got_at(j, c, depth), size)
                    if stage < min(bits, last_stage):
                        self.down(j, c, stage).start()
                    elif stage < last_stage:
                        self.raise_up(j, c, halvings - 1)
                else:
                    depth = bits + halvings - stage
                    self.up(j, c, depth).wait_recv()
                    if depth > 0:
                        self.raise_up(j, c, depth - 1)
            if stage == bits + halvings:
                layer = self.layer_of(j)
                at_core(self.core, layer, lambda j=j, layer=layer: self.put(j, layer).start())
                at_core(self.core, 1 - layer, lambda j=j, layer=layer: self.give(j, 1 - layer).start())
        for j, (start, first_stage, _) in self.jobs.items():
            if start == now + 1 and first_stage == 0:
                self.prepare(j)

    def small_step(self, k):
        friend = self.across if k == 0 else self.partner(k - 1)
        return copy_far(
            self.small_out, self.small_got.at[k], self.small_send.at[k], self.small_recv.at[k], friend
        )

    def small_begin(self):
        for layer in range(2):

            def step(layer=layer):
                self.small_out[...] = self.small[layer]
                copy_far(
                    self.small.at[1 - layer], self.small_got.at[0], self.small_send.at[0], self.small_recv.at[0],
                    self.across,
                ).start()

            at_core(self.core, layer, step)

    def small_turn(self, k):
        self.small_step(k).wait()
        self.small_out[...] = self.small_out[...] + self.small_got[k]
        if k < self.bits:
            self.small_step(k + 1).start()

    def shown_keep(self, layer, k):
        return pltpu.make_async_copy(self.shown[2 * k + layer], self.shown_out[k].at[self.core], self.shown_sem.at[k])

    def shown_give(self, layer, k):
        return copy_far(
            self.shown[2 * k + 1 - layer], self.shown_out[k].at[self.core], self.shown_send.at[k],
            self.shown_recv.at[k], self.across,
        )

    def show(self):
        for layer in range(2):

            def step(layer=layer):
                for k in range(2):
                    self.shown_keep(layer, k).start()
                    self.shown_give(layer, k).start()

            at_core(self.core, layer, step)

    def close(self):
        for k in range(2):
            self.shown_keep(0, k).wait()
            self.shown_give(0, k).wait()
        for j in range(GROUPS):
            layer = self.layer_of(j)

            def kept(j=j, layer=layer):
                self.put(j, layer).wait()
                self.give(j, 1 - layer).wait_recv()

            at_core(self.core, layer, kept)
            at_core(self.core, 1 - layer, lambda j=j, layer=layer: self.give(j, 1 - layer).wait_send())
            for c in self.each(j):
                for depth in range(self.halvings):
                    self.up(j, c, depth).wait_send()


def cast_kernel(first, second, small, acts, slopes, qkv, out, up, down, *refs):
    gains, biases, router, means, acts_out, slopes_out, low, high, bounce, in_sem, out_sem, copy_sem = refs
    rows = low.shape[1]
    per = LANES // rows
    slots = low.shape[0]
    count = 12 * per
    core = lax.axis_index("section")
    passed = [
        (
            pltpu.make_async_copy(source, bounce.at[k], copy_sem.at[k]),
            pltpu.make_async_copy(bounce.at[k], target.at[0], copy_sem.at[k]),
        )
        for k, (source, target) in enumerate(((acts, acts_out), (slopes, slopes_out)))
    ]

    def take(k, source=first):
        return pltpu.make_async_copy(source.at[pl.ds(k * rows, rows), :], low.at[k % slots], in_sem.at[k % slots])

    def give(k):
        block, part = divmod(k, per)
        if block < 4:
            target = down.at[0, pl.ds(k * rows, rows), :]
        elif block < 8:
            target = up.at[0, pl.ds(part * rows, rows), pl.ds((block - 4) * LANES, LANES)]
        elif block < 9:
            target = out.at[0, pl.ds(part * rows, rows), :]
        else:
            target = qkv.at[0, pl.ds(part * rows, rows), pl.ds((block - 9) * LANES, LANES)]
        return pltpu.make_async_copy(high.at[k % slots], target, out_sem.at[k % slots])

    def fetch(k):
        at_core(core, 0, lambda: take(k).start())
        at_core(core, 1, lambda: take(k, second).start())

    for k in range(slots):
        fetch(k)
    for copy, _ in passed:
        copy.start()
    held = gains.shape[1] // LANES
    for row in range(held):
        gains[:, row * LANES : (row + 1) * LANES] = small[row : row + 1, :]
    for row in range(biases.shape[1] // LANES):
        biases[:, row * LANES : (row + 1) * LANES] = small[held + row : held + row + 1, :]
    row = held + biases.shape[1] // LANES
    router[...] = small[row : row + 1, :]
    micro = means.shape[1]
    means[...] = small[row + 1 : row + 2, :micro] / small[row + 1 : row + 2, micro : 2 * micro]
    for k in range(count):
        take(k).wait()
        if k >= slots:
            give(k - slots).wait()
        high[k % slots] = low[k % slots].astype(F32)
        give(k).start()
        if k + slots < count:
            fetch(k + slots)
        if k < 2:
            passed[k][0].wait()
            passed[k][1].start()
    for k in range(count - slots, count):
        give(k).wait()
    for _, copy in passed:
        copy.wait()


def cast_sums(sums, small, acts, slopes, shapes, micro):
    anywhere = pl.BlockSpec(memory_space=pl.ANY)
    inside = pl.BlockSpec(memory_space=pltpu.VMEM)
    outs = [(shape, F32) for shape in shapes] + [((1, LANES), F32), ((1, micro), F32)]
    outs += [((1, *value.shape), BF16) for value in (acts, slopes)]
    return pl.pallas_call(
        cast_kernel,
        out_shape=[jax.ShapeDtypeStruct(*one) for one in outs],
        in_specs=[anywhere] * 2 + [inside] + [anywhere] * 2,
        out_specs=[anywhere] * 4 + [inside] * 4 + [anywhere] * 2,
        scratch_shapes=[
            pltpu.VMEM((4, LANES, LANES), BF16),
            pltpu.VMEM((4, LANES, LANES), F32),
            pltpu.VMEM((2, *acts.shape), BF16),
            pltpu.SemaphoreType.DMA((4,)),
            pltpu.SemaphoreType.DMA((4,)),
            pltpu.SemaphoreType.DMA((2,)),
        ],
        compiler_params=pltpu.CompilerParams(vmem_limit_bytes=60 * 1024 * 1024),
        cost_estimate=pl.CostEstimate(flops=0, bytes_accessed=50 * 10**6, transcendentals=0),
        name="cast",
    )(*sums, small, acts, slopes)


STEP = 256
NEGATIVE = -1e30


def dot(left, right, dims=NN):
    return lax.dot_general(left, right, dims, preferred_element_type=F32)


def gelu_parts(pre):
    bell = jnp.exp(pre * pre * -0.5)
    t = pl.reciprocal(1.0 + jnp.abs(pre) * (0.3275911 * 0.7071067811865476))
    poly = t * (0.1274147960 + t * (-0.142248368 + t * (0.710706871 + t * (-0.7265760135 + t * 0.5307027145))))
    tail = poly * bell
    return jnp.where(pre >= 0.0, 1.0 - tail, tail), bell


def norm_stats(values):
    centred = values - jnp.mean(values, axis=-1, keepdims=True)
    recip = lax.rsqrt(jnp.mean(centred * centred, axis=-1, keepdims=True) + 1e-06)
    return centred * recip, recip


def fold(tile):
    return jnp.sum(tile.reshape(tile.shape[0] // 8, 8, tile.shape[1]), axis=0)


def front_names(r, given):
    r.weights = [next(given) for _ in range(4)]
    r.w_sem, r.n1, r.qkv, r.probs, r.mask, r.mix, r.between, r.n2, r.act = (next(given) for _ in range(9))
    r.pre = [next(given) for _ in range(2)]
    r.act_part = [next(given) for _ in range(2)]


def back_names(r, given, scaled):
    r.n1t, r.n2t = (next(given) for _ in range(2))
    r.mixt = r.n2t
    r.dmlp = next(given) if scaled else r.dout
    r.dpre, r.dn = (next(given) for _ in range(2))
    r.dqkv = r.dpre.at[:, pl.ds(0, 3 * LANES)]
    r.datt, r.dmix = r.n1, r.mix
    r.dpre_part = [next(given) for _ in range(2)]
    r.down_stage, r.up_stage, r.down_sem, r.up_sem = (next(given) for _ in range(4))


def use_weights(r, layer):
    core = lax.axis_index("section")

    def weight(which, source):
        return pltpu.make_async_copy(source[which].at[0], r.weights[which], r.w_sem.at[which])

    for near, source in ((core == layer, r.own), (core != layer, r.far)):

        @pl.when(near)
        def _():
            for which in range(4):
                weight(which, source).start()

    r.ready = lambda which: weight(which, r.own).wait()


def layer_kernel(groups, window, chunks, *refs):
    r = Names()
    given = iter(refs)
    r.x, r.col_code, r.row_code, r.vec = (next(given) for _ in range(4))
    r.own = [next(given) for _ in range(4)]
    r.far = [next(given) for _ in range(4)]
    r.unsort, r.dout = (next(given) for _ in range(2))
    r.shown_du, r.small, r.grads, r.du, r.shown_y, landed, carry = (next(given) for _ in range(7))
    front_names(r, given)
    back_names(r, given, False)
    r.y, r.shown_sem = r.n2, next(given)
    jobs = {j: (start, 0, stage) for j, (start, stage) in enumerate(REDUCED)}
    sums = Sums(chunks, jobs, {0: 0}, given, False)
    sums.grads, sums.landed, sums.carry = (None, r.grads), (None, landed), carry
    use_weights(r, 1)
    sums.open()
    r.tile_out = functools.partial(sums.tile_out, 1)
    r.hooks = {at: sums.moment for at in (4, 8)}
    r.hooks[3] = lambda: sums.prepare(0)
    layer_body(r, groups, window, True, False)
    while sums.now < sums.end:
        sums.moment()
    for j in jobs:
        for c in sums.each(j):
            sums.carried(j, c, True).start()
    sums.wait_tiles(1, 12)
    sums.wait_tiles(1, 24)
    for j in jobs:
        for c in sums.each(j):
            sums.carried(j, c, True).wait()


def start_kernel(groups, window, *refs):
    r = Names()
    given = iter(refs)
    lengths, route_mask, tokens, cotangent, router, own_vec = (next(given) for _ in range(6))
    own = [next(given) for _ in range(4)]
    far = [next(given) for _ in range(4)]
    vecs = [next(given) for _ in range(2)]
    r.all_y, r.shown_y, r.delta, cot, r.x = (next(given) for _ in range(5))
    col_codes = [next(given) for _ in range(2)]
    row_codes = [next(given) for _ in range(2)]
    r.unsort, pick, r.unpick, r.skipped, r.scale, factor, extra = (next(given) for _ in range(7))
    front_names(r, given)
    r.y, r.all_x, order, raw, far_vec, raw_sem = (next(given) for _ in range(6))
    far_send, far_recv, vec_sem = (next(given) for _ in range(3))
    core = lax.axis_index("section")
    across = (1 - core, lax.axis_index("dp"))
    rows, width = r.all_x.shape
    half = rows // 2

    def fetch(k, source):
        return pltpu.make_async_copy(source.at[core], raw.at[k], raw_sem.at[k])

    fetch(0, tokens).start()
    fetch(1, cotangent).start()
    barrier = pltpu.get_barrier_semaphore()
    pl.semaphore_signal(barrier, inc=1, device_id=across, device_id_type=pl.DeviceIdType.MESH)
    pl.semaphore_wait(barrier, 1)

    def lend(which):
        return copy_far(own[which], far[which], far_send.at[which], far_recv.at[which], across)

    lend_vec = copy_far(own_vec, far_vec, vec_sem.at[0], vec_sem.at[1], across)
    lend_vec.start()
    lend(0).start()

    def weight(which, source):
        return pltpu.make_async_copy(source[which].at[0], r.weights[which], r.w_sem.at[which])

    def take_own():
        for which in range(4):
            weight(which, own).start()

    at_core(core, 0, take_own)

    def ready(which):
        def arrive():
            lend(which).wait_recv()
            weight(which, far).start()

        at_core(core, 1, arrive)
        weight(which, own).wait()

    r.ready = ready

    starts, bases, total, longs, short = [], [], 0, 0, 0
    count = lengths.shape[2]
    sizes = [lengths[core, 0, c] for c in range(count)]
    for size in sizes:
        is_long = size == LONG
        starts.append(total)
        bases.append(jnp.where(is_long, longs * LONG, 2 * LONG + short))
        total = total + size
        longs = longs + jnp.where(is_long, 1, 0)
        short = short + jnp.where(is_long, 0, size)

    def place(shape, dim):
        return lax.broadcasted_iota(jnp.int32, shape, dim)

    def target(at):
        moved = at
        for start, size, base in zip(starts, sizes, bases):
            moved = moved + jnp.where((at >= start) & (at < start + size), base - start, 0)
        return moved

    def code_of(at):
        return sum(jnp.where(at >= base, 1, 0) for base in bases)

    row_at, col_at = place((1, rows), 1), place((rows, 1), 0)

    def one_hot(left, right):
        return jnp.where(left == right, 1.0, 0.0).astype(BF16)

    goes_row, goes_col = target(row_at), target(col_at)
    row_codes[1][...] = code_of(row_at)
    col_codes[1][...] = code_of(col_at)
    for start in range(0, rows, 128):
        here = slice(start, start + 128)
        order[here, :] = one_hot(col_at[here], goes_row)
        r.unsort[here, :] = one_hot(goes_col[here], row_at)
    lend(1).start()
    for k, (source, moved) in enumerate(((tokens, r.all_x), (cotangent, cot))):
        fetch(k, source).wait()
        moved[...] = dot(order[...], raw[k]).astype(BF16)

    mask = jnp.where(route_mask[pl.ds(core, 1), :] == 1, 1.0, 0.0)
    masks = jnp.broadcast_to(mask, (8, rows)).astype(BF16)
    chosen_row = dot(masks, r.unsort[...])
    chosen_col = dot(order[...], masks, NT)
    earlier = jnp.where(place((rows, rows), 0) < place((rows, rows), 1), 1.0, 0.0).astype(BF16)
    rank_row = dot(chosen_row.astype(BF16), earlier)[:1]
    later = jnp.where(place((rows, rows), 0) > place((rows, rows), 1), 1.0, 0.0).astype(BF16)
    rank_col = dot(later, chosen_col.astype(BF16))[:, :1]
    chosen_row, chosen_col = chosen_row[:1], chosen_col[:, :1]
    r.skipped[...] = 1.0 - chosen_col
    key_row = jnp.where(chosen_row > 0.5, rank_row, -1.0)
    key_col = jnp.where(chosen_col > 0.5, rank_col, -1.0)
    pick[...] = one_hot(place((half, 1), 0).astype(F32), key_row)
    r.unpick[...] = one_hot(key_col, place((1, half), 1).astype(F32))
    names_row = jnp.broadcast_to(code_of(row_at).astype(F32), (8, rows)).astype(BF16)
    routed_row = dot(names_row, r.unpick[...])[:1]
    routed_col = dot(pick[...], names_row, NT)[:, :1]
    row_codes[0][...] = routed_row.astype(jnp.int32)
    col_codes[0][...] = routed_col.astype(jnp.int32)
    r.x[...] = dot(pick[...], r.all_x[...]).astype(BF16)
    logit = jnp.sum(r.x[...].astype(F32) * router[...], axis=1, keepdims=True)
    gate = 1.0 / (1.0 + jnp.exp(-logit))
    held = jnp.where(routed_col > 0.5, 1.0, 0.0)
    r.scale[...] = held * gate
    factor[...] = held * gate * (1.0 - gate)
    gates, counts = jnp.sum(held * gate, axis=0, keepdims=True), jnp.sum(mask, axis=1, keepdims=True)
    lane = place((1, width), 1)
    micro = tokens.shape[0]
    extra[...] = jnp.where(lane == core, gates, jnp.where(lane == core + micro, counts, 0.0))

    lend_vec.wait()
    for layer in range(2):
        vecs[layer][...] = jnp.where(core == layer, own_vec[...], far_vec[...])
    r.vec, r.col_code, r.row_code, r.own = vecs[0], col_codes[0], row_codes[0], own
    r.hooks = {0: lambda: lend(2).start(), 1: lambda: lend(3).start()}
    layer_body(r, groups, window, False, True)
    for which in range(4):
        lend(which).wait_send()
        at_core(core, 0, lambda which=which: lend(which).wait_recv())


def fused_kernel(groups, window, chunks, *refs):
    r = Names()
    given = iter(refs)
    r.x, r.col_code, r.row_code, r.vec, r.scale = (next(given) for _ in range(5))
    r.own = [next(given) for _ in range(4)]
    r.far = [next(given) for _ in range(4)]
    r.unsort = next(given)
    r.all_dout, r.pick, r.unpick, r.skipped, r.delta, r.factor, r.router = (next(given) for _ in range(7))
    second, second_landed, carry, second_small, extra = (next(given) for _ in range(5))
    shown = [next(given) for _ in range(3)]
    full = [next(given) for _ in range(2)]
    first_landed, first, small_out = (next(given) for _ in range(3))
    shown_out = [next(given) for _ in range(2)]
    front_names(r, given)
    back_names(r, given, True)
    r.dout, r.du, r.shown_du, r.small, r.router_grad = (next(given) for _ in range(5))
    bits = len(chunks[0][0][2])
    last = bits + min(bits, HALVINGS)
    reduced = len(REDUCED)
    jobs = {j: (start, REDUCED[j][1] if j < reduced else 0, last) for j, start in enumerate(GROUP_STARTS)}
    sums = Sums(chunks, jobs, {3: 0, 4: 12, 5: 24}, given, True)
    sums.grads, sums.landed, sums.full = (first, second), (first_landed, second_landed), full
    sums.carry, sums.small_out = carry, small_out
    sums.shown, sums.shown_out = (shown[0], shown[1], r.shown_du, shown[2]), shown_out
    r.grads = first
    use_weights(r, 0)
    sums.open()
    for j in range(reduced):
        for c in sums.each(j):
            sums.carried(j, c, False).start()
    for j, (start, first_stage, _) in jobs.items():
        if start == 0 and first_stage == 0:
            sums.prepare(j)
    r.tile_out = functools.partial(sums.tile_out, 0)
    r.hooks = {at: sums.moment for at in (0, 1, 2, 3, 8, 9)}
    layer_body(r, groups, window, True, True)

    for index, source in enumerate((r.small, second_small)):
        for row in range(source.shape[1] // LANES):
            sums.small[index, row : row + 1, :] = source[:, row * LANES : (row + 1) * LANES]
        row = source.shape[1] // LANES
        sums.small[index, row : row + 1, :] = r.router_grad[...]
        sums.small[index, row + 1 : row + 2, :] = extra[...]
        left = sums.small.shape[1] - row - 2
        sums.small[index, row + 2 :, :] = jnp.zeros((left, LANES), F32)
    sums.small_begin()
    sums.show()

    for turn in range(max(sums.end - sums.now, sums.bits + 1)):
        if sums.now < sums.end:
            sums.moment()
        if turn <= sums.bits:
            sums.small_turn(turn)
    sums.close()


def layer_body(r, groups, window, full, is_router):
    def hook(at):
        if at in r.hooks:
            r.hooks[at]()

    rows, width = r.x.shape
    hidden = r.own[2].shape[2]
    pairs = width // 128
    row_tile = rows // 5

    def vec(start, count=width):
        return r.vec[:, start : start + count]

    g1, g2, b1, bq, bv, bo, b2 = (vec(k * width) for k in range(7))
    bu_at, bd_at = 7 * width, 7 * width + hidden

    def row_loop(step, init=0):
        def at(k, carry):
            return step(pl.ds(pl.multiple_of(k * row_tile, row_tile), row_tile), carry)

        return lax.fori_loop(0, rows // row_tile, at, init)

    def norm_step(source, gain, bias, target):
        def step(here, carry):
            normal, _ = norm_stats(source[here, :].astype(F32))
            target[here, :] = (normal * gain + bias).astype(BF16)
            return carry

        return step

    def tiles(step):
        for k in range(width // STEP):
            step(slice(k * STEP, (k + 1) * STEP))

    def show(source, target):
        def step(span):
            target[:, span] = dot(r.unsort[...], source[:, span]).astype(BF16)

        tiles(step)

    def spread(routed, others, target, shown):
        def step(span):
            value = dot(r.unpick[...], routed[:, span]) + others[:, span].astype(F32) * r.skipped[...]
            if target is not None:
                target[:, span] = value.astype(BF16)
            shown[:, span] = dot(r.unsort[...], value.astype(BF16)).astype(BF16)

        tiles(step)

    row_loop(norm_step(r.x, g1, b1, r.n1))
    if full and is_router:

        def route_step(span):
            r.dout[:, span] = dot(r.pick[...], r.all_dout[:, span]).astype(BF16)

        tiles(route_step)
    if full:

        def delta_step(here, carry):
            low = r.dout[here, :]
            if is_router:
                low = (low.astype(F32) * r.scale[here, :]).astype(BF16)
                r.dmlp[here, :] = low
            return carry + fold(low.astype(F32))

        dbd = row_loop(delta_step, jnp.zeros((8, width), F32))
        r.small[:, bd_at:] = jnp.sum(dbd, axis=0, keepdims=True)

    for k, (start, low, high) in enumerate(groups):
        col = r.col_code[start : start + window, :]
        row = r.row_code[:, start : start + window]
        place = lax.broadcasted_iota(jnp.int32, (window, 1), 0) + start
        col = jnp.where((place >= low) & (place < high), col, -1)
        r.mask[k] = jnp.where(col == row, 0.0, NEGATIVE)

    r.ready(0)
    for k in range(3 * width // STEP):
        span = slice(k * STEP, (k + 1) * STEP)
        value = dot(r.n1[...], r.weights[0][:, span])
        if k < width // STEP:
            value = (value + bq[:, span]).astype(BF16).astype(F32) * 0.125
        elif k >= 2 * width // STEP:
            value = value + bv[:, k * STEP - 2 * width : (k + 1) * STEP - 2 * width]
        r.qkv[:, span] = value.astype(BF16)

    hook(0)
    lane = lax.broadcasted_iota(jnp.int32, (1, 128), 1)

    def halves(block):
        zero = jnp.zeros_like(block)
        return jnp.concatenate([jnp.where(lane < 64, block, zero), jnp.where(lane < 64, zero, block)], axis=0)

    high_half = lax.broadcasted_iota(jnp.int32, (128, 1), 0) >= 64

    def own_half(both):
        return jnp.where(high_half, both[:, window:], both[:, :window]).T

    r.mix[...] = jnp.zeros_like(r.mix)

    def lanes(pair, part):
        return pl.ds(pl.multiple_of(pair * 128 + part * width, 128), 128)

    spots = [slice(start, start + window) for start, _, _ in groups]
    count = len(groups)

    def qkv_at(pair, part):
        return [r.qkv[here, lanes(pair, part)] for here in spots]

    def attend(pair, carry):
        q, key, v = (qkv_at(pair, part) for part in range(3))
        scores = [dot(key[k], halves(q[k]), NT) for k in range(count)]
        probs = []
        for k, (start, low, high) in enumerate(groups):
            mask = r.mask[k]
            masked = scores[k] + jnp.concatenate([mask, mask], axis=1)
            place = lax.broadcasted_iota(jnp.int32, (1, window), 1) + start
            valid = (place >= low) & (place < high)
            valid = jnp.concatenate([valid, valid], axis=1)
            power = jnp.exp(masked - jnp.max(masked, axis=0, keepdims=True))
            total = jnp.sum(power, axis=0, keepdims=True)
            prob = (power * jnp.where(valid, 1.0 / total, 0.0)).astype(BF16)
            if full:
                r.probs[pair * count + k] = prob
            probs.append(prob)
        mixed = [dot(v[k].T, probs[k]) for k in range(count)]
        for k, here in enumerate(spots):
            r.mix[here, lanes(pair, 0)] = r.mix[here, lanes(pair, 0)] + own_half(mixed[k]).astype(BF16)
        return carry

    lax.fori_loop(0, pairs, attend, 0)

    r.ready(1)
    for k in range(width // STEP):
        span = slice(k * STEP, (k + 1) * STEP)
        value = dot(r.mix[...], r.weights[1][:, span]) + bo[:, span]
        r.between[:, span] = r.x[:, span].astype(F32) + value
    row_loop(norm_step(r.between, g2, b2, r.n2))
    if full:
        r.n1t[...] = r.n1[...].T
        r.n2t[...] = r.n2[...].T
    hook(1)

    r.ready(2)
    if full:
        r.ready(3)

    def down_out(k, slot):
        r.tile_out(
            r.down_stage.at[slot], pl.multiple_of(k * STEP, STEP), 0, (STEP, width), r.down_sem.at[slot], k
        )

    def side_out(block, k, slot):
        row = pl.multiple_of((block + k // 3) * width, width)
        column = pl.multiple_of(k % 3 * STEP, STEP)
        tile = k + {4: 12, 8: 24, 9: 27}[block]
        r.tile_out(r.up_stage.at[slot], row, column, (width, STEP), r.up_sem.at[slot], tile)

    def down_free(slot):
        target = r.grads.at[pl.ds(0, STEP), pl.ds(0, width)]
        pltpu.make_async_copy(r.down_stage.at[slot], target, r.down_sem.at[slot]).wait()

    def side_free(slot):
        target = r.grads.at[pl.ds(0, width), pl.ds(0, STEP)]
        pltpu.make_async_copy(r.up_stage.at[slot], target, r.up_sem.at[slot]).wait()

    steps = hidden // STEP

    def part_at(k):
        return pl.multiple_of(k * STEP, STEP)

    def ahead(k, side):
        at = part_at(k)
        r.pre[side][...] = dot(r.n2[...], r.weights[2][:, pl.ds(at, STEP)]) + r.vec[:, pl.ds(at + bu_at, STEP)]

    def middle(k, side):
        at = part_at(k)
        span = pl.ds(at, STEP)
        pre = r.pre[side][...]
        cdf, bell = gelu_parts(pre)
        act = (pre * cdf).astype(BF16)
        if not (full and is_router):
            r.act[:, span] = act
        if full:
            r.act_part[side][...] = act
            slope = cdf + pre * bell * 0.3989422804014327
            dact = dot(r.dmlp[...], r.weights[3][span, :], NT)
            dpre = (dact * slope).astype(BF16)
            r.dpre[:, span] = dpre
            r.dpre_part[side][...] = dpre
            r.small[:, pl.ds(at + bu_at, STEP)] = jnp.sum(dpre.astype(F32), axis=0, keepdims=True)

    def weigh(side):
        r.down_stage[side] = dot(r.act_part[side][...], r.dmlp[...], TN).astype(BF16)
        r.up_stage[side] = dot(r.n2t[...], r.dpre_part[side][...]).astype(BF16)

    def send_out(k, side):
        down_out(k, side)
        side_out(4, k, side)

    def two_steps(kk, first=False):
        even, odd = kk, kk + steps // 2
        if full and not first:

            @pl.when(kk >= 2)
            def _():
                down_free(1)
                side_free(1)

            down_free(0)
            side_free(0)
        middle(even, 0)
        ahead(odd, 1)
        if full and not first:
            weigh(1)
        middle(odd, 1)
        ahead(jnp.minimum(even + 1, steps // 2 - 1), 0)
        if full:
            weigh(0)
            if not first:
                send_out(odd - 1, 1)
            send_out(even, 0)

    def more_steps(kk, carry):
        two_steps(kk)
        return carry

    ahead(0, 0)
    two_steps(0, True)
    if 2 in r.hooks:
        lax.fori_loop(1, steps // 4, more_steps, 0)
        hook(2)
        lax.fori_loop(steps // 4, steps // 2, more_steps, 0)
    else:
        lax.fori_loop(1, steps // 2, more_steps, 0)
    if full:
        down_free(1)
        side_free(1)
        weigh(1)
        send_out(steps - 1, 1)
        for side in range(2):
            down_free(side)
            side_free(side)
        hook(3)
    if not full:
        r.ready(3)
    if not (full and is_router):
        for k in range(width // STEP):
            span = slice(k * STEP, (k + 1) * STEP)
            value = dot(r.act[...], r.weights[3][:, span]) + vec(bd_at)[:, span]
            source = r.x[:, span].astype(F32)
            value = r.between[:, span] - source + value
            if not full:
                r.delta[:, span] = value
            r.y[:, span] = (source + (r.scale[...] * value if is_router else value)).astype(BF16)
    if not full:
        spread(r.y, r.all_x, r.all_y, r.shown_y)
        return
    if not is_router:
        show(r.y, r.shown_du)
        r.shown_copy = pltpu.make_async_copy(r.shown_du, r.shown_y, r.shown_sem.at[0])
        r.shown_copy.start()

    r.dn[...] = dot(r.dpre[...], r.weights[2][...], NT)
    hook(4)

    def norm_back(source, gain, here):
        normal, recip = norm_stats(source[here, :].astype(F32))
        grad = r.dn[here, :]
        hat = grad * gain
        back = recip * (
            hat - jnp.mean(hat, axis=-1, keepdims=True) - normal * jnp.mean(hat * normal, axis=-1, keepdims=True)
        )
        return back, fold(grad * normal), fold(grad)

    def second_back(here, carry):
        back, dg, db = norm_back(r.between, g2, here)
        r.between[here, :] = back
        delta = r.dout[here, :].astype(F32)
        total = ((delta * r.scale[here, :] if is_router else delta) + back).astype(BF16)
        r.datt[here, :] = total
        return carry[0] + dg, carry[1] + db, carry[2] + fold(total.astype(F32))

    zero = jnp.zeros((8, width), F32)
    dg2, db2, dbo = row_loop(second_back, (zero, zero, zero))
    r.small[:, width : 2 * width] = jnp.sum(dg2, axis=0, keepdims=True)
    r.small[:, 6 * width : 7 * width] = jnp.sum(db2, axis=0, keepdims=True)
    r.small[:, 5 * width : 6 * width] = jnp.sum(dbo, axis=0, keepdims=True)

    hook(5)
    r.mixt[...] = r.mix[...].T
    r.dmix[...] = dot(r.datt[...], r.weights[1][...], NT).astype(BF16)
    for k in range(width // STEP):
        span = slice(k * STEP, (k + 1) * STEP)
        slot = k % 2
        if k >= 2:
            side_free(slot)
        r.up_stage[slot] = dot(r.mixt[...], r.datt[:, span]).astype(BF16)
        side_out(8, k, slot)
    hook(6)

    r.dqkv[...] = jnp.zeros((rows, 3 * width), BF16)

    def attend_back(pair, carry):
        q, key, v = (qkv_at(pair, part) for part in range(3))
        dm = [halves(r.dmix[here, lanes(pair, 0)]) for here in spots]
        dprobs = [dot(v[k], dm[k], NT) for k in range(count)]
        dv = [dot(r.probs[pair * count + k], dm[k]) for k in range(count)]
        ds = []
        for k in range(count):
            wide = r.probs[pair * count + k].astype(F32)
            product = wide * dprobs[k]
            ds.append((product - wide * jnp.sum(product, axis=0, keepdims=True)).astype(BF16))
        dk = [dot(ds[k], halves(q[k])) for k in range(count)]
        dq = [dot(key[k].T, ds[k]) for k in range(count)]
        for k, here in enumerate(spots):
            for part, value in enumerate((own_half(dq[k]) * 0.125, dk[k], dv[k])):
                spot = lanes(pair, part)
                r.dqkv[here, spot] = r.dqkv[here, spot] + value.astype(BF16)
        return carry

    if 7 in r.hooks:
        lax.fori_loop(0, pairs // 2, attend_back, 0)
        hook(7)
        lax.fori_loop(pairs // 2, pairs, attend_back, 0)
    else:
        lax.fori_loop(0, pairs, attend_back, 0)
    hook(8)

    for k in range(3 * width // STEP):
        span = slice(k * STEP, (k + 1) * STEP)
        block = r.dqkv[:, span]
        if not width <= k * STEP < 2 * width:
            at = 3 * width + k * STEP - (width if k * STEP >= width else 0)
            r.small[:, at : at + STEP] = jnp.sum(block.astype(F32), axis=0, keepdims=True)
        slot = (k + 1) % 2
        side_free(slot)
        r.up_stage[slot] = dot(r.n1t[...], block).astype(BF16)
        side_out(9, k, slot)
    side_free(0)
    side_free(1)
    hook(9)

    r.dn[...] = dot(r.dqkv[...], r.weights[0][...], NT)

    def first_back(here, carry):
        back, dg, db = norm_back(r.x, g1, here)
        dout = r.dout[here, :].astype(F32)
        total = dout + r.between[here, :] + back
        sums = [carry[0] + dg, carry[1] + db]
        if is_router:
            slope = jnp.sum(dout * r.delta[here, :], axis=1, keepdims=True) * r.factor[here, :]
            total = total + slope * r.router[...]
            sums.append(carry[2] + fold(slope * r.x[here, :].astype(F32)))
        r.du[here, :] = total.astype(BF16)
        return tuple(sums)

    sums = row_loop(first_back, (zero,) * (3 if is_router else 2))
    r.small[:, :width] = jnp.sum(sums[0], axis=0, keepdims=True)
    r.small[:, 2 * width : 3 * width] = jnp.sum(sums[1], axis=0, keepdims=True)
    if is_router:
        r.router_grad[...] = jnp.sum(sums[2], axis=0, keepdims=True)
        spread(r.du, r.all_dout, None, r.shown_du)
    else:
        r.shown_copy.wait()
        show(r.du, r.shown_du)


def front_scratch(rows, width, hidden, groups, window, full, keep_act):
    sizes = [(width, 3 * width), (width, width), (width, hidden), (hidden, width)]
    held = [pltpu.VMEM(size, BF16) for size in sizes]
    held += [pltpu.SemaphoreType.DMA((4,))]
    held += [pltpu.VMEM((rows, width), BF16), pltpu.VMEM((rows, 3 * width), BF16)]
    held += [pltpu.VMEM((HEADS // 2 * len(groups) if full else 1, window, 2 * window), BF16)]
    held += [pltpu.VMEM((len(groups), window, window), F32), pltpu.VMEM((rows, width), BF16)]
    held += [pltpu.VMEM((rows, width), F32), pltpu.VMEM((rows, width), BF16)]
    held += [pltpu.VMEM((rows, hidden) if keep_act else (TILE, LANES), BF16)]
    held += [pltpu.VMEM((rows, STEP), F32)] * 2
    return held + [pltpu.VMEM((rows, STEP), BF16)] * 2


def back_scratch(rows, width, hidden, scaled):
    held = [pltpu.VMEM((width, rows), BF16)] * 2 + [pltpu.VMEM((rows, width), BF16)] * int(scaled)
    held += [pltpu.VMEM((rows, hidden), BF16), pltpu.VMEM((rows, width), F32)]
    held += [pltpu.VMEM((rows, STEP), BF16)] * 2
    held += [pltpu.VMEM((2, STEP, width), BF16), pltpu.VMEM((2, width, STEP), BF16)]
    return held + [pltpu.SemaphoreType.DMA((2,))] * 2


def run_start(groups, window, lengths, route_mask, tokens, cotangent, router_row, own_vec, own):
    _, rows, width = tokens.shape
    half, hidden = rows // 2, own[2].shape[2]
    inside = pl.BlockSpec(memory_space=pltpu.VMEM)
    anywhere = pl.BlockSpec(memory_space=pl.ANY)
    outs = [(value.shape, BF16) for value in own] + [(own_vec.shape, F32)] * 2
    outs += [((rows, width), BF16)] * 2 + [((half, width), F32), ((rows, width), BF16), ((half, width), BF16)]
    outs += [((half, 1), jnp.int32), ((rows, 1), jnp.int32), ((1, half), jnp.int32), ((1, rows), jnp.int32)]
    outs += [((rows, rows), BF16), ((half, rows), BF16), ((rows, half), BF16), ((rows, 1), F32)]
    outs += [((half, 1), F32)] * 2 + [((1, width), F32)]
    scratch = front_scratch(half, width, hidden, groups, window, False, True)
    scratch += [pltpu.VMEM((half, width), BF16), pltpu.VMEM((rows, width), BF16), pltpu.VMEM((rows, rows), BF16)]
    scratch += [pltpu.VMEM((2, rows, width), BF16), pltpu.VMEM(own_vec.shape, F32), pltpu.SemaphoreType.DMA((2,))]
    scratch += [pltpu.SemaphoreType.DMA((4,))] * 2 + [pltpu.SemaphoreType.DMA((2,))]
    return pl.pallas_call(
        functools.partial(start_kernel, groups, window),
        out_shape=[jax.ShapeDtypeStruct(*one) for one in outs],
        in_specs=[pl.BlockSpec(memory_space=pltpu.SMEM), inside] + [anywhere] * 2 + [inside] * 2 + [anywhere] * 4,
        out_specs=[anywhere] * 4 + [inside] * (len(outs) - 4),
        scratch_shapes=scratch,
        compiler_params=pltpu.CompilerParams(
            collective_id=1, has_side_effects=True, vmem_limit_bytes=60 * 1024 * 1024
        ),
        cost_estimate=pl.CostEstimate(flops=5 * 10**9, bytes_accessed=6 * 10**7, transcendentals=0),
        name="start",
    )(lengths, route_mask, tokens, cotangent, router_row, own_vec, *own)


def run_layer(axis_of, groups, window, x, col_code, row_code, vec, own, far, unsort, back):
    chunks = sum_plan(axis_of)
    reduced = len(REDUCED)
    rows, width = x.shape
    hidden = own[2].shape[2]
    inside = pl.BlockSpec(memory_space=pltpu.VMEM)
    anywhere = pl.BlockSpec(memory_space=pl.ANY)
    args = [x, col_code, row_code, vec, *own, *far, unsort, back]
    outs = [((rows, width), BF16), ((1, vec.shape[1]), F32), ((GRAD_ROWS, LANES), BF16)]
    outs += [((rows, width), BF16)] * 2 + [((GRAD_ROWS, LANES), BF16), ((reduced * GROUP_ROWS, LANES), BF16)]
    scratch = front_scratch(rows, width, hidden, groups, window, True, True)
    scratch += back_scratch(rows, width, hidden, False) + [pltpu.SemaphoreType.DMA((1,))]
    scratch += Sums.scratch(chunks, reduced, 0)
    flops = rows * width * (3 * width + width + 2 * hidden) * 6
    return pl.pallas_call(
        functools.partial(layer_kernel, groups, window, chunks),
        out_shape=[jax.ShapeDtypeStruct(*one) for one in outs],
        in_specs=[inside] * 4 + [anywhere] * 8 + [inside] * 2,
        out_specs=[inside] * 2 + [anywhere] + [inside] + [anywhere] * 3,
        scratch_shapes=scratch,
        compiler_params=pltpu.CompilerParams(
            collective_id=2, has_side_effects=True, vmem_limit_bytes=64 * 1024 * 1024
        ),
        cost_estimate=pl.CostEstimate(flops=flops, bytes_accessed=3 * 10**7, transcendentals=0),
        name="layer",
    )(*args)


def run_fused(axis_of, groups, window, x, col_code, row_code, vec, scale, own, far, rows_of, back, router, second, extra, shown):
    rows, width = x.shape
    hidden = own[2].shape[2]
    chunks = sum_plan(axis_of)
    inside = pl.BlockSpec(memory_space=pltpu.VMEM)
    anywhere = pl.BlockSpec(memory_space=pl.ANY)
    unsort, pick, unpick, skipped = rows_of
    delta, factor, router_row = router
    every = unsort.shape[0]
    args = [x, col_code, row_code, vec, scale, *own, *far, unsort]
    args += [back, pick, unpick, skipped, delta, factor, router_row]
    args += [*second, extra, *shown]
    small_rows = -(-(vec.shape[1] // LANES + 2) // 8) * 8
    outs = [((GRAD_ROWS, LANES), BF16)] * 4
    outs += [((small_rows, LANES), F32)] + [((2, every, width), BF16)] * 2
    scratch = front_scratch(rows, width, hidden, groups, window, True, False)
    scratch += back_scratch(rows, width, hidden, True)
    scratch += [pltpu.VMEM((rows, width), BF16)] * 2 + [pltpu.VMEM((every, width), BF16)]
    scratch += [pltpu.VMEM((1, vec.shape[1]), F32), pltpu.VMEM((1, width), F32)]
    scratch += Sums.scratch(chunks, GROUPS, small_rows)
    *sums, _, _, small, acts, grads = pl.pallas_call(
        functools.partial(fused_kernel, groups, window, chunks),
        out_shape=[jax.ShapeDtypeStruct(*one) for one in outs],
        in_specs=[inside] * 5 + [anywhere] * 8 + [inside] * 8 + [anywhere] * 3 + [inside] * 2 + [anywhere] * 3,
        out_specs=[anywhere] * 4 + [inside] + [anywhere] * 2,
        scratch_shapes=scratch,
        compiler_params=pltpu.CompilerParams(
            collective_id=0, has_side_effects=True, vmem_limit_bytes=64 * 1024 * 1024
        ),
        cost_estimate=pl.CostEstimate(flops=10**10, bytes_accessed=6 * 10**8, transcendentals=0),
        name="fused",
    )(*args)
    return sums, small, (acts, grads)


def body(axis_of, tokens, lengths, route_mask, router_weight, gains, biases, w_qkv, w_out, w_up, w_down, cotangent):
    micro, rows, width = tokens.shape
    own = (w_qkv, w_out, w_up, w_down)
    own_vec = jnp.concatenate([gains, biases], axis=1)
    router_row = router_weight.astype(F32)[None, :]
    half = LONG // 2
    groups_one = ((0, 0, half), (96, half, 2 * half), (192, 2 * half, rows // 2))
    groups_two = ((0, 0, LONG), (192, LONG, 2 * LONG), (384, 2 * LONG, rows))
    made = run_start(groups_one, 128, lengths, route_mask, tokens, cotangent, router_row, own_vec, own)
    far, (vec_one, vec_two), (y1, shown_y1, delta_one, cot, routed) = made[:4], made[4:6], made[6:11]
    col_one, col_two, row_one, row_two, *others = made[11:]
    unsort, pick, unpick, skipped, scale, factor, extra = others
    shown_du2, small_two, grads_two, dout, shown_y2, landed_two, carry = run_layer(
        axis_of, groups_two, 256, y1, col_two, row_two, vec_two, own, far, unsort, cot
    )
    sums, small, (activations, input_grads) = run_fused(
        axis_of, groups_one, 128, routed, col_one, row_one, vec_one, scale, own, far,
        (unsort, pick, unpick, skipped), dout, (delta_one, factor, router_row),
        (grads_two, landed_two, carry, small_two), extra,
        (shown_y1, shown_y2, shown_du2),
    )
    *grads, router_grad, means, activations, input_grads = cast_sums(
        sums, small, activations, input_grads,
        [value.shape for value in (*own, gains, biases)], micro,
    )
    return (activations, input_grads, *grads, router_grad[0], means[0])


def solution(mesh):
    in_specs = (
        P(None, "dp", None),
        P(None, "dp", None),
        P(None, "dp"),
        P(),
        P("section", None),
        P("section", None),
        P("section", None, None),
        P("section", None, None),
        P("section", None, None),
        P("section", None, None),
        P(None, "dp", None),
    )
    out_specs = (
        P("section", None, "dp", None),
        P("section", None, "dp", None),
        P("section", None, None),
        P("section", None, None),
        P("section", None, None),
        P("section", None, None),
        P("section", None),
        P("section", None),
        P(),
        P(),
    )
    step = functools.partial(body, axis_bits(mesh))
    return jax.shard_map(step, mesh=mesh, in_specs=in_specs, out_specs=out_specs, check_vma=False)
```

```python
import functools

import jax
import jax.numpy as jnp
from jax import lax
from jax.experimental import pallas as pl
from jax.experimental.pallas import tpu as pltpu
from jax.sharding import PartitionSpec as P

HEADS = 12
HEAD = 64
LONG = 197
F32 = jnp.float32
BF16 = jnp.bfloat16
NT = (((1,), (1,)), ((), ()))
TN = (((0,), (0,)), ((), ()))
NN = (((1,), (0,)), ((), ()))


LANES = 768
TILE = 16
GRAD_ROWS = 12 * LANES


def axis_bits(mesh):
    line = mesh.devices[0]
    bits = len(line).bit_length() - 1
    try:
        spots = [tuple(device.coords) for device in line]
    except AttributeError:
        return [0] * bits
    return [
        next((w for w in range(3) if spots[1 << b][w] != spots[0][w]), 0) for b in range(bits)
    ]


HALVINGS = 4
GROUPS = 6
SLOTS = 4


GROUP_PLAN = (
    ((768, 1023), (768, 132)),
    ((768, 123), (512, 1023), (256, 1203)),
    ((768, 123), (768, 1032)),
    ((512, 2103), (512, 123), (512, 1032)),
    ((768, 1023), (512, 2103), (256, 132)),
    ((512, 2013), (512, 132), (512, 1203)),
)
REDUCED = ((0, 3), (2, 1))
GROUP_STARTS = (0, 1, 2, 4, 5, 7)


def sum_plan(axis_of):
    lists = {}
    for bit, axis in enumerate(axis_of):
        lists.setdefault(axis, []).append(bit)
    lists = sorted(lists.values(), key=len)
    while len(lists) < 3:
        lists.append([])
    roles = [lists[0][:1], lists[1][:1], lists[2][:1], lists[2][1:2]]
    plan = []
    for group in GROUP_PLAN:
        chunks, start = [], 0
        for size, code in group:
            order = [bit for place in (1000, 100, 10, 1) for bit in roles[code // place % 10]]
            order += [bit for bit in range(len(axis_of)) if bit not in order]
            chunks.append((start, size, order))
            start += size
        plan.append(chunks)
    return plan


def add_rows(into, into_start, source, start, other, other_start, count):
    tile = next(t for t in (64, 32, 16) if count % t == 0)

    def step(k, carry):
        target, here, there = (
            pl.ds(pl.multiple_of(first + k * tile, TILE), tile) for first in (into_start, start, other_start)
        )
        into[target, :] = source[here, :] + other[there, :]
        return carry

    lax.fori_loop(0, count // tile, step, 0)


class Names:
    pass


def copy_far(source, target, one, two, friend):
    return pltpu.make_async_remote_copy(
        src_ref=source,
        dst_ref=target,
        send_sem=one,
        recv_sem=two,
        device_id=friend,
        device_id_type=pl.DeviceIdType.MESH,
    )


def at_core(core, index, step):
    pl.when(core == index)(step)


GRAD_TILES = 36
GROUP_ROWS = GRAD_ROWS // GROUPS


class Sums:
    def __init__(self, chunks, jobs, tiles, given, whole):
        self.chunks, self.jobs, self.tiles = chunks, jobs, tiles
        self.bits = bits = len(chunks[0][0][2])
        self.halvings = min(bits, HALVINGS)
        self.acc, self.mate = next(given), next(given)
        self.got = [next(given) for _ in range(bits)]
        self.load_sem, self.mate_sem = (next(given) for _ in range(2))
        self.send, self.recv, self.back_send, self.back_recv = (next(given) for _ in range(4))
        self.tile_recv, self.ready = (next(given) for _ in range(2))
        if whole:
            self.small_got, self.small = next(given), next(given)
            self.small_send, self.small_recv = (next(given) for _ in range(2))
            self.shown_sem, self.shown_send, self.shown_recv = (next(given) for _ in range(3))
            self.give_send, self.give_recv, self.put_sem = (next(given) for _ in range(3))
        self.core = lax.axis_index("section")
        self.me = lax.axis_index("dp")
        self.across = (1 - self.core, self.me)
        self.end = max(start + last - first + 1 for start, first, last in jobs.values())
        self.now = 0

    @staticmethod
    def scratch(chunks, held_groups, small_rows):
        bits = len(chunks[0][0][2])
        count = sum(len(group) for group in chunks)
        rows = min(held_groups, SLOTS) * GROUP_ROWS
        held = [pltpu.VMEM((held_groups * GROUP_ROWS, LANES), BF16), pltpu.VMEM((GROUP_ROWS, LANES), BF16)]
        held += [pltpu.VMEM((rows >> min(depth + 1, HALVINGS), LANES), BF16) for depth in range(bits)]
        held += [pltpu.SemaphoreType.DMA((count,))] * 2
        held += [pltpu.SemaphoreType.DMA((count, bits))] * 4
        held += [pltpu.SemaphoreType.DMA((GRAD_TILES,))]
        held += [pltpu.SemaphoreType.REGULAR((count, min(bits, HALVINGS)))]
        if small_rows:
            held += [pltpu.VMEM((bits + 1, small_rows, LANES), F32), pltpu.VMEM((2, small_rows, LANES), F32)]
            held += [pltpu.SemaphoreType.DMA((bits + 1,))] * 2
            held += [pltpu.SemaphoreType.DMA((2,))] * 3
            held += [pltpu.SemaphoreType.DMA((GROUPS,))] * 3
        return held

    def bit_at(self, bit):
        return lax.rem(self.me // (1 << bit), 2)

    def partner(self, bit):
        return (self.core, self.me + (1 - 2 * self.bit_at(bit)) * (1 << bit))

    def open(self):
        friends = [self.across] + [self.partner(bit) for bit in range(self.bits)]
        barrier = pltpu.get_barrier_semaphore()
        for friend in friends:
            pl.semaphore_signal(barrier, inc=1, device_id=friend, device_id_type=pl.DeviceIdType.MESH)

    def meet(self):
        pl.semaphore_wait(pltpu.get_barrier_semaphore(), 1 + self.bits)

    @staticmethod
    def layer_of(j):
        return 1 if j < GROUPS // 2 else 0

    def base(self, j, core):
        return (2 * (j % (GROUPS // 2)) + core) * GROUP_ROWS

    def rows_at(self, j, core, c):
        start, size, _ = self.chunks[j][c]
        return pl.ds(pl.multiple_of(self.base(j, core) + start, TILE), size)

    def index(self, j, c):
        return sum(len(group) for group in self.chunks[:j]) + c

    def load(self, j, c):
        start, size, _ = self.chunks[j][c]
        target = self.acc.at[pl.ds(j * GROUP_ROWS + start, size), :]
        source = self.grads[self.layer_of(j)].at[self.rows_at(j, self.core, c), :]
        return pltpu.make_async_copy(source, target, self.load_sem.at[self.index(j, c)])

    def load_mate(self, j, c):
        source = self.landed[self.layer_of(j)].at[self.rows_at(j, self.core, c), :]
        start, size, _ = self.chunks[j][c]
        target = self.mate.at[pl.ds(start, size), :]
        return pltpu.make_async_copy(source, target, self.mate_sem.at[self.index(j, c)])

    def span(self, j, c, depth):
        start, size, order = self.chunks[j][c]
        for bit in order[: min(depth, self.halvings)]:
            size //= 2
            start = start + self.bit_at(bit) * size
        return start, size

    def in_acc(self, j, start, size):
        return pl.ds(pl.multiple_of(j * GROUP_ROWS + start, TILE), size)

    def got_at(self, j, c, depth):
        return (j % SLOTS * GROUP_ROWS + self.chunks[j][c][0]) >> min(depth + 1, HALVINGS)

    def down(self, j, c, depth):
        bit = self.chunks[j][c][2][depth]
        start, size = self.span(j, c, depth)
        if depth < self.halvings:
            size //= 2
            start = start + (1 - self.bit_at(bit)) * size
        k = self.index(j, c)
        return copy_far(
            self.acc.at[self.in_acc(j, start, size), :],
            self.got[depth].at[pl.ds(self.got_at(j, c, depth), size), :],
            self.send.at[k, depth],
            self.recv.at[k, depth],
            self.partner(bit),
        )

    def up(self, j, c, depth):
        bit = self.chunks[j][c][2][depth]
        start, size = self.span(j, c, depth + 1)
        here = self.acc.at[self.in_acc(j, start, size), :]
        k = self.index(j, c)
        return copy_far(here, here, self.back_send.at[k, depth], self.back_recv.at[k, depth], self.partner(bit))

    def left(self, j, c, depth):
        self.down(j, c, depth).wait_send()
        if self.jobs[j][2] > self.bits:
            partner = self.partner(self.chunks[j][c][2][depth])
            pl.semaphore_signal(
                self.ready.at[self.index(j, c), depth], inc=1, device_id=partner, device_id_type=pl.DeviceIdType.MESH
            )

    def raise_up(self, j, c, depth):
        if depth >= self.jobs[j][1]:
            pl.semaphore_wait(self.ready.at[self.index(j, c), depth], 1)
        self.up(j, c, depth).start()

    def carried(self, j, c, keep):
        start, size = self.span(j, c, REDUCED[j][1])
        here = self.in_acc(j, start, size)
        pair = (self.acc.at[here, :], self.carry.at[here, :])
        return pltpu.make_async_copy(*(pair if keep else pair[::-1]), self.load_sem.at[self.index(j, c)])

    def wait_tiles(self, layer, first):
        for tile in range(6):
            area = self.landed[layer].at[pl.ds(0, LANES), pl.ds(0, STEP)]
            sem = self.tile_recv.at[first + self.core * 6 + tile]
            copy_far(area, area, sem, sem, self.across).wait_recv()

    def tile_out(self, layer, stage, row, column, shape, sem, tile):
        area = (pl.ds(row, shape[0]), pl.ds(column, shape[1]))
        owner = lax.rem(tile // 6, 2)

        @pl.when(self.core == owner)
        def _():
            pltpu.make_async_copy(stage, self.grads[layer].at[area], sem).start()

        @pl.when(self.core != owner)
        def _():
            copy_far(stage, self.landed[layer].at[area], sem, self.tile_recv.at[tile], self.across).start()

    def give(self, j, core):
        rows = pl.ds(self.base(j, core), GROUP_ROWS)
        source = self.acc.at[pl.ds(j * GROUP_ROWS, GROUP_ROWS), :]
        target = self.full[self.layer_of(j)].at[rows, :]
        return copy_far(source, target, self.give_send.at[j], self.give_recv.at[j], self.across)

    def put(self, j, core):
        rows = pl.ds(self.base(j, core), GROUP_ROWS)
        source = self.acc.at[pl.ds(j * GROUP_ROWS, GROUP_ROWS), :]
        return pltpu.make_async_copy(source, self.full[self.layer_of(j)].at[rows, :], self.put_sem.at[j])

    def each(self, j):
        return range(len(self.chunks[j]))

    def prepare(self, j):
        for c in self.each(j):
            self.load(j, c).start()
        if j in self.tiles:
            self.wait_tiles(self.layer_of(j), self.tiles[j])
        for c in self.each(j):
            self.load_mate(j, c).start()

    def moment(self):
        now, self.now = self.now, self.now + 1
        bits, halvings = self.bits, self.halvings
        order = sorted(self.jobs, key=lambda j: self.jobs[j][:2] != (now, 0))
        for j in order:
            start, first_stage, last_stage = self.jobs[j]
            stage = now - start + first_stage
            if not first_stage <= stage <= last_stage:
                continue
            for c in self.each(j):
                if stage == 0:
                    self.load(j, c).wait()
                    self.load_mate(j, c).wait()
                    first, size, _ = self.chunks[j][c]
                    at = j * GROUP_ROWS + first
                    add_rows(self.acc, at, self.acc, at, self.mate, first, size)
                    self.down(j, c, 0).start()
                elif stage == first_stage:
                    self.carried(j, c, False).wait()
                    self.down(j, c, stage).start()
                elif stage <= bits:
                    depth = stage - 1
                    if depth < halvings:
                        self.down(j, c, depth).wait_recv()
                        self.left(j, c, depth)
                    else:
                        self.down(j, c, depth).wait()
                    first, size = self.span(j, c, stage)
                    at = j * GROUP_ROWS + first
                    add_rows(self.acc, at, self.acc, at, self.got[depth], self.got_at(j, c, depth), size)
                    if stage < min(bits, last_stage):
                        self.down(j, c, stage).start()
                    elif stage < last_stage:
                        self.raise_up(j, c, halvings - 1)
                else:
                    depth = bits + halvings - stage
                    self.up(j, c, depth).wait_recv()
                    if depth > 0:
                        self.raise_up(j, c, depth - 1)
            if stage == bits + halvings:
                layer = self.layer_of(j)
                at_core(self.core, layer, lambda j=j, layer=layer: self.put(j, layer).start())
                at_core(self.core, 1 - layer, lambda j=j, layer=layer: self.give(j, 1 - layer).start())
        for j, (start, first_stage, _) in self.jobs.items():
            if start == now + 1 and first_stage == 0:
                self.prepare(j)

    def small_step(self, k):
        friend = self.across if k == 0 else self.partner(k - 1)
        return copy_far(
            self.small_out, self.small_got.at[k], self.small_send.at[k], self.small_recv.at[k], friend
        )

    def small_begin(self):
        for layer in range(2):

            def step(layer=layer):
                self.small_out[...] = self.small[layer]
                copy_far(
                    self.small.at[1 - layer], self.small_got.at[0], self.small_send.at[0], self.small_recv.at[0],
                    self.across,
                ).start()

            at_core(self.core, layer, step)

    def small_turn(self, k):
        self.small_step(k).wait()
        self.small_out[...] = self.small_out[...] + self.small_got[k]
        if k < self.bits:
            self.small_step(k + 1).start()

    def shown_keep(self, layer, k):
        return pltpu.make_async_copy(self.shown[2 * k + layer], self.shown_out[k].at[self.core], self.shown_sem.at[k])

    def shown_give(self, layer, k):
        return copy_far(
            self.shown[2 * k + 1 - layer], self.shown_out[k].at[self.core], self.shown_send.at[k],
            self.shown_recv.at[k], self.across,
        )

    def show(self):
        for layer in range(2):

            def step(layer=layer):
                for k in range(2):
                    self.shown_keep(layer, k).start()
                    self.shown_give(layer, k).start()

            at_core(self.core, layer, step)

    def close(self):
        for k in range(2):
            self.shown_keep(0, k).wait()
            self.shown_give(0, k).wait()
        for j in range(GROUPS):
            layer = self.layer_of(j)

            def kept(j=j, layer=layer):
                self.put(j, layer).wait()
                self.give(j, 1 - layer).wait_recv()

            at_core(self.core, layer, kept)
            at_core(self.core, 1 - layer, lambda j=j, layer=layer: self.give(j, 1 - layer).wait_send())
            for c in self.each(j):
                for depth in range(self.halvings):
                    self.up(j, c, depth).wait_send()


def cast_kernel(first, second, small, acts, slopes, qkv, out, up, down, *refs):
    gains, biases, router, means, acts_out, slopes_out, low, high, bounce, in_sem, out_sem, copy_sem = refs
    rows = low.shape[1]
    per = LANES // rows
    slots = low.shape[0]
    count = 12 * per
    core = lax.axis_index("section")
    passed = [
        (
            pltpu.make_async_copy(source, bounce.at[k], copy_sem.at[k]),
            pltpu.make_async_copy(bounce.at[k], target.at[0], copy_sem.at[k]),
        )
        for k, (source, target) in enumerate(((acts, acts_out), (slopes, slopes_out)))
    ]

    def take(k, source=first):
        return pltpu.make_async_copy(source.at[pl.ds(k * rows, rows), :], low.at[k % slots], in_sem.at[k % slots])

    def give(k):
        block, part = divmod(k, per)
        if block < 4:
            target = down.at[0, pl.ds(k * rows, rows), :]
        elif block < 8:
            target = up.at[0, pl.ds(part * rows, rows), pl.ds((block - 4) * LANES, LANES)]
        elif block < 9:
            target = out.at[0, pl.ds(part * rows, rows), :]
        else:
            target = qkv.at[0, pl.ds(part * rows, rows), pl.ds((block - 9) * LANES, LANES)]
        return pltpu.make_async_copy(high.at[k % slots], target, out_sem.at[k % slots])

    def fetch(k):
        at_core(core, 0, lambda: take(k).start())
        at_core(core, 1, lambda: take(k, second).start())

    for k in range(slots):
        fetch(k)
    for copy, _ in passed:
        copy.start()
    held = gains.shape[1] // LANES
    for row in range(held):
        gains[:, row * LANES : (row + 1) * LANES] = small[row : row + 1, :]
    for row in range(biases.shape[1] // LANES):
        biases[:, row * LANES : (row + 1) * LANES] = small[held + row : held + row + 1, :]
    row = held + biases.shape[1] // LANES
    router[...] = small[row : row + 1, :]
    micro = means.shape[1]
    means[...] = small[row + 1 : row + 2, :micro] / small[row + 1 : row + 2, micro : 2 * micro]
    for k in range(count):
        take(k).wait()
        if k >= slots:
            give(k - slots).wait()
        high[k % slots] = low[k % slots].astype(F32)
        give(k).start()
        if k + slots < count:
            fetch(k + slots)
        if k < 2:
            passed[k][0].wait()
            passed[k][1].start()
    for k in range(count - slots, count):
        give(k).wait()
    for _, copy in passed:
        copy.wait()


def cast_sums(sums, small, acts, slopes, shapes, micro):
    anywhere = pl.BlockSpec(memory_space=pl.ANY)
    inside = pl.BlockSpec(memory_space=pltpu.VMEM)
    outs = [(shape, F32) for shape in shapes] + [((1, LANES), F32), ((1, micro), F32)]
    outs += [((1, *value.shape), BF16) for value in (acts, slopes)]
    return pl.pallas_call(
        cast_kernel,
        out_shape=[jax.ShapeDtypeStruct(*one) for one in outs],
        in_specs=[anywhere] * 2 + [inside] + [anywhere] * 2,
        out_specs=[anywhere] * 4 + [inside] * 4 + [anywhere] * 2,
        scratch_shapes=[
            pltpu.VMEM((6, 256, LANES), BF16),
            pltpu.VMEM((6, 256, LANES), F32),
            pltpu.VMEM((2, *acts.shape), BF16),
            pltpu.SemaphoreType.DMA((6,)),
            pltpu.SemaphoreType.DMA((6,)),
            pltpu.SemaphoreType.DMA((2,)),
        ],
        compiler_params=pltpu.CompilerParams(vmem_limit_bytes=60 * 1024 * 1024),
        cost_estimate=pl.CostEstimate(flops=0, bytes_accessed=50 * 10**6, transcendentals=0),
        name="cast",
    )(*sums, small, acts, slopes)


STEP = 256
NEGATIVE = -1e30


def dot(left, right, dims=NN):
    return lax.dot_general(left, right, dims, preferred_element_type=F32)


def gelu_parts(pre):
    bell = jnp.exp(pre * pre * -0.5)
    t = pl.reciprocal(1.0 + jnp.abs(pre) * (0.3275911 * 0.7071067811865476))
    poly = t * (0.1274147960 + t * (-0.142248368 + t * (0.710706871 + t * (-0.7265760135 + t * 0.5307027145))))
    tail = poly * bell
    return jnp.where(pre >= 0.0, 1.0 - tail, tail), bell


def norm_stats(values):
    centred = values - jnp.mean(values, axis=-1, keepdims=True)
    recip = lax.rsqrt(jnp.mean(centred * centred, axis=-1, keepdims=True) + 1e-06)
    return centred * recip, recip


def fold(tile):
    return jnp.sum(tile.reshape(tile.shape[0] // 8, 8, tile.shape[1]), axis=0)


def front_names(r, given, full):
    r.weights = [next(given) for _ in range(4)]
    r.w_sem, r.n1, r.qkv, r.probs, r.mask, r.mix, r.between, r.n2, r.act = (next(given) for _ in range(9))
    if not full:
        r.pre = [next(given) for _ in range(2)]
    r.act_part = [next(given) for _ in range(2)]


def back_names(r, given, scaled):
    r.n1t, r.n2t = (next(given) for _ in range(2))
    r.mixt = r.n2t
    r.dmlp = next(given) if scaled else r.dout
    r.dpre, r.dn = (next(given) for _ in range(2))
    r.pre = [r.dn.at[:, pl.ds(side * STEP, STEP)] for side in range(2)]
    r.dqkv = r.dpre.at[:, pl.ds(0, 3 * LANES)]
    r.datt, r.dmix = r.n1, r.mix
    r.dpre_part = [next(given) for _ in range(2)]
    r.down_stage, r.up_stage, r.down_sem, r.up_sem = (next(given) for _ in range(4))


def use_weights(r, layer):
    core = lax.axis_index("section")

    def weight(which, source):
        return pltpu.make_async_copy(source[which].at[0], r.weights[which], r.w_sem.at[which])

    for near, source in ((core == layer, r.own), (core != layer, r.far)):

        @pl.when(near)
        def _():
            for which in range(4):
                weight(which, source).start()

    r.ready = lambda which: weight(which, r.own).wait()


def layer_kernel(groups, window, chunks, *refs):
    r = Names()
    given = iter(refs)
    r.x, r.col_code, r.row_code, r.vec = (next(given) for _ in range(4))
    r.own = [next(given) for _ in range(4)]
    r.far = [next(given) for _ in range(4)]
    r.unsort, r.dout = (next(given) for _ in range(2))
    r.shown_du, r.small, r.grads, r.du, r.shown_y, landed, carry = (next(given) for _ in range(7))
    front_names(r, given, True)
    back_names(r, given, False)
    r.y, r.shown_sem = r.n2, next(given)
    jobs = {j: (start, 0, stage) for j, (start, stage) in enumerate(REDUCED)}
    sums = Sums(chunks, jobs, {0: 0, 1: 12}, given, False)
    sums.grads, sums.landed, sums.carry = (None, r.grads), (None, landed), carry
    use_weights(r, 1)
    sums.open()
    r.tile_out = functools.partial(sums.tile_out, 1)
    r.hooks = {at: sums.moment for at in (4, 7, 8)}
    r.hooks[1] = sums.meet
    r.hooks[3] = lambda: sums.prepare(0)
    layer_body(r, groups, window, True, False)
    while sums.now < sums.end:
        sums.moment()
    for j in jobs:
        for c in sums.each(j):
            sums.carried(j, c, True).start()
    sums.wait_tiles(1, 24)
    for j in jobs:
        for c in sums.each(j):
            sums.carried(j, c, True).wait()


def start_kernel(groups, window, *refs):
    r = Names()
    given = iter(refs)
    lengths, route_mask, tokens, cotangent, router, own_vec = (next(given) for _ in range(6))
    own = [next(given) for _ in range(4)]
    far = [next(given) for _ in range(4)]
    vecs = [next(given) for _ in range(2)]
    r.all_y, r.shown_y, r.delta, cot, r.x = (next(given) for _ in range(5))
    col_codes = [next(given) for _ in range(2)]
    row_codes = [next(given) for _ in range(2)]
    r.unsort, pick, r.unpick, r.skipped, r.scale, factor, extra = (next(given) for _ in range(7))
    front_names(r, given, False)
    r.y, r.all_x, order, raw, far_vec, raw_sem = (next(given) for _ in range(6))
    far_send, far_recv, vec_sem = (next(given) for _ in range(3))
    core = lax.axis_index("section")
    across = (1 - core, lax.axis_index("dp"))
    rows, width = r.all_x.shape
    half = rows // 2

    def fetch(k, source):
        return pltpu.make_async_copy(source.at[core], raw.at[k], raw_sem.at[k])

    fetch(0, tokens).start()
    fetch(1, cotangent).start()
    barrier = pltpu.get_barrier_semaphore()
    pl.semaphore_signal(barrier, inc=1, device_id=across, device_id_type=pl.DeviceIdType.MESH)
    pl.semaphore_wait(barrier, 1)

    def lend(which):
        return copy_far(own[which], far[which], far_send.at[which], far_recv.at[which], across)

    lend_vec = copy_far(own_vec, far_vec, vec_sem.at[0], vec_sem.at[1], across)
    lend_vec.start()
    lend(0).start()

    def weight(which, source):
        return pltpu.make_async_copy(source[which].at[0], r.weights[which], r.w_sem.at[which])

    def take_own():
        for which in range(4):
            weight(which, own).start()

    at_core(core, 0, take_own)

    def ready(which):
        def arrive():
            lend(which).wait_recv()
            weight(which, far).start()

        at_core(core, 1, arrive)
        weight(which, own).wait()

    r.ready = ready

    starts, bases, total, longs, short = [], [], 0, 0, 0
    count = lengths.shape[2]
    sizes = [lengths[core, 0, c] for c in range(count)]
    for size in sizes:
        is_long = size == LONG
        starts.append(total)
        bases.append(jnp.where(is_long, longs * LONG, 2 * LONG + short))
        total = total + size
        longs = longs + jnp.where(is_long, 1, 0)
        short = short + jnp.where(is_long, 0, size)

    def place(shape, dim):
        return lax.broadcasted_iota(jnp.int32, shape, dim)

    def target(at):
        moved = at
        for start, size, base in zip(starts, sizes, bases):
            moved = moved + jnp.where((at >= start) & (at < start + size), base - start, 0)
        return moved

    def code_of(at):
        return sum(jnp.where(at >= base, 1, 0) for base in bases)

    row_at, col_at = place((1, rows), 1), place((rows, 1), 0)

    def one_hot(left, right):
        return jnp.where(left == right, 1.0, 0.0).astype(BF16)

    goes_row, goes_col = target(row_at), target(col_at)
    row_codes[1][...] = code_of(row_at)
    col_codes[1][...] = code_of(col_at)
    for start in range(0, rows, 128):
        here = slice(start, start + 128)
        order[here, :] = one_hot(col_at[here], goes_row)
        r.unsort[here, :] = one_hot(goes_col[here], row_at)
    lend(1).start()
    lend(2).start()
    lend(3).start()
    for k, (source, moved) in enumerate(((tokens, r.all_x), (cotangent, cot))):
        fetch(k, source).wait()
        moved[...] = dot(order[...], raw[k]).astype(BF16)

    mask = jnp.where(route_mask[pl.ds(core, 1), :] == 1, 1.0, 0.0)
    masks = jnp.broadcast_to(mask, (8, rows)).astype(BF16)
    chosen_row = dot(masks, r.unsort[...])
    chosen_col = dot(order[...], masks, NT)
    earlier = jnp.where(place((rows, rows), 0) < place((rows, rows), 1), 1.0, 0.0).astype(BF16)
    rank_row = dot(chosen_row.astype(BF16), earlier)[:1]
    later = jnp.where(place((rows, rows), 0) > place((rows, rows), 1), 1.0, 0.0).astype(BF16)
    rank_col = dot(later, chosen_col.astype(BF16))[:, :1]
    chosen_row, chosen_col = chosen_row[:1], chosen_col[:, :1]
    r.skipped[...] = 1.0 - chosen_col
    key_row = jnp.where(chosen_row > 0.5, rank_row, -1.0)
    key_col = jnp.where(chosen_col > 0.5, rank_col, -1.0)
    pick[...] = one_hot(place((half, 1), 0).astype(F32), key_row)
    r.unpick[...] = one_hot(key_col, place((1, half), 1).astype(F32))
    names_row = jnp.broadcast_to(code_of(row_at).astype(F32), (8, rows)).astype(BF16)
    routed_row = dot(names_row, r.unpick[...])[:1]
    routed_col = dot(pick[...], names_row, NT)[:, :1]
    row_codes[0][...] = routed_row.astype(jnp.int32)
    col_codes[0][...] = routed_col.astype(jnp.int32)
    r.x[...] = dot(pick[...], r.all_x[...]).astype(BF16)
    logit = jnp.sum(r.x[...].astype(F32) * router[...], axis=1, keepdims=True)
    gate = 1.0 / (1.0 + jnp.exp(-logit))
    held = jnp.where(routed_col > 0.5, 1.0, 0.0)
    r.scale[...] = held * gate
    factor[...] = held * gate * (1.0 - gate)
    gates, counts = jnp.sum(held * gate, axis=0, keepdims=True), jnp.sum(mask, axis=1, keepdims=True)
    lane = place((1, width), 1)
    micro = tokens.shape[0]
    extra[...] = jnp.where(lane == core, gates, jnp.where(lane == core + micro, counts, 0.0))

    lend_vec.wait()
    for layer in range(2):
        vecs[layer][...] = jnp.where(core == layer, own_vec[...], far_vec[...])
    r.vec, r.col_code, r.row_code, r.own = vecs[0], col_codes[0], row_codes[0], own
    r.hooks = {}
    layer_body(r, groups, window, False, True)
    for which in range(4):
        lend(which).wait_send()
        at_core(core, 0, lambda which=which: lend(which).wait_recv())


def fused_kernel(groups, window, chunks, *refs):
    r = Names()
    given = iter(refs)
    r.x, r.col_code, r.row_code, r.vec, r.scale = (next(given) for _ in range(5))
    r.own = [next(given) for _ in range(4)]
    r.far = [next(given) for _ in range(4)]
    r.unsort = next(given)
    r.all_dout, r.pick, r.unpick, r.skipped, r.delta, r.factor, r.router = (next(given) for _ in range(7))
    second, second_landed, carry, second_small, extra = (next(given) for _ in range(5))
    shown = [next(given) for _ in range(3)]
    full = [next(given) for _ in range(2)]
    first_landed, first, small_out = (next(given) for _ in range(3))
    shown_out = [next(given) for _ in range(2)]
    front_names(r, given, True)
    back_names(r, given, True)
    r.dout, r.du, r.shown_du, r.small, r.router_grad = (next(given) for _ in range(5))
    bits = len(chunks[0][0][2])
    last = bits + min(bits, HALVINGS)
    reduced = len(REDUCED)
    jobs = {j: (start, REDUCED[j][1] if j < reduced else 0, last) for j, start in enumerate(GROUP_STARTS)}
    sums = Sums(chunks, jobs, {3: 0, 4: 12, 5: 24}, given, True)
    sums.grads, sums.landed, sums.full = (first, second), (first_landed, second_landed), full
    sums.carry, sums.small_out = carry, small_out
    sums.shown, sums.shown_out = (shown[0], shown[1], r.shown_du, shown[2]), shown_out
    r.grads = first
    use_weights(r, 0)
    sums.open()
    sums.meet()
    for j in range(reduced):
        for c in sums.each(j):
            sums.carried(j, c, False).start()
    for j, (start, first_stage, _) in jobs.items():
        if start == 0 and first_stage == 0:
            sums.prepare(j)
    r.tile_out = functools.partial(sums.tile_out, 0)
    r.hooks = {at: sums.moment for at in (0, 1, 2, 3, 8, 9)}
    layer_body(r, groups, window, True, True)

    for index, source in enumerate((r.small, second_small)):
        for row in range(source.shape[1] // LANES):
            sums.small[index, row : row + 1, :] = source[:, row * LANES : (row + 1) * LANES]
        row = source.shape[1] // LANES
        sums.small[index, row : row + 1, :] = r.router_grad[...]
        sums.small[index, row + 1 : row + 2, :] = extra[...]
        left = sums.small.shape[1] - row - 2
        sums.small[index, row + 2 :, :] = jnp.zeros((left, LANES), F32)
    sums.small_begin()
    sums.show()

    for turn in range(max(sums.end - sums.now, sums.bits + 1)):
        if sums.now < sums.end:
            sums.moment()
        if turn <= sums.bits:
            sums.small_turn(turn)
    sums.close()


def layer_body(r, groups, window, full, is_router):
    def hook(at):
        if at in r.hooks:
            r.hooks[at]()

    rows, width = r.x.shape
    hidden = r.own[2].shape[2]
    pairs = width // 128
    row_tile = rows // 5

    def vec(start, count=width):
        return r.vec[:, start : start + count]

    g1, g2, b1, bq, bv, bo, b2 = (vec(k * width) for k in range(7))
    bu_at, bd_at = 7 * width, 7 * width + hidden

    def row_loop(step, init=0):
        def at(k, carry):
            return step(pl.ds(pl.multiple_of(k * row_tile, row_tile), row_tile), carry)

        return lax.fori_loop(0, rows // row_tile, at, init)

    def norm_step(source, gain, bias, target):
        def step(here, carry):
            normal, _ = norm_stats(source[here, :].astype(F32))
            target[here, :] = (normal * gain + bias).astype(BF16)
            return carry

        return step

    def tiles(step):
        for k in range(width // STEP):
            step(slice(k * STEP, (k + 1) * STEP))

    def show(source, target):
        def step(span):
            target[:, span] = dot(r.unsort[...], source[:, span]).astype(BF16)

        tiles(step)

    def spread(routed, others, target, shown):
        def step(span):
            value = dot(r.unpick[...], routed[:, span]) + others[:, span].astype(F32) * r.skipped[...]
            if target is not None:
                target[:, span] = value.astype(BF16)
            shown[:, span] = dot(r.unsort[...], value.astype(BF16)).astype(BF16)

        tiles(step)

    row_loop(norm_step(r.x, g1, b1, r.n1))
    if full and is_router:

        def route_step(span):
            r.dout[:, span] = dot(r.pick[...], r.all_dout[:, span]).astype(BF16)

        tiles(route_step)
    if full:

        def delta_step(here, carry):
            low = r.dout[here, :]
            if is_router:
                low = (low.astype(F32) * r.scale[here, :]).astype(BF16)
                r.dmlp[here, :] = low
            return carry + fold(low.astype(F32))

        dbd = row_loop(delta_step, jnp.zeros((8, width), F32))
        r.small[:, bd_at:] = jnp.sum(dbd, axis=0, keepdims=True)

    for k, (start, low, high) in enumerate(groups):
        col = r.col_code[start : start + window, :]
        row = r.row_code[:, start : start + window]
        place = lax.broadcasted_iota(jnp.int32, (window, 1), 0) + start
        col = jnp.where((place >= low) & (place < high), col, -1)
        r.mask[k] = jnp.where(col == row, 0.0, NEGATIVE)

    r.ready(0)
    for k in range(3 * width // STEP):
        span = slice(k * STEP, (k + 1) * STEP)
        value = dot(r.n1[...], r.weights[0][:, span])
        if k < width // STEP:
            value = (value + bq[:, span]).astype(BF16).astype(F32) * 0.125
        elif k >= 2 * width // STEP:
            value = value + bv[:, k * STEP - 2 * width : (k + 1) * STEP - 2 * width]
        r.qkv[:, span] = value.astype(BF16)

    hook(0)
    lane = lax.broadcasted_iota(jnp.int32, (1, 128), 1)

    def halves(block):
        zero = jnp.zeros_like(block)
        return jnp.concatenate([jnp.where(lane < 64, block, zero), jnp.where(lane < 64, zero, block)], axis=0)

    high_half = lax.broadcasted_iota(jnp.int32, (128, 1), 0) >= 64

    def own_half(both):
        return jnp.where(high_half, both[:, window:], both[:, :window]).T

    r.mix[...] = jnp.zeros_like(r.mix)

    def lanes(pair, part):
        return pl.ds(pl.multiple_of(pair * 128 + part * width, 128), 128)

    spots = [slice(start, start + window) for start, _, _ in groups]
    count = len(groups)

    def qkv_at(pair, part):
        return [r.qkv[here, lanes(pair, part)] for here in spots]

    def attend(pair, carry):
        q, key, v = (qkv_at(pair, part) for part in range(3))
        scores = [dot(key[k], halves(q[k]), NT) for k in range(count)]
        probs = []
        for k, (start, low, high) in enumerate(groups):
            mask = r.mask[k]
            masked = scores[k] + jnp.concatenate([mask, mask], axis=1)
            place = lax.broadcasted_iota(jnp.int32, (1, window), 1) + start
            valid = (place >= low) & (place < high)
            valid = jnp.concatenate([valid, valid], axis=1)
            power = jnp.exp(masked - jnp.max(masked, axis=0, keepdims=True))
            total = jnp.sum(power, axis=0, keepdims=True)
            prob = (power * jnp.where(valid, 1.0 / total, 0.0)).astype(BF16)
            if full:
                r.probs[pair * count + k] = prob
            probs.append(prob)
        mixed = [dot(v[k].T, probs[k]) for k in range(count)]
        for k, here in enumerate(spots):
            r.mix[here, lanes(pair, 0)] = r.mix[here, lanes(pair, 0)] + own_half(mixed[k]).astype(BF16)
        return carry

    lax.fori_loop(0, pairs, attend, 0)

    r.ready(1)
    for k in range(width // STEP):
        span = slice(k * STEP, (k + 1) * STEP)
        value = dot(r.mix[...], r.weights[1][:, span]) + bo[:, span]
        r.between[:, span] = r.x[:, span].astype(F32) + value
    row_loop(norm_step(r.between, g2, b2, r.n2))
    if full:
        r.n1t[...] = r.n1[...].T
        r.n2t[...] = r.n2[...].T
    hook(1)

    r.ready(2)
    if full:
        r.ready(3)

    def down_out(k, slot):
        r.tile_out(
            r.down_stage.at[slot], pl.multiple_of(k * STEP, STEP), 0, (STEP, width), r.down_sem.at[slot], k
        )

    def side_out(block, k, slot):
        row = pl.multiple_of((block + k // 3) * width, width)
        column = pl.multiple_of(k % 3 * STEP, STEP)
        tile = k + {4: 12, 8: 24, 9: 27}[block]
        r.tile_out(r.up_stage.at[slot], row, column, (width, STEP), r.up_sem.at[slot], tile)

    def down_free(slot):
        target = r.grads.at[pl.ds(0, STEP), pl.ds(0, width)]
        pltpu.make_async_copy(r.down_stage.at[slot], target, r.down_sem.at[slot]).wait()

    def side_free(slot):
        target = r.grads.at[pl.ds(0, width), pl.ds(0, STEP)]
        pltpu.make_async_copy(r.up_stage.at[slot], target, r.up_sem.at[slot]).wait()

    steps = hidden // STEP

    def part_at(k):
        return pl.multiple_of(k * STEP, STEP)

    def ahead(k, side):
        at = part_at(k)
        r.pre[side][...] = dot(r.n2[...], r.weights[2][:, pl.ds(at, STEP)]) + r.vec[:, pl.ds(at + bu_at, STEP)]

    def middle(k, side):
        at = part_at(k)
        span = pl.ds(at, STEP)
        pre = r.pre[side][...]
        cdf, bell = gelu_parts(pre)
        act = (pre * cdf).astype(BF16)
        if not (full and is_router):
            r.act[:, span] = act
        if full:
            r.act_part[side][...] = act
            slope = cdf + pre * bell * 0.3989422804014327
            dact = dot(r.dmlp[...], r.weights[3][span, :], NT)
            dpre = (dact * slope).astype(BF16)
            r.dpre[:, span] = dpre
            r.dpre_part[side][...] = dpre
            r.small[:, pl.ds(at + bu_at, STEP)] = jnp.sum(dpre.astype(F32), axis=0, keepdims=True)

    def weigh(side):
        r.down_stage[side] = dot(r.act_part[side][...], r.dmlp[...], TN).astype(BF16)
        r.up_stage[side] = dot(r.n2t[...], r.dpre_part[side][...]).astype(BF16)

    def send_out(k, side):
        down_out(k, side)
        side_out(4, k, side)

    def two_steps(kk, first=False):
        even, odd = kk, kk + steps // 2
        if full and not first:

            @pl.when(kk >= 2)
            def _():
                down_free(1)
                side_free(1)

            down_free(0)
            side_free(0)
        middle(even, 0)
        ahead(odd, 1)
        if full and not first:
            weigh(1)
        middle(odd, 1)
        ahead(jnp.minimum(even + 1, steps // 2 - 1), 0)
        if full:
            weigh(0)
            if not first:
                send_out(odd - 1, 1)
            send_out(even, 0)

    def more_steps(kk, carry):
        two_steps(kk)
        return carry

    ahead(0, 0)
    two_steps(0, True)
    if 2 in r.hooks:
        lax.fori_loop(1, steps // 4, more_steps, 0)
        hook(2)
        lax.fori_loop(steps // 4, steps // 2, more_steps, 0)
    else:
        lax.fori_loop(1, steps // 2, more_steps, 0)
    if full:
        down_free(1)
        side_free(1)
        weigh(1)
        send_out(steps - 1, 1)
    if not full:
        r.ready(3)
    if not (full and is_router):
        for k in range(width // STEP):
            span = slice(k * STEP, (k + 1) * STEP)
            value = dot(r.act[...], r.weights[3][:, span]) + vec(bd_at)[:, span]
            source = r.x[:, span].astype(F32)
            value = r.between[:, span] - source + value
            if not full:
                r.delta[:, span] = value
            r.y[:, span] = (source + (r.scale[...] * value if is_router else value)).astype(BF16)
    if not full:
        spread(r.y, r.all_x, r.all_y, r.shown_y)
        return
    if not is_router:
        show(r.y, r.shown_du)
        r.shown_copy = pltpu.make_async_copy(r.shown_du, r.shown_y, r.shown_sem.at[0])
        r.shown_copy.start()

    for side in range(2):
        down_free(side)
        side_free(side)
    hook(3)
    r.dn[...] = dot(r.dpre[...], r.weights[2][...], NT)
    hook(4)

    def norm_back(source, gain, here):
        normal, recip = norm_stats(source[here, :].astype(F32))
        grad = r.dn[here, :]
        hat = grad * gain
        back = recip * (
            hat - jnp.mean(hat, axis=-1, keepdims=True) - normal * jnp.mean(hat * normal, axis=-1, keepdims=True)
        )
        return back, fold(grad * normal), fold(grad)

    def second_back(here, carry):
        back, dg, db = norm_back(r.between, g2, here)
        r.between[here, :] = back
        delta = r.dout[here, :].astype(F32)
        total = ((delta * r.scale[here, :] if is_router else delta) + back).astype(BF16)
        r.datt[here, :] = total
        return carry[0] + dg, carry[1] + db, carry[2] + fold(total.astype(F32))

    zero = jnp.zeros((8, width), F32)
    dg2, db2, dbo = row_loop(second_back, (zero, zero, zero))
    r.small[:, width : 2 * width] = jnp.sum(dg2, axis=0, keepdims=True)
    r.small[:, 6 * width : 7 * width] = jnp.sum(db2, axis=0, keepdims=True)
    r.small[:, 5 * width : 6 * width] = jnp.sum(dbo, axis=0, keepdims=True)

    hook(5)
    r.mixt[...] = r.mix[...].T
    r.dmix[...] = dot(r.datt[...], r.weights[1][...], NT).astype(BF16)
    for k in range(width // STEP):
        span = slice(k * STEP, (k + 1) * STEP)
        slot = k % 2
        if k >= 2:
            side_free(slot)
        r.up_stage[slot] = dot(r.mixt[...], r.datt[:, span]).astype(BF16)
        side_out(8, k, slot)
    hook(6)

    r.dqkv[...] = jnp.zeros((rows, 3 * width), BF16)

    def attend_back(pair, carry):
        q, key, v = (qkv_at(pair, part) for part in range(3))
        dm = [halves(r.dmix[here, lanes(pair, 0)]) for here in spots]
        dprobs = [dot(v[k], dm[k], NT) for k in range(count)]
        dv = [dot(r.probs[pair * count + k], dm[k]) for k in range(count)]
        ds = []
        for k in range(count):
            wide = r.probs[pair * count + k].astype(F32)
            product = wide * dprobs[k]
            ds.append((product - wide * jnp.sum(product, axis=0, keepdims=True)).astype(BF16))
        dk = [dot(ds[k], halves(q[k])) for k in range(count)]
        dq = [dot(key[k].T, ds[k]) for k in range(count)]
        for k, here in enumerate(spots):
            for part, value in enumerate((own_half(dq[k]) * 0.125, dk[k], dv[k])):
                spot = lanes(pair, part)
                r.dqkv[here, spot] = r.dqkv[here, spot] + value.astype(BF16)
        return carry

    if 7 in r.hooks:
        lax.fori_loop(0, pairs // 2, attend_back, 0)
        hook(7)
        lax.fori_loop(pairs // 2, pairs, attend_back, 0)
    else:
        lax.fori_loop(0, pairs, attend_back, 0)
    hook(8)

    for k in range(3 * width // STEP):
        span = slice(k * STEP, (k + 1) * STEP)
        block = r.dqkv[:, span]
        if not width <= k * STEP < 2 * width:
            at = 3 * width + k * STEP - (width if k * STEP >= width else 0)
            r.small[:, at : at + STEP] = jnp.sum(block.astype(F32), axis=0, keepdims=True)
        slot = (k + 1) % 2
        side_free(slot)
        r.up_stage[slot] = dot(r.n1t[...], block).astype(BF16)
        side_out(9, k, slot)
    if is_router:
        side_free(0)
        side_free(1)
    hook(9)

    r.dn[...] = dot(r.dqkv[...], r.weights[0][...], NT)

    def first_back(here, carry):
        back, dg, db = norm_back(r.x, g1, here)
        dout = r.dout[here, :].astype(F32)
        total = dout + r.between[here, :] + back
        sums = [carry[0] + dg, carry[1] + db]
        if is_router:
            slope = jnp.sum(dout * r.delta[here, :], axis=1, keepdims=True) * r.factor[here, :]
            total = total + slope * r.router[...]
            sums.append(carry[2] + fold(slope * r.x[here, :].astype(F32)))
        r.du[here, :] = total.astype(BF16)
        return tuple(sums)

    sums = row_loop(first_back, (zero,) * (3 if is_router else 2))
    r.small[:, :width] = jnp.sum(sums[0], axis=0, keepdims=True)
    r.small[:, 2 * width : 3 * width] = jnp.sum(sums[1], axis=0, keepdims=True)
    if is_router:
        r.router_grad[...] = jnp.sum(sums[2], axis=0, keepdims=True)
        spread(r.du, r.all_dout, None, r.shown_du)
    else:
        r.shown_copy.wait()
        show(r.du, r.shown_du)
        side_free(0)
        side_free(1)


def front_scratch(rows, width, hidden, groups, window, full, keep_act):
    sizes = [(width, 3 * width), (width, width), (width, hidden), (hidden, width)]
    held = [pltpu.VMEM(size, BF16) for size in sizes]
    held += [pltpu.SemaphoreType.DMA((4,))]
    held += [pltpu.VMEM((rows, width), BF16), pltpu.VMEM((rows, 3 * width), BF16)]
    held += [pltpu.VMEM((HEADS // 2 * len(groups) if full else 1, window, 2 * window), BF16)]
    held += [pltpu.VMEM((len(groups), window, window), F32), pltpu.VMEM((rows, width), BF16)]
    held += [pltpu.VMEM((rows, width), F32), pltpu.VMEM((rows, width), BF16)]
    held += [pltpu.VMEM((rows, hidden) if keep_act else (TILE, LANES), BF16)]
    held += [pltpu.VMEM((rows, STEP), F32)] * (0 if full else 2)
    return held + [pltpu.VMEM((rows, STEP), BF16)] * 2


def back_scratch(rows, width, hidden, scaled):
    held = [pltpu.VMEM((width, rows), BF16)] * 2 + [pltpu.VMEM((rows, width), BF16)] * int(scaled)
    held += [pltpu.VMEM((rows, hidden), BF16), pltpu.VMEM((rows, width), F32)]
    held += [pltpu.VMEM((rows, STEP), BF16)] * 2
    held += [pltpu.VMEM((2, STEP, width), BF16), pltpu.VMEM((2, width, STEP), BF16)]
    return held + [pltpu.SemaphoreType.DMA((2,))] * 2


def run_start(groups, window, lengths, route_mask, tokens, cotangent, router_row, own_vec, own):
    _, rows, width = tokens.shape
    half, hidden = rows // 2, own[2].shape[2]
    inside = pl.BlockSpec(memory_space=pltpu.VMEM)
    anywhere = pl.BlockSpec(memory_space=pl.ANY)
    outs = [(value.shape, BF16) for value in own] + [(own_vec.shape, F32)] * 2
    outs += [((rows, width), BF16)] * 2 + [((half, width), F32), ((rows, width), BF16), ((half, width), BF16)]
    outs += [((half, 1), jnp.int32), ((rows, 1), jnp.int32), ((1, half), jnp.int32), ((1, rows), jnp.int32)]
    outs += [((rows, rows), BF16), ((half, rows), BF16), ((rows, half), BF16), ((rows, 1), F32)]
    outs += [((half, 1), F32)] * 2 + [((1, width), F32)]
    scratch = front_scratch(half, width, hidden, groups, window, False, True)
    scratch += [pltpu.VMEM((half, width), BF16), pltpu.VMEM((rows, width), BF16), pltpu.VMEM((rows, rows), BF16)]
    scratch += [pltpu.VMEM((2, rows, width), BF16), pltpu.VMEM(own_vec.shape, F32), pltpu.SemaphoreType.DMA((2,))]
    scratch += [pltpu.SemaphoreType.DMA((4,))] * 2 + [pltpu.SemaphoreType.DMA((2,))]
    return pl.pallas_call(
        functools.partial(start_kernel, groups, window),
        out_shape=[jax.ShapeDtypeStruct(*one) for one in outs],
        in_specs=[pl.BlockSpec(memory_space=pltpu.SMEM), inside] + [anywhere] * 2 + [inside] * 2 + [anywhere] * 4,
        out_specs=[anywhere] * 4 + [inside] * (len(outs) - 4),
        scratch_shapes=scratch,
        compiler_params=pltpu.CompilerParams(
            collective_id=1, has_side_effects=True, vmem_limit_bytes=60 * 1024 * 1024
        ),
        cost_estimate=pl.CostEstimate(flops=5 * 10**9, bytes_accessed=6 * 10**7, transcendentals=0),
        name="start",
    )(lengths, route_mask, tokens, cotangent, router_row, own_vec, *own)


def run_layer(axis_of, groups, window, x, col_code, row_code, vec, own, far, unsort, back):
    chunks = sum_plan(axis_of)
    reduced = len(REDUCED)
    rows, width = x.shape
    hidden = own[2].shape[2]
    inside = pl.BlockSpec(memory_space=pltpu.VMEM)
    anywhere = pl.BlockSpec(memory_space=pl.ANY)
    args = [x, col_code, row_code, vec, *own, *far, unsort, back]
    outs = [((rows, width), BF16), ((1, vec.shape[1]), F32), ((GRAD_ROWS, LANES), BF16)]
    outs += [((rows, width), BF16)] * 2 + [((GRAD_ROWS, LANES), BF16), ((reduced * GROUP_ROWS, LANES), BF16)]
    scratch = front_scratch(rows, width, hidden, groups, window, True, True)
    scratch += back_scratch(rows, width, hidden, False) + [pltpu.SemaphoreType.DMA((1,))]
    scratch += Sums.scratch(chunks, reduced, 0)
    flops = rows * width * (3 * width + width + 2 * hidden) * 6
    return pl.pallas_call(
        functools.partial(layer_kernel, groups, window, chunks),
        out_shape=[jax.ShapeDtypeStruct(*one) for one in outs],
        in_specs=[inside] * 4 + [anywhere] * 8 + [inside] * 2,
        out_specs=[inside] * 2 + [anywhere] + [inside] + [anywhere] * 3,
        scratch_shapes=scratch,
        compiler_params=pltpu.CompilerParams(
            collective_id=2, has_side_effects=True, vmem_limit_bytes=64 * 1024 * 1024
        ),
        cost_estimate=pl.CostEstimate(flops=flops, bytes_accessed=3 * 10**7, transcendentals=0),
        name="layer",
    )(*args)


def run_fused(axis_of, groups, window, x, col_code, row_code, vec, scale, own, far, rows_of, back, router, second, extra, shown):
    rows, width = x.shape
    hidden = own[2].shape[2]
    chunks = sum_plan(axis_of)
    inside = pl.BlockSpec(memory_space=pltpu.VMEM)
    anywhere = pl.BlockSpec(memory_space=pl.ANY)
    unsort, pick, unpick, skipped = rows_of
    delta, factor, router_row = router
    every = unsort.shape[0]
    args = [x, col_code, row_code, vec, scale, *own, *far, unsort]
    args += [back, pick, unpick, skipped, delta, factor, router_row]
    args += [*second, extra, *shown]
    small_rows = -(-(vec.shape[1] // LANES + 2) // 8) * 8
    outs = [((GRAD_ROWS, LANES), BF16)] * 4
    outs += [((small_rows, LANES), F32)] + [((2, every, width), BF16)] * 2
    scratch = front_scratch(rows, width, hidden, groups, window, True, False)
    scratch += back_scratch(rows, width, hidden, True)
    scratch += [pltpu.VMEM((rows, width), BF16)] * 2 + [pltpu.VMEM((every, width), BF16)]
    scratch += [pltpu.VMEM((1, vec.shape[1]), F32), pltpu.VMEM((1, width), F32)]
    scratch += Sums.scratch(chunks, GROUPS, small_rows)
    *sums, _, _, small, acts, grads = pl.pallas_call(
        functools.partial(fused_kernel, groups, window, chunks),
        out_shape=[jax.ShapeDtypeStruct(*one) for one in outs],
        in_specs=[inside] * 5 + [anywhere] * 8 + [inside] * 8 + [anywhere] * 3 + [inside] * 2 + [anywhere] * 3,
        out_specs=[anywhere] * 4 + [inside] + [anywhere] * 2,
        scratch_shapes=scratch,
        compiler_params=pltpu.CompilerParams(
            collective_id=0, has_side_effects=True, vmem_limit_bytes=64 * 1024 * 1024
        ),
        cost_estimate=pl.CostEstimate(flops=10**10, bytes_accessed=6 * 10**8, transcendentals=0),
        name="fused",
    )(*args)
    return sums, small, (acts, grads)


def body(axis_of, tokens, lengths, route_mask, router_weight, gains, biases, w_qkv, w_out, w_up, w_down, cotangent):
    micro, rows, width = tokens.shape
    own = (w_qkv, w_out, w_up, w_down)
    own_vec = jnp.concatenate([gains, biases], axis=1)
    router_row = router_weight.astype(F32)[None, :]
    half = LONG // 2
    groups_one = ((0, 0, half), (96, half, 2 * half), (192, 2 * half, rows // 2))
    groups_two = ((0, 0, LONG), (192, LONG, 2 * LONG), (384, 2 * LONG, rows))
    made = run_start(groups_one, 128, lengths, route_mask, tokens, cotangent, router_row, own_vec, own)
    far, (vec_one, vec_two), (y1, shown_y1, delta_one, cot, routed) = made[:4], made[4:6], made[6:11]
    col_one, col_two, row_one, row_two, *others = made[11:]
    unsort, pick, unpick, skipped, scale, factor, extra = others
    shown_du2, small_two, grads_two, dout, shown_y2, landed_two, carry = run_layer(
        axis_of, groups_two, 256, y1, col_two, row_two, vec_two, own, far, unsort, cot
    )
    sums, small, (activations, input_grads) = run_fused(
        axis_of, groups_one, 128, routed, col_one, row_one, vec_one, scale, own, far,
        (unsort, pick, unpick, skipped), dout, (delta_one, factor, router_row),
        (grads_two, landed_two, carry, small_two), extra,
        (shown_y1, shown_y2, shown_du2),
    )
    *grads, router_grad, means, activations, input_grads = cast_sums(
        sums, small, activations, input_grads,
        [value.shape for value in (*own, gains, biases)], micro,
    )
    return (activations, input_grads, *grads, router_grad[0], means[0])


def solution(mesh):
    in_specs = (
        P(None, "dp", None),
        P(None, "dp", None),
        P(None, "dp"),
        P(),
        P("section", None),
        P("section", None),
        P("section", None, None),
        P("section", None, None),
        P("section", None, None),
        P("section", None, None),
        P(None, "dp", None),
    )
    out_specs = (
        P("section", None, "dp", None),
        P("section", None, "dp", None),
        P("section", None, None),
        P("section", None, None),
        P("section", None, None),
        P("section", None, None),
        P("section", None),
        P("section", None),
        P(),
        P(),
    )
    step = functools.partial(body, axis_bits(mesh))
    return jax.shard_map(step, mesh=mesh, in_specs=in_specs, out_specs=out_specs, check_vma=False)
```
